32 devices in a mesh: dp: 4 (over z), rep: 2 (over x), sub: 4 (over y, core).
Axes of the slice: x: 2, y: 2, z: 4, core: 2. Of those that a mesh axis runs over, the one named last changes fastest.
Arguments:
- byte_ids: int32 [8192], P(('dp', 'rep', 'sub')), may hold values from 0 to 255
- hash_ids: int32 [8192, 6], P(('dp', 'rep', 'sub')), may hold values from 0 to 62527, as said below
- lengths: int32 [32, 64], P(('dp', 'rep', 'sub')), may hold values from 1 to 64, 256 in all within a row
- byte_table: bfloat16 [256, 1024], replicated, may hold values from -2.390625 to 2.390625
- hash_table: bfloat16 [62528, 1024], P(('dp', 'rep', 'sub')), may hold values from -2.390625 to 2.390625
- norm_attn: float32 [1024], replicated, may hold values from 0.1 to 1.9
- norm_ffn: float32 [1024], replicated, may hold values from 0.1 to 1.9
- norm_cross: float32 [1024], replicated, may hold values from 0.1 to 1.9
- w_query: bfloat16 [1024, 1024], P('dp'), may hold values from -0.1875 to 0.1875
- w_key: bfloat16 [1024, 1024], P('dp'), may hold values from -0.1875 to 0.1875
- w_value: bfloat16 [1024, 1024], P('dp'), may hold values from -0.1875 to 0.1875
- w_out: bfloat16 [1024, 1024], P('dp'), may hold values from -1 to 1
- w_gate: bfloat16 [1024, 2816], P('dp'), may hold values from -0.1875 to 0.1875
- w_up: bfloat16 [1024, 2816], P('dp'), may hold values from -0.1875 to 0.1875
- w_down: bfloat16 [2816, 1024], P('dp'), may hold values from -0.109375 to 0.109375
- c_query: bfloat16 [1024, 1024], P('dp'), may hold values from -0.1875 to 0.1875
- c_key: bfloat16 [1024, 1024], P('dp'), may hold values from -0.1875 to 0.1875
- c_value: bfloat16 [1024, 1024], P('dp'), may hold values from -0.1875 to 0.1875
- c_out: bfloat16 [1024, 1024], P('dp'), may hold values from -0.375 to 0.375
- cot_bytes: bfloat16 [8192, 1024], P(('dp', 'rep', 'sub')), may hold values from -6 to 6
- cot_patches: bfloat16 [2048, 1024], P(('dp', 'rep', 'sub')), may hold values from -6 to 6
Outputs:
- byte_states: bfloat16 [8192, 1024], P(('dp', 'rep', 'sub'))
- patch_states: bfloat16 [2048, 1024], P(('dp', 'rep', 'sub'))
- embed_grad: bfloat16 [8192, 1024], P(('dp', 'rep', 'sub'))
- byte_table_grad: float32 [256, 1024], P(('dp', 'rep', 'sub'))
- hash_table_grad: float32 [62528, 1024], P(('dp', 'rep', 'sub'))
- row_counts: int32 [62528], P(('dp', 'rep', 'sub'))
- norm_attn_grad: float32 [1024], P(('dp', 'rep', 'sub'))
- norm_ffn_grad: float32 [1024], P(('dp', 'rep', 'sub'))
- norm_cross_grad: float32 [1024], P(('dp', 'rep', 'sub'))
- w_query_grad: float32 [1024, 1024], P(('dp', 'rep', 'sub'))
- w_key_grad: float32 [1024, 1024], P(('dp', 'rep', 'sub'))
- w_value_grad: float32 [1024, 1024], P(('dp', 'rep', 'sub'))
- w_out_grad: float32 [1024, 1024], P(('dp', 'rep', 'sub'))
- w_gate_grad: float32 [1024, 2816], P(('dp', 'rep', 'sub'))
- w_up_grad: float32 [1024, 2816], P(('dp', 'rep', 'sub'))
- w_down_grad: float32 [2816, 1024], P(('dp', 'rep', 'sub'))
- c_query_grad: float32 [1024, 1024], P(('dp', 'rep', 'sub'))
- c_key_grad: float32 [1024, 1024], P(('dp', 'rep', 'sub'))
- c_value_grad: float32 [1024, 1024], P(('dp', 'rep', 'sub'))
- c_out_grad: float32 [1024, 1024], P(('dp', 'rep', 'sub'))
The draws below stay inside these ranges and needn't reach their ends.
Inputs may be any that keep to these rules, and one draw needn't show every extreme that they name: `hash_ids`: of the 1536 ids of one device's bytes, at most 96 fall in the 1954 rows held by any one device (rows d * 1954 onward for device d in the order dp, rep, sub), and in every draw some device's rows receive exactly 96 from every device. Row b holds the lengths of the 64 patches of bytes b * 256 to (b + 1) * 256 - 1, in order; each row sums to 256 and its largest is 64.
All inputs are finite; a program needn't handle non-finite values.
Results may differ from the reference program's by a relative error of at most 0.02.
Values may be sent and summed in bfloat16 or wider, within the bound.
A program may use at most 384 MiB of HBM per device.

```python
import math
from functools import partial
import jax
import jax.numpy as jnp
import numpy as np
from jax import lax

D = 1024
HEADS = 16
HD = 64
FF = 2816
WIN = 512
NGRAM = 6
MAXP = 64
BYTE_VALUES = 256
ROWS_DEV = 1954
TOK_DEV = 256
PDEV = 64
SEQ = 2048
TOKENS = 8192
PATCHES = 2048
HASH_ROWS = 62528
N_DP = 4
N_REP = 2
N_SUB = 4
DEVICES = 32


def draw_hash_ids(key, part):
    key = jax.random.fold_in(key, 7)
    request_count = TOK_DEV * NGRAM
    mean_load = request_count // DEVICES
    half_count = DEVICES // 2
    key_pair, key_swing, key_order, key_row = jax.random.split(key, 4)
    pairing = jax.random.permutation(key_pair, DEVICES)
    swing = jax.random.randint(key_swing, (DEVICES, half_count), 0, mean_load + 1)
    swing = swing.at[:, 0].set(mean_load)
    loads = jnp.zeros((DEVICES, DEVICES), jnp.int32)
    loads = loads.at[:, pairing[:half_count]].set(mean_load + swing)
    loads = loads.at[:, pairing[half_count:]].set(mean_load - swing)
    bounds = jnp.cumsum(loads, axis=1)
    slot_index = jnp.arange(request_count, dtype=jnp.int32)
    owners = jax.vmap(partial(jnp.searchsorted, v=slot_index, side='right'))(bounds).astype(jnp.int32)
    order_keys = jax.random.split(key_order, DEVICES)
    shuffles = jax.vmap(partial(jax.random.permutation, x=request_count))(order_keys)
    owners = jnp.take_along_axis(owners, shuffles, axis=1)
    within = jax.random.randint(key_row, (DEVICES, request_count), 0, ROWS_DEV)
    return (owners * ROWS_DEV + within).reshape(TOKENS, NGRAM).astype(jnp.int32)


def touch_ends(result, rng, least, high):
    index_at = [jax.random.randint(jax.random.fold_in(rng, axis), (), 0, length) for axis, length in enumerate(result.shape)]
    widest = result.shape.index(max(result.shape))
    neighbour = index_at[:widest] + [(index_at[widest] + 1) % result.shape[widest]] + index_at[widest + 1:]
    return result.at[tuple(index_at)].set(least).at[tuple(neighbour)].set(high)


def shard_levels(own_key, extent, cuts, smallest, largest):
    level = 1.0
    for position, shards_of in cuts:
        steps = jax.random.uniform(jax.random.fold_in(jax.random.fold_in(own_key, 6), position), (shards_of,), jnp.float32, smallest / len(cuts), largest / len(cuts))
        level = level * jnp.repeat(jnp.exp(steps), extent[position] // shards_of).reshape((-1,) + (1,) * (len(extent) - 1 - position))
    return level


def profile(number_of, total, bound, skew):
    weights = [(1 << 20) // math.isqrt(standing ** skew) + 1 for standing in range(2, number_of + 1)]
    rest, given = total - bound - (number_of - 1), [1] * (number_of - 1)
    while rest > 0:
        candidates = [i for i in range(number_of - 1) if given[i] < bound]
        pool, remaining = sum([weights[i] for i in candidates]), rest
        for i in candidates:
            more = min(bound - given[i], max(1, remaining * weights[i] // pool), rest)
            given[i] = given[i] + more
            rest = rest - more
    return np.array([bound] + given)


def ragged_sizes(rng, count, total, reach, skew):
    if count == 2:
        one = jax.random.randint(rng, (), max(1, total - reach), min(reach, total - 1) + 1)
        return jnp.stack([one, total - one])
    sizes = jnp.asarray(profile(count, total, reach, skew), jnp.int32)
    pairs = (count - 1) // 2
    source_of, sink = sizes[1:1 + 2 * pairs:2], sizes[2:2 + 2 * pairs:2]
    room = jnp.minimum(source_of - 1, reach - sink)
    moved = jax.random.randint(jax.random.fold_in(rng, 1), (pairs,), 0, 1 << 20) % (room + 1)
    sizes = sizes.at[1:1 + 2 * pairs:2].set(source_of - moved).at[2:2 + 2 * pairs:2].set(sink + moved)
    return sizes[jax.random.permutation(jax.random.fold_in(rng, 2), count)]


def gaussian(rng, dims, scale, most, cuts=(), kind=jnp.bfloat16):
    array = jax.random.normal(rng, dims, jnp.float32) * scale
    if len(cuts) > 0:
        array = shard_levels(rng, dims, cuts, -0.22, 0.18) * array
    return jnp.clip(array, min=-most, max=most).astype(kind)


def setup_inputs(seed: int = 0) -> dict:
    keys = jax.random.split(jax.random.key(seed), 22)
    return {
        "byte_ids": touch_ends(jax.random.randint(keys[0], (TOKENS,), 0, BYTE_VALUES), jax.random.fold_in(keys[0], 1), 0, BYTE_VALUES - 1).astype(jnp.int32),
        "hash_ids": draw_hash_ids(jax.random.fold_in(keys[21], 71), 0),
        "lengths": jax.vmap(lambda own: ragged_sizes(own, PDEV, TOK_DEV, MAXP, 2))(jax.random.split(keys[2], DEVICES)).reshape((DEVICES, PDEV)).astype(jnp.int32),
        "byte_table": gaussian(keys[3], (BYTE_VALUES, D), 0.4, 2.390625),
        "hash_table": gaussian(keys[4], (HASH_ROWS, D), 0.4, 2.390625, ((0, 32),)),
        "norm_attn": jnp.clip(1.0 + 0.18 * jax.random.normal(keys[5], (D,), jnp.float32), 0.1, 1.9),
        "norm_ffn": jnp.clip(1.0 + 0.18 * jax.random.normal(keys[6], (D,), jnp.float32), 0.1, 1.9),
        "norm_cross": jnp.clip(1.0 + 0.18 * jax.random.normal(keys[7], (D,), jnp.float32), 0.1, 1.9),
        "w_query": gaussian(keys[8], (D, D), D ** -0.5, 0.1875, ((0, 4),)),
        "w_key": gaussian(keys[9], (D, D), D ** -0.5, 0.1875, ((0, 4),)),
        "w_value": gaussian(keys[10], (D, D), D ** -0.5, 0.1875, ((0, 4),)),
        "w_out": gaussian(keys[11], (D, D), (D // 32) ** -0.5, 1.0, ((0, 4),)),
        "w_gate": gaussian(keys[12], (D, FF), D ** -0.5, 0.1875, ((0, 4),)),
        "w_up": gaussian(keys[13], (D, FF), D ** -0.5, 0.1875, ((0, 4),)),
        "w_down": gaussian(keys[14], (FF, D), FF ** -0.5, 0.109375, ((0, 4),)),
        "c_query": gaussian(keys[15], (D, D), D ** -0.5, 0.1875, ((0, 4),)),
        "c_key": gaussian(keys[16], (D, D), D ** -0.5, 0.1875, ((0, 4),)),
        "c_value": gaussian(keys[17], (D, D), D ** -0.5, 0.1875, ((0, 4),)),
        "c_out": gaussian(keys[18], (D, D), (D // 4) ** -0.5, 0.375, ((0, 4),)),
        "cot_bytes": gaussian(keys[19], (TOKENS, D), 1.0, 6.0, ((0, 32),)),
        "cot_patches": gaussian(keys[20], (PATCHES, D), 1.0, 6.0, ((0, 32),)),
    }


PRECISE = lax.Precision.HIGHEST
NEG_BIG = -1e+30
EPSILON = 1e-06
SCORE_SCALE = 0.125

@jax.custom_vjp
def low(v):
    return lax.optimization_barrier(v.astype(jnp.bfloat16)).astype(jnp.float32)

@jax.custom_vjp
def low_back(v):
    return v

def low_keep(v):
    return (low(v), None)

def low_pass(kept, grad):
    return (grad,)

def back_keep(v):
    return (v, None)

def back_low(kept, grad):
    return (low(grad),)
low.defvjp(low_keep, low_pass)
low_back.defvjp(back_keep, back_low)

def both_round(values):
    return low(low_back(values))

def matmul(matrix_a, matrix_b):
    return jnp.dot(matrix_a, matrix_b, precision=PRECISE)

def normalize(values, gains):
    return values * lax.rsqrt(lax.optimization_barrier(jnp.mean(values * values, axis=-1, keepdims=True)) + EPSILON) * gains

def window_block(start, queries, keys_pad, values_pad, q_rows, key_span):
    query_part = lax.dynamic_slice_in_dim(queries, start, q_rows, 0)
    key_part = lax.dynamic_slice_in_dim(keys_pad, start, q_rows + key_span, 0)
    value_part = lax.dynamic_slice_in_dim(values_pad, start, q_rows + key_span, 0)
    scores = low_back(jnp.einsum('qhd,khd->hqk', query_part, key_part, precision=PRECISE) * SCORE_SCALE)
    query_pos = start + jnp.arange(q_rows, dtype=jnp.int32)
    key_pos = start - key_span + jnp.arange(q_rows + key_span, dtype=jnp.int32)
    allowed = (key_pos[None, :] <= query_pos[:, None]) & (key_pos[None, :] > query_pos[:, None] - WIN) & (key_pos[None, :] >= 0)
    scores = jnp.where(allowed[None], scores, NEG_BIG)
    probs_low = low(jax.nn.softmax(scores, axis=-1))
    return jnp.einsum('hqk,khd->qhd', probs_low, value_part, precision=PRECISE)

def cross_block(pair, weights):
    x_block, patch_len = pair
    cq_weight, ck_weight, cv_weight, co_weight = weights
    patch_end = jnp.cumsum(patch_len)
    patch_start = patch_end - patch_len
    byte_pos = jnp.arange(TOK_DEV, dtype=jnp.int32)
    member = (byte_pos[None, :] >= patch_start[:, None]) & (byte_pos[None, :] < patch_end[:, None])
    pooled = matmul(member.astype(jnp.float32), x_block) / patch_len.astype(jnp.float32)[:, None]
    p_query = both_round(matmul(both_round(pooled), cq_weight)).reshape(PDEV, HEADS, HD)
    p_key = both_round(matmul(x_block, ck_weight)).reshape(TOK_DEV, HEADS, HD)
    p_value = both_round(matmul(x_block, cv_weight)).reshape(TOK_DEV, HEADS, HD)
    scores = low_back(jnp.einsum('phd,thd->hpt', p_query, p_key, precision=PRECISE) * SCORE_SCALE)
    scores = jnp.where(member[None], scores, NEG_BIG)
    probs_low = low(jax.nn.softmax(scores, axis=-1))
    attended = both_round(jnp.einsum('hpt,thd->phd', probs_low, p_value, precision=PRECISE).reshape(PDEV, D))
    return pooled + low_back(matmul(attended, co_weight))

def sequence_layer(pair, params):
    embedded, seq_lengths = pair
    norm_attn, norm_ffn, norm_cross, w_query, w_key, w_value, w_out, w_gate, w_up, w_down, c_query, c_key, c_value, c_out = params
    x_attn = both_round(normalize(embedded, norm_attn))
    queries = both_round(matmul(x_attn, w_query)).reshape(SEQ, HEADS, HD)
    key_rows = both_round(matmul(x_attn, w_key)).reshape(SEQ, HEADS, HD)
    value_rows = both_round(matmul(x_attn, w_value)).reshape(SEQ, HEADS, HD)
    q_rows = min(TOK_DEV, 512)
    key_span = (WIN - 1 + q_rows - 1) // q_rows * q_rows
    padding = jnp.zeros((key_span, HEADS, HD), jnp.float32)
    keys_pad = jnp.concatenate([padding, key_rows], axis=0)
    values_pad = jnp.concatenate([padding, value_rows], axis=0)
    starts = jnp.arange(SEQ // q_rows, dtype=jnp.int32) * q_rows
    attend = jax.checkpoint(partial(window_block, queries=queries, keys_pad=keys_pad, values_pad=values_pad, q_rows=q_rows, key_span=key_span))
    attended = both_round(lax.map(attend, starts).reshape(SEQ, D))
    h_mid = embedded + low_back(matmul(attended, w_out))
    x_ffn = both_round(normalize(h_mid, norm_ffn))
    gate_pre = low_back(matmul(x_ffn, w_gate))
    up_pre = low_back(matmul(x_ffn, w_up))
    hidden = both_round(jax.nn.silu(gate_pre) * up_pre)
    h_out = h_mid + low_back(matmul(hidden, w_down))
    x_cross = both_round(normalize(h_out, norm_cross))
    cross = jax.checkpoint(partial(cross_block, weights=(c_query, c_key, c_value, c_out)))
    patch_out = lax.map(cross, (x_cross.reshape(N_REP * N_SUB, TOK_DEV, D), seq_lengths))
    return (h_out, patch_out.reshape(N_REP * N_SUB * PDEV, D))

def reference(byte_ids, hash_ids, lengths, byte_table, hash_table, norm_attn, norm_ffn, norm_cross, w_query, w_key, w_value, w_out, w_gate, w_up, w_down, c_query, c_key, c_value, c_out, cot_bytes, cot_patches):
    params = tuple((tensor.astype(jnp.float32) for tensor in (norm_attn, norm_ffn, norm_cross, w_query, w_key, w_value, w_out, w_gate, w_up, w_down, c_query, c_key, c_value, c_out)))

    def embed(table_bytes, table_hash):
        summed = table_bytes[byte_ids]
        for gram_index in range(NGRAM):
            summed = summed + table_hash[hash_ids[:, gram_index]]
        return summed
    embedded, embed_back = jax.vjp(embed, byte_table.astype(jnp.float32), hash_table.astype(jnp.float32))

    def whole_layer(inputs, weights):
        layer_fn = jax.checkpoint(partial(sequence_layer, params=weights))
        states, patches = lax.map(layer_fn, (inputs.reshape(N_DP, SEQ, D), lengths.reshape(N_DP, N_REP * N_SUB, PDEV)))
        return (states.reshape(TOKENS, D), patches.reshape(PATCHES, D))
    (states, patches), layer_back = jax.vjp(whole_layer, embedded, params)
    grad_embed, grad_params = layer_back((cot_bytes.astype(jnp.float32), cot_patches.astype(jnp.float32)))
    grad_bytes, grad_hash = embed_back(grad_embed)
    row_counts = jnp.zeros((HASH_ROWS,), jnp.int32).at[hash_ids.reshape(-1)].add(jnp.ones((TOKENS * NGRAM,), jnp.int32))
    grad_norm_attn, grad_norm_ffn, grad_norm_cross, grad_query, grad_key, grad_value, grad_out, grad_gate, grad_up, grad_down, grad_cquery, grad_ckey, grad_cvalue, grad_cout = grad_params
    return (states.astype(jnp.bfloat16), patches.astype(jnp.bfloat16), grad_embed.astype(jnp.bfloat16), grad_bytes, grad_hash, row_counts, grad_norm_attn, grad_norm_ffn, grad_norm_cross, grad_query, grad_key, grad_value, grad_out, grad_gate, grad_up, grad_down, grad_cquery, grad_ckey, grad_cvalue, grad_cout)
```

```python
import functools

import jax
import jax.numpy as jnp
from jax import lax
from jax.experimental import pallas as pl
from jax.experimental.pallas import tpu as pltpu
from jax.sharding import PartitionSpec as P

HD = 64
WIN = 512
BYTE_VALUES = 256


PRECISE = lax.Precision.HIGHEST
NEG_BIG = -1e30
EPSILON = 1e-06
SCORE_SCALE = 0.125


def passed_along(x, axis, by):
    devices = lax.axis_size(axis)
    pairs = [(i, i + by) for i in range(devices) if 0 <= i + by < devices]
    return lax.ppermute(x, axis, pairs)


def matmul(matrix_a, matrix_b):
    return jnp.dot(matrix_a, matrix_b, preferred_element_type=jnp.float32)


def times_t(matrix_a, matrix_b):
    return lax.dot_general(
        matrix_a, matrix_b, (((1,), (1,)), ((), ())), preferred_element_type=jnp.float32
    )


def t_times(matrix_a, matrix_b):
    return lax.dot_general(
        matrix_a, matrix_b, (((0,), (0,)), ((), ())), preferred_element_type=jnp.float32
    )


def normalize(values, gains):
    inv_rms = lax.rsqrt(jnp.mean(values * values, axis=-1, keepdims=True) + EPSILON)
    normed = values * inv_rms
    return ((normed * gains).astype(jnp.bfloat16), normed, inv_rms)


def norm_back(grad_out, normed, inv_rms, gains):
    grad_gain = jnp.sum(grad_out * normed, axis=0)
    scaled_grad = grad_out * gains
    grad_in = inv_rms * (
        scaled_grad - normed * jnp.mean(scaled_grad * normed, axis=-1, keepdims=True)
    )
    return (grad_in, grad_gain)


def soft_forward(scores, allowed):
    masked = jnp.where(allowed, scores, NEG_BIG)
    row_max = jnp.max(masked, axis=-1, keepdims=True)
    exps = jnp.exp(masked - row_max)
    row_sum = jnp.sum(exps, axis=-1, keepdims=True)
    return (exps / row_sum, row_max + jnp.log(row_sum))


def soft_again(scores, allowed, log_total):
    return jnp.where(allowed, jnp.exp(scores - log_total), 0.0)


def soft_back(probs_full, grad_probs):
    row_total = jnp.sum(probs_full * grad_probs, axis=-1, keepdims=True)
    return (probs_full * (grad_probs - row_total)).astype(jnp.bfloat16)


def window_mask(first_query, first_key, row_count, col_count):
    query_pos = first_query + jnp.arange(row_count, dtype=jnp.int32)
    key_pos = first_key + jnp.arange(col_count, dtype=jnp.int32)
    near = (
        (key_pos[None, :] <= query_pos[:, None])
        & (key_pos[None, :] > query_pos[:, None] - WIN)
        & (key_pos[None, :] >= 0)
    )
    return near[None]


MESH_ID = pl.DeviceIdType.MESH
SLOTS = 96
VMEM_CAP = 60 * 1024 * 1024


class Place:
    def __init__(self, dp_count):
        self.n = dp_count
        self.z = lax.axis_index("dp")
        self.x = lax.axis_index("rep")
        sub = lax.axis_index("sub")
        self.y = sub // 2
        self.c = sub % 2
        self.started = []

    def at(self, dz=0, dx=0, dy=0, dc=0):
        z = lax.rem(self.z + dz, self.n) if dz else self.z
        x = 1 - self.x if dx else self.x
        y = 1 - self.y if dy else self.y
        c = 1 - self.c if dc else self.c
        return (z, x, y * 2 + c)

    def greet(self):
        barrier = pltpu.get_barrier_semaphore()
        peers = [self.at(dx=1), self.at(dy=1), self.at(dc=1)]
        peers += [self.at(dz=j) for j in range(1, self.n)]
        for peer in peers:
            pl.semaphore_signal(barrier, inc=1, device_id=peer, device_id_type=MESH_ID)
        pl.semaphore_wait(barrier, len(peers))

    def send(self, src, dst, send_sem, recv_sem, peer):
        copy = pltpu.make_async_remote_copy(
            src_ref=src,
            dst_ref=dst,
            send_sem=send_sem,
            recv_sem=recv_sem,
            device_id=peer,
            device_id_type=MESH_ID,
        )
        copy.start()
        self.started.append(copy)
        return copy

    def expect(self, dst, recv_sem):
        pltpu.make_async_remote_copy(
            src_ref=dst,
            dst_ref=dst,
            send_sem=recv_sem,
            recv_sem=recv_sem,
            device_id=self.at(dc=1),
            device_id_type=MESH_ID,
        ).wait_recv()

    def sent(self, copy):
        copy.wait_send()
        self.started = [other for other in self.started if other is not copy]

    def finish(self):
        for copy in self.started:
            copy.wait_send()
        self.started = []


def add_into(dst, src, blocks, width):
    def step(i, carry):
        total = dst(i)[...].astype(jnp.float32) + src(i)[...].astype(jnp.float32)
        dst(i)[...] = total.astype(jnp.bfloat16)
        return carry

    lax.fori_loop(0, blocks, step, 0)


class Reduction:
    def __init__(self, here, p0, r1a, r1b, r2a, r2b, sems, index):
        self.here, self.p0 = here, p0
        self.r1a, self.r1b, self.r2a, self.r2b = r1a, r1b, r2a, r2b
        self.sems, self.i = sems, index
        self.planes, _, _, self.rows, cols = p0.shape
        self.half = cols // 2
        self.left = pl.ds(0, self.half)
        self.right = pl.ds(self.half, self.half)

    def sem(self, k):
        return self.sems.at[self.i, k, 0], self.sems.at[self.i, k, 1]

    def first(self):
        h = self.here
        self.s1a = h.send(
            self.p0.at[:, 1 - h.x, :, :, self.left], self.r1a, *self.sem(0), h.at(dx=1)
        )
        self.s1b = h.send(
            self.p0.at[:, :, 1 - h.y, :, self.right], self.r1b, *self.sem(1), h.at(dy=1)
        )

    def second(self):
        h = self.here
        self.s1a.wait_recv()
        add_into(
            lambda i: self.p0.at[i // 2, h.x, i % 2, :, self.left],
            lambda i: self.r1a.at[i // 2, i % 2],
            2 * self.planes,
            self.half,
        )
        self.s2a = h.send(
            self.p0.at[:, h.x, 1 - h.y, :, self.left], self.r2a, *self.sem(2), h.at(dy=1)
        )
        self.s1b.wait_recv()
        add_into(
            lambda i: self.p0.at[i // 2, i % 2, h.y, :, self.right],
            lambda i: self.r1b.at[i // 2, i % 2],
            2 * self.planes,
            self.half,
        )
        self.s2b = h.send(
            self.p0.at[:, 1 - h.x, h.y, :, self.right], self.r2b, *self.sem(3), h.at(dx=1)
        )

    def third(self):
        h = self.here
        self.s2a.wait_recv()
        add_into(
            lambda i: self.p0.at[i, h.x, h.y, :, self.left],
            lambda i: self.r2a.at[i],
            self.planes,
            self.half,
        )
        self.s2b.wait_recv()
        add_into(
            lambda i: self.p0.at[i, h.x, h.y, :, self.right],
            lambda i: self.r2b.at[i],
            self.planes,
            self.half,
        )
        return self.p0.at[:, h.x, h.y]


def fetch_kernel(dp_count, weight_count, gram_tokens, *refs):
    shards = refs[:weight_count]
    lists, table = refs[weight_count : weight_count + 2]
    fulls = refs[weight_count + 2 : 2 * weight_count + 2]
    (
        summed,
        send0,
        p0,
        r1a,
        r1b,
        r2a,
        r2b,
        r3,
        g_rows,
        core_sems,
        stage_sems,
        z_sems,
        local_sems,
        w_send,
        w_recv,
    ) = refs[2 * weight_count + 2 :]
    here = Place(dp_count)
    n = dp_count
    z, x, y, c = here.z, here.x, here.y, here.c
    tokens = gram_tokens

    class Weight:
        def __init__(self, i):
            self.i = i
            self.shard, self.full = shards[i], fulls[i]
            self.kind = i % 2
            rows, cols = self.shard.shape
            self.by_cols = rows % 128 != 0
            self.step = (cols if self.by_cols else rows) // 8
            near, far = (x, y) if self.kind == 0 else (y, x)
            self.q = (c * 2 + far) * 2 + near

        def cut(self, ref, start, count):
            span = pl.ds(start * self.step, count * self.step)
            if self.by_cols:
                return ref.at[:, span]
            return ref.at[span, :]

        def local(self):
            self.copy = pltpu.make_async_copy(
                self.shard, self.full.at[z], local_sems.at[self.i]
            )
            self.copy.start()

        def stage(self, k, j, start, count, src_ref, plane, peer):
            here.send(
                self.cut(src_ref, start, count),
                self.cut(self.full.at[plane], start, count),
                w_send.at[self.i, k, j - 1],
                w_recv.at[self.i, k, j - 1],
                peer,
            )

        def came(self, k, j, start, count):
            plane = lax.rem(z + n - j, n)
            here.expect(
                self.cut(self.full.at[plane], start, count), w_recv.at[self.i, k, j - 1]
            )
            return plane

        def along_z(self):
            for j in range(1, n):
                self.stage(0, j, self.q, 1, self.shard, z, here.at(dz=j))

        def near(self):
            for j in range(1, n):
                plane = self.came(0, j, self.q, 1)
                peer = here.at(dx=1) if self.kind == 0 else here.at(dy=1)
                self.stage(1, j, self.q, 1, self.full.at[plane], plane, peer)

        def far(self):
            other = self.q + 1 - 2 * (self.q % 2)
            for j in range(1, n):
                plane = self.came(1, j, other, 1)
                peer = here.at(dy=1) if self.kind == 0 else here.at(dx=1)
                self.stage(2, j, self.q // 2 * 2, 2, self.full.at[plane], plane, peer)

        def across(self):
            pair = self.q // 2
            other = pair + 1 - 2 * (pair % 2)
            for j in range(1, n):
                plane = self.came(2, j, other * 2, 2)
                self.stage(3, j, c * 4, 4, self.full.at[plane], plane, here.at(dc=1))

        def done(self):
            for j in range(1, n):
                self.came(3, j, (1 - c) * 4, 4)
            self.copy.wait()

    weights = [Weight(i) for i in range(weight_count)]

    row_iota = lax.broadcasted_iota(jnp.int32, (SLOTS, table.shape[0]), 1)
    byte_iota = lax.broadcasted_iota(jnp.int32, (SLOTS, tokens), 1)

    def partial_sums(plane, core, write):
        for place in range(4):
            source = plane * 8 + place * 2 + core
            entry = lists[source]
            pick = (jnp.right_shift(entry, 8) == row_iota).astype(jnp.bfloat16)
            g_rows[place * SLOTS : (place + 1) * SLOTS, :] = matmul(pick, table[...]).astype(
                jnp.bfloat16
            )
        for place in range(4):
            source = plane * 8 + place * 2 + core
            entry = lists[source]
            to_byte = (jnp.bitwise_and(entry, 255) == byte_iota).astype(jnp.bfloat16)
            sums = t_times(to_byte, g_rows[place * SLOTS : (place + 1) * SLOTS, :])
            write(place, sums)

    units = []
    for u in range(n):
        units.append(
            Reduction(
                here,
                p0.at[pl.ds(u, 1)],
                r1a.at[pl.ds(u, 1)],
                r1b.at[pl.ds(u, 1)],
                r2a.at[pl.ds(u, 1)],
                r2b.at[pl.ds(u, 1)],
                stage_sems,
                u,
            )
        )
    core_copies = [None] * n
    z_copies = [None] * n

    def plane_of(u):
        return lax.rem(z + u + 1, n)

    def hash_a(u):
        slot = u % 2
        if u >= 2:
            here.sent(core_copies[u - 2])

        def write(place, sums):
            send0[slot, place // 2, place % 2] = sums.astype(jnp.bfloat16)

        partial_sums(plane_of(u), 1 - c, write)
        core_copies[u] = here.send(
            send0.at[slot], p0.at[u], core_sems.at[u, 0], core_sems.at[u, 1], here.at(dc=1)
        )

    def hash_b(u):
        core_copies[u].wait_recv()

        def write(place, sums):
            total = sums + p0[u, place // 2, place % 2].astype(jnp.float32)
            p0[u, place // 2, place % 2] = total.astype(jnp.bfloat16)

        partial_sums(plane_of(u), c, write)
        units[u].first()

    def hash_c(u):
        units[u].second()

    def hash_d(u):
        mine = units[u].third()
        if u < n - 1:
            z_copies[u] = here.send(
                mine.at[0], r3.at[u], z_sems.at[u, 0], z_sems.at[u, 1], here.at(dz=u + 1)
            )

    def hash_e():
        for u in range(n - 1):
            z_copies[u].wait_recv()
        total = p0[n - 1, x, y].astype(jnp.float32)
        for u in range(n - 1):
            total = total + r3[u].astype(jnp.float32)
        summed[...] = total

    here.greet()
    for w in weights:
        w.local()
    for w in weights[:2]:
        w.along_z()
    steps = []
    hash_steps = []
    for t in range(n + 3):
        group = []
        for u, stage in ((t, hash_a), (t - 1, hash_b), (t - 2, hash_c), (t - 3, hash_d)):
            if 0 <= u < n:
                group.append(lambda u=u, stage=stage: stage(u))
        hash_steps.append(group)
    hash_steps.append([hash_e])
    for t in range(max(weight_count + 3, len(hash_steps))):
        if t + 2 < weight_count:
            weights[t + 2].along_z()
        if t < len(hash_steps):
            for run in hash_steps[t]:
                run()
        if t < weight_count:
            weights[t].near()
        if 0 <= t - 1 < weight_count:
            weights[t - 1].far()
        if 0 <= t - 2 < weight_count:
            weights[t - 2].across()
        if 0 <= t - 3 < weight_count:
            weights[t - 3].done()
    here.finish()


def fetch(lists, table, shards, dp_count, tokens):
    width = table.shape[1]
    count = len(shards)
    hbm = pl.BlockSpec(memory_space=pl.ANY)
    vmem = pl.BlockSpec(memory_space=pltpu.VMEM)
    n, half = dp_count, width // 2
    low = jnp.bfloat16
    dma = pltpu.SemaphoreType.DMA
    results = pl.pallas_call(
        functools.partial(fetch_kernel, dp_count, count, tokens),
        out_shape=[jax.ShapeDtypeStruct((n, *w.shape), w.dtype) for w in shards]
        + [jax.ShapeDtypeStruct((tokens, width), jnp.float32)],
        in_specs=[hbm] * count + [vmem, vmem],
        out_specs=[hbm] * count + [vmem],
        scratch_shapes=[
            pltpu.VMEM((2, 2, 2, tokens, width), low),
            pltpu.VMEM((n, 2, 2, tokens, width), low),
            pltpu.VMEM((n, 2, tokens, half), low),
            pltpu.VMEM((n, 2, tokens, half), low),
            pltpu.VMEM((n, tokens, half), low),
            pltpu.VMEM((n, tokens, half), low),
            pltpu.VMEM((n - 1, tokens, width), low),
            pltpu.VMEM((4 * SLOTS, width), low),
            dma((n, 2)),
            dma((n, 4, 2)),
            dma((n - 1, 2)),
            dma((count,)),
            dma((count, 4, n - 1)),
            dma((count, 4, n - 1)),
        ],
        compiler_params=pltpu.CompilerParams(
            collective_id=0, has_side_effects=True, vmem_limit_bytes=VMEM_CAP
        ),
        name="fetch",
    )(*shards, lists, table)
    fulls = [w.reshape(n * w.shape[1], w.shape[2]) for w in results[:count]]
    return fulls, results[count]


def grads_kernel(dp_count, units, left_count, right_count, slots_of, *refs):
    n = dp_count
    count = len(units)
    refs = list(refs)

    def take(number):
        taken = refs[:number]
        del refs[:number]
        return taken

    lefts_in, rights_in = take(left_count), take(right_count)
    embed_in, gains_in = take(2)
    outs = take(count)
    gathered, gains_out = take(2)
    lefts, rights = take(left_count), take(right_count)
    pools = take(len(slots_of))
    r1a, r1b, r2a, r2b, r3 = (take(count) for _ in range(5))
    gain_send, gain_recv = take(2)
    (
        left_sems,
        right_sems,
        stage_sems,
        z_sems,
        gain_sems,
        own_sem,
        near_sems,
        plane_sems,
    ) = refs
    here = Place(n)
    z, x, y, c = here.z, here.x, here.y, here.c

    here.greet()

    def bring(source, target, sems, i, split):
        mine = source.at[c] if split else source
        theirs = source.at[1 - c] if split else source
        local = pltpu.make_async_copy(mine, target.at[0], sems.at[i, 0])
        local.start()
        remote = here.send(
            theirs, target.at[1], sems.at[i, 1], sems.at[i, 2], here.at(dc=1)
        )
        return [local, remote]

    left_copies, right_copies = {}, {}

    def need(i):
        left, right = units[i][0], units[i][1]
        if left not in left_copies:
            left_copies[left] = bring(lefts_in[left], lefts[left], left_sems, left, True)
        if right not in right_copies:
            right_copies[right] = bring(rights_in[right], rights[right], right_sems, right, False)

    def have(i):
        for copies in (left_copies[units[i][0]], right_copies[units[i][1]]):
            if copies:
                copies[0].wait()
                copies[1].wait_recv()
                copies.clear()

    own = pltpu.make_async_copy(embed_in, gathered.at[z, x, y, c], own_sem)
    own.start()
    for j in range(1, n):
        here.send(
            embed_in,
            gathered.at[z, x, y, c],
            plane_sems.at[j - 1, 0],
            plane_sems.at[j - 1, 1],
            here.at(dz=j),
        )
    width = embed_in.shape[1]
    left_half, right_half = pl.ds(0, width // 2), pl.ds(width // 2, width // 2)

    def embed_near(j):
        plane = lax.rem(z + n - j, n)
        if j:
            here.expect(gathered.at[plane, x, y, c], plane_sems.at[j - 1, 1])
        else:
            own.wait()
        a = gathered.at[plane, x, y, c, :, left_half]
        b = gathered.at[plane, x, y, c, :, right_half]
        here.send(a, a, near_sems.at[j, 0, 0], near_sems.at[j, 0, 1], here.at(dx=1))
        here.send(b, b, near_sems.at[j, 1, 0], near_sems.at[j, 1, 1], here.at(dy=1))

    def embed_far(j):
        plane = lax.rem(z + n - j, n)
        here.expect(gathered.at[plane, 1 - x, y, c, :, left_half], near_sems.at[j, 0, 1])
        here.expect(gathered.at[plane, x, 1 - y, c, :, right_half], near_sems.at[j, 1, 1])
        a = gathered.at[plane, :, y, c, :, left_half]
        b = gathered.at[plane, x, :, c, :, right_half]
        here.send(a, a, near_sems.at[j, 2, 0], near_sems.at[j, 2, 1], here.at(dy=1))
        here.send(b, b, near_sems.at[j, 3, 0], near_sems.at[j, 3, 1], here.at(dx=1))

    def embed_across(j):
        plane = lax.rem(z + n - j, n)
        here.expect(gathered.at[plane, :, 1 - y, c, :, left_half], near_sems.at[j, 2, 1])
        here.expect(gathered.at[plane, 1 - x, :, c, :, right_half], near_sems.at[j, 3, 1])
        a = gathered.at[plane, :, :, c]
        here.send(a, a, near_sems.at[j, 4, 0], near_sems.at[j, 4, 1], here.at(dc=1))

    def embed_done(j):
        plane = lax.rem(z + n - j, n)
        here.expect(gathered.at[plane, :, :, 1 - c], near_sems.at[j, 4, 1])

    def gains(stage):
        if stage == 0:
            gain_send[0] = gains_in[...]
        elif stage <= 3:
            here.expect(gain_recv.at[stage - 1], gain_sems.at[stage - 1, 1])
            gain_send[stage] = gain_send[stage - 1] + gain_recv[stage - 1]
        if stage < 3:
            peer = (here.at(dc=1), here.at(dx=1), here.at(dy=1))[stage]
            here.send(
                gain_send.at[stage],
                gain_recv.at[stage],
                gain_sems.at[stage, 0],
                gain_sems.at[stage, 1],
                peer,
            )
        elif stage == 3:
            for j in range(1, n):
                here.send(
                    gain_send.at[3],
                    gain_recv.at[2 + j],
                    gain_sems.at[2 + j, 0],
                    gain_sems.at[2 + j, 1],
                    here.at(dz=j),
                )
        else:
            total = gain_send[3]
            for j in range(1, n):
                here.expect(gain_recv.at[2 + j], gain_sems.at[2 + j, 1])
                total = total + gain_recv[2 + j]
            gains_out[...] = total

    sums = [None] * count
    using = {}
    mine_of = [None] * count
    sent_of = [None] * count

    def product(i):
        left, right, pool, slot = units[i]
        have(i)
        if (pool, slot) in using:
            for copy in using[(pool, slot)]:
                here.sent(copy)
        p0 = pools[pool].at[slot]
        xt, g = lefts[left], rights[right]
        k, depth = xt.shape[2], xt.shape[3]
        cols = g.shape[2]
        chunks = 1 if k <= 32 else n
        planes = n // chunks
        tile = 256

        def columns(t, carry):
            span = pl.ds(pl.multiple_of(t * tile, tile), tile)
            for chunk in range(chunks):
                total = None
                for who in range(2):
                    rows = xt[who, chunk * planes * 4 : (chunk + 1) * planes * 4]
                    part = matmul(rows.reshape(planes * 4 * k, depth), g[who, :, span])
                    total = part if total is None else total + part
                p0[chunk * planes : (chunk + 1) * planes, :, :, :, span] = total.astype(
                    jnp.bfloat16
                ).reshape(planes, 2, 2, k, tile)
            return carry

        lax.fori_loop(0, cols // tile, columns, 0)
        sums[i] = Reduction(here, p0, r1a[i], r1b[i], r2a[i], r2b[i], stage_sems, i)
        sums[i].first()
        using[(pool, slot)] = [sums[i].s1a, sums[i].s1b]

    def second(i):
        sums[i].second()
        using[units[i][2:]] += [sums[i].s2a, sums[i].s2b]

    def third(i):
        mine = sums[i].third()
        sent_of[i] = []
        for j in range(1, n):
            sent_of[i].append(
                here.send(
                    mine.at[lax.rem(z + j, n)],
                    r3[i].at[j - 1],
                    z_sems.at[i, j - 1, 0],
                    z_sems.at[i, j - 1, 1],
                    here.at(dz=j),
                )
            )
        using[units[i][2:]] += sent_of[i]
        mine_of[i] = mine

    def final(i):
        total = mine_of[i][z].astype(jnp.float32)
        for j in range(1, n):
            sent_of[i][j - 1].wait_recv()
            total = total + r3[i][j - 1].astype(jnp.float32)
        outs[i][...] = total

    ahead = 2
    for i in range(ahead):
        need(i)
    for t in range(count + 4):
        if t + ahead < count:
            need(t + ahead)
        if t < 5:
            gains(t)
        if 0 <= t - 4 < count:
            final(t - 4)
        if t < count:
            product(t)
        if t < n:
            embed_near(t)
        if 0 <= t - 1 < n:
            embed_far(t - 1)
        if 0 <= t - 2 < n:
            embed_across(t - 2)
        if 0 <= t - 3 < n:
            embed_done(t - 3)
        if 0 <= t - 1 < count:
            second(t - 1)
        if 0 <= t - 3 < count:
            third(t - 3)
    here.finish()


def reduce_grads(pairs, lefts, rights, embed_low, gains, dp_count):
    n = dp_count
    low = jnp.bfloat16
    dma = pltpu.SemaphoreType.DMA
    hbm = pl.BlockSpec(memory_space=pl.ANY)
    vmem = pl.BlockSpec(memory_space=pltpu.VMEM)
    shapes, units, pools = [], [], []
    seen = {}
    for left, right in pairs:
        shape = (lefts[left].shape[2], rights[right].shape[1])
        number = seen.get(shape, 0)
        seen[shape] = number + 1
        shapes.append(shape)
    classes = list(seen)
    slots = [min(seen[s], 5) for s in classes]
    used = {s: 0 for s in classes}
    for (left, right), shape in zip(pairs, shapes):
        pool = classes.index(shape)
        units.append((left, right, pool, used[shape] % slots[pool]))
        used[shape] += 1
    count = len(pairs)
    tokens, width = embed_low.shape
    scratch = [pltpu.VMEM(a.shape, low) for a in lefts]
    scratch += [pltpu.VMEM((2, *a.shape), low) for a in rights]
    scratch += [pltpu.VMEM((s, n, 2, 2, *shape), low) for s, shape in zip(slots, classes)]
    halves = [(k, cols // 2) for k, cols in shapes]
    for _ in range(2):
        scratch += [pltpu.VMEM((n, 2, *half), low) for half in halves]
    for _ in range(2):
        scratch += [pltpu.VMEM((n, *half), low) for half in halves]
    scratch += [pltpu.VMEM((n - 1, *shape), low) for shape in shapes]
    scratch += [
        pltpu.VMEM((4, 8, width), jnp.float32),
        pltpu.VMEM((2 + n, 8, width), jnp.float32),
        dma((len(lefts), 3)),
        dma((len(rights), 3)),
        dma((count, 4, 2)),
        dma((count, n - 1, 2)),
        dma((2 + n, 2)),
        dma,
        dma((n, 5, 2)),
        dma((n - 1, 2)),
    ]
    results = pl.pallas_call(
        functools.partial(grads_kernel, n, units, len(lefts), len(rights), slots),
        out_shape=[jax.ShapeDtypeStruct(shape, jnp.float32) for shape in shapes]
        + [
            jax.ShapeDtypeStruct((n, 2, 2, 2, tokens, width), low),
            jax.ShapeDtypeStruct((8, width), jnp.float32),
        ],
        in_specs=[hbm] * (len(lefts) + len(rights) + 1) + [vmem],
        out_specs=[vmem] * count + [hbm, vmem],
        scratch_shapes=scratch,
        compiler_params=pltpu.CompilerParams(
            collective_id=1, has_side_effects=True, vmem_limit_bytes=VMEM_CAP
        ),
        name="reduce_grads",
    )(*lefts, *rights, embed_low, gains)
    return results[:count], results[count], results[count + 1]


def spread_kernel(lists, rows_of, grads, out, counts, stacked):
    step = pl.program_id(0)
    group, tokens = grads.shape[0], grads.shape[1]

    @pl.when(step == 0)
    def _():
        out[...] = jnp.zeros_like(out)
        counts[...] = jnp.zeros_like(counts)

    byte_iota = lax.broadcasted_iota(jnp.int32, (SLOTS, tokens), 1)
    for s in range(group):
        pick = (jnp.bitwise_and(lists[s], 255) == byte_iota).astype(jnp.bfloat16)
        stacked[s * SLOTS : (s + 1) * SLOTS, :] = matmul(pick, grads[s]).astype(jnp.bfloat16)
    row_iota = lax.broadcasted_iota(jnp.int32, (out.shape[0], group * SLOTS), 0)
    onto = (rows_of[0] == row_iota).astype(jnp.float32)
    counts[...] += jnp.sum(onto, axis=1, keepdims=True)
    out[...] += matmul(onto.astype(jnp.bfloat16), stacked[...])


def spread(entries, gathered, rows_dev):
    sources, tokens, width = gathered.shape
    group = 8
    steps = sources // group
    rows_of = jnp.right_shift(entries, 8).reshape(steps, 1, group * SLOTS)
    out, counts = pl.pallas_call(
        spread_kernel,
        grid=(steps,),
        out_shape=[
            jax.ShapeDtypeStruct((rows_dev, width), jnp.float32),
            jax.ShapeDtypeStruct((rows_dev, 1), jnp.float32),
        ],
        in_specs=[
            pl.BlockSpec((group, SLOTS, 1), lambda i: (i, 0, 0)),
            pl.BlockSpec((1, 1, group * SLOTS), lambda i: (i, 0, 0)),
            pl.BlockSpec((group, tokens, width), lambda i: (i, 0, 0)),
        ],
        out_specs=[
            pl.BlockSpec((rows_dev, width), lambda i: (0, 0)),
            pl.BlockSpec((rows_dev, 1), lambda i: (0, 0)),
        ],
        scratch_shapes=[pltpu.VMEM((group * SLOTS, width), jnp.bfloat16)],
        compiler_params=pltpu.CompilerParams(vmem_limit_bytes=VMEM_CAP),
        name="spread",
    )(entries[:, :, None], rows_of, gathered)
    return out, counts[:, 0].astype(jnp.int32)


def asked_rows(all_ids, first_row, rows_dev, gram_count):
    requests = all_ids.shape[1]
    local = all_ids - first_row
    inside = (local >= 0) & (local < rows_dev)
    index = jnp.arange(requests, dtype=jnp.int32)
    earlier = (index[:, None] < index[None, :]).astype(jnp.bfloat16)
    place = matmul(inside.astype(jnp.bfloat16), earlier).astype(jnp.int32)
    place = jnp.where(inside, place, -1)
    entry = local * 256 + (index // gram_count)[None, :] + 1
    slots = jnp.arange(SLOTS, dtype=jnp.int32)
    chosen = place[:, None, :] == slots[None, :, None]
    return jnp.sum(jnp.where(chosen, entry[:, None, :], 0), axis=2) - 1


def by_rows(a, dp_count):
    depth, total = a.shape
    pairs = dp_count * 4
    both = total // pairs
    a = a.T.reshape(pairs, both, depth)
    rows = -(-(both // 2) // 16) * 16
    return jnp.stack([a[:, :rows], a[:, both - rows :]])


def own_rows(block, rows):
    core = lax.axis_index("sub") % 2
    return jnp.where(core == 0, block[:rows], block[block.shape[0] - rows :])


def body(
    byte_ids,
    hash_ids,
    lengths,
    byte_table,
    hash_table,
    norm_attn,
    norm_ffn,
    norm_cross,
    w_query,
    w_key,
    w_value,
    w_out,
    w_gate,
    w_up,
    w_down,
    c_query,
    c_key,
    c_value,
    c_out,
    cot_bytes,
    cot_patches,
):
    dp_count = lax.axis_size("dp")
    rs_count = lax.axis_size(("rep", "sub"))
    all_count = dp_count * rs_count
    rank_seq = lax.axis_index(("rep", "sub"))
    rank_table = lax.axis_index("dp") * rs_count + rank_seq
    tokens, gram_count = hash_ids.shape
    rows_dev, model_width = hash_table.shape
    head_count = model_width // HD
    request_count = tokens * gram_count
    slot_count = 2 * request_count // all_count
    flat_ids = hash_ids.reshape(request_count)
    owners = flat_ids // rows_dev
    ordering = jnp.argsort(owners, stable=True)
    owners_sorted = owners[ordering]
    per_owner = jnp.sum(
        (owners[:, None] == jnp.arange(all_count, dtype=jnp.int32)[None, :]).astype(jnp.int32),
        axis=0,
    )
    first_slot = jnp.cumsum(per_owner) - per_owner
    place_sorted = (
        owners_sorted * slot_count
        + jnp.arange(request_count, dtype=jnp.int32)
        - first_slot[owners_sorted]
    )
    placement = jnp.zeros((request_count,), jnp.int32).at[ordering].set(place_sorted)
    requests = jnp.full((all_count * slot_count,), -1, jnp.int32).at[placement].set(flat_ids)
    requests = requests.reshape(dp_count, rs_count, slot_count)
    incoming = lax.all_to_all(
        lax.all_to_all(requests, "dp", split_axis=0, concat_axis=0, tiled=True),
        ("rep", "sub"),
        split_axis=1,
        concat_axis=1,
        tiled=True,
    )
    present = incoming >= 0
    safe_rows = jnp.where(present, incoming - rank_table * rows_dev, 0)
    served = jnp.where(present[..., None], hash_table[safe_rows], jnp.zeros((), jnp.bfloat16))
    returned = lax.all_to_all(
        lax.all_to_all(served, "dp", split_axis=0, concat_axis=0, tiled=True),
        ("rep", "sub"),
        split_axis=1,
        concat_axis=1,
        tiled=True,
    )
    fetched = returned.reshape(all_count * slot_count, model_width)[placement]
    fetched = fetched.astype(jnp.float32).reshape(tokens, gram_count, model_width)
    one_hot = byte_ids[:, None] == jnp.arange(BYTE_VALUES, dtype=jnp.int32)[None, :]
    embedded = matmul(one_hot.astype(jnp.bfloat16), byte_table) + jnp.sum(fetched, axis=1)
    row_counts = (
        jnp.zeros((rows_dev,), jnp.int32)
        .at[safe_rows.reshape(-1)]
        .add(present.reshape(-1).astype(jnp.int32))
    )
    weight_list = (
        w_query,
        w_key,
        w_value,
        w_out,
        w_gate,
        w_up,
        w_down,
        c_query,
        c_key,
        c_value,
        c_out,
    )
    gathered = (
        lax.all_gather(weight_list[0], "dp", axis=0, tiled=True),
        lax.all_gather(weight_list[1], "dp", axis=0, tiled=True),
        lax.all_gather(weight_list[2], "dp", axis=0, tiled=True),
        lax.all_gather(weight_list[3], "dp", axis=0, tiled=True),
        lax.all_gather(weight_list[4], "dp", axis=0, tiled=True),
        lax.all_gather(weight_list[5], "dp", axis=0, tiled=True),
        lax.all_gather(weight_list[6], "dp", axis=0, tiled=True),
        lax.all_gather(weight_list[7], "dp", axis=0, tiled=True),
        lax.all_gather(weight_list[8], "dp", axis=0, tiled=True),
        lax.all_gather(weight_list[9], "dp", axis=0, tiled=True),
        lax.all_gather(weight_list[10], "dp", axis=0, tiled=True),
    )
    (
        full_query,
        full_key,
        full_value,
        full_out,
        full_gate,
        full_up,
        full_down,
        full_cquery,
        full_ckey,
        full_cvalue,
        full_cout,
    ) = gathered
    x_attn, normed_attn, scale_attn = normalize(embedded, norm_attn)
    queries = matmul(x_attn, full_query).astype(jnp.bfloat16).reshape(tokens, head_count, HD)
    key_rows = matmul(x_attn, full_key).astype(jnp.bfloat16).reshape(tokens, head_count, HD)
    value_rows = matmul(x_attn, full_value).astype(jnp.bfloat16).reshape(tokens, head_count, HD)
    behind = (WIN - 2) // tokens + 1
    key_parts = []
    value_parts = []
    for offset_back in range(behind, 0, -1):
        far_keys, far_values = passed_along((key_rows, value_rows), ("rep", "sub"), offset_back)
        key_parts.append(far_keys)
        value_parts.append(far_values)
    all_keys = jnp.concatenate(key_parts + [key_rows], axis=0)
    all_values = jnp.concatenate(value_parts + [value_rows], axis=0)
    q_rows = min(tokens, 512)
    key_span = (WIN - 1 + q_rows - 1) // q_rows * q_rows
    base_key = (rank_seq - behind) * tokens
    block_index = 0
    q_start = block_index * q_rows
    k_start = behind * tokens + q_start - key_span
    allowed = window_mask(
        rank_seq * tokens + q_start, base_key + k_start, q_rows, q_rows + key_span
    )
    scores = (
        jnp.einsum("qhd,khd->hqk", queries, all_keys, preferred_element_type=jnp.float32)
        * SCORE_SCALE
    )
    prob_block, log_total = soft_forward(scores, allowed)
    attended_parts = jnp.einsum(
        "hqk,khd->qhd",
        prob_block.astype(jnp.bfloat16),
        all_values,
        preferred_element_type=jnp.float32,
    )
    lse_parts = [log_total]
    attended = attended_parts.astype(jnp.bfloat16).reshape(tokens, model_width)
    h_mid = embedded + matmul(attended, full_out)
    x_ffn, normed_ffn, scale_ffn = normalize(h_mid, norm_ffn)
    gate_pre = matmul(x_ffn, full_gate)
    up_pre = matmul(x_ffn, full_up)
    gate_sig = jax.nn.sigmoid(gate_pre)
    silu_val = gate_pre * gate_sig
    hidden = (silu_val * up_pre).astype(jnp.bfloat16)
    h_out = h_mid + matmul(hidden, full_down)
    byte_states = h_out.astype(jnp.bfloat16)
    x_cross, normed_cross, scale_cross = normalize(h_out, norm_cross)
    patch_len = lengths[0]
    patch_count = patch_len.shape[0]
    patch_end = jnp.cumsum(patch_len)
    patch_start = patch_end - patch_len
    byte_pos = jnp.arange(tokens, dtype=jnp.int32)
    member = (byte_pos[None, :] >= patch_start[:, None]) & (byte_pos[None, :] < patch_end[:, None])
    length_f = patch_len.astype(jnp.float32)[:, None]
    pooled = matmul(member.astype(jnp.bfloat16), x_cross) / length_f
    pooled_low = pooled.astype(jnp.bfloat16)
    p_query = (
        matmul(pooled_low, full_cquery).astype(jnp.bfloat16).reshape(patch_count, head_count, HD)
    )
    p_key = matmul(x_cross, full_ckey).astype(jnp.bfloat16).reshape(tokens, head_count, HD)
    p_value = matmul(x_cross, full_cvalue).astype(jnp.bfloat16).reshape(tokens, head_count, HD)
    cross_scores = (
        jnp.einsum("phd,thd->hpt", p_query, p_key, preferred_element_type=jnp.float32) * SCORE_SCALE
    )
    cross_prob, cross_lse = soft_forward(cross_scores, member[None])
    p_attended = (
        jnp.einsum(
            "hpt,thd->phd",
            cross_prob.astype(jnp.bfloat16),
            p_value,
            preferred_element_type=jnp.float32,
        )
        .astype(jnp.bfloat16)
        .reshape(patch_count, model_width)
    )
    patch_states = (pooled + matmul(p_attended, full_cout)).astype(jnp.bfloat16)
    grad_c_out = t_times(p_attended, cot_patches)
    grad_patt = (
        times_t(cot_patches, full_cout).astype(jnp.bfloat16).reshape(patch_count, head_count, HD)
    )
    cross_again = (
        jnp.einsum("phd,thd->hpt", p_query, p_key, preferred_element_type=jnp.float32) * SCORE_SCALE
    )
    cross_full = soft_again(cross_again, member[None], cross_lse)
    grad_cprob = jnp.einsum("phd,thd->hpt", grad_patt, p_value, preferred_element_type=jnp.float32)
    grad_cscore = soft_back(cross_full, grad_cprob)
    grad_pquery = (
        (
            jnp.einsum("hpt,thd->phd", grad_cscore, p_key, preferred_element_type=jnp.float32)
            * SCORE_SCALE
        )
        .astype(jnp.bfloat16)
        .reshape(patch_count, model_width)
    )
    grad_pkey = (
        (
            jnp.einsum("hpt,phd->thd", grad_cscore, p_query, preferred_element_type=jnp.float32)
            * SCORE_SCALE
        )
        .astype(jnp.bfloat16)
        .reshape(tokens, model_width)
    )
    grad_pvalue = (
        jnp.einsum(
            "hpt,phd->thd",
            cross_full.astype(jnp.bfloat16),
            grad_patt,
            preferred_element_type=jnp.float32,
        )
        .astype(jnp.bfloat16)
        .reshape(tokens, model_width)
    )
    grad_c_query = t_times(pooled_low, grad_pquery)
    grad_c_key = t_times(x_cross, grad_pkey)
    grad_c_value = t_times(x_cross, grad_pvalue)
    grad_pooled = cot_patches.astype(jnp.float32) + times_t(grad_pquery, full_cquery).astype(
        jnp.bfloat16
    ).astype(jnp.float32)
    to_bytes = lax.dot_general(
        member.astype(jnp.float32),
        grad_pooled / length_f,
        (((0,), (0,)), ((), ())),
        precision=PRECISE,
    )
    grad_xcross = (
        times_t(grad_pkey, full_ckey) + times_t(grad_pvalue, full_cvalue) + to_bytes
    ).astype(jnp.bfloat16)
    grad_hout_norm, grad_norm_cross = norm_back(
        grad_xcross.astype(jnp.float32), normed_cross, scale_cross, norm_cross
    )
    grad_hout = cot_bytes.astype(jnp.float32) + grad_hout_norm
    grad_branch_f = grad_hout.astype(jnp.bfloat16)
    grad_w_down = t_times(hidden, grad_branch_f)
    grad_hidden = times_t(grad_branch_f, full_down).astype(jnp.bfloat16).astype(jnp.float32)
    grad_gate = (grad_hidden * up_pre * gate_sig * (1.0 + gate_pre * (1.0 - gate_sig))).astype(
        jnp.bfloat16
    )
    grad_up = (grad_hidden * silu_val).astype(jnp.bfloat16)
    grad_w_gate = t_times(x_ffn, grad_gate)
    grad_w_up = t_times(x_ffn, grad_up)
    grad_xffn = (times_t(grad_gate, full_gate) + times_t(grad_up, full_up)).astype(jnp.bfloat16)
    grad_hmid_norm, grad_norm_ffn = norm_back(
        grad_xffn.astype(jnp.float32), normed_ffn, scale_ffn, norm_ffn
    )
    grad_hmid = grad_hout + grad_hmid_norm
    grad_branch_a = grad_hmid.astype(jnp.bfloat16)
    grad_w_out = t_times(attended, grad_branch_a)
    grad_att = times_t(grad_branch_a, full_out).astype(jnp.bfloat16).reshape(tokens, head_count, HD)
    grad_keys_all = jnp.zeros(((behind + 1) * tokens, head_count, HD), jnp.float32)
    grad_values_all = jnp.zeros(((behind + 1) * tokens, head_count, HD), jnp.float32)
    block_index = 0
    q_start = block_index * q_rows
    k_start = behind * tokens + q_start - key_span
    k_stop = k_start + q_rows + key_span
    allowed = window_mask(
        rank_seq * tokens + q_start, base_key + k_start, q_rows, q_rows + key_span
    )
    scores = (
        jnp.einsum("qhd,khd->hqk", queries, all_keys, preferred_element_type=jnp.float32)
        * SCORE_SCALE
    )
    prob_block = soft_again(scores, allowed, lse_parts[block_index])
    grad_prob = jnp.einsum("qhd,khd->hqk", grad_att, all_values, preferred_element_type=jnp.float32)
    grad_score = soft_back(prob_block, grad_prob)
    grad_q_parts = (
        jnp.einsum("hqk,khd->qhd", grad_score, all_keys, preferred_element_type=jnp.float32)
        * SCORE_SCALE
    )
    grad_keys_all = grad_keys_all.at[k_start:k_stop].add(
        jnp.einsum("hqk,qhd->khd", grad_score, queries, preferred_element_type=jnp.float32)
        * SCORE_SCALE
    )
    grad_values_all = grad_values_all.at[k_start:k_stop].add(
        jnp.einsum(
            "hqk,qhd->khd",
            prob_block.astype(jnp.bfloat16),
            grad_att,
            preferred_element_type=jnp.float32,
        )
    )
    grad_keys = grad_keys_all[behind * tokens :]
    grad_values = grad_values_all[behind * tokens :]
    for offset_back in range(behind, 0, -1):
        part_index = behind - offset_back
        far_grad_k, far_grad_v = (
            passed_along(
                grad_keys_all[part_index * tokens : (part_index + 1) * tokens].astype(jnp.bfloat16),
                ("rep", "sub"),
                -offset_back,
            ).astype(jnp.float32),
            passed_along(
                grad_values_all[part_index * tokens : (part_index + 1) * tokens].astype(
                    jnp.bfloat16
                ),
                ("rep", "sub"),
                -offset_back,
            ).astype(jnp.float32),
        )
        grad_keys = grad_keys + far_grad_k
        grad_values = grad_values + far_grad_v
    grad_queries = grad_q_parts.astype(jnp.bfloat16).reshape(tokens, model_width)
    grad_keys_low = grad_keys.astype(jnp.bfloat16).reshape(tokens, model_width)
    grad_values_low = grad_values.astype(jnp.bfloat16).reshape(tokens, model_width)
    grad_w_query = t_times(x_attn, grad_queries)
    grad_w_key = t_times(x_attn, grad_keys_low)
    grad_w_value = t_times(x_attn, grad_values_low)
    grad_xattn = (
        times_t(grad_queries, full_query)
        + times_t(grad_keys_low, full_key)
        + times_t(grad_values_low, full_value)
    ).astype(jnp.bfloat16)
    grad_embed_norm, grad_norm_attn = norm_back(
        grad_xattn.astype(jnp.float32), normed_attn, scale_attn, norm_attn
    )
    grad_embed = grad_hmid + grad_embed_norm
    embed_grad = grad_embed.astype(jnp.bfloat16)
    grad_byte_table = lax.dot_general(
        one_hot.astype(jnp.float32), grad_embed, (((0,), (0,)), ((), ())), precision=PRECISE
    )
    per_request = jnp.broadcast_to(
        grad_embed[:, None, :], (tokens, gram_count, model_width)
    ).reshape(request_count, model_width)
    outgoing = (
        jnp.zeros((all_count * slot_count, model_width), jnp.float32).at[placement].set(per_request)
    )
    outgoing = outgoing.reshape(dp_count, rs_count, slot_count, model_width)
    arrived = lax.all_to_all(
        lax.all_to_all(
            outgoing.astype(jnp.bfloat16), "dp", split_axis=0, concat_axis=0, tiled=True
        ),
        ("rep", "sub"),
        split_axis=1,
        concat_axis=1,
        tiled=True,
    ).astype(outgoing.dtype)
    hash_table_grad = (
        jnp.zeros((rows_dev, model_width), jnp.float32)
        .at[safe_rows.reshape(-1)]
        .add(jnp.where(present[..., None], arrived, 0.0).reshape(-1, model_width))
    )
    summed_all = (
        lax.psum_scatter(grad_norm_attn, ("dp", "rep", "sub"), scatter_dimension=0, tiled=True),
        lax.psum_scatter(grad_norm_ffn, ("dp", "rep", "sub"), scatter_dimension=0, tiled=True),
        lax.psum_scatter(grad_norm_cross, ("dp", "rep", "sub"), scatter_dimension=0, tiled=True),
        lax.psum_scatter(grad_w_query, ("dp", "rep", "sub"), scatter_dimension=0, tiled=True),
        lax.psum_scatter(grad_w_key, ("dp", "rep", "sub"), scatter_dimension=0, tiled=True),
        lax.psum_scatter(grad_w_value, ("dp", "rep", "sub"), scatter_dimension=0, tiled=True),
        lax.psum_scatter(grad_w_out, ("dp", "rep", "sub"), scatter_dimension=0, tiled=True),
        lax.psum_scatter(grad_w_gate, ("dp", "rep", "sub"), scatter_dimension=0, tiled=True),
        lax.psum_scatter(grad_w_up, ("dp", "rep", "sub"), scatter_dimension=0, tiled=True),
        lax.psum_scatter(grad_w_down, ("dp", "rep", "sub"), scatter_dimension=0, tiled=True),
        lax.psum_scatter(grad_c_query, ("dp", "rep", "sub"), scatter_dimension=0, tiled=True),
        lax.psum_scatter(grad_c_key, ("dp", "rep", "sub"), scatter_dimension=0, tiled=True),
        lax.psum_scatter(grad_c_value, ("dp", "rep", "sub"), scatter_dimension=0, tiled=True),
        lax.psum_scatter(grad_c_out, ("dp", "rep", "sub"), scatter_dimension=0, tiled=True),
        lax.psum_scatter(grad_byte_table, ("dp", "rep", "sub"), scatter_dimension=0, tiled=True),
    )
    (
        out_norm_attn,
        out_norm_ffn,
        out_norm_cross,
        out_query,
        out_key,
        out_value,
        out_proj,
        out_gate,
        out_up,
        out_down,
        out_cquery,
        out_ckey,
        out_cvalue,
        out_cout,
        out_bytes,
    ) = summed_all
    return (
        byte_states,
        patch_states,
        embed_grad,
        out_bytes,
        hash_table_grad,
        row_counts,
        out_norm_attn,
        out_norm_ffn,
        out_norm_cross,
        out_query,
        out_key,
        out_value,
        out_proj,
        out_gate,
        out_up,
        out_down,
        out_cquery,
        out_ckey,
        out_cvalue,
        out_cout,
    )


def fast_body(
    byte_ids,
    hash_ids,
    lengths,
    byte_table,
    hash_table,
    norm_attn,
    norm_ffn,
    norm_cross,
    w_query,
    w_key,
    w_value,
    w_out,
    w_gate,
    w_up,
    w_down,
    c_query,
    c_key,
    c_value,
    c_out,
    cot_bytes,
    cot_patches,
):
    dp_count = lax.axis_size("dp")
    rs_count = lax.axis_size(("rep", "sub"))
    all_count = dp_count * rs_count
    rank_seq = lax.axis_index(("rep", "sub"))
    rank_table = lax.axis_index("dp") * rs_count + rank_seq
    tokens, gram_count = hash_ids.shape
    rows_dev, model_width = hash_table.shape
    head_count = model_width // HD
    request_count = tokens * gram_count
    all_ids = lax.all_gather(hash_ids.reshape(1, request_count), ("dp", "rep", "sub"), tiled=True)
    entries = asked_rows(all_ids, rank_table * rows_dev, rows_dev, gram_count)
    weight_list = (
        w_query,
        w_key,
        w_value,
        w_out,
        w_gate,
        w_up,
        w_down,
        c_query,
        c_key,
        c_value,
        c_out,
    )
    order = (0, 1, 2, 3, 4, 5, 7, 8, 9, 6, 10)
    got, hash_sum = fetch(
        entries[:, :, None], hash_table, [weight_list[i] for i in order], dp_count, tokens
    )
    gathered = [got[order.index(i)] for i in range(len(order))]
    one_hot = byte_ids[:, None] == jnp.arange(BYTE_VALUES, dtype=jnp.int32)[None, :]
    embedded = matmul(one_hot.astype(jnp.bfloat16), byte_table) + hash_sum
    (
        full_query,
        full_key,
        full_value,
        full_out,
        full_gate,
        full_up,
        full_down,
        full_cquery,
        full_ckey,
        full_cvalue,
        full_cout,
    ) = gathered
    x_attn, normed_attn, scale_attn = normalize(embedded, norm_attn)
    queries = matmul(x_attn, full_query).astype(jnp.bfloat16).reshape(tokens, head_count, HD)
    key_rows = matmul(x_attn, full_key).astype(jnp.bfloat16).reshape(tokens, head_count, HD)
    value_rows = matmul(x_attn, full_value).astype(jnp.bfloat16).reshape(tokens, head_count, HD)
    behind = (WIN - 2) // tokens + 1
    key_parts = []
    value_parts = []
    for offset_back in range(behind, 0, -1):
        far_keys, far_values = passed_along((key_rows, value_rows), ("rep", "sub"), offset_back)
        key_parts.append(far_keys)
        value_parts.append(far_values)
    all_keys = jnp.concatenate(key_parts + [key_rows], axis=0)
    all_values = jnp.concatenate(value_parts + [value_rows], axis=0)
    q_rows = min(tokens, 512)
    key_span = (WIN - 1 + q_rows - 1) // q_rows * q_rows
    base_key = (rank_seq - behind) * tokens
    block_index = 0
    q_start = block_index * q_rows
    k_start = behind * tokens + q_start - key_span
    allowed = window_mask(
        rank_seq * tokens + q_start, base_key + k_start, q_rows, q_rows + key_span
    )
    scores = (
        jnp.einsum("qhd,khd->hqk", queries, all_keys, preferred_element_type=jnp.float32)
        * SCORE_SCALE
    )
    prob_block, log_total = soft_forward(scores, allowed)
    attended_parts = jnp.einsum(
        "hqk,khd->qhd",
        prob_block.astype(jnp.bfloat16),
        all_values,
        preferred_element_type=jnp.float32,
    )
    lse_parts = [log_total]
    attended = attended_parts.astype(jnp.bfloat16).reshape(tokens, model_width)
    h_mid = embedded + matmul(attended, full_out)
    x_ffn, normed_ffn, scale_ffn = normalize(h_mid, norm_ffn)
    gate_pre = matmul(x_ffn, full_gate)
    up_pre = matmul(x_ffn, full_up)
    gate_sig = jax.nn.sigmoid(gate_pre)
    silu_val = gate_pre * gate_sig
    hidden = (silu_val * up_pre).astype(jnp.bfloat16)
    h_out = h_mid + matmul(hidden, full_down)
    byte_states = h_out.astype(jnp.bfloat16)
    x_cross, normed_cross, scale_cross = normalize(h_out, norm_cross)
    patch_len = lengths[0]
    patch_count = patch_len.shape[0]
    patch_end = jnp.cumsum(patch_len)
    patch_start = patch_end - patch_len
    byte_pos = jnp.arange(tokens, dtype=jnp.int32)
    member = (byte_pos[None, :] >= patch_start[:, None]) & (byte_pos[None, :] < patch_end[:, None])
    length_f = patch_len.astype(jnp.float32)[:, None]
    pooled = matmul(member.astype(jnp.bfloat16), x_cross) / length_f
    pooled_low = pooled.astype(jnp.bfloat16)
    p_query = (
        matmul(pooled_low, full_cquery).astype(jnp.bfloat16).reshape(patch_count, head_count, HD)
    )
    p_key = matmul(x_cross, full_ckey).astype(jnp.bfloat16).reshape(tokens, head_count, HD)
    p_value = matmul(x_cross, full_cvalue).astype(jnp.bfloat16).reshape(tokens, head_count, HD)
    cross_scores = (
        jnp.einsum("phd,thd->hpt", p_query, p_key, preferred_element_type=jnp.float32) * SCORE_SCALE
    )
    cross_prob, cross_lse = soft_forward(cross_scores, member[None])
    p_attended = (
        jnp.einsum(
            "hpt,thd->phd",
            cross_prob.astype(jnp.bfloat16),
            p_value,
            preferred_element_type=jnp.float32,
        )
        .astype(jnp.bfloat16)
        .reshape(patch_count, model_width)
    )
    patch_states = (pooled + matmul(p_attended, full_cout)).astype(jnp.bfloat16)
    grad_patt = (
        times_t(cot_patches, full_cout).astype(jnp.bfloat16).reshape(patch_count, head_count, HD)
    )
    cross_again = (
        jnp.einsum("phd,thd->hpt", p_query, p_key, preferred_element_type=jnp.float32) * SCORE_SCALE
    )
    cross_full = soft_again(cross_again, member[None], cross_lse)
    grad_cprob = jnp.einsum("phd,thd->hpt", grad_patt, p_value, preferred_element_type=jnp.float32)
    grad_cscore = soft_back(cross_full, grad_cprob)
    grad_pquery = (
        (
            jnp.einsum("hpt,thd->phd", grad_cscore, p_key, preferred_element_type=jnp.float32)
            * SCORE_SCALE
        )
        .astype(jnp.bfloat16)
        .reshape(patch_count, model_width)
    )
    grad_pkey = (
        (
            jnp.einsum("hpt,phd->thd", grad_cscore, p_query, preferred_element_type=jnp.float32)
            * SCORE_SCALE
        )
        .astype(jnp.bfloat16)
        .reshape(tokens, model_width)
    )
    grad_pvalue = (
        jnp.einsum(
            "hpt,phd->thd",
            cross_full.astype(jnp.bfloat16),
            grad_patt,
            preferred_element_type=jnp.float32,
        )
        .astype(jnp.bfloat16)
        .reshape(tokens, model_width)
    )
    grad_pooled = cot_patches.astype(jnp.float32) + times_t(grad_pquery, full_cquery).astype(
        jnp.bfloat16
    ).astype(jnp.float32)
    to_bytes = lax.dot_general(
        member.astype(jnp.float32),
        grad_pooled / length_f,
        (((0,), (0,)), ((), ())),
        precision=PRECISE,
    )
    grad_xcross = (
        times_t(grad_pkey, full_ckey) + times_t(grad_pvalue, full_cvalue) + to_bytes
    ).astype(jnp.bfloat16)
    grad_hout_norm, grad_norm_cross = norm_back(
        grad_xcross.astype(jnp.float32), normed_cross, scale_cross, norm_cross
    )
    grad_hout = cot_bytes.astype(jnp.float32) + grad_hout_norm
    grad_branch_f = grad_hout.astype(jnp.bfloat16)
    grad_hidden = times_t(grad_branch_f, full_down).astype(jnp.bfloat16).astype(jnp.float32)
    grad_gate = (grad_hidden * up_pre * gate_sig * (1.0 + gate_pre * (1.0 - gate_sig))).astype(
        jnp.bfloat16
    )
    grad_up = (grad_hidden * silu_val).astype(jnp.bfloat16)
    grad_xffn = (times_t(grad_gate, full_gate) + times_t(grad_up, full_up)).astype(jnp.bfloat16)
    grad_hmid_norm, grad_norm_ffn = norm_back(
        grad_xffn.astype(jnp.float32), normed_ffn, scale_ffn, norm_ffn
    )
    grad_hmid = grad_hout + grad_hmid_norm
    grad_branch_a = grad_hmid.astype(jnp.bfloat16)
    grad_att = times_t(grad_branch_a, full_out).astype(jnp.bfloat16).reshape(tokens, head_count, HD)
    grad_keys_all = jnp.zeros(((behind + 1) * tokens, head_count, HD), jnp.float32)
    grad_values_all = jnp.zeros(((behind + 1) * tokens, head_count, HD), jnp.float32)
    block_index = 0
    q_start = block_index * q_rows
    k_start = behind * tokens + q_start - key_span
    k_stop = k_start + q_rows + key_span
    allowed = window_mask(
        rank_seq * tokens + q_start, base_key + k_start, q_rows, q_rows + key_span
    )
    scores = (
        jnp.einsum("qhd,khd->hqk", queries, all_keys, preferred_element_type=jnp.float32)
        * SCORE_SCALE
    )
    prob_block = soft_again(scores, allowed, lse_parts[block_index])
    grad_prob = jnp.einsum("qhd,khd->hqk", grad_att, all_values, preferred_element_type=jnp.float32)
    grad_score = soft_back(prob_block, grad_prob)
    grad_q_parts = (
        jnp.einsum("hqk,khd->qhd", grad_score, all_keys, preferred_element_type=jnp.float32)
        * SCORE_SCALE
    )
    grad_keys_all = grad_keys_all.at[k_start:k_stop].add(
        jnp.einsum("hqk,qhd->khd", grad_score, queries, preferred_element_type=jnp.float32)
        * SCORE_SCALE
    )
    grad_values_all = grad_values_all.at[k_start:k_stop].add(
        jnp.einsum(
            "hqk,qhd->khd",
            prob_block.astype(jnp.bfloat16),
            grad_att,
            preferred_element_type=jnp.float32,
        )
    )
    grad_keys = grad_keys_all[behind * tokens :]
    grad_values = grad_values_all[behind * tokens :]
    for offset_back in range(behind, 0, -1):
        part_index = behind - offset_back
        far_grad_k, far_grad_v = (
            passed_along(
                grad_keys_all[part_index * tokens : (part_index + 1) * tokens].astype(jnp.bfloat16),
                ("rep", "sub"),
                -offset_back,
            ).astype(jnp.float32),
            passed_along(
                grad_values_all[part_index * tokens : (part_index + 1) * tokens].astype(
                    jnp.bfloat16
                ),
                ("rep", "sub"),
                -offset_back,
            ).astype(jnp.float32),
        )
        grad_keys = grad_keys + far_grad_k
        grad_values = grad_values + far_grad_v
    grad_queries = grad_q_parts.astype(jnp.bfloat16).reshape(tokens, model_width)
    grad_keys_low = grad_keys.astype(jnp.bfloat16).reshape(tokens, model_width)
    grad_values_low = grad_values.astype(jnp.bfloat16).reshape(tokens, model_width)
    grad_xattn = (
        times_t(grad_queries, full_query)
        + times_t(grad_keys_low, full_key)
        + times_t(grad_values_low, full_value)
    ).astype(jnp.bfloat16)
    grad_embed_norm, grad_norm_attn = norm_back(
        grad_xattn.astype(jnp.float32), normed_attn, scale_attn, norm_attn
    )
    grad_embed = grad_hmid + grad_embed_norm
    embed_grad = grad_embed.astype(jnp.bfloat16)
    lefts = [
        by_rows(a, dp_count)
        for a in (
            x_attn,
            attended,
            x_ffn,
            hidden,
            pooled_low,
            x_cross,
            p_attended,
            one_hot.astype(jnp.bfloat16),
        )
    ]
    rights = [
        grad_queries,
        grad_keys_low,
        grad_values_low,
        grad_branch_a,
        grad_gate,
        grad_up,
        grad_branch_f,
        grad_pquery,
        grad_pkey,
        grad_pvalue,
        cot_patches,
        embed_grad,
    ]
    pairs = [
        (5, 8),
        (2, 4),
        (5, 9),
        (2, 5),
        (6, 10),
        (3, 6),
        (4, 7),
        (1, 3),
        (0, 0),
        (0, 1),
        (0, 2),
        (7, 11),
    ]
    gain_rows = jnp.concatenate(
        [grad_norm_attn[None], grad_norm_ffn[None], grad_norm_cross[None]]
        + [jnp.zeros((5, model_width), jnp.float32)]
    )
    sums, all_embed, gain_sums = reduce_grads(pairs, lefts, rights, embed_grad, gain_rows, dp_count)
    (
        out_ckey,
        out_gate,
        out_cvalue,
        out_up,
        out_cout,
        down_rows,
        out_cquery,
        out_proj,
        out_query,
        out_key,
        out_value,
        byte_rows,
    ) = sums
    out_down = own_rows(down_rows, hidden.shape[1] // all_count)
    out_bytes = own_rows(byte_rows, BYTE_VALUES // all_count)
    hash_table_grad, row_counts = spread(
        entries, all_embed.reshape(all_count, tokens, model_width), rows_dev
    )
    own_gains = lax.dynamic_slice_in_dim(
        gain_sums, rank_table * (model_width // all_count), model_width // all_count, 1
    )
    out_norm_attn, out_norm_ffn, out_norm_cross = own_gains[0], own_gains[1], own_gains[2]
    return (
        byte_states,
        patch_states,
        embed_grad,
        out_bytes,
        hash_table_grad,
        row_counts,
        out_norm_attn,
        out_norm_ffn,
        out_norm_cross,
        out_query,
        out_key,
        out_value,
        out_proj,
        out_gate,
        out_up,
        out_down,
        out_cquery,
        out_ckey,
        out_cvalue,
        out_cout,
    )


def solution(mesh):
    fits = mesh.shape["rep"] == 2 and mesh.shape["sub"] == 4 and mesh.shape["dp"] <= 4
    return jax.shard_map(
        fast_body if fits else body,
        mesh=mesh,
        in_specs=(
            P(("dp", "rep", "sub")),
            P(("dp", "rep", "sub"), None),
            P(("dp", "rep", "sub"), None),
            P(),
            P(("dp", "rep", "sub"), None),
            P(),
            P(),
            P(),
            P("dp", None),
            P("dp", None),
            P("dp", None),
            P("dp", None),
            P("dp", None),
            P("dp", None),
            P("dp", None),
            P("dp", None),
            P("dp", None),
            P("dp", None),
            P("dp", None),
            P(("dp", "rep", "sub"), None),
            P(("dp", "rep", "sub"), None),
        ),
        out_specs=(
            P(("dp", "rep", "sub"), None),
            P(("dp", "rep", "sub"), None),
            P(("dp", "rep", "sub"), None),
            P(("dp", "rep", "sub"), None),
            P(("dp", "rep", "sub"), None),
            P(("dp", "rep", "sub")),
            P(("dp", "rep", "sub")),
            P(("dp", "rep", "sub")),
            P(("dp", "rep", "sub")),
            P(("dp", "rep", "sub"), None),
            P(("dp", "rep", "sub"), None),
            P(("dp", "rep", "sub"), None),
            P(("dp", "rep", "sub"), None),
            P(("dp", "rep", "sub"), None),
            P(("dp", "rep", "sub"), None),
            P(("dp", "rep", "sub"), None),
            P(("dp", "rep", "sub"), None),
            P(("dp", "rep", "sub"), None),
            P(("dp", "rep", "sub"), None),
            P(("dp", "rep", "sub"), None),
        ),
        check_vma=False,
    )
```

```python
import functools
import typing

import jax
import jax.numpy as jnp
from jax import lax
from jax.experimental import pallas as pl
from jax.experimental.pallas import tpu as pltpu
from jax.sharding import PartitionSpec as P

DP, REP, SUB = "dp", "rep", "sub"
SEQ = (REP, SUB)
ALL = (DP, REP, SUB)
HD = 64
WIN = 512
BYTE_VALUES = 256


PRECISE = lax.Precision.HIGHEST
NEG_BIG = -1e30
EPSILON = 1e-06
SCORE_SCALE = 0.125


def passed_along(x, axis, by):
    devices = lax.axis_size(axis)
    pairs = [(i, i + by) for i in range(devices) if 0 <= i + by < devices]
    return lax.ppermute(x, axis, pairs)


def matmul(matrix_a, matrix_b):
    return jnp.dot(matrix_a, matrix_b, preferred_element_type=jnp.float32)


def times_t(matrix_a, matrix_b):
    return lax.dot_general(
        matrix_a, matrix_b, (((1,), (1,)), ((), ())), preferred_element_type=jnp.float32
    )


def t_times(matrix_a, matrix_b):
    return lax.dot_general(
        matrix_a, matrix_b, (((0,), (0,)), ((), ())), preferred_element_type=jnp.float32
    )


def normalize(values, gains):
    inv_rms = lax.rsqrt(jnp.mean(values * values, axis=-1, keepdims=True) + EPSILON)
    normed = values * inv_rms
    return ((normed * gains).astype(jnp.bfloat16), normed, inv_rms)


def norm_back(grad_out, normed, inv_rms, gains):
    grad_gain = jnp.sum(grad_out * normed, axis=0)
    scaled_grad = grad_out * gains
    grad_in = inv_rms * (
        scaled_grad - normed * jnp.mean(scaled_grad * normed, axis=-1, keepdims=True)
    )
    return (grad_in, grad_gain)


def soft_forward(scores, allowed):
    masked = jnp.where(allowed, scores, NEG_BIG)
    row_max = jnp.max(masked, axis=-1, keepdims=True)
    exps = jnp.exp(masked - row_max)
    row_sum = jnp.sum(exps, axis=-1, keepdims=True)
    return (exps / row_sum, row_max + jnp.log(row_sum))


def soft_again(scores, allowed, log_total):
    return jnp.where(allowed, jnp.exp(scores - log_total), 0.0)


def soft_back(probs_full, grad_probs):
    row_total = jnp.sum(probs_full * grad_probs, axis=-1, keepdims=True)
    return (probs_full * (grad_probs - row_total)).astype(jnp.bfloat16)


def window_mask(first_query, first_key, row_count, col_count):
    query_pos = first_query + jnp.arange(row_count, dtype=jnp.int32)
    key_pos = first_key + jnp.arange(col_count, dtype=jnp.int32)
    near = (
        (key_pos[None, :] <= query_pos[:, None])
        & (key_pos[None, :] > query_pos[:, None] - WIN)
        & (key_pos[None, :] >= 0)
    )
    return near[None]


MESH_ID = pl.DeviceIdType.MESH
SLOTS = 96
GATHER_LAGS = (1, 1, 2, 3)


HASH, GATHER, FORWARD = range(3)


SCHEDULE = (
    (HASH, 0),
    (GATHER, 0),
    (HASH, 1),
    (GATHER, 1),
    (HASH, 2),
    (GATHER, 2),
    (HASH, 3),
    (GATHER, 3),
    (HASH, 4),
    (GATHER, 4),
    (HASH, 5),
    (GATHER, 5),
    (HASH, 6),
    (GATHER, 6),
    (HASH, 7),
    (GATHER, 7),
    (FORWARD, 1),
    (GATHER, 8),
    (FORWARD, 1),
    (GATHER, 9),
    (FORWARD, 1),
    (GATHER, 10),
    (FORWARD, 1),
    (GATHER, 11),
    (FORWARD, 1),
    (GATHER, 12),
    (FORWARD, 1),
    (GATHER, 13),
    (FORWARD, 5),
)
VMEM_CAP = 60 * 1024 * 1024


class Place:
    def __init__(self, dp_count):
        self.n = dp_count
        self.z = lax.axis_index(DP)
        self.x = lax.axis_index(REP)
        sub = lax.axis_index(SUB)
        self.y = sub // 2
        self.c = sub % 2
        self.started, self.maybe = [], []

    def at(self, dz=0, dx=0, dy=0, dc=0):
        z = lax.rem(self.z + dz, self.n) if dz else self.z
        x = 1 - self.x if dx else self.x
        y = 1 - self.y if dy else self.y
        c = 1 - self.c if dc else self.c
        return (z, x, y * 2 + c)

    def greet(self):
        barrier = pltpu.get_barrier_semaphore()
        peers = [
            self.at(dx=dx, dy=dy, dc=dc)
            for dx in range(2)
            for dy in range(2)
            for dc in range(2)
            if dx + dy + dc > 0
        ]
        peers += [self.at(dz=j) for j in range(1, self.n)]
        for peer in peers:
            pl.semaphore_signal(barrier, inc=1, device_id=peer, device_id_type=MESH_ID)
        pl.semaphore_wait(barrier, len(peers))

    def send_if(self, there, src, dst, send_sem, recv_sem, peer):
        copy = pltpu.make_async_remote_copy(
            src_ref=src,
            dst_ref=dst,
            send_sem=send_sem,
            recv_sem=recv_sem,
            device_id=peer,
            device_id_type=MESH_ID,
        )
        pl.when(there)(copy.start)
        self.maybe.append((there, copy))

    def send(self, src, dst, send_sem, recv_sem, peer):
        copy = pltpu.make_async_remote_copy(
            src_ref=src,
            dst_ref=dst,
            send_sem=send_sem,
            recv_sem=recv_sem,
            device_id=peer,
            device_id_type=MESH_ID,
        )
        copy.start()
        self.started.append(copy)
        return copy

    def expect(self, dst, recv_sem):
        pltpu.make_async_remote_copy(
            src_ref=dst,
            dst_ref=dst,
            send_sem=recv_sem,
            recv_sem=recv_sem,
            device_id=self.at(dc=1),
            device_id_type=MESH_ID,
        ).wait_recv()

    def sent(self, copy):
        copy.wait_send()
        self.started = [other for other in self.started if other is not copy]

    def finish(self):
        for copy in self.started:
            copy.wait_send()
        for there, copy in self.maybe:
            pl.when(there)(copy.wait_send)
        self.started, self.maybe = [], []


def add_into(dst, src, blocks, width):
    def step(i, carry):
        total = dst(i)[...].astype(jnp.float32) + src(i)[...].astype(jnp.float32)
        dst(i)[...] = total.astype(jnp.bfloat16)
        return carry

    lax.fori_loop(0, blocks, step, 0)


class Reduction:
    def __init__(self, here, p0, r1a, r1b, r2a, r2b, sems, index):
        self.here, self.p0 = here, p0
        self.r1a, self.r1b, self.r2a, self.r2b = r1a, r1b, r2a, r2b
        self.sems, self.i = sems, index
        self.planes, _, _, self.rows, cols = p0.shape
        self.half = cols // 2
        self.left = pl.ds(0, self.half)
        self.right = pl.ds(self.half, self.half)

    def sem(self, k):
        return self.sems.at[self.i, k, 0], self.sems.at[self.i, k, 1]

    def first(self):
        h = self.here
        self.s1a = h.send(
            self.p0.at[:, 1 - h.x, :, :, self.left], self.r1a, *self.sem(0), h.at(dx=1)
        )
        self.s1b = h.send(
            self.p0.at[:, :, 1 - h.y, :, self.right], self.r1b, *self.sem(1), h.at(dy=1)
        )

    def second(self):
        h = self.here
        self.s1a.wait_recv()
        add_into(
            lambda i: self.p0.at[i // 2, h.x, i % 2, :, self.left],
            lambda i: self.r1a.at[i // 2, i % 2],
            2 * self.planes,
            self.half,
        )
        self.s2a = h.send(
            self.p0.at[:, h.x, 1 - h.y, :, self.left], self.r2a, *self.sem(2), h.at(dy=1)
        )
        self.s1b.wait_recv()
        add_into(
            lambda i: self.p0.at[i // 2, i % 2, h.y, :, self.right],
            lambda i: self.r1b.at[i // 2, i % 2],
            2 * self.planes,
            self.half,
        )
        self.s2b = h.send(
            self.p0.at[:, 1 - h.x, h.y, :, self.right], self.r2b, *self.sem(3), h.at(dx=1)
        )

    def third(self):
        h = self.here
        self.s2a.wait_recv()
        add_into(
            lambda i: self.p0.at[i, h.x, h.y, :, self.left],
            lambda i: self.r2a.at[i],
            self.planes,
            self.half,
        )
        self.s2b.wait_recv()
        add_into(
            lambda i: self.p0.at[i, h.x, h.y, :, self.right],
            lambda i: self.r2b.at[i],
            self.planes,
            self.half,
        )
        return self.p0.at[:, h.x, h.y]


EXTRA_IN = 5
F32, LOW = jnp.float32, jnp.bfloat16
class Kept(typing.NamedTuple):
    x_attn: typing.Any
    queries: typing.Any
    key_values: typing.Any
    lse: typing.Any
    attended: typing.Any
    h_mid: typing.Any
    x_ffn: typing.Any
    gate_pre: typing.Any
    up_pre: typing.Any
    hidden: typing.Any
    h_out: typing.Any
    byte_states: typing.Any
    x_cross: typing.Any
    pooled: typing.Any
    p_query: typing.Any
    p_key: typing.Any
    p_value: typing.Any
    cross_lse: typing.Any
    p_attended: typing.Any
    patch_states: typing.Any


def kept_shapes(t, w, f, p):
    one = jax.ShapeDtypeStruct
    return Kept(
        x_attn=one((t, w), LOW),
        queries=one((t, w), LOW),
        key_values=one((2, 3 * t, w), LOW),
        lse=one((t, 128), F32),
        attended=one((t, w), LOW),
        h_mid=one((t, w), F32),
        x_ffn=one((t, w), LOW),
        gate_pre=one((t, f), F32),
        up_pre=one((t, f), F32),
        hidden=one((t, f), LOW),
        h_out=one((t, w), F32),
        byte_states=one((t, w), LOW),
        x_cross=one((t, w), LOW),
        pooled=one((p, w), LOW),
        p_query=one((p, w), LOW),
        p_key=one((t, w), LOW),
        p_value=one((t, w), LOW),
        cross_lse=one((p, 128), F32),
        p_attended=one((p, w), LOW),
        patch_states=one((p, w), LOW),
    )


def forward_steps(here, fulls, embedded, extra_in, extra_out, slots, scratch):
    byte_ids, byte_table, gains, starts, ends = extra_in
    out = Kept(*extra_out)
    gate_w, up_w, load_sems, halo_sems = scratch
    tokens, width = embedded.shape
    heads = width // HD
    n = here.n
    z, x, y, c = here.z, here.x, here.y, here.c
    rank = (x * 2 + y) * 2 + c
    loads = {}
    kv = out.key_values

    def load(i, *targets):
        copies = []
        for b, target in enumerate(targets):
            rows = target.shape[0]
            copy = pltpu.make_async_copy(
                fulls[i].at[pl.ds(b * rows, rows)], target, load_sems.at[i, b]
            )
            copy.start()
            copies.append(copy)
        loads[i] = copies

    def load_slot(i, slot):
        for b in range(4):
            copy = pltpu.make_async_copy(
                fulls[i].at[pl.ds(b * (width // 4), width // 4)],
                slots[slot].at[b // 2, b % 2],
                load_sems.at[i, b],
            )
            copy.start()
            loads.setdefault(i, []).append(copy)

    def wait(*weights):
        for i in weights:
            for copy in loads[i]:
                copy.wait()

    def through(a, slot):
        total = None
        for b in range(4):
            part = matmul(
                a[:, b * (width // 4) : (b + 1) * (width // 4)], slots[slot][b // 2, b % 2]
            )
            total = part if total is None else total + part
        return total

    def embed():
        load_slot(0, 0)
        load_slot(1, 1)
        load_slot(2, 2)
        ids = lax.broadcasted_iota(jnp.int32, (tokens, BYTE_VALUES), 1)
        pick = jnp.where(byte_ids[...] == ids, 1.0, 0.0).astype(LOW)
        embedded[...] = embedded[...] + matmul(pick, byte_table[...])
        out.x_attn[...] = normalize(embedded[...], gains[0:1])[0]

    def project():
        wait(0, 1, 2)
        a = out.x_attn[...]
        kv[0, 2 * tokens :] = through(a, 1).astype(LOW)
        kv[1, 2 * tokens :] = through(a, 2).astype(LOW)
        for back in (1, 2):
            target = rank + back
            here.send_if(
                target < 8,
                kv.at[:, pl.ds(2 * tokens, tokens)],
                kv.at[:, pl.ds((2 - back) * tokens, tokens)],
                halo_sems.at[back - 1, 0],
                halo_sems.at[back - 1, 1],
                (z, target // 4, lax.rem(target, 4)),
            )
        out.queries[...] = through(a, 0).astype(LOW)
        for back in (1, 2):
            part = kv.at[:, pl.ds((2 - back) * tokens, tokens)]

            @pl.when(rank >= back)
            def _():
                here.expect(part, halo_sems.at[back - 1, 1])

            @pl.when(rank < back)
            def _():
                part[...] = jnp.zeros_like(part)

    lane = lax.broadcasted_iota(jnp.int32, (1, 128), 1)
    sides = [jnp.where(lane < HD, 1.0, 0.0).astype(LOW), jnp.where(lane < HD, 0.0, 1.0).astype(LOW)]

    def attend(first):
        row = lax.broadcasted_iota(jnp.int32, (tokens, tokens), 0)
        col = lax.broadcasted_iota(jnp.int32, (tokens, tokens), 1)
        mine = col <= row
        far_bias = jnp.where(rank >= 2, 0.0, NEG_BIG)
        near_bias = jnp.where(rank >= 1, 0.0, NEG_BIG)
        if first == 0:
            out.lse[...] = jnp.zeros_like(out.lse)
        else:
            load_slot(3, 3)

        def heads_pair(pair, carry):
            span = pl.ds(pl.multiple_of(pair * 128, 128), 128)
            q2 = out.queries[:, span]
            k2, v2 = kv[0, :, span], kv[1, :, span]
            halves = []
            for side in range(2):
                scores = times_t(q2 * sides[side], k2) * SCORE_SCALE
                edge = jnp.where(mine, scores[:, 2 * tokens :], scores[:, :tokens] + far_bias)
                middle = scores[:, tokens : 2 * tokens] + near_bias
                top = jnp.maximum(
                    jnp.max(edge, axis=1, keepdims=True), jnp.max(middle, axis=1, keepdims=True)
                )
                edge, middle = jnp.exp(edge - top), jnp.exp(middle - top)
                total = jnp.sum(edge, axis=1, keepdims=True) + jnp.sum(
                    middle, axis=1, keepdims=True
                )
                inverse = 1.0 / total
                edge, middle = edge * inverse, middle * inverse
                probs = jnp.concatenate(
                    [
                        jnp.where(mine, 0.0, edge).astype(LOW),
                        middle.astype(LOW),
                        jnp.where(mine, edge, 0.0).astype(LOW),
                    ],
                    axis=1,
                )
                halves.append(matmul(probs, v2))
                where = lane == pair * 2 + side
                out.lse[...] = jnp.where(where, top + jnp.log(total), out.lse[...])
            out.attended[:, span] = jnp.where(lane < HD, halves[0], halves[1]).astype(LOW)
            return carry

        lax.fori_loop(first * heads // 4, (first + 1) * heads // 4, heads_pair, 0)

    def attention_out():
        wait(3)
        h_mid = embedded[...] + through(out.attended[...], 3)
        out.h_mid[...] = h_mid
        out.x_ffn[...] = normalize(h_mid, gains[1:2])[0]

    def down_block(t):
        return slots[t // 4].at[t // 2 % 2, t % 2]

    tile = 256
    tiles = gate_w.shape[1] // tile

    def feed_forward():
        for t in range(tiles):
            copy = pltpu.make_async_copy(
                fulls[6].at[pl.ds(t * tile, tile)], down_block(t), down_sems.at[t]
            )
            copy.start()
            loads.setdefault(6, []).append(copy)
        wait(4, 5)
        a = out.x_ffn[...]

        def columns(t, carry):
            span = pl.ds(pl.multiple_of(t * tile, tile), tile)
            gate = matmul(a, gate_w[:, span])
            up = matmul(a, up_w[:, span])
            out.gate_pre[:, span] = gate
            out.up_pre[:, span] = up
            out.hidden[:, span] = (gate * jax.nn.sigmoid(gate) * up).astype(LOW)
            return carry

        lax.fori_loop(0, tiles, columns, 0)

    def feed_out():
        wait(6)
        total = out.h_mid[...]
        for t in range(tiles):
            total = total + matmul(
                out.hidden[:, t * tile : (t + 1) * tile], down_block(t)[...]
            )
        out.h_out[...] = total
        out.byte_states[...] = total.astype(LOW)
        out.x_cross[...] = normalize(total, gains[2:3])[0]

    byte_pos = lax.broadcasted_iota(jnp.int32, (starts.shape[0], tokens), 1)

    def member():
        return (byte_pos >= starts[...]) & (byte_pos < ends[...])

    pooled_f = []

    def cross_keys():
        load_slot(8, 4)
        load_slot(9, 5)
        inside = jnp.where(member(), 1.0, 0.0).astype(LOW)
        length = (ends[...] - starts[...]).astype(F32)
        pooled = matmul(inside, out.x_cross[...]) / length
        pooled_f.append(pooled)
        out.pooled[...] = pooled.astype(LOW)
        wait(8, 9)
        a = out.x_cross[...]
        out.p_key[...] = through(a, 4).astype(LOW)
        out.p_value[...] = through(a, 5).astype(LOW)

    def cross_query():
        load_slot(7, 3)
        load_slot(10, 0)
        wait(7)
        out.p_query[...] = through(out.pooled[...], 3).astype(LOW)
        allowed = member()
        out.cross_lse[...] = jnp.zeros_like(out.cross_lse)

        def heads_pair(pair, carry):
            span = pl.ds(pl.multiple_of(pair * 128, 128), 128)
            q2, k2, v2 = out.p_query[:, span], out.p_key[:, span], out.p_value[:, span]
            halves = []
            for side in range(2):
                scores = times_t(q2 * sides[side], k2) * SCORE_SCALE
                masked = jnp.where(allowed, scores, NEG_BIG)
                top = jnp.max(masked, axis=1, keepdims=True)
                exps = jnp.exp(masked - top)
                total = jnp.sum(exps, axis=1, keepdims=True)
                halves.append(matmul((exps / total).astype(LOW), v2))
                where = lane == pair * 2 + side
                out.cross_lse[...] = jnp.where(
                    where, top + jnp.log(total), out.cross_lse[...]
                )
            out.p_attended[:, span] = jnp.where(lane < HD, halves[0], halves[1]).astype(LOW)
            return carry

        lax.fori_loop(0, heads // 2, heads_pair, 0)

    def cross_out():
        wait(10)
        states = pooled_f[0] + through(out.p_attended[...], 0)
        out.patch_states[...] = states.astype(LOW)

    down_sems = load_sems.at[6]
    return [
        ((0, 1, 2), embed),
        ((), project),
        ((), lambda: attend(0)),
        ((3,), lambda: attend(1)),
        ((), attention_out),
        ((4, 5), lambda: (load(4, gate_w), load(5, up_w))),
        ((6,), feed_forward),
        ((), feed_out),
        ((8, 9), cross_keys),
        ((7, 10), cross_query),
        ((), cross_out),
    ]


def fetch_kernel(dp_count, weight_count, steps_of, tokens, gram_count, used_lines, *refs):
    shards = refs[:weight_count]
    refs = list(refs[weight_count:])

    def take(number):
        taken = refs[:number]
        del refs[:number]
        return taken

    ids, table = take(2)
    extra_in = take(EXTRA_IN)
    fulls = take(weight_count)
    embedded, lists = take(2)
    extra_out = take(len(Kept._fields))
    (
        all_ids,
        send0,
        p0,
        r1a,
        r1b,
        r2a,
        r2b,
        r3,
        g_rows,
        core_sems,
        stage_sems,
        z_sems,
        local_sems,
        w_send,
        w_recv,
        id_sems,
        places,
        entries,
        *extra_scratch,
    ) = refs
    here = Place(dp_count)
    n = dp_count
    z, x, y, c = here.z, here.x, here.y, here.c

    class Weight:
        def __init__(self, number, i, part, parts, kind):
            self.i = number
            self.kind = kind
            rows, cols = shards[i].shape
            self.by_cols = rows // 8 % 16 != 0
            self.all_rows, self.count = rows, rows // parts
            self.first = part * self.count
            self.shard = shards[i].at[pl.ds(self.first, self.count)]
            self.full = fulls[i]
            self.step = (cols if self.by_cols else rows // parts) // 8
            near, far = (x, y) if kind == 0 else (y, x)
            self.q = (c * 2 + far) * 2 + near

        def on(self, plane):
            return self.full.at[pl.ds(plane * self.all_rows + self.first, self.count)]

        def cut(self, ref, start, count):
            span = pl.ds(start * self.step, count * self.step)
            if self.by_cols:
                return ref.at[:, span]
            return ref.at[span, :]

        def local(self):
            here.send(
                self.shard,
                self.on(z),
                local_sems.at[self.i, 0],
                local_sems.at[self.i, 1],
                here.at(dc=1),
            )

        def stage(self, k, j, start, count, src_ref, plane, peer):
            here.send(
                self.cut(src_ref, start, count),
                self.cut(self.on(plane), start, count),
                w_send.at[self.i, k, j - 1],
                w_recv.at[self.i, k, j - 1],
                peer,
            )

        def came(self, k, j, start, count):
            plane = lax.rem(z + n - j, n)
            here.expect(
                self.cut(self.on(plane), start, count), w_recv.at[self.i, k, j - 1]
            )
            return plane

        def along_z(self):
            for j in range(1, n):
                self.stage(0, j, self.q, 1, self.shard, z, here.at(dz=j))

        def near(self):
            for j in range(1, n):
                plane = self.came(0, j, self.q, 1)
                peer = here.at(dx=1) if self.kind == 0 else here.at(dy=1)
                self.stage(1, j, self.q, 1, self.on(plane), plane, peer)

        def far(self):
            other = self.q + 1 - 2 * (self.q % 2)
            for j in range(1, n):
                plane = self.came(1, j, other, 1)
                peer = here.at(dy=1) if self.kind == 0 else here.at(dx=1)
                self.stage(2, j, self.q // 2 * 2, 2, self.on(plane), plane, peer)

        def across(self):
            pair = self.q // 2
            other = pair + 1 - 2 * (pair % 2)
            for j in range(1, n):
                plane = self.came(2, j, other * 2, 2)
                self.stage(3, j, c * 4, 4, self.on(plane), plane, here.at(dc=1))

        def done(self):
            for j in range(1, n):
                self.came(3, j, (1 - c) * 4, 4)
            here.expect(self.on(z), local_sems.at[self.i, 1])

    weights = []
    for first, second in steps_of:
        pair = []
        for kind, (i, part, parts) in enumerate((first, second)):
            pair.append(Weight(2 * len(weights) + kind, i, part, parts, kind))
        weights.append(pair)

    def each(t, name):
        if 0 <= t < len(weights):
            for w in weights[t]:
                name(w)

    def gather_ids():
        all_ids[z, x, y, c] = ids[...]
        mine = all_ids.at[z, x, y, c]
        here.send(mine, mine, id_sems.at[0, 0], id_sems.at[0, 1], here.at(dc=1))
        here.expect(all_ids.at[z, x, y, 1 - c], id_sems.at[0, 1])
        pair = all_ids.at[z, x, y]
        here.send(pair, pair, id_sems.at[1, 0], id_sems.at[1, 1], here.at(dx=1))
        here.expect(all_ids.at[z, 1 - x, y], id_sems.at[1, 1])
        four = all_ids.at[z, :, y]
        here.send(four, four, id_sems.at[2, 0], id_sems.at[2, 1], here.at(dy=1))
        here.expect(all_ids.at[z, :, 1 - y], id_sems.at[2, 1])
        plane = all_ids.at[z]
        for j in range(1, n):
            here.send(plane, plane, id_sems.at[2 + j, 0], id_sems.at[2 + j, 1], here.at(dz=j))
        for j in range(1, n):
            here.expect(all_ids.at[lax.rem(z + n - j, n)], id_sems.at[2 + j, 1])

    def list_rows():
        lines, lanes = ids.shape
        sources = n * 8
        total = sources * lines
        rows_dev = table.shape[0]
        local = all_ids[...].reshape(total, lanes) - ((z * 2 + x) * 4 + y * 2 + c) * rows_dev
        inside = (local >= 0) & (local < rows_dev)
        flags = jnp.where(inside, 1.0, 0.0).astype(jnp.bfloat16)
        row = lax.broadcasted_iota(jnp.int32, (lanes, lanes), 0)
        col = lax.broadcasted_iota(jnp.int32, (lanes, lanes), 1)
        place = matmul(flags, jnp.where(row < col, 1.0, 0.0).astype(jnp.bfloat16))
        held = matmul(flags, jnp.ones((lanes, lanes), jnp.bfloat16)).astype(jnp.bfloat16)
        row = lax.broadcasted_iota(jnp.int32, (total, total), 0)
        col = lax.broadcasted_iota(jnp.int32, (total, total), 1)
        before = (row // lines == col // lines) & (col < row)
        place = place + matmul(jnp.where(before, 1.0, 0.0).astype(jnp.bfloat16), held)
        places[...] = jnp.where(inside, place.astype(jnp.int32), -1)
        line = lax.broadcasted_iota(jnp.int32, (total, lanes), 0)
        lane = lax.broadcasted_iota(jnp.int32, (total, lanes), 1)
        index = lax.rem(line, lines) * lanes + lane
        entries[...] = local * 256 + index // gram_count + 1
        slot = lax.broadcasted_iota(jnp.int32, (SLOTS, lanes), 0)

        def source(s, carry):
            span = pl.ds(pl.multiple_of(s * lines, lines), lines)
            where, what = places[span], entries[span]
            found = jnp.zeros((SLOTS, lanes), jnp.int32)
            for line in range(used_lines):
                hit = where[line : line + 1] == slot
                found = found + jnp.where(hit, what[line : line + 1], 0)
            lists[s] = jnp.sum(found, axis=1, keepdims=True) - 1
            return carry

        lax.fori_loop(0, sources, source, 0)

    row_iota = lax.broadcasted_iota(jnp.int32, (SLOTS, table.shape[0]), 1)
    byte_iota = lax.broadcasted_iota(jnp.int32, (SLOTS, tokens), 1)

    def partial_sums(plane, core, write):
        for place in range(4):
            source = plane * 8 + place * 2 + core
            entry = lists[source]
            pick = (jnp.right_shift(entry, 8) == row_iota).astype(jnp.bfloat16)
            g_rows[place * SLOTS : (place + 1) * SLOTS, :] = matmul(pick, table[...]).astype(
                jnp.bfloat16
            )
        for place in range(4):
            source = plane * 8 + place * 2 + core
            entry = lists[source]
            to_byte = (jnp.bitwise_and(entry, 255) == byte_iota).astype(jnp.bfloat16)
            sums = t_times(to_byte, g_rows[place * SLOTS : (place + 1) * SLOTS, :])
            write(place, sums)

    units = []
    for u in range(n):
        units.append(
            Reduction(
                here,
                p0.at[pl.ds(u, 1)],
                r1a.at[pl.ds(u, 1)],
                r1b.at[pl.ds(u, 1)],
                r2a.at[pl.ds(u, 1)],
                r2b.at[pl.ds(u, 1)],
                stage_sems,
                u,
            )
        )
    core_copies = [None] * n
    z_copies = [None] * n

    def plane_of(u):
        return lax.rem(z + u + 1, n)

    def hash_a(u):
        slot = u % 2
        if u >= 2:
            here.sent(core_copies[u - 2])

        def write(place, sums):
            send0[slot, place // 2, place % 2] = sums.astype(jnp.bfloat16)

        partial_sums(plane_of(u), 1 - c, write)
        core_copies[u] = here.send(
            send0.at[slot], p0.at[u], core_sems.at[u, 0], core_sems.at[u, 1], here.at(dc=1)
        )

    def hash_b(u):
        core_copies[u].wait_recv()

        def write(place, sums):
            total = sums + p0[u, place // 2, place % 2].astype(jnp.float32)
            p0[u, place // 2, place % 2] = total.astype(jnp.bfloat16)

        partial_sums(plane_of(u), c, write)
        units[u].first()

    def hash_c(u):
        units[u].second()

    def hash_d(u):
        mine = units[u].third()
        if u < n - 1:
            z_copies[u] = here.send(
                mine.at[0], r3.at[u], z_sems.at[u, 0], z_sems.at[u, 1], here.at(dz=u + 1)
            )

    def hash_e():
        for u in range(n - 1):
            z_copies[u].wait_recv()
        total = p0[n - 1, x, y].astype(jnp.float32)
        for u in range(n - 1):
            total = total + r3[u].astype(jnp.float32)
        embedded[...] = total
        for copy in core_copies[-2:] + z_copies[:-1]:
            here.sent(copy)
        for unit in units:
            for copy in (unit.s1a, unit.s1b, unit.s2a, unit.s2b):
                here.sent(copy)

    here.greet()
    for t in range(len(weights)):
        each(t, Weight.local)
    lead, lag1, lag2, lag3 = GATHER_LAGS
    for t in range(lead):
        each(t, Weight.along_z)
    gather_ids()
    list_rows()
    hash_steps = []
    for t in range(n + 3):
        group = []
        for u, stage in ((t, hash_a), (t - 1, hash_b), (t - 2, hash_c), (t - 3, hash_d)):
            if 0 <= u < n:
                group.append(lambda u=u, stage=stage: stage(u))
        hash_steps.append(group)
    hash_steps.append([hash_e])
    layer = forward_steps(
        here,
        fulls,
        embedded,
        extra_in,
        extra_out,
        [p0.at[u] for u in range(n)] + [send0.at[u] for u in range(2)],
        extra_scratch,
    )
    gather_done, runs = set(), iter(layer)
    for what, number in SCHEDULE:
        if what == HASH:
            for run in hash_steps[number]:
                run()
        elif what == GATHER:
            each(number + lead, Weight.along_z)
            each(number, Weight.near)
            each(number - lag1, Weight.far)
            each(number - lag2, Weight.across)
            each(number - lag3, Weight.done)
            if 0 <= number - lag3 < len(steps_of):
                gather_done |= {i for i, _, _ in steps_of[number - lag3]}
        else:
            for _ in range(number):
                needs, run = next(runs)
                assert gather_done.issuperset(needs)
                run()
    assert next(runs, None) is None
    here.finish()


def fetch(hash_ids, table, shards, extra, steps_of, dp_count):
    width = table.shape[1]
    tokens, gram_count = hash_ids.shape
    count = len(shards)
    hbm = pl.BlockSpec(memory_space=pl.ANY)
    vmem = pl.BlockSpec(memory_space=pltpu.VMEM)
    n, half = dp_count, width // 2
    low = jnp.bfloat16
    dma = pltpu.SemaphoreType.DMA
    used_lines = tokens * gram_count // 128
    lines = -(-used_lines // 8) * 8
    ids = hash_ids.reshape(used_lines, 128)
    ids = jnp.concatenate([ids, jnp.full((lines - used_lines, 128), -1, jnp.int32)])
    gathers = 2 * len(steps_of)
    ff = shards[4].shape[1]
    extra_out = list(kept_shapes(tokens, width, ff, extra[3].shape[0]))
    results = pl.pallas_call(
        functools.partial(fetch_kernel, n, count, steps_of, tokens, gram_count, used_lines),
        out_shape=[jax.ShapeDtypeStruct((n * w.shape[0], w.shape[1]), w.dtype) for w in shards]
        + [
            jax.ShapeDtypeStruct((tokens, width), jnp.float32),
            jax.ShapeDtypeStruct((n * 8, SLOTS, 1), jnp.int32),
        ]
        + extra_out,
        in_specs=[hbm] * count + [vmem, vmem] + [vmem] * len(extra),
        out_specs=[hbm] * count + [vmem, vmem] + [vmem] * len(extra_out),
        scratch_shapes=[
            pltpu.VMEM((n, 2, 2, 2, lines, 128), jnp.int32),
            pltpu.VMEM((2, 2, 2, tokens, width), low),
            pltpu.VMEM((n, 2, 2, tokens, width), low),
            pltpu.VMEM((n, 2, tokens, half), low),
            pltpu.VMEM((n, 2, tokens, half), low),
            pltpu.VMEM((n, tokens, half), low),
            pltpu.VMEM((n, tokens, half), low),
            pltpu.VMEM((n - 1, tokens, width), low),
            pltpu.VMEM((4 * SLOTS, width), low),
            dma((n, 2)),
            dma((n, 4, 2)),
            dma((n - 1, 2)),
            dma((gathers, 2)),
            dma((gathers, 4, n - 1)),
            dma((gathers, 4, n - 1)),
            dma((2 + n, 2)),
            pltpu.VMEM((n * 8 * lines, 128), jnp.int32),
            pltpu.VMEM((n * 8 * lines, 128), jnp.int32),
            pltpu.VMEM((n * shards[4].shape[0], ff), low),
            pltpu.VMEM((n * shards[5].shape[0], ff), low),
            dma((count, max(n, ff // 256))),
            dma((2, 2)),
        ],
        compiler_params=pltpu.CompilerParams(
            collective_id=0, has_side_effects=True, vmem_limit_bytes=VMEM_CAP
        ),
        name="fetch",
    )(*shards, ids, table, *extra)
    return results[:count], results[count], results[count + 1], Kept(*results[count + 2 :])


LAGS = (2, 3, 5)


class GradSums:
    def __init__(self, here, units, lefts_in, rights_in, outs, take, pool_count):
        count = len(units)
        self.here, self.units = here, units
        self.lefts_in, self.rights_in, self.outs = lefts_in, rights_in, outs
        self.lefts, self.rights = take(len(lefts_in)), take(len(rights_in))
        self.pools = take(pool_count)
        self.r1a, self.r1b, self.r2a, self.r2b, self.r3 = (take(count) for _ in range(5))
        self.left_sems, self.right_sems, self.stage_sems, self.z_sems = take(4)
        self.left_copies, self.right_copies = {}, {}
        self.sums = [None] * count
        self.using = {}
        self.mine_of = [None] * count
        self.sent_of = [None] * count

    def bring(self, source, target, sems, i, split):
        here = self.here
        copies = []
        theirs = target.at[0]
        if source is not None:
            theirs = source.at[1 - here.c] if split else source
            mine = source.at[here.c] if split else source
            local = pltpu.make_async_copy(mine, target.at[0], sems.at[i, 0])
            local.start()
            copies.append(local.wait)
        remote = here.send(theirs, target.at[1], sems.at[i, 1], sems.at[i, 2], here.at(dc=1))
        copies.append(remote.wait_recv)
        return copies

    def left(self, i):
        if i not in self.left_copies:
            self.left_copies[i] = self.bring(
                self.lefts_in[i], self.lefts[i], self.left_sems, i, True
            )

    def right(self, i):
        if i not in self.right_copies:
            self.right_copies[i] = self.bring(
                self.rights_in[i], self.rights[i], self.right_sems, i, False
            )

    def need(self, i):
        self.left(self.units[i][0])
        self.right(self.units[i][1])

    def product(self, i):
        here, n = self.here, self.here.n
        left, right, pool, slot = self.units[i]
        self.need(i)
        for copies in (self.left_copies[left], self.right_copies[right]):
            for wait in copies:
                wait()
            copies.clear()
        for copy in self.using.get((pool, slot), []):
            here.sent(copy)
        p0 = self.pools[pool].at[slot]
        xt, g = self.lefts[left], self.rights[right]
        k, depth = xt.shape[2], xt.shape[3]
        cols = g.shape[2]
        chunks = 1 if k <= 32 else n
        planes = n // chunks
        tile = 256

        def columns(t, carry):
            span = pl.ds(pl.multiple_of(t * tile, tile), tile)
            for chunk in range(chunks):
                total = None
                for who in range(2):
                    rows = xt[who, chunk * planes * 4 : (chunk + 1) * planes * 4]
                    part = matmul(rows.reshape(planes * 4 * k, depth), g[who, :, span])
                    total = part if total is None else total + part
                p0[chunk * planes : (chunk + 1) * planes, :, :, :, span] = total.astype(
                    jnp.bfloat16
                ).reshape(planes, 2, 2, k, tile)
            return carry

        lax.fori_loop(0, cols // tile, columns, 0)
        unit = Reduction(
            here, p0, self.r1a[i], self.r1b[i], self.r2a[i], self.r2b[i], self.stage_sems, i
        )
        unit.first()
        self.sums[i] = unit
        self.using[(pool, slot)] = [unit.s1a, unit.s1b]

    def second(self, i):
        self.sums[i].second()
        self.using[self.units[i][2:]] += [self.sums[i].s2a, self.sums[i].s2b]

    def third(self, i):
        here, n = self.here, self.here.n
        mine = self.sums[i].third()
        self.sent_of[i] = []
        for j in range(1, n):
            self.sent_of[i].append(
                here.send(
                    mine.at[lax.rem(here.z + j, n)],
                    self.r3[i].at[j - 1],
                    self.z_sems.at[i, j - 1, 0],
                    self.z_sems.at[i, j - 1, 1],
                    here.at(dz=j),
                )
            )
        self.using[self.units[i][2:]] += self.sent_of[i]
        self.mine_of[i] = mine

    def final(self, i):
        total = self.mine_of[i][self.here.z].astype(jnp.float32)
        for j in range(1, self.here.n):
            self.sent_of[i][j - 1].wait_recv()
            total = total + self.r3[i][j - 1].astype(jnp.float32)
        self.outs[i][...] = total

    def move(self, t, lags):
        lag2, lag3, lag4 = lags
        count = len(self.units)
        if 0 <= t - lag2 < count:
            self.second(t - lag2)
        if 0 <= t - lag3 < count:
            self.third(t - lag3)
        if 0 <= t - lag4 < count:
            self.final(t - lag4)


def plan_sums(pairs, left_shapes, right_shapes, n, most):
    low = jnp.bfloat16
    dma = pltpu.SemaphoreType.DMA
    shapes, units, seen = [], [], {}
    for left, right in pairs:
        shape = (left_shapes[left][2], right_shapes[right][1])
        seen[shape] = seen.get(shape, 0) + 1
        shapes.append(shape)
    classes = list(seen)
    slots = [min(seen[s], most) for s in classes]
    used = {s: 0 for s in classes}
    for (left, right), shape in zip(pairs, shapes):
        pool = classes.index(shape)
        units.append((left, right, pool, used[shape] % slots[pool]))
        used[shape] += 1
    count = len(pairs)
    scratch = [pltpu.VMEM(shape, low) for shape in left_shapes]
    scratch += [pltpu.VMEM((2, *shape), low) for shape in right_shapes]
    scratch += [pltpu.VMEM((s, n, 2, 2, *shape), low) for s, shape in zip(slots, classes)]
    halves = [(k, cols // 2) for k, cols in shapes]
    for _ in range(2):
        scratch += [pltpu.VMEM((n, 2, *half), low) for half in halves]
    for _ in range(2):
        scratch += [pltpu.VMEM((n, *half), low) for half in halves]
    scratch += [pltpu.VMEM((n - 1, *shape), low) for shape in shapes]
    scratch += [
        dma((len(left_shapes), 3)),
        dma((len(right_shapes), 3)),
        dma((count, 4, 2)),
        dma((count, n - 1, 2)),
    ]
    return units, shapes, scratch, len(classes)


def taker(refs):
    refs = list(refs)

    def take(number):
        taken = refs[:number]
        del refs[:number]
        return taken

    return take


def last_kernel(dp_count, units, left_count, right_count, pool_count, *refs):
    n = dp_count
    count = len(units)
    take = taker(refs)
    lefts_in, rights_in = take(left_count), take(right_count)
    embed_in, gains_in = take(2)
    outs = take(count)
    gathered, gains_out = take(2)
    here = Place(n)
    sums = GradSums(here, units, lefts_in, rights_in, outs, take, pool_count)
    gain_send, gain_recv, gain_sems, own_sem, near_sems, plane_sems = take(6)
    z, x, y, c = here.z, here.x, here.y, here.c

    here.greet()

    own = pltpu.make_async_copy(embed_in, gathered.at[z, x, y, c], own_sem)
    own.start()
    for j in range(1, n):
        here.send(
            embed_in,
            gathered.at[z, x, y, c],
            plane_sems.at[j - 1, 0],
            plane_sems.at[j - 1, 1],
            here.at(dz=j),
        )
    width = embed_in.shape[1]
    left_half, right_half = pl.ds(0, width // 2), pl.ds(width // 2, width // 2)

    def embed_near(j):
        plane = lax.rem(z + n - j, n)
        if j:
            here.expect(gathered.at[plane, x, y, c], plane_sems.at[j - 1, 1])
        else:
            own.wait()
        a = gathered.at[plane, x, y, c, :, left_half]
        b = gathered.at[plane, x, y, c, :, right_half]
        here.send(a, a, near_sems.at[j, 0, 0], near_sems.at[j, 0, 1], here.at(dx=1))
        here.send(b, b, near_sems.at[j, 1, 0], near_sems.at[j, 1, 1], here.at(dy=1))

    def embed_far(j):
        plane = lax.rem(z + n - j, n)
        here.expect(gathered.at[plane, 1 - x, y, c, :, left_half], near_sems.at[j, 0, 1])
        here.expect(gathered.at[plane, x, 1 - y, c, :, right_half], near_sems.at[j, 1, 1])
        a = gathered.at[plane, :, y, c, :, left_half]
        b = gathered.at[plane, x, :, c, :, right_half]
        here.send(a, a, near_sems.at[j, 2, 0], near_sems.at[j, 2, 1], here.at(dy=1))
        here.send(b, b, near_sems.at[j, 3, 0], near_sems.at[j, 3, 1], here.at(dx=1))

    def embed_across(j):
        plane = lax.rem(z + n - j, n)
        here.expect(gathered.at[plane, :, 1 - y, c, :, left_half], near_sems.at[j, 2, 1])
        here.expect(gathered.at[plane, 1 - x, :, c, :, right_half], near_sems.at[j, 3, 1])
        a = gathered.at[plane, :, :, c]
        here.send(a, a, near_sems.at[j, 4, 0], near_sems.at[j, 4, 1], here.at(dc=1))

    def embed_done(j):
        plane = lax.rem(z + n - j, n)
        here.expect(gathered.at[plane, :, :, 1 - c], near_sems.at[j, 4, 1])

    def gains(stage):
        if stage == 0:
            gain_send[0] = gains_in[...]
        elif stage <= 3:
            here.expect(gain_recv.at[stage - 1], gain_sems.at[stage - 1, 1])
            gain_send[stage] = gain_send[stage - 1] + gain_recv[stage - 1]
        if stage < 3:
            peer = (here.at(dc=1), here.at(dx=1), here.at(dy=1))[stage]
            here.send(
                gain_send.at[stage],
                gain_recv.at[stage],
                gain_sems.at[stage, 0],
                gain_sems.at[stage, 1],
                peer,
            )
        elif stage == 3:
            for j in range(1, n):
                here.send(
                    gain_send.at[3],
                    gain_recv.at[2 + j],
                    gain_sems.at[2 + j, 0],
                    gain_sems.at[2 + j, 1],
                    here.at(dz=j),
                )
        else:
            total = gain_send[3]
            for j in range(1, n):
                here.expect(gain_recv.at[2 + j], gain_sems.at[2 + j, 1])
                total = total + gain_recv[2 + j]
            gains_out[...] = total

    for i in range(count):
        sums.need(i)
    for t in range(max(count + LAGS[2], n + 5)):
        if t < count:
            sums.product(t)
        if t == 0:
            embed_near(0)
        if 0 <= t - 1 < 5:
            gains(t - 1)
        if 1 <= t - 2 < n:
            embed_near(t - 2)
        sums.move(t, LAGS)
        if 0 <= t - 3 < n:
            embed_far(t - 3)
        if 0 <= t - 4 < n:
            embed_across(t - 4)
        if 0 <= t - 5 < n:
            embed_done(t - 5)
    here.finish()


def last_sums(pairs, lefts, rights, embed_low, gains, dp_count):
    n = dp_count
    low = jnp.bfloat16
    dma = pltpu.SemaphoreType.DMA
    hbm = pl.BlockSpec(memory_space=pl.ANY)
    vmem = pl.BlockSpec(memory_space=pltpu.VMEM)
    units, shapes, scratch, pool_count = plan_sums(
        pairs, [a.shape for a in lefts], [a.shape for a in rights], n, 6
    )
    count = len(pairs)
    tokens, width = embed_low.shape
    scratch += [
        pltpu.VMEM((4, 8, width), jnp.float32),
        pltpu.VMEM((2 + n, 8, width), jnp.float32),
        dma((2 + n, 2)),
        dma,
        dma((n, 5, 2)),
        dma((n - 1, 2)),
    ]
    results = pl.pallas_call(
        functools.partial(last_kernel, n, units, len(lefts), len(rights), pool_count),
        out_shape=[jax.ShapeDtypeStruct(shape, jnp.float32) for shape in shapes]
        + [
            jax.ShapeDtypeStruct((n, 2, 2, 2, tokens, width), low),
            jax.ShapeDtypeStruct((8, width), jnp.float32),
        ],
        in_specs=[hbm] * (len(lefts) + len(rights)) + [vmem, vmem],
        out_specs=[vmem] * count + [hbm, vmem],
        scratch_shapes=scratch,
        compiler_params=pltpu.CompilerParams(
            collective_id=2, has_side_effects=True, vmem_limit_bytes=VMEM_CAP
        ),
        name="last_sums",
    )(*lefts, *rights, embed_low, gains)
    return results[:count], results[count], results[count + 1]


BACK_PAIRS = ((4, 8), (3, 6), (3, 7), (2, 5), (1, 4), (0, 0), (0, 1), (0, 2), (0, 3))


class Streamed(typing.NamedTuple):
    gate_pre: typing.Any
    up_pre: typing.Any
    h_out: typing.Any
    h_mid: typing.Any
    embedded: typing.Any
    key_values: typing.Any
    w_query: typing.Any
    w_key: typing.Any
    w_value: typing.Any
    w_out: typing.Any
    w_gate: typing.Any
    w_up: typing.Any
    w_down: typing.Any
    c_query: typing.Any
    c_key: typing.Any
    c_value: typing.Any
    c_out: typing.Any
    cot_patches: typing.Any


def back_kernel(dp_count, units, pool_count, *refs):
    n = dp_count
    take = taker(refs)
    lefts_in = take(5)
    hbm = Streamed(*take(len(Streamed._fields)))
    (cot_bytes, p_query, p_key, p_value, cross_lse, gains, starts, ends, queries, lse) = take(10)
    outs = take(len(units))
    grad_gains, g_attn, g_query, g_key, g_value, g_embed = take(6)
    here = Place(n)
    sums = GradSums(here, units, lefts_in, [None] * 8 + [hbm.cot_patches], outs, take, pool_count)
    w, tile_pre, grad_out, grad_ffn, grad_mid, kv, halo = take(7)
    w_sems, tile_sems, pre_sems, kv_sems, halo_sems = take(5)
    g_gate = [sums.rights[0].at[0], sums.rights[2].at[0]]
    g_up = [sums.rights[1].at[0], sums.rights[3].at[0]]
    g_branch, g_pquery, g_pkey, g_pvalue, cot_patches = [ref.at[0] for ref in sums.rights[4:]]
    tokens, width = cot_bytes.shape
    patches = p_query.shape[0]
    tile = 256
    first_tiles = g_gate[0].shape[1] // tile
    tiles = first_tiles + g_gate[1].shape[1] // tile
    rank = (here.x * 2 + here.y) * 2 + here.c
    lane = lax.broadcasted_iota(jnp.int32, (1, 128), 1)
    sides = [jnp.where(lane < HD, 1.0, 0.0).astype(LOW), jnp.where(lane < HD, 0.0, 1.0).astype(LOW)]
    byte_pos = lax.broadcasted_iota(jnp.int32, (patches, tokens), 1)

    here.greet()

    def load_w(slot, source):
        copy = pltpu.make_async_copy(source, w.at[slot], w_sems.at[slot])
        copy.start()
        return copy

    def load_pre(source):
        copies = []
        for b in range(width // tile):
            copy = pltpu.make_async_copy(
                source.at[:, pl.ds(b * tile, tile)],
                tile_pre.at[b // 2, b % 2],
                pre_sems.at[b],
            )
            copy.start()
            copies.append(copy)
        return copies

    def pre_rows(copies):
        for copy in copies:
            copy.wait()
        return jnp.concatenate([tile_pre[b // 2, b % 2] for b in range(width // tile)], axis=1)

    for i in (4, 3, 2, 1, 0):
        sums.left(i)
    sums.right(8)
    cross = [load_w(i, a) for i, a in enumerate((hbm.c_out, hbm.c_query, hbm.c_key, hbm.c_value))]
    h_out_copies = load_pre(hbm.h_out)

    def tile_copies(t):
        slot = lax.rem(t, 2)
        span = pl.ds(pl.multiple_of(t * tile, tile), tile)
        return [
            pltpu.make_async_copy(source, target, tile_sems.at[slot, k])
            for k, (source, target) in enumerate(
                (
                    (hbm.w_gate.at[:, span], w.at[slot, :, pl.ds(0, tile)]),
                    (hbm.w_up.at[:, span], w.at[slot, :, pl.ds(tile, tile)]),
                    (hbm.w_down.at[span], w.at[2, pl.ds(pl.multiple_of(slot * tile, tile), tile)]),
                    (hbm.gate_pre.at[:, span], tile_pre.at[slot, 0]),
                    (hbm.up_pre.at[:, span], tile_pre.at[slot, 1]),
                )
            )
        ]

    def member():
        return (byte_pos >= starts[...]) & (byte_pos < ends[...])

    def head_lse(ref, head):
        return jnp.sum(jnp.where(lane == head, ref[...], 0.0), axis=1, keepdims=True)

    def cross_heads():
        cross[0].wait()
        allowed = member()
        grad_ffn[:patches] = times_t(cot_patches[...], w[0]).astype(LOW).astype(F32)

        def heads_pair(pair, carry):
            span = pl.ds(pl.multiple_of(pair * 128, 128), 128)
            q2, k2, v2 = p_query[:, span], p_key[:, span], p_value[:, span]
            gp2 = grad_ffn[:patches, span].astype(LOW)
            parts = []
            for side in range(2):
                total = head_lse(cross_lse, pair * 2 + side)
                scores = times_t(q2 * sides[side], k2) * SCORE_SCALE
                probs = jnp.where(allowed, jnp.exp(jnp.where(allowed, scores, total) - total), 0.0)
                grad_score = soft_back(probs, times_t(gp2 * sides[side], v2))
                parts.append(
                    (
                        matmul(grad_score, k2),
                        t_times(grad_score, q2),
                        t_times(probs.astype(LOW), gp2),
                    )
                )
            mine = lane < HD
            g_pquery[:, span] = (jnp.where(mine, parts[0][0], parts[1][0]) * SCORE_SCALE).astype(LOW)
            g_pkey[:, span] = (jnp.where(mine, parts[0][1], parts[1][1]) * SCORE_SCALE).astype(LOW)
            g_pvalue[:, span] = jnp.where(mine, parts[0][2], parts[1][2]).astype(LOW)
            return carry

        lax.fori_loop(0, width // 128, heads_pair, 0)
        for i in (5, 6, 7):
            sums.right(i)

    def split(v):
        high = v.astype(LOW)
        return high, (v - high.astype(F32)).astype(LOW)

    def unit_of(v):
        inv_rms = lax.rsqrt(jnp.mean(v * v, axis=-1, keepdims=True) + EPSILON)
        return v * inv_rms, inv_rms

    def through_norm(grad, rows, number):
        normed, inv_rms = unit_of(rows)
        grad_in, grad_gain = norm_back(
            grad.astype(LOW).astype(F32), normed, inv_rms, gains[number : number + 1]
        )
        grad_gains[number : number + 1] = grad_gain[None]
        return grad_in

    loaded = {}

    def cross_in():
        for copy in cross[1:]:
            copy.wait()
        length = (ends[...] - starts[...]).astype(F32)
        grad_pooled = cot_patches[...].astype(F32) + times_t(g_pquery[...], w[1]).astype(
            LOW
        ).astype(F32)
        high, rest = split(grad_pooled / length)
        inside = jnp.where(member(), 1.0, 0.0).astype(LOW)
        grad_x = t_times(inside, high) + t_times(inside, rest)
        grad_x = grad_x + times_t(g_pkey[...], w[2]) + times_t(g_pvalue[...], w[3])
        grad_gains[...] = jnp.zeros_like(grad_gains)
        total = cot_bytes[...].astype(F32) + through_norm(grad_x, pre_rows(h_out_copies), 2)
        grad_out[...] = total
        g_branch[...] = total.astype(LOW)
        grad_ffn[...] = jnp.zeros_like(grad_ffn)
        sums.right(4)
        loaded[3] = load_w(3, hbm.w_out)

    def feed(part):
        first, last = ((0, first_tiles), (first_tiles, tiles))[part]
        for copy in tile_copies(first):
            copy.start()

        def one(t, carry):
            slot = lax.rem(t, 2)
            for copy in tile_copies(t):
                copy.wait()

            @pl.when(t + 1 < last)
            def _():
                for copy in tile_copies(t + 1):
                    copy.start()

            span = pl.ds(pl.multiple_of((t - first) * tile, tile), tile)
            down_rows = w[2, pl.ds(pl.multiple_of(slot * tile, tile), tile)]
            grad_hidden = times_t(g_branch[...], down_rows).astype(LOW).astype(F32)
            gate, up = tile_pre[slot, 0], tile_pre[slot, 1]
            sig = jax.nn.sigmoid(gate)
            gg = (grad_hidden * up * sig * (1.0 + gate * (1.0 - sig))).astype(LOW)
            gu = (grad_hidden * (gate * sig)).astype(LOW)
            g_gate[part][:, span] = gg
            g_up[part][:, span] = gu
            grad_ffn[...] += times_t(gg, w[slot, :, :tile]) + times_t(
                gu, w[slot, :, tile : 2 * tile]
            )
            return carry

        lax.fori_loop(first, last, one, 0)
        sums.right(2 * part)
        sums.right(2 * part + 1)

    def feed_in():
        copies = load_pre(hbm.h_mid)
        loaded[3].wait()
        grad_mid[...] = grad_out[...] + through_norm(grad_ffn[...], pre_rows(copies), 1)
        g_attn[...] = grad_mid[...].astype(LOW)
        g_query[...] = times_t(g_attn[...], w[3]).astype(LOW)
        loaded[1] = load_w(1, hbm.w_query)
        loaded[2] = load_w(2, hbm.w_key)
        loaded[3] = load_w(3, hbm.w_value)
        loaded[0] = load_pre(hbm.embedded)

    own_key, own_value = grad_ffn, grad_out
    sent = w.at[0]

    def kv_copy(pair):
        slot = lax.rem(pair, 2)
        span = pl.ds(pl.multiple_of(pair * 128, 128), 128)
        return pltpu.make_async_copy(hbm.key_values.at[:, :, span], kv.at[slot], kv_sems.at[slot])

    def attend(first, last):
        row = lax.broadcasted_iota(jnp.int32, (tokens, tokens), 0)
        col = lax.broadcasted_iota(jnp.int32, (tokens, tokens), 1)
        mine = col <= row
        far_bias = jnp.where(rank >= 2, 0.0, NEG_BIG)
        near_bias = jnp.where(rank >= 1, 0.0, NEG_BIG)
        kv_copy(first).start()

        def three(edge, middle):
            return jnp.concatenate(
                [
                    jnp.where(mine, 0.0, edge).astype(LOW),
                    middle.astype(LOW),
                    jnp.where(mine, edge, 0.0).astype(LOW),
                ],
                axis=1,
            )

        def heads_pair(pair, carry):
            kv_copy(pair).wait()

            @pl.when(pair + 1 < last)
            def _():
                kv_copy(pair + 1).start()

            slot = lax.rem(pair, 2)
            span = pl.ds(pl.multiple_of(pair * 128, 128), 128)
            q2, ga2 = queries[:, span], g_query[:, span]
            k2, v2 = kv[slot, 0], kv[slot, 1]
            parts = []
            for side in range(2):
                total = head_lse(lse, pair * 2 + side)
                scores = times_t(q2 * sides[side], k2) * SCORE_SCALE
                edge = jnp.where(mine, scores[:, 2 * tokens :], scores[:, :tokens] + far_bias)
                edge = jnp.exp(edge - total)
                middle = jnp.exp(scores[:, tokens : 2 * tokens] + near_bias - total)
                grad_prob = times_t(ga2 * sides[side], v2)
                grad_edge = jnp.where(mine, grad_prob[:, 2 * tokens :], grad_prob[:, :tokens])
                grad_middle = grad_prob[:, tokens : 2 * tokens]
                row_total = jnp.sum(edge * grad_edge, axis=1, keepdims=True) + jnp.sum(
                    middle * grad_middle, axis=1, keepdims=True
                )
                grad_score = three(edge * (grad_edge - row_total), middle * (grad_middle - row_total))
                parts.append(
                    (
                        matmul(grad_score, k2),
                        t_times(grad_score, q2),
                        t_times(three(edge, middle), ga2),
                    )
                )
            left = lane < HD
            g_query[:, span] = (jnp.where(left, parts[0][0], parts[1][0]) * SCORE_SCALE).astype(LOW)
            for number, own, scale in ((1, own_key, SCORE_SCALE), (2, own_value, 1.0)):
                grad = jnp.where(left, parts[0][number], parts[1][number]) * scale
                own[:, span] = grad[2 * tokens :]
                start = (number - 1) * 2 * tokens
                sent[start : start + 2 * tokens, span] = grad[: 2 * tokens].astype(LOW)
            return carry

        lax.fori_loop(first, last, heads_pair, 0)

    def halo_send():
        for back in (1, 2):
            target = rank - back
            for number in range(2):
                here.send_if(
                    target >= 0,
                    sent.at[pl.ds((2 * number + 2 - back) * tokens, tokens)],
                    halo.at[back - 1, number],
                    halo_sems.at[back - 1, number, 0],
                    halo_sems.at[back - 1, number, 1],
                    (here.z, jnp.maximum(target, 0) // 4, lax.rem(jnp.maximum(target, 0), 4)),
                )

    def halo_add():
        for back in (1, 2):

            @pl.when(rank + back < 8)
            def _():
                for number, own in ((0, own_key), (1, own_value)):
                    here.expect(halo.at[back - 1, number], halo_sems.at[back - 1, number, 1])
                    own[...] += halo[back - 1, number].astype(F32)

        g_key[...] = own_key[...].astype(LOW)
        g_value[...] = own_value[...].astype(LOW)

    def embed_in():
        for slot in (1, 2, 3):
            loaded[slot].wait()
        grad = times_t(g_query[...], w[1]) + times_t(g_key[...], w[2]) + times_t(g_value[...], w[3])
        total = grad_mid[...] + through_norm(grad, pre_rows(loaded[0]), 0)
        g_embed[...] = total.astype(LOW)

    sums.product(0)
    cross_heads()
    sums.product(1)
    sums.product(2)
    sums.product(3)
    cross_in()
    sums.second(0)
    sums.product(4)
    sums.second(1)
    feed(0)
    sums.product(5)
    sums.product(6)
    sums.second(2)
    sums.third(0)
    feed(1)
    sums.product(7)
    sums.product(8)
    sums.second(3)
    sums.third(1)
    feed_in()
    sums.second(4)
    sums.third(2)
    pairs = width // 128
    attend(0, pairs // 2)
    sums.second(5)
    sums.third(3)
    attend(pairs // 2, pairs)
    halo_send()
    sums.second(6)
    sums.third(4)
    for i in range(4):
        sums.final(i)
    halo_add()
    sums.second(7)
    sums.third(5)
    embed_in()
    sums.second(8)
    sums.third(6)
    sums.third(7)
    sums.third(8)
    for i in range(4, 9):
        sums.final(i)
    here.finish()


def back_sums(lefts, streamed, kept, dp_count):
    n = dp_count
    low = jnp.bfloat16
    dma = pltpu.SemaphoreType.DMA
    hbm = pl.BlockSpec(memory_space=pl.ANY)
    vmem = pl.BlockSpec(memory_space=pltpu.VMEM)
    tokens, ff = streamed.gate_pre.shape
    patches, width = streamed.cot_patches.shape
    tile = 256
    first = (ff // tile + 1) // 2 * tile
    one = jax.ShapeDtypeStruct
    right_shapes = [(tokens, first)] * 2 + [(tokens, ff - first)] * 2
    right_shapes += [(tokens, width), (patches, width)]
    right_shapes += [(tokens, width)] * 2 + [(patches, width)]
    units, shapes, scratch, pool_count = plan_sums(
        BACK_PAIRS, [a.shape for a in lefts], right_shapes, n, 4
    )
    count = len(units)
    scratch += [
        pltpu.VMEM((4, width, width), low),
        pltpu.VMEM((2, 2, tokens, tile), F32),
        pltpu.VMEM((tokens, width), F32),
        pltpu.VMEM((tokens, width), F32),
        pltpu.VMEM((tokens, width), F32),
        pltpu.VMEM((2, 2, 3 * tokens, 128), low),
        pltpu.VMEM((2, 2, tokens, width), low),
        dma((4,)),
        dma((2, 5)),
        dma((width // tile,)),
        dma((2,)),
        dma((2, 2, 2)),
    ]
    results = pl.pallas_call(
        functools.partial(back_kernel, n, units, pool_count),
        out_shape=[one(shape, F32) for shape in shapes]
        + [one((8, width), F32)]
        + [one((tokens, width), low)] * 5,
        in_specs=[hbm] * (len(lefts) + len(streamed)) + [vmem] * len(kept),
        out_specs=[vmem] * (count + 6),
        scratch_shapes=scratch,
        compiler_params=pltpu.CompilerParams(
            collective_id=1, has_side_effects=True, vmem_limit_bytes=63 * 1024 * 1024
        ),
        name="back_sums",
    )(*lefts, *streamed, *kept)
    return results[:count], results[count:]


def spread_kernel(lists, rows_of, grads, out, counts, stacked):
    step = pl.program_id(0)
    group, tokens = grads.shape[0], grads.shape[1]

    @pl.when(step == 0)
    def _():
        out[...] = jnp.zeros_like(out)
        counts[...] = jnp.zeros_like(counts)

    byte_iota = lax.broadcasted_iota(jnp.int32, (SLOTS, tokens), 1)
    for s in range(group):
        pick = (jnp.bitwise_and(lists[s], 255) == byte_iota).astype(jnp.bfloat16)
        stacked[s * SLOTS : (s + 1) * SLOTS, :] = matmul(pick, grads[s]).astype(jnp.bfloat16)
    row_iota = lax.broadcasted_iota(jnp.int32, (out.shape[0], group * SLOTS), 0)
    onto = (rows_of[0] == row_iota).astype(jnp.float32)
    counts[...] += jnp.sum(onto, axis=1, keepdims=True)
    out[...] += matmul(onto.astype(jnp.bfloat16), stacked[...])


def spread(entries, gathered, rows_dev):
    sources, tokens, width = gathered.shape
    group = 8
    steps = sources // group
    rows_of = jnp.right_shift(entries, 8).reshape(steps, 1, group * SLOTS)
    out, counts = pl.pallas_call(
        spread_kernel,
        grid=(steps,),
        out_shape=[
            jax.ShapeDtypeStruct((rows_dev, width), jnp.float32),
            jax.ShapeDtypeStruct((rows_dev, 1), jnp.float32),
        ],
        in_specs=[
            pl.BlockSpec((group, SLOTS, 1), lambda i: (i, 0, 0)),
            pl.BlockSpec((1, 1, group * SLOTS), lambda i: (i, 0, 0)),
            pl.BlockSpec((group, tokens, width), lambda i: (i, 0, 0)),
        ],
        out_specs=[
            pl.BlockSpec((rows_dev, width), lambda i: (0, 0)),
            pl.BlockSpec((rows_dev, 1), lambda i: (0, 0)),
        ],
        scratch_shapes=[pltpu.VMEM((group * SLOTS, width), jnp.bfloat16)],
        compiler_params=pltpu.CompilerParams(vmem_limit_bytes=VMEM_CAP),
        name="spread",
    )(entries, rows_of, gathered)
    return out, counts[:, 0].astype(jnp.int32)


WEIGHT_STEPS = tuple(((i, 0, 2), (i, 1, 2)) for i in (0, 1, 2, 3, 4, 5, 6, 8, 9, 7, 10))


def by_rows(a, dp_count):
    depth, total = a.shape
    pairs = dp_count * 4
    both = total // pairs
    a = a.T.reshape(pairs, both, depth)
    rows = -(-(both // 2) // 16) * 16
    return jnp.stack([a[:, :rows], a[:, both - rows :]])


def own_rows(block, rows):
    core = lax.axis_index(SUB) % 2
    return jnp.where(core == 0, block[:rows], block[block.shape[0] - rows :])


def body(
    byte_ids,
    hash_ids,
    lengths,
    byte_table,
    hash_table,
    norm_attn,
    norm_ffn,
    norm_cross,
    w_query,
    w_key,
    w_value,
    w_out,
    w_gate,
    w_up,
    w_down,
    c_query,
    c_key,
    c_value,
    c_out,
    cot_bytes,
    cot_patches,
):
    dp_count = lax.axis_size(DP)
    rs_count = lax.axis_size(SEQ)
    all_count = dp_count * rs_count
    rank_seq = lax.axis_index(SEQ)
    rank_table = lax.axis_index(DP) * rs_count + rank_seq
    tokens, gram_count = hash_ids.shape
    rows_dev, model_width = hash_table.shape
    head_count = model_width // HD
    request_count = tokens * gram_count
    slot_count = 2 * request_count // all_count
    flat_ids = hash_ids.reshape(request_count)
    owners = flat_ids // rows_dev
    ordering = jnp.argsort(owners, stable=True)
    owners_sorted = owners[ordering]
    per_owner = jnp.sum(
        (owners[:, None] == jnp.arange(all_count, dtype=jnp.int32)[None, :]).astype(jnp.int32),
        axis=0,
    )
    first_slot = jnp.cumsum(per_owner) - per_owner
    place_sorted = (
        owners_sorted * slot_count
        + jnp.arange(request_count, dtype=jnp.int32)
        - first_slot[owners_sorted]
    )
    placement = jnp.zeros((request_count,), jnp.int32).at[ordering].set(place_sorted)
    requests = jnp.full((all_count * slot_count,), -1, jnp.int32).at[placement].set(flat_ids)
    requests = requests.reshape(dp_count, rs_count, slot_count)
    incoming = lax.all_to_all(
        lax.all_to_all(requests, DP, split_axis=0, concat_axis=0, tiled=True),
        SEQ,
        split_axis=1,
        concat_axis=1,
        tiled=True,
    )
    present = incoming >= 0
    safe_rows = jnp.where(present, incoming - rank_table * rows_dev, 0)
    served = jnp.where(present[..., None], hash_table[safe_rows], jnp.zeros((), jnp.bfloat16))
    returned = lax.all_to_all(
        lax.all_to_all(served, DP, split_axis=0, concat_axis=0, tiled=True),
        SEQ,
        split_axis=1,
        concat_axis=1,
        tiled=True,
    )
    fetched = returned.reshape(all_count * slot_count, model_width)[placement]
    fetched = fetched.astype(jnp.float32).reshape(tokens, gram_count, model_width)
    one_hot = byte_ids[:, None] == jnp.arange(BYTE_VALUES, dtype=jnp.int32)[None, :]
    embedded = matmul(one_hot.astype(jnp.bfloat16), byte_table) + jnp.sum(fetched, axis=1)
    row_counts = (
        jnp.zeros((rows_dev,), jnp.int32)
        .at[safe_rows.reshape(-1)]
        .add(present.reshape(-1).astype(jnp.int32))
    )
    weight_list = (
        w_query,
        w_key,
        w_value,
        w_out,
        w_gate,
        w_up,
        w_down,
        c_query,
        c_key,
        c_value,
        c_out,
    )
    gathered = (
        lax.all_gather(weight_list[0], DP, axis=0, tiled=True),
        lax.all_gather(weight_list[1], DP, axis=0, tiled=True),
        lax.all_gather(weight_list[2], DP, axis=0, tiled=True),
        lax.all_gather(weight_list[3], DP, axis=0, tiled=True),
        lax.all_gather(weight_list[4], DP, axis=0, tiled=True),
        lax.all_gather(weight_list[5], DP, axis=0, tiled=True),
        lax.all_gather(weight_list[6], DP, axis=0, tiled=True),
        lax.all_gather(weight_list[7], DP, axis=0, tiled=True),
        lax.all_gather(weight_list[8], DP, axis=0, tiled=True),
        lax.all_gather(weight_list[9], DP, axis=0, tiled=True),
        lax.all_gather(weight_list[10], DP, axis=0, tiled=True),
    )
    (
        full_query,
        full_key,
        full_value,
        full_out,
        full_gate,
        full_up,
        full_down,
        full_cquery,
        full_ckey,
        full_cvalue,
        full_cout,
    ) = gathered
    x_attn, normed_attn, scale_attn = normalize(embedded, norm_attn)
    queries = matmul(x_attn, full_query).astype(jnp.bfloat16).reshape(tokens, head_count, HD)
    key_rows = matmul(x_attn, full_key).astype(jnp.bfloat16).reshape(tokens, head_count, HD)
    value_rows = matmul(x_attn, full_value).astype(jnp.bfloat16).reshape(tokens, head_count, HD)
    behind = (WIN - 2) // tokens + 1
    key_parts = []
    value_parts = []
    for offset_back in range(behind, 0, -1):
        far_keys, far_values = passed_along((key_rows, value_rows), SEQ, offset_back)
        key_parts.append(far_keys)
        value_parts.append(far_values)
    all_keys = jnp.concatenate(key_parts + [key_rows], axis=0)
    all_values = jnp.concatenate(value_parts + [value_rows], axis=0)
    q_rows = min(tokens, 512)
    key_span = (WIN - 1 + q_rows - 1) // q_rows * q_rows
    base_key = (rank_seq - behind) * tokens
    block_index = 0
    q_start = block_index * q_rows
    k_start = behind * tokens + q_start - key_span
    allowed = window_mask(
        rank_seq * tokens + q_start, base_key + k_start, q_rows, q_rows + key_span
    )
    scores = (
        jnp.einsum("qhd,khd->hqk", queries, all_keys, preferred_element_type=jnp.float32)
        * SCORE_SCALE
    )
    prob_block, log_total = soft_forward(scores, allowed)
    attended_parts = jnp.einsum(
        "hqk,khd->qhd",
        prob_block.astype(jnp.bfloat16),
        all_values,
        preferred_element_type=jnp.float32,
    )
    lse_parts = [log_total]
    attended = attended_parts.astype(jnp.bfloat16).reshape(tokens, model_width)
    h_mid = embedded + matmul(attended, full_out)
    x_ffn, normed_ffn, scale_ffn = normalize(h_mid, norm_ffn)
    gate_pre = matmul(x_ffn, full_gate)
    up_pre = matmul(x_ffn, full_up)
    gate_sig = jax.nn.sigmoid(gate_pre)
    silu_val = gate_pre * gate_sig
    hidden = (silu_val * up_pre).astype(jnp.bfloat16)
    h_out = h_mid + matmul(hidden, full_down)
    byte_states = h_out.astype(jnp.bfloat16)
    x_cross, normed_cross, scale_cross = normalize(h_out, norm_cross)
    patch_len = lengths[0]
    patch_count = patch_len.shape[0]
    patch_end = jnp.cumsum(patch_len)
    patch_start = patch_end - patch_len
    byte_pos = jnp.arange(tokens, dtype=jnp.int32)
    member = (byte_pos[None, :] >= patch_start[:, None]) & (byte_pos[None, :] < patch_end[:, None])
    length_f = patch_len.astype(jnp.float32)[:, None]
    pooled = matmul(member.astype(jnp.bfloat16), x_cross) / length_f
    pooled_low = pooled.astype(jnp.bfloat16)
    p_query = (
        matmul(pooled_low, full_cquery).astype(jnp.bfloat16).reshape(patch_count, head_count, HD)
    )
    p_key = matmul(x_cross, full_ckey).astype(jnp.bfloat16).reshape(tokens, head_count, HD)
    p_value = matmul(x_cross, full_cvalue).astype(jnp.bfloat16).reshape(tokens, head_count, HD)
    cross_scores = (
        jnp.einsum("phd,thd->hpt", p_query, p_key, preferred_element_type=jnp.float32) * SCORE_SCALE
    )
    cross_prob, cross_lse = soft_forward(cross_scores, member[None])
    p_attended = (
        jnp.einsum(
            "hpt,thd->phd",
            cross_prob.astype(jnp.bfloat16),
            p_value,
            preferred_element_type=jnp.float32,
        )
        .astype(jnp.bfloat16)
        .reshape(patch_count, model_width)
    )
    patch_states = (pooled + matmul(p_attended, full_cout)).astype(jnp.bfloat16)
    grad_c_out = t_times(p_attended, cot_patches)
    grad_patt = (
        times_t(cot_patches, full_cout).astype(jnp.bfloat16).reshape(patch_count, head_count, HD)
    )
    cross_again = (
        jnp.einsum("phd,thd->hpt", p_query, p_key, preferred_element_type=jnp.float32) * SCORE_SCALE
    )
    cross_full = soft_again(cross_again, member[None], cross_lse)
    grad_cprob = jnp.einsum("phd,thd->hpt", grad_patt, p_value, preferred_element_type=jnp.float32)
    grad_cscore = soft_back(cross_full, grad_cprob)
    grad_pquery = (
        (
            jnp.einsum("hpt,thd->phd", grad_cscore, p_key, preferred_element_type=jnp.float32)
            * SCORE_SCALE
        )
        .astype(jnp.bfloat16)
        .reshape(patch_count, model_width)
    )
    grad_pkey = (
        (
            jnp.einsum("hpt,phd->thd", grad_cscore, p_query, preferred_element_type=jnp.float32)
            * SCORE_SCALE
        )
        .astype(jnp.bfloat16)
        .reshape(tokens, model_width)
    )
    grad_pvalue = (
        jnp.einsum(
            "hpt,phd->thd",
            cross_full.astype(jnp.bfloat16),
            grad_patt,
            preferred_element_type=jnp.float32,
        )
        .astype(jnp.bfloat16)
        .reshape(tokens, model_width)
    )
    grad_c_query = t_times(pooled_low, grad_pquery)
    grad_c_key = t_times(x_cross, grad_pkey)
    grad_c_value = t_times(x_cross, grad_pvalue)
    grad_pooled = cot_patches.astype(jnp.float32) + times_t(grad_pquery, full_cquery).astype(
        jnp.bfloat16
    ).astype(jnp.float32)
    to_bytes = lax.dot_general(
        member.astype(jnp.float32),
        grad_pooled / length_f,
        (((0,), (0,)), ((), ())),
        precision=PRECISE,
    )
    grad_xcross = (
        times_t(grad_pkey, full_ckey) + times_t(grad_pvalue, full_cvalue) + to_bytes
    ).astype(jnp.bfloat16)
    grad_hout_norm, grad_norm_cross = norm_back(
        grad_xcross.astype(jnp.float32), normed_cross, scale_cross, norm_cross
    )
    grad_hout = cot_bytes.astype(jnp.float32) + grad_hout_norm
    grad_branch_f = grad_hout.astype(jnp.bfloat16)
    grad_w_down = t_times(hidden, grad_branch_f)
    grad_hidden = times_t(grad_branch_f, full_down).astype(jnp.bfloat16).astype(jnp.float32)
    grad_gate = (grad_hidden * up_pre * gate_sig * (1.0 + gate_pre * (1.0 - gate_sig))).astype(
        jnp.bfloat16
    )
    grad_up = (grad_hidden * silu_val).astype(jnp.bfloat16)
    grad_w_gate = t_times(x_ffn, grad_gate)
    grad_w_up = t_times(x_ffn, grad_up)
    grad_xffn = (times_t(grad_gate, full_gate) + times_t(grad_up, full_up)).astype(jnp.bfloat16)
    grad_hmid_norm, grad_norm_ffn = norm_back(
        grad_xffn.astype(jnp.float32), normed_ffn, scale_ffn, norm_ffn
    )
    grad_hmid = grad_hout + grad_hmid_norm
    grad_branch_a = grad_hmid.astype(jnp.bfloat16)
    grad_w_out = t_times(attended, grad_branch_a)
    grad_att = times_t(grad_branch_a, full_out).astype(jnp.bfloat16).reshape(tokens, head_count, HD)
    grad_keys_all = jnp.zeros(((behind + 1) * tokens, head_count, HD), jnp.float32)
    grad_values_all = jnp.zeros(((behind + 1) * tokens, head_count, HD), jnp.float32)
    block_index = 0
    q_start = block_index * q_rows
    k_start = behind * tokens + q_start - key_span
    k_stop = k_start + q_rows + key_span
    allowed = window_mask(
        rank_seq * tokens + q_start, base_key + k_start, q_rows, q_rows + key_span
    )
    scores = (
        jnp.einsum("qhd,khd->hqk", queries, all_keys, preferred_element_type=jnp.float32)
        * SCORE_SCALE
    )
    prob_block = soft_again(scores, allowed, lse_parts[block_index])
    grad_prob = jnp.einsum("qhd,khd->hqk", grad_att, all_values, preferred_element_type=jnp.float32)
    grad_score = soft_back(prob_block, grad_prob)
    grad_q_parts = (
        jnp.einsum("hqk,khd->qhd", grad_score, all_keys, preferred_element_type=jnp.float32)
        * SCORE_SCALE
    )
    grad_keys_all = grad_keys_all.at[k_start:k_stop].add(
        jnp.einsum("hqk,qhd->khd", grad_score, queries, preferred_element_type=jnp.float32)
        * SCORE_SCALE
    )
    grad_values_all = grad_values_all.at[k_start:k_stop].add(
        jnp.einsum(
            "hqk,qhd->khd",
            prob_block.astype(jnp.bfloat16),
            grad_att,
            preferred_element_type=jnp.float32,
        )
    )
    grad_keys = grad_keys_all[behind * tokens :]
    grad_values = grad_values_all[behind * tokens :]
    for offset_back in range(behind, 0, -1):
        part_index = behind - offset_back
        far_grad_k, far_grad_v = (
            passed_along(
                grad_keys_all[part_index * tokens : (part_index + 1) * tokens].astype(jnp.bfloat16),
                SEQ,
                -offset_back,
            ).astype(jnp.float32),
            passed_along(
                grad_values_all[part_index * tokens : (part_index + 1) * tokens].astype(
                    jnp.bfloat16
                ),
                SEQ,
                -offset_back,
            ).astype(jnp.float32),
        )
        grad_keys = grad_keys + far_grad_k
        grad_values = grad_values + far_grad_v
    grad_queries = grad_q_parts.astype(jnp.bfloat16).reshape(tokens, model_width)
    grad_keys_low = grad_keys.astype(jnp.bfloat16).reshape(tokens, model_width)
    grad_values_low = grad_values.astype(jnp.bfloat16).reshape(tokens, model_width)
    grad_w_query = t_times(x_attn, grad_queries)
    grad_w_key = t_times(x_attn, grad_keys_low)
    grad_w_value = t_times(x_attn, grad_values_low)
    grad_xattn = (
        times_t(grad_queries, full_query)
        + times_t(grad_keys_low, full_key)
        + times_t(grad_values_low, full_value)
    ).astype(jnp.bfloat16)
    grad_embed_norm, grad_norm_attn = norm_back(
        grad_xattn.astype(jnp.float32), normed_attn, scale_attn, norm_attn
    )
    grad_embed = grad_hmid + grad_embed_norm
    embed_grad = grad_embed.astype(jnp.bfloat16)
    grad_byte_table = lax.dot_general(
        one_hot.astype(jnp.float32), grad_embed, (((0,), (0,)), ((), ())), precision=PRECISE
    )
    per_request = jnp.broadcast_to(
        grad_embed[:, None, :], (tokens, gram_count, model_width)
    ).reshape(request_count, model_width)
    outgoing = (
        jnp.zeros((all_count * slot_count, model_width), jnp.float32).at[placement].set(per_request)
    )
    outgoing = outgoing.reshape(dp_count, rs_count, slot_count, model_width)
    arrived = lax.all_to_all(
        lax.all_to_all(
            outgoing.astype(jnp.bfloat16), DP, split_axis=0, concat_axis=0, tiled=True
        ),
        SEQ,
        split_axis=1,
        concat_axis=1,
        tiled=True,
    ).astype(outgoing.dtype)
    hash_table_grad = (
        jnp.zeros((rows_dev, model_width), jnp.float32)
        .at[safe_rows.reshape(-1)]
        .add(jnp.where(present[..., None], arrived, 0.0).reshape(-1, model_width))
    )
    summed_all = (
        lax.psum_scatter(grad_norm_attn, ALL, scatter_dimension=0, tiled=True),
        lax.psum_scatter(grad_norm_ffn, ALL, scatter_dimension=0, tiled=True),
        lax.psum_scatter(grad_norm_cross, ALL, scatter_dimension=0, tiled=True),
        lax.psum_scatter(grad_w_query, ALL, scatter_dimension=0, tiled=True),
        lax.psum_scatter(grad_w_key, ALL, scatter_dimension=0, tiled=True),
        lax.psum_scatter(grad_w_value, ALL, scatter_dimension=0, tiled=True),
        lax.psum_scatter(grad_w_out, ALL, scatter_dimension=0, tiled=True),
        lax.psum_scatter(grad_w_gate, ALL, scatter_dimension=0, tiled=True),
        lax.psum_scatter(grad_w_up, ALL, scatter_dimension=0, tiled=True),
        lax.psum_scatter(grad_w_down, ALL, scatter_dimension=0, tiled=True),
        lax.psum_scatter(grad_c_query, ALL, scatter_dimension=0, tiled=True),
        lax.psum_scatter(grad_c_key, ALL, scatter_dimension=0, tiled=True),
        lax.psum_scatter(grad_c_value, ALL, scatter_dimension=0, tiled=True),
        lax.psum_scatter(grad_c_out, ALL, scatter_dimension=0, tiled=True),
        lax.psum_scatter(grad_byte_table, ALL, scatter_dimension=0, tiled=True),
    )
    (
        out_norm_attn,
        out_norm_ffn,
        out_norm_cross,
        out_query,
        out_key,
        out_value,
        out_proj,
        out_gate,
        out_up,
        out_down,
        out_cquery,
        out_ckey,
        out_cvalue,
        out_cout,
        out_bytes,
    ) = summed_all
    return (
        byte_states,
        patch_states,
        embed_grad,
        out_bytes,
        hash_table_grad,
        row_counts,
        out_norm_attn,
        out_norm_ffn,
        out_norm_cross,
        out_query,
        out_key,
        out_value,
        out_proj,
        out_gate,
        out_up,
        out_down,
        out_cquery,
        out_ckey,
        out_cvalue,
        out_cout,
    )


def fast_body(
    byte_ids,
    hash_ids,
    lengths,
    byte_table,
    hash_table,
    norm_attn,
    norm_ffn,
    norm_cross,
    w_query,
    w_key,
    w_value,
    w_out,
    w_gate,
    w_up,
    w_down,
    c_query,
    c_key,
    c_value,
    c_out,
    cot_bytes,
    cot_patches,
):
    dp_count = lax.axis_size(DP)
    rs_count = lax.axis_size(SEQ)
    all_count = dp_count * rs_count
    rank_table = lax.axis_index(ALL)
    tokens = hash_ids.shape[0]
    rows_dev, model_width = hash_table.shape
    patch_len = lengths[0]
    patch_end = jnp.cumsum(patch_len)[:, None]
    patch_start = patch_end - patch_len[:, None]
    gains = jnp.concatenate(
        [norm_attn[None], norm_ffn[None], norm_cross[None], jnp.zeros((5, model_width), jnp.float32)]
    )
    full, embedded, entries, kept = fetch(
        hash_ids,
        hash_table,
        (
            w_query,
            w_key,
            w_value,
            w_out,
            w_gate,
            w_up,
            w_down,
            c_query,
            c_key,
            c_value,
            c_out,
        ),
        (byte_ids[:, None], byte_table, gains, patch_start, patch_end),
        WEIGHT_STEPS,
        dp_count,
    )
    lefts = [
        by_rows(a, dp_count)
        for a in (kept.x_ffn, kept.hidden, kept.pooled, kept.x_cross, kept.p_attended)
    ]
    sums, results = back_sums(
        lefts,
        Streamed(
            kept.gate_pre,
            kept.up_pre,
            kept.h_out,
            kept.h_mid,
            embedded,
            kept.key_values,
            *full,
            cot_patches,
        ),
        (
            cot_bytes,
            kept.p_query,
            kept.p_key,
            kept.p_value,
            kept.cross_lse,
            gains,
            patch_start,
            patch_end,
            kept.queries,
            kept.lse,
        ),
        dp_count,
    )
    out_cout, out_ckey, out_cvalue, out_cquery, down_rows = sums[:5]
    out_gate = jnp.concatenate([sums[5], sums[7]], axis=1)
    out_up = jnp.concatenate([sums[6], sums[8]], axis=1)
    gain_rows, grad_branch_a, grad_queries, grad_keys, grad_values, embed_grad = results
    one_hot = byte_ids[:, None] == jnp.arange(BYTE_VALUES, dtype=jnp.int32)[None, :]
    lefts = [
        by_rows(a, dp_count) for a in (kept.x_attn, kept.attended, one_hot.astype(jnp.bfloat16))
    ]
    rights = [grad_queries, grad_keys, grad_values, grad_branch_a, embed_grad]
    sums, all_embed, gain_sums = last_sums(
        [(1, 3), (0, 0), (0, 1), (0, 2), (2, 4)],
        lefts,
        rights,
        embed_grad,
        gain_rows,
        dp_count,
    )
    out_proj, out_query, out_key, out_value, byte_rows = sums
    out_down = own_rows(down_rows, kept.hidden.shape[1] // all_count)
    out_bytes = own_rows(byte_rows, BYTE_VALUES // all_count)
    hash_table_grad, row_counts = spread(
        entries, all_embed.reshape(all_count, tokens, model_width), rows_dev
    )
    own_gains = lax.dynamic_slice_in_dim(
        gain_sums, rank_table * (model_width // all_count), model_width // all_count, 1
    )
    return (
        kept.byte_states,
        kept.patch_states,
        embed_grad,
        out_bytes,
        hash_table_grad,
        row_counts,
        own_gains[0],
        own_gains[1],
        own_gains[2],
        out_query,
        out_key,
        out_value,
        out_proj,
        out_gate,
        out_up,
        out_down,
        out_cquery,
        out_ckey,
        out_cvalue,
        out_cout,
    )


def solution(mesh):
    fits = mesh.shape[REP] == 2 and mesh.shape[SUB] == 4 and mesh.shape[DP] <= 4
    return jax.shard_map(
        fast_body if fits else body,
        mesh=mesh,
        in_specs=(
            P(ALL),
            P(ALL, None),
            P(ALL, None),
            P(),
            P(ALL, None),
            P(),
            P(),
            P(),
            P(DP, None),
            P(DP, None),
            P(DP, None),
            P(DP, None),
            P(DP, None),
            P(DP, None),
            P(DP, None),
            P(DP, None),
            P(DP, None),
            P(DP, None),
            P(DP, None),
            P(ALL, None),
            P(ALL, None),
        ),
        out_specs=(
            P(ALL, None),
            P(ALL, None),
            P(ALL, None),
            P(ALL, None),
            P(ALL, None),
            P(ALL),
            P(ALL),
            P(ALL),
            P(ALL),
            P(ALL, None),
            P(ALL, None),
            P(ALL, None),
            P(ALL, None),
            P(ALL, None),
            P(ALL, None),
            P(ALL, None),
            P(ALL, None),
            P(ALL, None),
            P(ALL, None),
            P(ALL, None),
        ),
        check_vma=False,
    )
```

```python
import functools
import typing

import jax
import jax.numpy as jnp
from jax import lax
from jax.experimental import pallas as pl
from jax.experimental.pallas import tpu as pltpu
from jax.sharding import PartitionSpec as P

DP, REP, SUB = "dp", "rep", "sub"
SEQ = (REP, SUB)
ALL = (DP, REP, SUB)
HD = 64
WIN = 512
BYTE_VALUES = 256


PRECISE = lax.Precision.HIGHEST
NEG_BIG = -1e30
EPSILON = 1e-06
SCORE_SCALE = 0.125


def passed_along(x, axis, by):
    devices = lax.axis_size(axis)
    pairs = [(i, i + by) for i in range(devices) if 0 <= i + by < devices]
    return lax.ppermute(x, axis, pairs)


def matmul(matrix_a, matrix_b):
    return jnp.dot(matrix_a, matrix_b, preferred_element_type=jnp.float32)


def times_t(matrix_a, matrix_b):
    return lax.dot_general(
        matrix_a, matrix_b, (((1,), (1,)), ((), ())), preferred_element_type=jnp.float32
    )


def t_times(matrix_a, matrix_b):
    return lax.dot_general(
        matrix_a, matrix_b, (((0,), (0,)), ((), ())), preferred_element_type=jnp.float32
    )


def normalize(values, gains):
    inv_rms = lax.rsqrt(jnp.mean(values * values, axis=-1, keepdims=True) + EPSILON)
    normed = values * inv_rms
    return ((normed * gains).astype(jnp.bfloat16), normed, inv_rms)


def norm_back(grad_out, normed, inv_rms, gains):
    grad_gain = jnp.sum(grad_out * normed, axis=0)
    scaled_grad = grad_out * gains
    grad_in = inv_rms * (
        scaled_grad - normed * jnp.mean(scaled_grad * normed, axis=-1, keepdims=True)
    )
    return (grad_in, grad_gain)


def soft_forward(scores, allowed):
    masked = jnp.where(allowed, scores, NEG_BIG)
    row_max = jnp.max(masked, axis=-1, keepdims=True)
    exps = jnp.exp(masked - row_max)
    row_sum = jnp.sum(exps, axis=-1, keepdims=True)
    return (exps / row_sum, row_max + jnp.log(row_sum))


def soft_again(scores, allowed, log_total):
    return jnp.where(allowed, jnp.exp(scores - log_total), 0.0)


def soft_back(probs_full, grad_probs):
    row_total = jnp.sum(probs_full * grad_probs, axis=-1, keepdims=True)
    return (probs_full * (grad_probs - row_total)).astype(jnp.bfloat16)


def window_mask(first_query, first_key, row_count, col_count):
    query_pos = first_query + jnp.arange(row_count, dtype=jnp.int32)
    key_pos = first_key + jnp.arange(col_count, dtype=jnp.int32)
    near = (
        (key_pos[None, :] <= query_pos[:, None])
        & (key_pos[None, :] > query_pos[:, None] - WIN)
        & (key_pos[None, :] >= 0)
    )
    return near[None]


MESH_ID = pl.DeviceIdType.MESH
SLOTS = 96
GATHER_LAGS = (1, 1, 2, 3)


HASH, GATHER, FORWARD = range(3)


SCHEDULE = (
    (GATHER, 0),
    (HASH, 0),
    (GATHER, 1),
    (HASH, 1),
    (HASH, 2),
    (GATHER, 2),
    (HASH, 3),
    (GATHER, 3),
    (HASH, 4),
    (GATHER, 4),
    (HASH, 5),
    (GATHER, 5),
    (HASH, 6),
    (GATHER, 6),
    (HASH, 7),
    (FORWARD, 2),
    (GATHER, 7),
    (FORWARD, 2),
    (GATHER, 8),
    (FORWARD, 1),
    (GATHER, 9),
    (FORWARD, 2),
    (GATHER, 10),
    (FORWARD, 1),
    (GATHER, 11),
    (FORWARD, 2),
    (GATHER, 12),
    (FORWARD, 2),
    (GATHER, 13),
    (FORWARD, 3),
)
VMEM_CAP = 60 * 1024 * 1024


class Place:
    def __init__(self, dp_count):
        self.n = dp_count
        self.z = lax.axis_index(DP)
        self.x = lax.axis_index(REP)
        sub = lax.axis_index(SUB)
        self.y = sub // 2
        self.c = sub % 2
        self.started, self.maybe = [], []

    def at(self, dz=0, dx=0, dy=0, dc=0):
        z = lax.rem(self.z + dz, self.n) if dz else self.z
        x = 1 - self.x if dx else self.x
        y = 1 - self.y if dy else self.y
        c = 1 - self.c if dc else self.c
        return (z, x, y * 2 + c)

    def greet(self):
        barrier = pltpu.get_barrier_semaphore()
        peers = [
            self.at(dx=dx, dy=dy, dc=dc)
            for dx in range(2)
            for dy in range(2)
            for dc in range(2)
            if dx + dy + dc > 0
        ]
        peers += [self.at(dz=j) for j in range(1, self.n)]
        for peer in peers:
            pl.semaphore_signal(barrier, inc=1, device_id=peer, device_id_type=MESH_ID)
        pl.semaphore_wait(barrier, len(peers))

    def send_if(self, there, src, dst, send_sem, recv_sem, peer):
        copy = pltpu.make_async_remote_copy(
            src_ref=src,
            dst_ref=dst,
            send_sem=send_sem,
            recv_sem=recv_sem,
            device_id=peer,
            device_id_type=MESH_ID,
        )
        pl.when(there)(copy.start)
        self.maybe.append((there, copy))

    def send(self, src, dst, send_sem, recv_sem, peer):
        copy = pltpu.make_async_remote_copy(
            src_ref=src,
            dst_ref=dst,
            send_sem=send_sem,
            recv_sem=recv_sem,
            device_id=peer,
            device_id_type=MESH_ID,
        )
        copy.start()
        self.started.append(copy)
        return copy

    def expect(self, dst, recv_sem):
        pltpu.make_async_remote_copy(
            src_ref=dst,
            dst_ref=dst,
            send_sem=recv_sem,
            recv_sem=recv_sem,
            device_id=self.at(dc=1),
            device_id_type=MESH_ID,
        ).wait_recv()

    def sent(self, copy):
        copy.wait_send()
        self.started = [other for other in self.started if other is not copy]

    def finish(self):
        for copy in self.started:
            copy.wait_send()
        for there, copy in self.maybe:
            pl.when(there)(copy.wait_send)
        self.started, self.maybe = [], []


def add_into(dst, src, blocks, width):
    def step(i, carry):
        total = dst(i)[...].astype(jnp.float32) + src(i)[...].astype(jnp.float32)
        dst(i)[...] = total.astype(jnp.bfloat16)
        return carry

    lax.fori_loop(0, blocks, step, 0)


class Reduction:
    def __init__(self, here, p0, r1a, r1b, r2a, r2b, sems, index):
        self.here, self.p0 = here, p0
        self.r1a, self.r1b, self.r2a, self.r2b = r1a, r1b, r2a, r2b
        self.sems, self.i = sems, index
        self.planes, _, _, self.rows, cols = p0.shape
        self.half = cols // 2
        self.left = pl.ds(0, self.half)
        self.right = pl.ds(self.half, self.half)

    def sem(self, k):
        return self.sems.at[self.i, k, 0], self.sems.at[self.i, k, 1]

    def first(self):
        h = self.here
        self.s1a = h.send(
            self.p0.at[:, 1 - h.x, :, :, self.left], self.r1a, *self.sem(0), h.at(dx=1)
        )
        self.s1b = h.send(
            self.p0.at[:, :, 1 - h.y, :, self.right], self.r1b, *self.sem(1), h.at(dy=1)
        )

    def second(self):
        h = self.here
        self.s1a.wait_recv()
        add_into(
            lambda i: self.p0.at[i // 2, h.x, i % 2, :, self.left],
            lambda i: self.r1a.at[i // 2, i % 2],
            2 * self.planes,
            self.half,
        )
        self.s2a = h.send(
            self.p0.at[:, h.x, 1 - h.y, :, self.left], self.r2a, *self.sem(2), h.at(dy=1)
        )
        self.s1b.wait_recv()
        add_into(
            lambda i: self.p0.at[i // 2, i % 2, h.y, :, self.right],
            lambda i: self.r1b.at[i // 2, i % 2],
            2 * self.planes,
            self.half,
        )
        self.s2b = h.send(
            self.p0.at[:, 1 - h.x, h.y, :, self.right], self.r2b, *self.sem(3), h.at(dx=1)
        )

    def third(self):
        h = self.here
        self.s2a.wait_recv()
        add_into(
            lambda i: self.p0.at[i, h.x, h.y, :, self.left],
            lambda i: self.r2a.at[i],
            self.planes,
            self.half,
        )
        self.s2b.wait_recv()
        add_into(
            lambda i: self.p0.at[i, h.x, h.y, :, self.right],
            lambda i: self.r2b.at[i],
            self.planes,
            self.half,
        )
        return self.p0.at[:, h.x, h.y]


EXTRA_IN = 5
F32, LOW = jnp.float32, jnp.bfloat16
class Kept(typing.NamedTuple):
    x_attn: typing.Any
    queries: typing.Any
    key_values: typing.Any
    lse: typing.Any
    attended: typing.Any
    h_mid: typing.Any
    x_ffn: typing.Any
    gate_pre: typing.Any
    up_pre: typing.Any
    hidden: typing.Any
    h_out: typing.Any
    byte_states: typing.Any
    x_cross: typing.Any
    pooled: typing.Any
    p_query: typing.Any
    p_key: typing.Any
    p_value: typing.Any
    cross_lse: typing.Any
    p_attended: typing.Any
    patch_states: typing.Any


def kept_shapes(t, w, f, p):
    one = jax.ShapeDtypeStruct
    return Kept(
        x_attn=one((t, w), LOW),
        queries=one((t, w), LOW),
        key_values=one((2, 3 * t, w), LOW),
        lse=one((t, 128), F32),
        attended=one((t, w), LOW),
        h_mid=one((t, w), F32),
        x_ffn=one((t, w), LOW),
        gate_pre=one((t, f), F32),
        up_pre=one((t, f), F32),
        hidden=one((t, f), LOW),
        h_out=one((t, w), F32),
        byte_states=one((t, w), LOW),
        x_cross=one((t, w), LOW),
        pooled=one((p, w), LOW),
        p_query=one((p, w), LOW),
        p_key=one((t, w), LOW),
        p_value=one((t, w), LOW),
        cross_lse=one((p, 128), F32),
        p_attended=one((p, w), LOW),
        patch_states=one((p, w), LOW),
    )


def forward_steps(here, fulls, embedded, extra_in, extra_out, slots, scratch):
    byte_ids, byte_table, gains, starts, ends = extra_in
    out = Kept(*extra_out)
    gate_w, up_w, x_halo, load_sems, halo_sems = scratch
    tokens, width = embedded.shape
    heads = width // HD
    n = here.n
    z, x, y, c = here.z, here.x, here.y, here.c
    rank = (x * 2 + y) * 2 + c
    loads = {}
    kv = out.key_values

    def load(i, *targets):
        copies = []
        for b, target in enumerate(targets):
            rows = target.shape[0]
            copy = pltpu.make_async_copy(
                fulls[i].at[pl.ds(b * rows, rows)], target, load_sems.at[i, b]
            )
            copy.start()
            copies.append(copy)
        loads[i] = copies

    def load_slot(i, slot):
        for b in range(4):
            copy = pltpu.make_async_copy(
                fulls[i].at[pl.ds(b * (width // 4), width // 4)],
                slots[slot].at[b // 2, b % 2],
                load_sems.at[i, b],
            )
            copy.start()
            loads.setdefault(i, []).append(copy)

    def wait(*weights):
        for i in weights:
            for copy in loads[i]:
                copy.wait()

    def through(a, slot):
        return matmul(a, slots[slot][...].reshape(width, width))

    def embed():
        load_slot(0, 0)
        load_slot(1, 1)
        load_slot(2, 2)
        ids = lax.broadcasted_iota(jnp.int32, (tokens, BYTE_VALUES), 1)
        pick = jnp.where(byte_ids[...] == ids, 1.0, 0.0).astype(LOW)
        embedded[...] = embedded[...] + matmul(pick, byte_table[...])
        out.x_attn[...] = normalize(embedded[...], gains[0:1])[0]
        halo_send()

    def halo_send():
        target = jnp.minimum(rank + 2, 7)
        here.send_if(
            rank + 2 < 8,
            out.x_attn,
            x_halo.at[0],
            halo_sems.at[0, 0],
            halo_sems.at[0, 1],
            (z, target // 4, lax.rem(target, 4)),
        )
        here.send_if(
            c == 0, out.x_attn, x_halo.at[1], halo_sems.at[1, 0], halo_sems.at[1, 1], here.at(dc=1)
        )

    def project():
        wait(0, 1, 2)
        a = out.x_attn[...]
        out.queries[...] = through(a, 0).astype(LOW)
        kv[0, 2 * tokens :] = through(a, 1).astype(LOW)
        kv[1, 2 * tokens :] = through(a, 2).astype(LOW)

    def halo():
        there = rank >= 2

        @pl.when(there)
        def _():
            here.expect(x_halo.at[0], halo_sems.at[0, 1])

        here.send_if(
            there & (c == 1),
            x_halo.at[0],
            x_halo.at[1],
            halo_sems.at[1, 0],
            halo_sems.at[1, 1],
            here.at(dc=1),
        )

        @pl.when(there | (c == 1))
        def _():
            here.expect(x_halo.at[1], halo_sems.at[1, 1])

        @pl.when(jnp.logical_not(there))
        def _():
            x_halo[0] = jnp.zeros_like(x_halo[0])

        @pl.when(rank == 0)
        def _():
            x_halo[1] = jnp.zeros_like(x_halo[1])

        a = x_halo[...].reshape(2 * tokens, width)
        kv[0, : 2 * tokens] = through(a, 1).astype(LOW)
        kv[1, : 2 * tokens] = through(a, 2).astype(LOW)

    lane = lax.broadcasted_iota(jnp.int32, (1, 128), 1)
    sides = [jnp.where(lane < HD, 1.0, 0.0).astype(LOW), jnp.where(lane < HD, 0.0, 1.0).astype(LOW)]

    def attend(first):
        row = lax.broadcasted_iota(jnp.int32, (tokens, tokens), 0)
        col = lax.broadcasted_iota(jnp.int32, (tokens, tokens), 1)
        mine = col <= row
        far_bias = jnp.where(rank >= 2, 0.0, NEG_BIG)
        near_bias = jnp.where(rank >= 1, 0.0, NEG_BIG)
        if first == 0:
            out.lse[...] = jnp.zeros_like(out.lse)
        else:
            load_slot(3, 3)

        def heads_pair(pair, carry):
            span = pl.ds(pl.multiple_of(pair * 128, 128), 128)
            q2 = out.queries[:, span]
            k2, v2 = kv[0, :, span], kv[1, :, span]
            halves = []
            for side in range(2):
                scores = times_t(q2 * sides[side], k2) * SCORE_SCALE
                edge = jnp.where(mine, scores[:, 2 * tokens :], scores[:, :tokens] + far_bias)
                middle = scores[:, tokens : 2 * tokens] + near_bias
                top = jnp.maximum(
                    jnp.max(edge, axis=1, keepdims=True), jnp.max(middle, axis=1, keepdims=True)
                )
                edge, middle = jnp.exp(edge - top), jnp.exp(middle - top)
                total = jnp.sum(edge, axis=1, keepdims=True) + jnp.sum(
                    middle, axis=1, keepdims=True
                )
                inverse = 1.0 / total
                edge, middle = edge * inverse, middle * inverse
                probs = jnp.concatenate(
                    [
                        jnp.where(mine, 0.0, edge).astype(LOW),
                        middle.astype(LOW),
                        jnp.where(mine, edge, 0.0).astype(LOW),
                    ],
                    axis=1,
                )
                halves.append(matmul(probs, v2))
                where = lane == pair * 2 + side
                out.lse[...] = jnp.where(where, top + jnp.log(total), out.lse[...])
            out.attended[:, span] = jnp.where(lane < HD, halves[0], halves[1]).astype(LOW)
            return carry

        lax.fori_loop(first * heads // 4, (first + 1) * heads // 4, heads_pair, 0)

    def attention_out():
        wait(3)
        h_mid = embedded[...] + through(out.attended[...], 3)
        out.h_mid[...] = h_mid
        out.x_ffn[...] = normalize(h_mid, gains[1:2])[0]

    def down_block(t):
        return slots[t // 4].at[t // 2 % 2, t % 2]

    tile = 256
    tiles = gate_w.shape[1] // tile

    def feed_forward():
        for t in range(tiles):
            copy = pltpu.make_async_copy(
                fulls[6].at[pl.ds(t * tile, tile)], down_block(t), down_sems.at[t]
            )
            copy.start()
            loads.setdefault(6, []).append(copy)
        wait(4, 5)
        a = out.x_ffn[...]

        def columns(t, carry):
            span = pl.ds(pl.multiple_of(t * tile, tile), tile)
            gate = matmul(a, gate_w[:, span])
            up = matmul(a, up_w[:, span])
            out.gate_pre[:, span] = gate
            out.up_pre[:, span] = up
            out.hidden[:, span] = (gate * jax.nn.sigmoid(gate) * up).astype(LOW)
            return carry

        lax.fori_loop(0, tiles, columns, 0)

    def feed_out():
        wait(6)
        total = out.h_mid[...]
        for t in range(tiles):
            total = total + matmul(
                out.hidden[:, t * tile : (t + 1) * tile], down_block(t)[...]
            )
        out.h_out[...] = total
        out.byte_states[...] = total.astype(LOW)
        out.x_cross[...] = normalize(total, gains[2:3])[0]

    byte_pos = lax.broadcasted_iota(jnp.int32, (starts.shape[0], tokens), 1)

    def member():
        return (byte_pos >= starts[...]) & (byte_pos < ends[...])

    pooled_f = []

    def cross_keys():
        inside = jnp.where(member(), 1.0, 0.0).astype(LOW)
        length = (ends[...] - starts[...]).astype(F32)
        pooled = matmul(inside, out.x_cross[...]) / length
        pooled_f.append(pooled)
        out.pooled[...] = pooled.astype(LOW)
        wait(8, 9)
        a = out.x_cross[...]
        out.p_key[...] = through(a, 4).astype(LOW)
        out.p_value[...] = through(a, 5).astype(LOW)

    def cross_query():
        wait(7)
        out.p_query[...] = through(out.pooled[...], 3).astype(LOW)
        allowed = member()
        out.cross_lse[...] = jnp.zeros_like(out.cross_lse)

        def heads_pair(pair, carry):
            span = pl.ds(pl.multiple_of(pair * 128, 128), 128)
            q2, k2, v2 = out.p_query[:, span], out.p_key[:, span], out.p_value[:, span]
            halves = []
            for side in range(2):
                scores = times_t(q2 * sides[side], k2) * SCORE_SCALE
                masked = jnp.where(allowed, scores, NEG_BIG)
                top = jnp.max(masked, axis=1, keepdims=True)
                exps = jnp.exp(masked - top)
                total = jnp.sum(exps, axis=1, keepdims=True)
                halves.append(matmul((exps / total).astype(LOW), v2))
                where = lane == pair * 2 + side
                out.cross_lse[...] = jnp.where(
                    where, top + jnp.log(total), out.cross_lse[...]
                )
            out.p_attended[:, span] = jnp.where(lane < HD, halves[0], halves[1]).astype(LOW)
            return carry

        lax.fori_loop(0, heads // 2, heads_pair, 0)

    def cross_out():
        wait(10)
        states = pooled_f[0] + through(out.p_attended[...], 0)
        out.patch_states[...] = states.astype(LOW)

    down_sems = load_sems.at[6]
    return [
        ((0, 1, 2), embed),
        ((), project),
        ((), halo),
        ((), lambda: attend(0)),
        ((3,), lambda: attend(1)),
        ((), attention_out),
        ((4, 5), lambda: (load(4, gate_w), load(5, up_w))),
        ((6,), feed_forward),
        ((8, 9), lambda: (load_slot(8, 4), load_slot(9, 5))),
        ((), feed_out),
        ((7,), lambda: load_slot(7, 3)),
        ((), cross_keys),
        ((10,), lambda: load_slot(10, 0)),
        ((), cross_query),
        ((), cross_out),
    ]


def fetch_kernel(dp_count, weight_count, steps_of, tokens, gram_count, used_lines, *refs):
    shards = refs[:weight_count]
    refs = list(refs[weight_count:])

    def take(number):
        taken = refs[:number]
        del refs[:number]
        return taken

    ids, table = take(2)
    extra_in = take(EXTRA_IN)
    fulls = take(weight_count)
    embedded, lists = take(2)
    extra_out = take(len(Kept._fields))
    (
        all_ids,
        send0,
        p0,
        r1a,
        r1b,
        r2a,
        r2b,
        r3,
        g_rows,
        core_sems,
        stage_sems,
        z_sems,
        local_sems,
        w_send,
        w_recv,
        id_sems,
        places,
        entries,
        *extra_scratch,
    ) = refs
    here = Place(dp_count)
    n = dp_count
    z, x, y, c = here.z, here.x, here.y, here.c

    class Weight:
        def __init__(self, number, i, part, parts, kind):
            self.i = number
            self.kind = kind
            rows, cols = shards[i].shape
            self.by_cols = rows // 8 % 16 != 0
            self.all_rows, self.count = rows, rows // parts
            self.first = part * self.count
            self.shard = shards[i].at[pl.ds(self.first, self.count)]
            self.full = fulls[i]
            self.step = (cols if self.by_cols else rows // parts) // 8
            near, far = (x, y) if kind == 0 else (y, x)
            self.q = (c * 2 + far) * 2 + near

        def on(self, plane):
            return self.full.at[pl.ds(plane * self.all_rows + self.first, self.count)]

        def cut(self, ref, start, count):
            span = pl.ds(start * self.step, count * self.step)
            if self.by_cols:
                return ref.at[:, span]
            return ref.at[span, :]

        def local(self):
            here.send(
                self.shard,
                self.on(z),
                local_sems.at[self.i, 0],
                local_sems.at[self.i, 1],
                here.at(dc=1),
            )

        def stage(self, k, j, start, count, src_ref, plane, peer):
            here.send(
                self.cut(src_ref, start, count),
                self.cut(self.on(plane), start, count),
                w_send.at[self.i, k, j - 1],
                w_recv.at[self.i, k, j - 1],
                peer,
            )

        def came(self, k, j, start, count):
            plane = lax.rem(z + n - j, n)
            here.expect(
                self.cut(self.on(plane), start, count), w_recv.at[self.i, k, j - 1]
            )
            return plane

        def along_z(self):
            for j in range(1, n):
                self.stage(0, j, self.q, 1, self.shard, z, here.at(dz=j))

        def near(self):
            for j in range(1, n):
                plane = self.came(0, j, self.q, 1)
                peer = here.at(dx=1) if self.kind == 0 else here.at(dy=1)
                self.stage(1, j, self.q, 1, self.on(plane), plane, peer)

        def far(self):
            other = self.q + 1 - 2 * (self.q % 2)
            for j in range(1, n):
                plane = self.came(1, j, other, 1)
                peer = here.at(dy=1) if self.kind == 0 else here.at(dx=1)
                self.stage(2, j, self.q // 2 * 2, 2, self.on(plane), plane, peer)

        def across(self):
            pair = self.q // 2
            other = pair + 1 - 2 * (pair % 2)
            for j in range(1, n):
                plane = self.came(2, j, other * 2, 2)
                self.stage(3, j, c * 4, 4, self.on(plane), plane, here.at(dc=1))

        def done(self):
            for j in range(1, n):
                self.came(3, j, (1 - c) * 4, 4)
            here.expect(self.on(z), local_sems.at[self.i, 1])

    weights = []
    for first, second in steps_of:
        pair = []
        for kind, (i, part, parts) in enumerate((first, second)):
            pair.append(Weight(2 * len(weights) + kind, i, part, parts, kind))
        weights.append(pair)

    def each(t, name):
        if 0 <= t < len(weights):
            for w in weights[t]:
                name(w)

    def gather_ids():
        all_ids[z, x, y, c] = ids[...]
        mine = all_ids.at[z, x, y, c]
        here.send(mine, mine, id_sems.at[0, 0], id_sems.at[0, 1], here.at(dc=1))
        here.expect(all_ids.at[z, x, y, 1 - c], id_sems.at[0, 1])
        pair = all_ids.at[z, x, y]
        here.send(pair, pair, id_sems.at[1, 0], id_sems.at[1, 1], here.at(dx=1))
        here.expect(all_ids.at[z, 1 - x, y], id_sems.at[1, 1])
        four = all_ids.at[z, :, y]
        here.send(four, four, id_sems.at[2, 0], id_sems.at[2, 1], here.at(dy=1))
        here.expect(all_ids.at[z, :, 1 - y], id_sems.at[2, 1])
        plane = all_ids.at[z]
        for j in range(1, n):
            here.send(plane, plane, id_sems.at[2 + j, 0], id_sems.at[2 + j, 1], here.at(dz=j))
        for j in range(1, n):
            here.expect(all_ids.at[lax.rem(z + n - j, n)], id_sems.at[2 + j, 1])

    def list_rows():
        lines, lanes = ids.shape
        sources = n * 8
        total = sources * lines
        rows_dev = table.shape[0]
        local = all_ids[...].reshape(total, lanes) - ((z * 2 + x) * 4 + y * 2 + c) * rows_dev
        inside = (local >= 0) & (local < rows_dev)
        flags = jnp.where(inside, 1.0, 0.0).astype(jnp.bfloat16)
        row = lax.broadcasted_iota(jnp.int32, (lanes, lanes), 0)
        col = lax.broadcasted_iota(jnp.int32, (lanes, lanes), 1)
        place = matmul(flags, jnp.where(row < col, 1.0, 0.0).astype(jnp.bfloat16))
        held = matmul(flags, jnp.ones((lanes, lanes), jnp.bfloat16)).astype(jnp.bfloat16)
        row = lax.broadcasted_iota(jnp.int32, (total, total), 0)
        col = lax.broadcasted_iota(jnp.int32, (total, total), 1)
        before = (row // lines == col // lines) & (col < row)
        place = place + matmul(jnp.where(before, 1.0, 0.0).astype(jnp.bfloat16), held)
        places[...] = jnp.where(inside, place.astype(jnp.int32), -1)
        line = lax.broadcasted_iota(jnp.int32, (total, lanes), 0)
        lane = lax.broadcasted_iota(jnp.int32, (total, lanes), 1)
        index = lax.rem(line, lines) * lanes + lane
        entries[...] = local * 256 + index // gram_count + 1
        slot = lax.broadcasted_iota(jnp.int32, (SLOTS, lanes), 0)

        def source(s, carry):
            span = pl.ds(pl.multiple_of(s * lines, lines), lines)
            where, what = places[span], entries[span]
            found = jnp.zeros((SLOTS, lanes), jnp.int32)
            for line in range(used_lines):
                hit = where[line : line + 1] == slot
                found = found + jnp.where(hit, what[line : line + 1], 0)
            lists[s] = jnp.sum(found, axis=1, keepdims=True) - 1
            return carry

        lax.fori_loop(0, sources, source, 0)

    row_iota = lax.broadcasted_iota(jnp.int32, (SLOTS, table.shape[0]), 1)
    byte_iota = lax.broadcasted_iota(jnp.int32, (SLOTS, tokens), 1)

    def partial_sums(plane, core, write):
        for place in range(4):
            source = plane * 8 + place * 2 + core
            entry = lists[source]
            pick = (jnp.right_shift(entry, 8) == row_iota).astype(jnp.bfloat16)
            g_rows[place * SLOTS : (place + 1) * SLOTS, :] = matmul(pick, table[...]).astype(
                jnp.bfloat16
            )
        for place in range(4):
            source = plane * 8 + place * 2 + core
            entry = lists[source]
            to_byte = (jnp.bitwise_and(entry, 255) == byte_iota).astype(jnp.bfloat16)
            sums = t_times(to_byte, g_rows[place * SLOTS : (place + 1) * SLOTS, :])
            write(place, sums)

    units = []
    for u in range(n):
        units.append(
            Reduction(
                here,
                p0.at[pl.ds(u, 1)],
                r1a.at[pl.ds(u, 1)],
                r1b.at[pl.ds(u, 1)],
                r2a.at[pl.ds(u, 1)],
                r2b.at[pl.ds(u, 1)],
                stage_sems,
                u,
            )
        )
    core_copies = [None] * n
    z_copies = [None] * n

    def plane_of(u):
        return lax.rem(z + u + 1, n)

    def hash_a(u):
        slot = u % 2
        if u >= 2:
            here.sent(core_copies[u - 2])

        def write(place, sums):
            send0[slot, place // 2, place % 2] = sums.astype(jnp.bfloat16)

        partial_sums(plane_of(u), 1 - c, write)
        core_copies[u] = here.send(
            send0.at[slot], p0.at[u], core_sems.at[u, 0], core_sems.at[u, 1], here.at(dc=1)
        )

    def hash_b(u):
        core_copies[u].wait_recv()

        def write(place, sums):
            total = sums + p0[u, place // 2, place % 2].astype(jnp.float32)
            p0[u, place // 2, place % 2] = total.astype(jnp.bfloat16)

        partial_sums(plane_of(u), c, write)
        units[u].first()

    def hash_c(u):
        units[u].second()

    def hash_d(u):
        mine = units[u].third()
        if u < n - 1:
            z_copies[u] = here.send(
                mine.at[0], r3.at[u], z_sems.at[u, 0], z_sems.at[u, 1], here.at(dz=u + 1)
            )

    def hash_e():
        for u in range(n - 1):
            z_copies[u].wait_recv()
        total = p0[n - 1, x, y].astype(jnp.float32)
        for u in range(n - 1):
            total = total + r3[u].astype(jnp.float32)
        embedded[...] = total
        for copy in core_copies[-2:] + z_copies[:-1]:
            here.sent(copy)
        for unit in units:
            for copy in (unit.s1a, unit.s1b, unit.s2a, unit.s2b):
                here.sent(copy)

    here.greet()
    lead, lag1, lag2, lag3 = GATHER_LAGS
    for t in range(lead):
        each(t, Weight.along_z)
    gather_ids()
    list_rows()
    hash_steps = []
    for t in range(n + 3):
        group = []
        for u, stage in ((t, hash_a), (t - 1, hash_b), (t - 2, hash_c), (t - 3, hash_d)):
            if 0 <= u < n:
                group.append(lambda u=u, stage=stage: stage(u))
        hash_steps.append(group)
    hash_steps.append([hash_e])
    layer = forward_steps(
        here,
        fulls,
        embedded,
        extra_in,
        extra_out,
        [p0.at[u] for u in range(n)] + [send0.at[u] for u in range(2)],
        extra_scratch,
    )
    gather_done, runs = set(), iter(layer)
    for what, number in SCHEDULE:
        if what == HASH:
            for run in hash_steps[number]:
                run()
        elif what == GATHER:
            each(number + lead, Weight.along_z)
            each(number, Weight.near)
            each(number - lag1, Weight.far)
            each(number - lag1, Weight.local)
            each(number - lag2, Weight.across)
            each(number - lag3, Weight.done)
            if 0 <= number - lag3 < len(steps_of):
                gather_done |= {i for i, _, _ in steps_of[number - lag3]}
        else:
            for _ in range(number):
                needs, run = next(runs)
                assert gather_done.issuperset(needs)
                run()
    assert next(runs, None) is None
    here.finish()


def fetch(hash_ids, table, shards, extra, steps_of, dp_count):
    width = table.shape[1]
    tokens, gram_count = hash_ids.shape
    count = len(shards)
    hbm = pl.BlockSpec(memory_space=pl.ANY)
    vmem = pl.BlockSpec(memory_space=pltpu.VMEM)
    n, half = dp_count, width // 2
    low = jnp.bfloat16
    dma = pltpu.SemaphoreType.DMA
    used_lines = tokens * gram_count // 128
    lines = -(-used_lines // 8) * 8
    ids = hash_ids.reshape(used_lines, 128)
    ids = jnp.concatenate([ids, jnp.full((lines - used_lines, 128), -1, jnp.int32)])
    gathers = 2 * len(steps_of)
    ff = shards[4].shape[1]
    extra_out = list(kept_shapes(tokens, width, ff, extra[3].shape[0]))
    results = pl.pallas_call(
        functools.partial(fetch_kernel, n, count, steps_of, tokens, gram_count, used_lines),
        out_shape=[jax.ShapeDtypeStruct((n * w.shape[0], w.shape[1]), w.dtype) for w in shards]
        + [
            jax.ShapeDtypeStruct((tokens, width), jnp.float32),
            jax.ShapeDtypeStruct((n * 8, SLOTS, 1), jnp.int32),
        ]
        + extra_out,
        in_specs=[hbm] * count + [vmem, vmem] + [vmem] * len(extra),
        out_specs=[hbm] * count + [vmem, vmem] + [vmem] * len(extra_out),
        scratch_shapes=[
            pltpu.VMEM((n, 2, 2, 2, lines, 128), jnp.int32),
            pltpu.VMEM((2, 2, 2, tokens, width), low),
            pltpu.VMEM((n, 2, 2, tokens, width), low),
            pltpu.VMEM((n, 2, tokens, half), low),
            pltpu.VMEM((n, 2, tokens, half), low),
            pltpu.VMEM((n, tokens, half), low),
            pltpu.VMEM((n, tokens, half), low),
            pltpu.VMEM((n - 1, tokens, width), low),
            pltpu.VMEM((4 * SLOTS, width), low),
            dma((n, 2)),
            dma((n, 4, 2)),
            dma((n - 1, 2)),
            dma((gathers, 2)),
            dma((gathers, 4, n - 1)),
            dma((gathers, 4, n - 1)),
            dma((2 + n, 2)),
            pltpu.VMEM((n * 8 * lines, 128), jnp.int32),
            pltpu.VMEM((n * 8 * lines, 128), jnp.int32),
            pltpu.VMEM((n * shards[4].shape[0], ff), low),
            pltpu.VMEM((n * shards[5].shape[0], ff), low),
            pltpu.VMEM((2, tokens, width), low),
            dma((count, max(n, ff // 256))),
            dma((2, 2)),
        ],
        compiler_params=pltpu.CompilerParams(
            collective_id=0, has_side_effects=True, vmem_limit_bytes=VMEM_CAP
        ),
        name="fetch",
    )(*shards, ids, table, *extra)
    return results[:count], results[count], results[count + 1], Kept(*results[count + 2 :])


LAGS = (2, 3, 5)


class GradSums:
    def __init__(self, here, units, lefts_in, rights_in, outs, take, pool_count):
        count = len(units)
        self.here, self.units = here, units
        self.lefts_in, self.rights_in, self.outs = lefts_in, rights_in, outs
        self.lefts, self.rights = take(len(lefts_in)), take(len(rights_in))
        self.pools = take(pool_count)
        self.r1a, self.r1b, self.r2a, self.r2b, self.r3 = (take(count) for _ in range(5))
        self.left_sems, self.right_sems, self.stage_sems, self.z_sems = take(4)
        self.left_copies, self.right_copies = {}, {}
        self.sums = [None] * count
        self.using = {}
        self.mine_of = [None] * count
        self.sent_of = [None] * count

    def bring(self, source, target, sems, i, split):
        here = self.here
        copies = []
        theirs = target.at[0]
        if source is not None:
            theirs = source.at[1 - here.c] if split else source
            mine = source.at[here.c] if split else source
            local = pltpu.make_async_copy(mine, target.at[0], sems.at[i, 0])
            local.start()
            copies.append(local.wait)
        remote = here.send(theirs, target.at[1], sems.at[i, 1], sems.at[i, 2], here.at(dc=1))
        copies.append(remote.wait_recv)
        return copies

    def left(self, i):
        if i not in self.left_copies:
            self.left_copies[i] = self.bring(
                self.lefts_in[i], self.lefts[i], self.left_sems, i, True
            )

    def right(self, i):
        if i not in self.right_copies:
            self.right_copies[i] = self.bring(
                self.rights_in[i], self.rights[i], self.right_sems, i, False
            )

    def need(self, i):
        self.left(self.units[i][0])
        self.right(self.units[i][1])

    def product(self, i):
        here, n = self.here, self.here.n
        left, right, pool, slot = self.units[i]
        self.need(i)
        for copies in (self.left_copies[left], self.right_copies[right]):
            for wait in copies:
                wait()
            copies.clear()
        for copy in self.using.get((pool, slot), []):
            here.sent(copy)
        p0 = self.pools[pool].at[slot]
        xt, g = self.lefts[left], self.rights[right]
        k, depth = xt.shape[2], xt.shape[3]
        cols = g.shape[2]
        chunks = 1 if k <= 32 else n
        planes = n // chunks
        tile = 256

        def columns(t, carry):
            span = pl.ds(pl.multiple_of(t * tile, tile), tile)
            for chunk in range(chunks):
                total = None
                for who in range(2):
                    rows = xt[who, chunk * planes * 4 : (chunk + 1) * planes * 4]
                    part = matmul(rows.reshape(planes * 4 * k, depth), g[who, :, span])
                    total = part if total is None else total + part
                p0[chunk * planes : (chunk + 1) * planes, :, :, :, span] = total.astype(
                    jnp.bfloat16
                ).reshape(planes, 2, 2, k, tile)
            return carry

        lax.fori_loop(0, cols // tile, columns, 0)
        unit = Reduction(
            here, p0, self.r1a[i], self.r1b[i], self.r2a[i], self.r2b[i], self.stage_sems, i
        )
        unit.first()
        self.sums[i] = unit
        self.using[(pool, slot)] = [unit.s1a, unit.s1b]

    def second(self, i):
        self.sums[i].second()
        self.using[self.units[i][2:]] += [self.sums[i].s2a, self.sums[i].s2b]

    def third(self, i):
        here, n = self.here, self.here.n
        mine = self.sums[i].third()
        self.sent_of[i] = []
        for j in range(1, n):
            self.sent_of[i].append(
                here.send(
                    mine.at[lax.rem(here.z + j, n)],
                    self.r3[i].at[j - 1],
                    self.z_sems.at[i, j - 1, 0],
                    self.z_sems.at[i, j - 1, 1],
                    here.at(dz=j),
                )
            )
        self.using[self.units[i][2:]] += self.sent_of[i]
        self.mine_of[i] = mine

    def final(self, i):
        total = self.mine_of[i][self.here.z].astype(jnp.float32)
        for j in range(1, self.here.n):
            self.sent_of[i][j - 1].wait_recv()
            total = total + self.r3[i][j - 1].astype(jnp.float32)
        self.outs[i][...] = total

    def move(self, t, lags):
        lag2, lag3, lag4 = lags
        count = len(self.units)
        if 0 <= t - lag2 < count:
            self.second(t - lag2)
        if 0 <= t - lag3 < count:
            self.third(t - lag3)
        if 0 <= t - lag4 < count:
            self.final(t - lag4)


def plan_sums(pairs, left_shapes, right_shapes, n, most):
    low = jnp.bfloat16
    dma = pltpu.SemaphoreType.DMA
    shapes, units, seen = [], [], {}
    for left, right in pairs:
        shape = (left_shapes[left][2], right_shapes[right][1])
        seen[shape] = seen.get(shape, 0) + 1
        shapes.append(shape)
    classes = list(seen)
    slots = [min(seen[s], most) for s in classes]
    used = {s: 0 for s in classes}
    for (left, right), shape in zip(pairs, shapes):
        pool = classes.index(shape)
        units.append((left, right, pool, used[shape] % slots[pool]))
        used[shape] += 1
    count = len(pairs)
    scratch = [pltpu.VMEM(shape, low) for shape in left_shapes]
    scratch += [pltpu.VMEM((2, *shape), low) for shape in right_shapes]
    scratch += [pltpu.VMEM((s, n, 2, 2, *shape), low) for s, shape in zip(slots, classes)]
    halves = [(k, cols // 2) for k, cols in shapes]
    for _ in range(2):
        scratch += [pltpu.VMEM((n, 2, *half), low) for half in halves]
    for _ in range(2):
        scratch += [pltpu.VMEM((n, *half), low) for half in halves]
    scratch += [pltpu.VMEM((n - 1, *shape), low) for shape in shapes]
    scratch += [
        dma((len(left_shapes), 3)),
        dma((len(right_shapes), 3)),
        dma((count, 4, 2)),
        dma((count, n - 1, 2)),
    ]
    return units, shapes, scratch, len(classes)


def taker(refs):
    refs = list(refs)

    def take(number):
        taken = refs[:number]
        del refs[:number]
        return taken

    return take


def last_kernel(dp_count, units, left_count, right_count, pool_count, *refs):
    n = dp_count
    count = len(units)
    take = taker(refs)
    lefts_in, rights_in = take(left_count), take(right_count)
    embed_in, gains_in, lists, rows_of = take(4)
    outs = take(count)
    gains_out, table_grad, counts = take(3)
    here = Place(n)
    sums = GradSums(here, units, lefts_in, rights_in, outs, take, pool_count)
    gathered, stacked = take(2)
    gain_send, gain_recv, gain_sems, own_sem, near_sems, plane_sems = take(6)
    z, x, y, c = here.z, here.x, here.y, here.c

    here.greet()

    own = pltpu.make_async_copy(embed_in, gathered.at[z, x, y, c], own_sem)
    own.start()
    for j in range(1, n):
        here.send(
            embed_in,
            gathered.at[z, x, y, c],
            plane_sems.at[j - 1, 0],
            plane_sems.at[j - 1, 1],
            here.at(dz=j),
        )
    width = embed_in.shape[1]
    left_half, right_half = pl.ds(0, width // 2), pl.ds(width // 2, width // 2)

    def embed_near(j):
        plane = lax.rem(z + n - j, n)
        if j:
            here.expect(gathered.at[plane, x, y, c], plane_sems.at[j - 1, 1])
        else:
            own.wait()
        a = gathered.at[plane, x, y, c, :, left_half]
        b = gathered.at[plane, x, y, c, :, right_half]
        here.send(a, a, near_sems.at[j, 0, 0], near_sems.at[j, 0, 1], here.at(dx=1))
        here.send(b, b, near_sems.at[j, 1, 0], near_sems.at[j, 1, 1], here.at(dy=1))

    def embed_far(j):
        plane = lax.rem(z + n - j, n)
        here.expect(gathered.at[plane, 1 - x, y, c, :, left_half], near_sems.at[j, 0, 1])
        here.expect(gathered.at[plane, x, 1 - y, c, :, right_half], near_sems.at[j, 1, 1])
        a = gathered.at[plane, :, y, c, :, left_half]
        b = gathered.at[plane, x, :, c, :, right_half]
        here.send(a, a, near_sems.at[j, 2, 0], near_sems.at[j, 2, 1], here.at(dy=1))
        here.send(b, b, near_sems.at[j, 3, 0], near_sems.at[j, 3, 1], here.at(dx=1))

    def embed_across(j):
        plane = lax.rem(z + n - j, n)
        here.expect(gathered.at[plane, :, 1 - y, c, :, left_half], near_sems.at[j, 2, 1])
        here.expect(gathered.at[plane, 1 - x, :, c, :, right_half], near_sems.at[j, 3, 1])
        a = gathered.at[plane, :, :, c]
        here.send(a, a, near_sems.at[j, 4, 0], near_sems.at[j, 4, 1], here.at(dc=1))

    def spread(j):
        plane = lax.rem(z + n - j, n)
        here.expect(gathered.at[plane, :, :, 1 - c], near_sems.at[j, 4, 1])
        byte_iota = lax.broadcasted_iota(jnp.int32, (SLOTS, embed_in.shape[0]), 1)
        for s in range(8):
            asked = jnp.bitwise_and(lists[plane * 8 + s], 255)
            pick = (asked == byte_iota).astype(jnp.bfloat16)
            grads = gathered[plane, s // 4, s // 2 % 2, s % 2]
            stacked[s * SLOTS : (s + 1) * SLOTS, :] = matmul(pick, grads).astype(jnp.bfloat16)
        row_iota = lax.broadcasted_iota(jnp.int32, (table_grad.shape[0], 8 * SLOTS), 0)
        onto = (rows_of[plane] == row_iota).astype(jnp.float32)
        uses = jnp.sum(onto, axis=1, keepdims=True)
        added = matmul(onto.astype(jnp.bfloat16), stacked[...])
        if j == 0:
            counts[...] = uses
            table_grad[...] = added
        else:
            counts[...] += uses
            table_grad[...] += added

    def gains(stage):
        if stage == 0:
            gain_send[0] = gains_in[...]
        elif stage <= 3:
            here.expect(gain_recv.at[stage - 1], gain_sems.at[stage - 1, 1])
            gain_send[stage] = gain_send[stage - 1] + gain_recv[stage - 1]
        if stage < 3:
            peer = (here.at(dc=1), here.at(dx=1), here.at(dy=1))[stage]
            here.send(
                gain_send.at[stage],
                gain_recv.at[stage],
                gain_sems.at[stage, 0],
                gain_sems.at[stage, 1],
                peer,
            )
        elif stage == 3:
            for j in range(1, n):
                here.send(
                    gain_send.at[3],
                    gain_recv.at[2 + j],
                    gain_sems.at[2 + j, 0],
                    gain_sems.at[2 + j, 1],
                    here.at(dz=j),
                )
        else:
            total = gain_send[3]
            for j in range(1, n):
                here.expect(gain_recv.at[2 + j], gain_sems.at[2 + j, 1])
                total = total + gain_recv[2 + j]
            gains_out[...] = total

    for i in range(count):
        sums.need(i)
    for t in range(max(count + LAGS[2], n + 5)):
        if t < count:
            sums.product(t)
        if t == 0:
            embed_near(0)
        if 0 <= t - 1 < 5:
            gains(t - 1)
        if 1 <= t - 2 < n:
            embed_near(t - 2)
        sums.move(t, LAGS)
        if 0 <= t - 3 < n:
            embed_far(t - 3)
        if 0 <= t - 4 < n:
            embed_across(t - 4)
        if 0 <= t - 5 < n:
            spread(t - 5)
    here.finish()


def last_sums(pairs, lefts, rights, embed_low, gains, entries, rows_dev, dp_count):
    n = dp_count
    low = jnp.bfloat16
    dma = pltpu.SemaphoreType.DMA
    hbm = pl.BlockSpec(memory_space=pl.ANY)
    vmem = pl.BlockSpec(memory_space=pltpu.VMEM)
    units, shapes, scratch, pool_count = plan_sums(
        pairs, [a.shape for a in lefts], [a.shape for a in rights], n, 6
    )
    count = len(pairs)
    tokens, width = embed_low.shape
    rows_of = jnp.right_shift(entries, 8).reshape(n, 1, 8 * SLOTS)
    scratch += [
        pltpu.VMEM((n, 2, 2, 2, tokens, width), low),
        pltpu.VMEM((8 * SLOTS, width), low),
        pltpu.VMEM((4, 8, width), jnp.float32),
        pltpu.VMEM((2 + n, 8, width), jnp.float32),
        dma((2 + n, 2)),
        dma,
        dma((n, 5, 2)),
        dma((n - 1, 2)),
    ]
    results = pl.pallas_call(
        functools.partial(last_kernel, n, units, len(lefts), len(rights), pool_count),
        out_shape=[jax.ShapeDtypeStruct(shape, jnp.float32) for shape in shapes]
        + [
            jax.ShapeDtypeStruct((8, width), jnp.float32),
            jax.ShapeDtypeStruct((rows_dev, width), jnp.float32),
            jax.ShapeDtypeStruct((rows_dev, 1), jnp.float32),
        ],
        in_specs=[hbm] * (len(lefts) + len(rights)) + [vmem] * 4,
        out_specs=[vmem] * (count + 3),
        scratch_shapes=scratch,
        compiler_params=pltpu.CompilerParams(
            collective_id=2, has_side_effects=True, vmem_limit_bytes=VMEM_CAP
        ),
        name="last_sums",
    )(*lefts, *rights, embed_low, gains, entries, rows_of)
    return results[:count], *results[count:]


BACK_PAIRS = ((4, 8), (3, 6), (3, 7), (2, 5), (1, 4), (0, 0), (0, 1), (0, 2), (0, 3))


class Streamed(typing.NamedTuple):
    gate_pre: typing.Any
    up_pre: typing.Any
    h_out: typing.Any
    h_mid: typing.Any
    embedded: typing.Any
    key_values: typing.Any
    w_query: typing.Any
    w_key: typing.Any
    w_value: typing.Any
    w_out: typing.Any
    w_gate: typing.Any
    w_up: typing.Any
    w_down: typing.Any
    c_query: typing.Any
    c_key: typing.Any
    c_value: typing.Any
    c_out: typing.Any
    cot_patches: typing.Any


def back_kernel(dp_count, units, pool_count, *refs):
    n = dp_count
    take = taker(refs)
    lefts_in = take(5)
    hbm = Streamed(*take(len(Streamed._fields)))
    (cot_bytes, p_query, p_key, p_value, cross_lse, gains, starts, ends, queries, lse) = take(10)
    outs = take(len(units))
    grad_gains, g_attn, g_query, g_key, g_value, g_embed = take(6)
    here = Place(n)
    sums = GradSums(here, units, lefts_in, [None] * 8 + [hbm.cot_patches], outs, take, pool_count)
    w, tile_pre, grad_out, grad_ffn, grad_mid, kv, halo = take(7)
    w_sems, tile_sems, pre_sems, kv_sems, halo_sems = take(5)
    g_gate = [sums.rights[0].at[0], sums.rights[2].at[0]]
    g_up = [sums.rights[1].at[0], sums.rights[3].at[0]]
    g_branch, g_pquery, g_pkey, g_pvalue, cot_patches = [ref.at[0] for ref in sums.rights[4:]]
    tokens, width = cot_bytes.shape
    patches = p_query.shape[0]
    tile = 256
    first_tiles = g_gate[0].shape[1] // tile
    tiles = first_tiles + g_gate[1].shape[1] // tile
    rank = (here.x * 2 + here.y) * 2 + here.c
    lane = lax.broadcasted_iota(jnp.int32, (1, 128), 1)
    sides = [jnp.where(lane < HD, 1.0, 0.0).astype(LOW), jnp.where(lane < HD, 0.0, 1.0).astype(LOW)]
    byte_pos = lax.broadcasted_iota(jnp.int32, (patches, tokens), 1)

    here.greet()

    def load_w(slot, source):
        copy = pltpu.make_async_copy(source, w.at[slot], w_sems.at[slot])
        copy.start()
        return copy

    def load_pre(source):
        copies = []
        for b in range(width // tile):
            copy = pltpu.make_async_copy(
                source.at[:, pl.ds(b * tile, tile)],
                tile_pre.at[b // 2, b % 2],
                pre_sems.at[b],
            )
            copy.start()
            copies.append(copy)
        return copies

    def pre_rows(copies):
        for copy in copies:
            copy.wait()
        return jnp.concatenate([tile_pre[b // 2, b % 2] for b in range(width // tile)], axis=1)

    for i in (4, 3, 2, 1, 0):
        sums.left(i)
    sums.right(8)
    cross = [load_w(i, a) for i, a in enumerate((hbm.c_out, hbm.c_query, hbm.c_key, hbm.c_value))]
    h_out_copies = load_pre(hbm.h_out)

    def tile_copies(t):
        slot = lax.rem(t, 2)
        span = pl.ds(pl.multiple_of(t * tile, tile), tile)
        return [
            pltpu.make_async_copy(source, target, tile_sems.at[slot, k])
            for k, (source, target) in enumerate(
                (
                    (hbm.w_gate.at[:, span], w.at[slot, :, pl.ds(0, tile)]),
                    (hbm.w_up.at[:, span], w.at[slot, :, pl.ds(tile, tile)]),
                    (hbm.w_down.at[span], w.at[2, pl.ds(pl.multiple_of(slot * tile, tile), tile)]),
                    (hbm.gate_pre.at[:, span], tile_pre.at[slot, 0]),
                    (hbm.up_pre.at[:, span], tile_pre.at[slot, 1]),
                )
            )
        ]

    def member():
        return (byte_pos >= starts[...]) & (byte_pos < ends[...])

    def head_lse(ref, head):
        return jnp.sum(jnp.where(lane == head, ref[...], 0.0), axis=1, keepdims=True)

    def cross_heads():
        cross[0].wait()
        allowed = member()
        grad_ffn[:patches] = times_t(cot_patches[...], w[0]).astype(LOW).astype(F32)

        def heads_pair(pair, carry):
            span = pl.ds(pl.multiple_of(pair * 128, 128), 128)
            q2, k2, v2 = p_query[:, span], p_key[:, span], p_value[:, span]
            gp2 = grad_ffn[:patches, span].astype(LOW)
            parts = []
            for side in range(2):
                total = head_lse(cross_lse, pair * 2 + side)
                scores = times_t(q2 * sides[side], k2) * SCORE_SCALE
                probs = jnp.where(allowed, jnp.exp(jnp.where(allowed, scores, total) - total), 0.0)
                grad_score = soft_back(probs, times_t(gp2 * sides[side], v2))
                parts.append(
                    (
                        matmul(grad_score, k2),
                        t_times(grad_score, q2),
                        t_times(probs.astype(LOW), gp2),
                    )
                )
            mine = lane < HD
            g_pquery[:, span] = (jnp.where(mine, parts[0][0], parts[1][0]) * SCORE_SCALE).astype(LOW)
            g_pkey[:, span] = (jnp.where(mine, parts[0][1], parts[1][1]) * SCORE_SCALE).astype(LOW)
            g_pvalue[:, span] = jnp.where(mine, parts[0][2], parts[1][2]).astype(LOW)
            return carry

        lax.fori_loop(0, width // 128, heads_pair, 0)
        for i in (5, 6, 7):
            sums.right(i)

    def split(v):
        high = v.astype(LOW)
        return high, (v - high.astype(F32)).astype(LOW)

    def unit_of(v):
        inv_rms = lax.rsqrt(jnp.mean(v * v, axis=-1, keepdims=True) + EPSILON)
        return v * inv_rms, inv_rms

    def through_norm(grad, rows, number):
        normed, inv_rms = unit_of(rows)
        grad_in, grad_gain = norm_back(
            grad.astype(LOW).astype(F32), normed, inv_rms, gains[number : number + 1]
        )
        grad_gains[number : number + 1] = grad_gain[None]
        return grad_in

    loaded = {}

    def cross_in():
        for copy in cross[1:]:
            copy.wait()
        length = (ends[...] - starts[...]).astype(F32)
        grad_pooled = cot_patches[...].astype(F32) + times_t(g_pquery[...], w[1]).astype(
            LOW
        ).astype(F32)
        high, rest = split(grad_pooled / length)
        inside = jnp.where(member(), 1.0, 0.0).astype(LOW)
        grad_x = t_times(inside, high) + t_times(inside, rest)
        grad_x = grad_x + times_t(g_pkey[...], w[2]) + times_t(g_pvalue[...], w[3])
        grad_gains[...] = jnp.zeros_like(grad_gains)
        total = cot_bytes[...].astype(F32) + through_norm(grad_x, pre_rows(h_out_copies), 2)
        grad_out[...] = total
        g_branch[...] = total.astype(LOW)
        grad_ffn[...] = jnp.zeros_like(grad_ffn)
        sums.right(4)
        loaded[3] = load_w(3, hbm.w_out)

    def feed(part):
        first, last = ((0, first_tiles), (first_tiles, tiles))[part]
        for copy in tile_copies(first):
            copy.start()

        def one(t, carry):
            slot = lax.rem(t, 2)
            for copy in tile_copies(t):
                copy.wait()

            @pl.when(t + 1 < last)
            def _():
                for copy in tile_copies(t + 1):
                    copy.start()

            span = pl.ds(pl.multiple_of((t - first) * tile, tile), tile)
            down_rows = w[2, pl.ds(pl.multiple_of(slot * tile, tile), tile)]
            grad_hidden = times_t(g_branch[...], down_rows).astype(LOW).astype(F32)
            gate, up = tile_pre[slot, 0], tile_pre[slot, 1]
            sig = jax.nn.sigmoid(gate)
            gg = (grad_hidden * up * sig * (1.0 + gate * (1.0 - sig))).astype(LOW)
            gu = (grad_hidden * (gate * sig)).astype(LOW)
            g_gate[part][:, span] = gg
            g_up[part][:, span] = gu
            grad_ffn[...] += times_t(gg, w[slot, :, :tile]) + times_t(
                gu, w[slot, :, tile : 2 * tile]
            )
            return carry

        lax.fori_loop(first, last, one, 0)
        sums.right(2 * part)
        sums.right(2 * part + 1)

    def feed_in():
        copies = load_pre(hbm.h_mid)
        loaded[3].wait()
        grad_mid[...] = grad_out[...] + through_norm(grad_ffn[...], pre_rows(copies), 1)
        g_attn[...] = grad_mid[...].astype(LOW)
        g_query[...] = times_t(g_attn[...], w[3]).astype(LOW)
        loaded[1] = load_w(1, hbm.w_query)
        loaded[2] = load_w(2, hbm.w_key)
        loaded[3] = load_w(3, hbm.w_value)
        loaded[0] = load_pre(hbm.embedded)

    own_key, own_value = grad_ffn, grad_out
    sent = w.at[0]

    def kv_copy(pair):
        slot = lax.rem(pair, 2)
        span = pl.ds(pl.multiple_of(pair * 128, 128), 128)
        return pltpu.make_async_copy(hbm.key_values.at[:, :, span], kv.at[slot], kv_sems.at[slot])

    def attend(first, last):
        row = lax.broadcasted_iota(jnp.int32, (tokens, tokens), 0)
        col = lax.broadcasted_iota(jnp.int32, (tokens, tokens), 1)
        mine = col <= row
        far_bias = jnp.where(rank >= 2, 0.0, NEG_BIG)
        near_bias = jnp.where(rank >= 1, 0.0, NEG_BIG)
        kv_copy(first).start()

        def three(edge, middle):
            return jnp.concatenate(
                [
                    jnp.where(mine, 0.0, edge).astype(LOW),
                    middle.astype(LOW),
                    jnp.where(mine, edge, 0.0).astype(LOW),
                ],
                axis=1,
            )

        def heads_pair(pair, carry):
            kv_copy(pair).wait()

            @pl.when(pair + 1 < last)
            def _():
                kv_copy(pair + 1).start()

            slot = lax.rem(pair, 2)
            span = pl.ds(pl.multiple_of(pair * 128, 128), 128)
            q2, ga2 = queries[:, span], g_query[:, span]
            k2, v2 = kv[slot, 0], kv[slot, 1]
            parts = []
            for side in range(2):
                total = head_lse(lse, pair * 2 + side)
                scores = times_t(q2 * sides[side], k2) * SCORE_SCALE
                edge = jnp.where(mine, scores[:, 2 * tokens :], scores[:, :tokens] + far_bias)
                edge = jnp.exp(edge - total)
                middle = jnp.exp(scores[:, tokens : 2 * tokens] + near_bias - total)
                grad_prob = times_t(ga2 * sides[side], v2)
                grad_edge = jnp.where(mine, grad_prob[:, 2 * tokens :], grad_prob[:, :tokens])
                grad_middle = grad_prob[:, tokens : 2 * tokens]
                row_total = jnp.sum(edge * grad_edge, axis=1, keepdims=True) + jnp.sum(
                    middle * grad_middle, axis=1, keepdims=True
                )
                grad_score = three(edge * (grad_edge - row_total), middle * (grad_middle - row_total))
                parts.append(
                    (
                        matmul(grad_score, k2),
                        t_times(grad_score, q2),
                        t_times(three(edge, middle), ga2),
                    )
                )
            left = lane < HD
            g_query[:, span] = (jnp.where(left, parts[0][0], parts[1][0]) * SCORE_SCALE).astype(LOW)
            for number, own, scale in ((1, own_key, SCORE_SCALE), (2, own_value, 1.0)):
                grad = jnp.where(left, parts[0][number], parts[1][number]) * scale
                own[:, span] = grad[2 * tokens :]
                start = (number - 1) * 2 * tokens
                sent[start : start + 2 * tokens, span] = grad[: 2 * tokens].astype(LOW)
            return carry

        lax.fori_loop(first, last, heads_pair, 0)

    there = rank >= 2

    def part_of(number, back):
        return sent.at[pl.ds((2 * number + 2 - back) * tokens, tokens)]

    def halo_pair():
        for number in range(2):
            here.send_if(
                there | (here.c == 1),
                part_of(number, 1),
                halo.at[1, number],
                halo_sems.at[1, number, 0],
                halo_sems.at[1, number, 1],
                here.at(dc=1),
            )

    def halo_send():
        for number in range(2):

            @pl.when(there | (here.c == 0))
            def _():
                here.expect(halo.at[1, number], halo_sems.at[1, number, 1])

            part = part_of(number, 2)

            @pl.when(there & (here.c == 1))
            def _():
                part[...] = (part[...].astype(F32) + halo[1, number].astype(F32)).astype(LOW)

            target = jnp.maximum(rank - 2, 0)
            here.send_if(
                there,
                part,
                halo.at[0, number],
                halo_sems.at[0, number, 0],
                halo_sems.at[0, number, 1],
                (here.z, target // 4, lax.rem(target, 4)),
            )

    def halo_add():
        for number, own, grad in ((0, own_key, g_key), (1, own_value, g_value)):

            @pl.when(here.c == 0)
            def _():
                own[...] += halo[1, number].astype(F32)

            @pl.when(rank + 2 < 8)
            def _():
                here.expect(halo.at[0, number], halo_sems.at[0, number, 1])
                own[...] += halo[0, number].astype(F32)

            grad[...] = own[...].astype(LOW)

    def embed_in():
        for slot in (1, 2, 3):
            loaded[slot].wait()
        grad = times_t(g_query[...], w[1]) + times_t(g_key[...], w[2]) + times_t(g_value[...], w[3])
        total = grad_mid[...] + through_norm(grad, pre_rows(loaded[0]), 0)
        g_embed[...] = total.astype(LOW)

    sums.product(0)
    cross_heads()
    sums.product(1)
    sums.product(2)
    sums.product(3)
    cross_in()
    sums.second(0)
    sums.product(4)
    sums.second(1)
    feed(0)
    sums.product(5)
    sums.product(6)
    sums.second(2)
    sums.third(0)
    feed(1)
    sums.product(7)
    sums.product(8)
    sums.second(3)
    sums.third(1)
    feed_in()
    sums.second(4)
    sums.third(2)
    pairs = width // 128
    attend(0, pairs // 2)
    sums.second(5)
    sums.third(3)
    attend(pairs // 2, pairs)
    halo_pair()
    halo_send()
    sums.second(6)
    sums.third(4)
    for i in range(4):
        sums.final(i)
    halo_add()
    sums.second(7)
    sums.third(5)
    embed_in()
    sums.second(8)
    sums.third(6)
    sums.third(7)
    sums.third(8)
    for i in range(4, 9):
        sums.final(i)
    here.finish()


def back_sums(lefts, streamed, kept, dp_count):
    n = dp_count
    low = jnp.bfloat16
    dma = pltpu.SemaphoreType.DMA
    hbm = pl.BlockSpec(memory_space=pl.ANY)
    vmem = pl.BlockSpec(memory_space=pltpu.VMEM)
    tokens, ff = streamed.gate_pre.shape
    patches, width = streamed.cot_patches.shape
    tile = 256
    first = (ff // tile + 1) // 2 * tile
    one = jax.ShapeDtypeStruct
    right_shapes = [(tokens, first)] * 2 + [(tokens, ff - first)] * 2
    right_shapes += [(tokens, width), (patches, width)]
    right_shapes += [(tokens, width)] * 2 + [(patches, width)]
    units, shapes, scratch, pool_count = plan_sums(
        BACK_PAIRS, [a.shape for a in lefts], right_shapes, n, 4
    )
    count = len(units)
    scratch += [
        pltpu.VMEM((4, width, width), low),
        pltpu.VMEM((2, 2, tokens, tile), F32),
        pltpu.VMEM((tokens, width), F32),
        pltpu.VMEM((tokens, width), F32),
        pltpu.VMEM((tokens, width), F32),
        pltpu.VMEM((2, 2, 3 * tokens, 128), low),
        pltpu.VMEM((2, 2, tokens, width), low),
        dma((4,)),
        dma((2, 5)),
        dma((width // tile,)),
        dma((2,)),
        dma((2, 2, 2)),
    ]
    results = pl.pallas_call(
        functools.partial(back_kernel, n, units, pool_count),
        out_shape=[one(shape, F32) for shape in shapes]
        + [one((8, width), F32)]
        + [one((tokens, width), low)] * 5,
        in_specs=[hbm] * (len(lefts) + len(streamed)) + [vmem] * len(kept),
        out_specs=[vmem] * (count + 6),
        scratch_shapes=scratch,
        compiler_params=pltpu.CompilerParams(
            collective_id=1, has_side_effects=True, vmem_limit_bytes=63 * 1024 * 1024
        ),
        name="back_sums",
    )(*lefts, *streamed, *kept)
    return results[:count], results[count:]


WEIGHT_STEPS = tuple(((i, 0, 2), (i, 1, 2)) for i in (0, 1, 2, 3, 4, 5, 6, 8, 9, 7, 10))


def by_rows(a, dp_count):
    depth, total = a.shape
    pairs = dp_count * 4
    both = total // pairs
    a = a.T.reshape(pairs, both, depth)
    rows = -(-(both // 2) // 16) * 16
    return jnp.stack([a[:, :rows], a[:, both - rows :]])


def own_rows(block, rows):
    core = lax.axis_index(SUB) % 2
    return jnp.where(core == 0, block[:rows], block[block.shape[0] - rows :])


def body(
    byte_ids,
    hash_ids,
    lengths,
    byte_table,
    hash_table,
    norm_attn,
    norm_ffn,
    norm_cross,
    w_query,
    w_key,
    w_value,
    w_out,
    w_gate,
    w_up,
    w_down,
    c_query,
    c_key,
    c_value,
    c_out,
    cot_bytes,
    cot_patches,
):
    dp_count = lax.axis_size(DP)
    rs_count = lax.axis_size(SEQ)
    all_count = dp_count * rs_count
    rank_seq = lax.axis_index(SEQ)
    rank_table = lax.axis_index(DP) * rs_count + rank_seq
    tokens, gram_count = hash_ids.shape
    rows_dev, model_width = hash_table.shape
    head_count = model_width // HD
    request_count = tokens * gram_count
    slot_count = 2 * request_count // all_count
    flat_ids = hash_ids.reshape(request_count)
    owners = flat_ids // rows_dev
    ordering = jnp.argsort(owners, stable=True)
    owners_sorted = owners[ordering]
    per_owner = jnp.sum(
        (owners[:, None] == jnp.arange(all_count, dtype=jnp.int32)[None, :]).astype(jnp.int32),
        axis=0,
    )
    first_slot = jnp.cumsum(per_owner) - per_owner
    place_sorted = (
        owners_sorted * slot_count
        + jnp.arange(request_count, dtype=jnp.int32)
        - first_slot[owners_sorted]
    )
    placement = jnp.zeros((request_count,), jnp.int32).at[ordering].set(place_sorted)
    requests = jnp.full((all_count * slot_count,), -1, jnp.int32).at[placement].set(flat_ids)
    requests = requests.reshape(dp_count, rs_count, slot_count)
    incoming = lax.all_to_all(
        lax.all_to_all(requests, DP, split_axis=0, concat_axis=0, tiled=True),
        SEQ,
        split_axis=1,
        concat_axis=1,
        tiled=True,
    )
    present = incoming >= 0
    safe_rows = jnp.where(present, incoming - rank_table * rows_dev, 0)
    served = jnp.where(present[..., None], hash_table[safe_rows], jnp.zeros((), jnp.bfloat16))
    returned = lax.all_to_all(
        lax.all_to_all(served, DP, split_axis=0, concat_axis=0, tiled=True),
        SEQ,
        split_axis=1,
        concat_axis=1,
        tiled=True,
    )
    fetched = returned.reshape(all_count * slot_count, model_width)[placement]
    fetched = fetched.astype(jnp.float32).reshape(tokens, gram_count, model_width)
    one_hot = byte_ids[:, None] == jnp.arange(BYTE_VALUES, dtype=jnp.int32)[None, :]
    embedded = matmul(one_hot.astype(jnp.bfloat16), byte_table) + jnp.sum(fetched, axis=1)
    row_counts = (
        jnp.zeros((rows_dev,), jnp.int32)
        .at[safe_rows.reshape(-1)]
        .add(present.reshape(-1).astype(jnp.int32))
    )
    weight_list = (
        w_query,
        w_key,
        w_value,
        w_out,
        w_gate,
        w_up,
        w_down,
        c_query,
        c_key,
        c_value,
        c_out,
    )
    gathered = (
        lax.all_gather(weight_list[0], DP, axis=0, tiled=True),
        lax.all_gather(weight_list[1], DP, axis=0, tiled=True),
        lax.all_gather(weight_list[2], DP, axis=0, tiled=True),
        lax.all_gather(weight_list[3], DP, axis=0, tiled=True),
        lax.all_gather(weight_list[4], DP, axis=0, tiled=True),
        lax.all_gather(weight_list[5], DP, axis=0, tiled=True),
        lax.all_gather(weight_list[6], DP, axis=0, tiled=True),
        lax.all_gather(weight_list[7], DP, axis=0, tiled=True),
        lax.all_gather(weight_list[8], DP, axis=0, tiled=True),
        lax.all_gather(weight_list[9], DP, axis=0, tiled=True),
        lax.all_gather(weight_list[10], DP, axis=0, tiled=True),
    )
    (
        full_query,
        full_key,
        full_value,
        full_out,
        full_gate,
        full_up,
        full_down,
        full_cquery,
        full_ckey,
        full_cvalue,
        full_cout,
    ) = gathered
    x_attn, normed_attn, scale_attn = normalize(embedded, norm_attn)
    queries = matmul(x_attn, full_query).astype(jnp.bfloat16).reshape(tokens, head_count, HD)
    key_rows = matmul(x_attn, full_key).astype(jnp.bfloat16).reshape(tokens, head_count, HD)
    value_rows = matmul(x_attn, full_value).astype(jnp.bfloat16).reshape(tokens, head_count, HD)
    behind = (WIN - 2) // tokens + 1
    key_parts = []
    value_parts = []
    for offset_back in range(behind, 0, -1):
        far_keys, far_values = passed_along((key_rows, value_rows), SEQ, offset_back)
        key_parts.append(far_keys)
        value_parts.append(far_values)
    all_keys = jnp.concatenate(key_parts + [key_rows], axis=0)
    all_values = jnp.concatenate(value_parts + [value_rows], axis=0)
    q_rows = min(tokens, 512)
    key_span = (WIN - 1 + q_rows - 1) // q_rows * q_rows
    base_key = (rank_seq - behind) * tokens
    block_index = 0
    q_start = block_index * q_rows
    k_start = behind * tokens + q_start - key_span
    allowed = window_mask(
        rank_seq * tokens + q_start, base_key + k_start, q_rows, q_rows + key_span
    )
    scores = (
        jnp.einsum("qhd,khd->hqk", queries, all_keys, preferred_element_type=jnp.float32)
        * SCORE_SCALE
    )
    prob_block, log_total = soft_forward(scores, allowed)
    attended_parts = jnp.einsum(
        "hqk,khd->qhd",
        prob_block.astype(jnp.bfloat16),
        all_values,
        preferred_element_type=jnp.float32,
    )
    lse_parts = [log_total]
    attended = attended_parts.astype(jnp.bfloat16).reshape(tokens, model_width)
    h_mid = embedded + matmul(attended, full_out)
    x_ffn, normed_ffn, scale_ffn = normalize(h_mid, norm_ffn)
    gate_pre = matmul(x_ffn, full_gate)
    up_pre = matmul(x_ffn, full_up)
    gate_sig = jax.nn.sigmoid(gate_pre)
    silu_val = gate_pre * gate_sig
    hidden = (silu_val * up_pre).astype(jnp.bfloat16)
    h_out = h_mid + matmul(hidden, full_down)
    byte_states = h_out.astype(jnp.bfloat16)
    x_cross, normed_cross, scale_cross = normalize(h_out, norm_cross)
    patch_len = lengths[0]
    patch_count = patch_len.shape[0]
    patch_end = jnp.cumsum(patch_len)
    patch_start = patch_end - patch_len
    byte_pos = jnp.arange(tokens, dtype=jnp.int32)
    member = (byte_pos[None, :] >= patch_start[:, None]) & (byte_pos[None, :] < patch_end[:, None])
    length_f = patch_len.astype(jnp.float32)[:, None]
    pooled = matmul(member.astype(jnp.bfloat16), x_cross) / length_f
    pooled_low = pooled.astype(jnp.bfloat16)
    p_query = (
        matmul(pooled_low, full_cquery).astype(jnp.bfloat16).reshape(patch_count, head_count, HD)
    )
    p_key = matmul(x_cross, full_ckey).astype(jnp.bfloat16).reshape(tokens, head_count, HD)
    p_value = matmul(x_cross, full_cvalue).astype(jnp.bfloat16).reshape(tokens, head_count, HD)
    cross_scores = (
        jnp.einsum("phd,thd->hpt", p_query, p_key, preferred_element_type=jnp.float32) * SCORE_SCALE
    )
    cross_prob, cross_lse = soft_forward(cross_scores, member[None])
    p_attended = (
        jnp.einsum(
            "hpt,thd->phd",
            cross_prob.astype(jnp.bfloat16),
            p_value,
            preferred_element_type=jnp.float32,
        )
        .astype(jnp.bfloat16)
        .reshape(patch_count, model_width)
    )
    patch_states = (pooled + matmul(p_attended, full_cout)).astype(jnp.bfloat16)
    grad_c_out = t_times(p_attended, cot_patches)
    grad_patt = (
        times_t(cot_patches, full_cout).astype(jnp.bfloat16).reshape(patch_count, head_count, HD)
    )
    cross_again = (
        jnp.einsum("phd,thd->hpt", p_query, p_key, preferred_element_type=jnp.float32) * SCORE_SCALE
    )
    cross_full = soft_again(cross_again, member[None], cross_lse)
    grad_cprob = jnp.einsum("phd,thd->hpt", grad_patt, p_value, preferred_element_type=jnp.float32)
    grad_cscore = soft_back(cross_full, grad_cprob)
    grad_pquery = (
        (
            jnp.einsum("hpt,thd->phd", grad_cscore, p_key, preferred_element_type=jnp.float32)
            * SCORE_SCALE
        )
        .astype(jnp.bfloat16)
        .reshape(patch_count, model_width)
    )
    grad_pkey = (
        (
            jnp.einsum("hpt,phd->thd", grad_cscore, p_query, preferred_element_type=jnp.float32)
            * SCORE_SCALE
        )
        .astype(jnp.bfloat16)
        .reshape(tokens, model_width)
    )
    grad_pvalue = (
        jnp.einsum(
            "hpt,phd->thd",
            cross_full.astype(jnp.bfloat16),
            grad_patt,
            preferred_element_type=jnp.float32,
        )
        .astype(jnp.bfloat16)
        .reshape(tokens, model_width)
    )
    grad_c_query = t_times(pooled_low, grad_pquery)
    grad_c_key = t_times(x_cross, grad_pkey)
    grad_c_value = t_times(x_cross, grad_pvalue)
    grad_pooled = cot_patches.astype(jnp.float32) + times_t(grad_pquery, full_cquery).astype(
        jnp.bfloat16
    ).astype(jnp.float32)
    to_bytes = lax.dot_general(
        member.astype(jnp.float32),
        grad_pooled / length_f,
        (((0,), (0,)), ((), ())),
        precision=PRECISE,
    )
    grad_xcross = (
        times_t(grad_pkey, full_ckey) + times_t(grad_pvalue, full_cvalue) + to_bytes
    ).astype(jnp.bfloat16)
    grad_hout_norm, grad_norm_cross = norm_back(
        grad_xcross.astype(jnp.float32), normed_cross, scale_cross, norm_cross
    )
    grad_hout = cot_bytes.astype(jnp.float32) + grad_hout_norm
    grad_branch_f = grad_hout.astype(jnp.bfloat16)
    grad_w_down = t_times(hidden, grad_branch_f)
    grad_hidden = times_t(grad_branch_f, full_down).astype(jnp.bfloat16).astype(jnp.float32)
    grad_gate = (grad_hidden * up_pre * gate_sig * (1.0 + gate_pre * (1.0 - gate_sig))).astype(
        jnp.bfloat16
    )
    grad_up = (grad_hidden * silu_val).astype(jnp.bfloat16)
    grad_w_gate = t_times(x_ffn, grad_gate)
    grad_w_up = t_times(x_ffn, grad_up)
    grad_xffn = (times_t(grad_gate, full_gate) + times_t(grad_up, full_up)).astype(jnp.bfloat16)
    grad_hmid_norm, grad_norm_ffn = norm_back(
        grad_xffn.astype(jnp.float32), normed_ffn, scale_ffn, norm_ffn
    )
    grad_hmid = grad_hout + grad_hmid_norm
    grad_branch_a = grad_hmid.astype(jnp.bfloat16)
    grad_w_out = t_times(attended, grad_branch_a)
    grad_att = times_t(grad_branch_a, full_out).astype(jnp.bfloat16).reshape(tokens, head_count, HD)
    grad_keys_all = jnp.zeros(((behind + 1) * tokens, head_count, HD), jnp.float32)
    grad_values_all = jnp.zeros(((behind + 1) * tokens, head_count, HD), jnp.float32)
    block_index = 0
    q_start = block_index * q_rows
    k_start = behind * tokens + q_start - key_span
    k_stop = k_start + q_rows + key_span
    allowed = window_mask(
        rank_seq * tokens + q_start, base_key + k_start, q_rows, q_rows + key_span
    )
    scores = (
        jnp.einsum("qhd,khd->hqk", queries, all_keys, preferred_element_type=jnp.float32)
        * SCORE_SCALE
    )
    prob_block = soft_again(scores, allowed, lse_parts[block_index])
    grad_prob = jnp.einsum("qhd,khd->hqk", grad_att, all_values, preferred_element_type=jnp.float32)
    grad_score = soft_back(prob_block, grad_prob)
    grad_q_parts = (
        jnp.einsum("hqk,khd->qhd", grad_score, all_keys, preferred_element_type=jnp.float32)
        * SCORE_SCALE
    )
    grad_keys_all = grad_keys_all.at[k_start:k_stop].add(
        jnp.einsum("hqk,qhd->khd", grad_score, queries, preferred_element_type=jnp.float32)
        * SCORE_SCALE
    )
    grad_values_all = grad_values_all.at[k_start:k_stop].add(
        jnp.einsum(
            "hqk,qhd->khd",
            prob_block.astype(jnp.bfloat16),
            grad_att,
            preferred_element_type=jnp.float32,
        )
    )
    grad_keys = grad_keys_all[behind * tokens :]
    grad_values = grad_values_all[behind * tokens :]
    for offset_back in range(behind, 0, -1):
        part_index = behind - offset_back
        far_grad_k, far_grad_v = (
            passed_along(
                grad_keys_all[part_index * tokens : (part_index + 1) * tokens].astype(jnp.bfloat16),
                SEQ,
                -offset_back,
            ).astype(jnp.float32),
            passed_along(
                grad_values_all[part_index * tokens : (part_index + 1) * tokens].astype(
                    jnp.bfloat16
                ),
                SEQ,
                -offset_back,
            ).astype(jnp.float32),
        )
        grad_keys = grad_keys + far_grad_k
        grad_values = grad_values + far_grad_v
    grad_queries = grad_q_parts.astype(jnp.bfloat16).reshape(tokens, model_width)
    grad_keys_low = grad_keys.astype(jnp.bfloat16).reshape(tokens, model_width)
    grad_values_low = grad_values.astype(jnp.bfloat16).reshape(tokens, model_width)
    grad_w_query = t_times(x_attn, grad_queries)
    grad_w_key = t_times(x_attn, grad_keys_low)
    grad_w_value = t_times(x_attn, grad_values_low)
    grad_xattn = (
        times_t(grad_queries, full_query)
        + times_t(grad_keys_low, full_key)
        + times_t(grad_values_low, full_value)
    ).astype(jnp.bfloat16)
    grad_embed_norm, grad_norm_attn = norm_back(
        grad_xattn.astype(jnp.float32), normed_attn, scale_attn, norm_attn
    )
    grad_embed = grad_hmid + grad_embed_norm
    embed_grad = grad_embed.astype(jnp.bfloat16)
    grad_byte_table = lax.dot_general(
        one_hot.astype(jnp.float32), grad_embed, (((0,), (0,)), ((), ())), precision=PRECISE
    )
    per_request = jnp.broadcast_to(
        grad_embed[:, None, :], (tokens, gram_count, model_width)
    ).reshape(request_count, model_width)
    outgoing = (
        jnp.zeros((all_count * slot_count, model_width), jnp.float32).at[placement].set(per_request)
    )
    outgoing = outgoing.reshape(dp_count, rs_count, slot_count, model_width)
    arrived = lax.all_to_all(
        lax.all_to_all(
            outgoing.astype(jnp.bfloat16), DP, split_axis=0, concat_axis=0, tiled=True
        ),
        SEQ,
        split_axis=1,
        concat_axis=1,
        tiled=True,
    ).astype(outgoing.dtype)
    hash_table_grad = (
        jnp.zeros((rows_dev, model_width), jnp.float32)
        .at[safe_rows.reshape(-1)]
        .add(jnp.where(present[..., None], arrived, 0.0).reshape(-1, model_width))
    )
    summed_all = (
        lax.psum_scatter(grad_norm_attn, ALL, scatter_dimension=0, tiled=True),
        lax.psum_scatter(grad_norm_ffn, ALL, scatter_dimension=0, tiled=True),
        lax.psum_scatter(grad_norm_cross, ALL, scatter_dimension=0, tiled=True),
        lax.psum_scatter(grad_w_query, ALL, scatter_dimension=0, tiled=True),
        lax.psum_scatter(grad_w_key, ALL, scatter_dimension=0, tiled=True),
        lax.psum_scatter(grad_w_value, ALL, scatter_dimension=0, tiled=True),
        lax.psum_scatter(grad_w_out, ALL, scatter_dimension=0, tiled=True),
        lax.psum_scatter(grad_w_gate, ALL, scatter_dimension=0, tiled=True),
        lax.psum_scatter(grad_w_up, ALL, scatter_dimension=0, tiled=True),
        lax.psum_scatter(grad_w_down, ALL, scatter_dimension=0, tiled=True),
        lax.psum_scatter(grad_c_query, ALL, scatter_dimension=0, tiled=True),
        lax.psum_scatter(grad_c_key, ALL, scatter_dimension=0, tiled=True),
        lax.psum_scatter(grad_c_value, ALL, scatter_dimension=0, tiled=True),
        lax.psum_scatter(grad_c_out, ALL, scatter_dimension=0, tiled=True),
        lax.psum_scatter(grad_byte_table, ALL, scatter_dimension=0, tiled=True),
    )
    (
        out_norm_attn,
        out_norm_ffn,
        out_norm_cross,
        out_query,
        out_key,
        out_value,
        out_proj,
        out_gate,
        out_up,
        out_down,
        out_cquery,
        out_ckey,
        out_cvalue,
        out_cout,
        out_bytes,
    ) = summed_all
    return (
        byte_states,
        patch_states,
        embed_grad,
        out_bytes,
        hash_table_grad,
        row_counts,
        out_norm_attn,
        out_norm_ffn,
        out_norm_cross,
        out_query,
        out_key,
        out_value,
        out_proj,
        out_gate,
        out_up,
        out_down,
        out_cquery,
        out_ckey,
        out_cvalue,
        out_cout,
    )


def fast_body(
    byte_ids,
    hash_ids,
    lengths,
    byte_table,
    hash_table,
    norm_attn,
    norm_ffn,
    norm_cross,
    w_query,
    w_key,
    w_value,
    w_out,
    w_gate,
    w_up,
    w_down,
    c_query,
    c_key,
    c_value,
    c_out,
    cot_bytes,
    cot_patches,
):
    dp_count = lax.axis_size(DP)
    rs_count = lax.axis_size(SEQ)
    all_count = dp_count * rs_count
    rank_table = lax.axis_index(ALL)
    rows_dev, model_width = hash_table.shape
    patch_len = lengths[0]
    patch_end = jnp.cumsum(patch_len)[:, None]
    patch_start = patch_end - patch_len[:, None]
    gains = jnp.concatenate(
        [norm_attn[None], norm_ffn[None], norm_cross[None], jnp.zeros((5, model_width), jnp.float32)]
    )
    full, embedded, entries, kept = fetch(
        hash_ids,
        hash_table,
        (
            w_query,
            w_key,
            w_value,
            w_out,
            w_gate,
            w_up,
            w_down,
            c_query,
            c_key,
            c_value,
            c_out,
        ),
        (byte_ids[:, None], byte_table, gains, patch_start, patch_end),
        WEIGHT_STEPS,
        dp_count,
    )
    lefts = [
        by_rows(a, dp_count)
        for a in (kept.x_ffn, kept.hidden, kept.pooled, kept.x_cross, kept.p_attended)
    ]
    sums, results = back_sums(
        lefts,
        Streamed(
            kept.gate_pre,
            kept.up_pre,
            kept.h_out,
            kept.h_mid,
            embedded,
            kept.key_values,
            *full,
            cot_patches,
        ),
        (
            cot_bytes,
            kept.p_query,
            kept.p_key,
            kept.p_value,
            kept.cross_lse,
            gains,
            patch_start,
            patch_end,
            kept.queries,
            kept.lse,
        ),
        dp_count,
    )
    out_cout, out_ckey, out_cvalue, out_cquery, down_rows = sums[:5]
    out_gate = jnp.concatenate([sums[5], sums[7]], axis=1)
    out_up = jnp.concatenate([sums[6], sums[8]], axis=1)
    gain_rows, grad_branch_a, grad_queries, grad_keys, grad_values, embed_grad = results
    one_hot = byte_ids[:, None] == jnp.arange(BYTE_VALUES, dtype=jnp.int32)[None, :]
    lefts = [
        by_rows(a, dp_count) for a in (kept.x_attn, kept.attended, one_hot.astype(jnp.bfloat16))
    ]
    rights = [grad_queries, grad_keys, grad_values, grad_branch_a, embed_grad]
    sums, gain_sums, hash_table_grad, counts = last_sums(
        [(1, 3), (0, 0), (0, 1), (0, 2), (2, 4)],
        lefts,
        rights,
        embed_grad,
        gain_rows,
        entries,
        rows_dev,
        dp_count,
    )
    out_proj, out_query, out_key, out_value, byte_rows = sums
    out_down = own_rows(down_rows, kept.hidden.shape[1] // all_count)
    out_bytes = own_rows(byte_rows, BYTE_VALUES // all_count)
    row_counts = counts[:, 0].astype(jnp.int32)
    own_gains = lax.dynamic_slice_in_dim(
        gain_sums, rank_table * (model_width // all_count), model_width // all_count, 1
    )
    return (
        kept.byte_states,
        kept.patch_states,
        embed_grad,
        out_bytes,
        hash_table_grad,
        row_counts,
        own_gains[0],
        own_gains[1],
        own_gains[2],
        out_query,
        out_key,
        out_value,
        out_proj,
        out_gate,
        out_up,
        out_down,
        out_cquery,
        out_ckey,
        out_cvalue,
        out_cout,
    )


def solution(mesh):
    fits = mesh.shape[REP] == 2 and mesh.shape[SUB] == 4 and mesh.shape[DP] <= 4
    return jax.shard_map(
        fast_body if fits else body,
        mesh=mesh,
        in_specs=(
            P(ALL),
            P(ALL, None),
            P(ALL, None),
            P(),
            P(ALL, None),
            P(),
            P(),
            P(),
            P(DP, None),
            P(DP, None),
            P(DP, None),
            P(DP, None),
            P(DP, None),
            P(DP, None),
            P(DP, None),
            P(DP, None),
            P(DP, None),
            P(DP, None),
            P(DP, None),
            P(ALL, None),
            P(ALL, None),
        ),
        out_specs=(
            P(ALL, None),
            P(ALL, None),
            P(ALL, None),
            P(ALL, None),
            P(ALL, None),
            P(ALL),
            P(ALL),
            P(ALL),
            P(ALL),
            P(ALL, None),
            P(ALL, None),
            P(ALL, None),
            P(ALL, None),
            P(ALL, None),
            P(ALL, None),
            P(ALL, None),
            P(ALL, None),
            P(ALL, None),
            P(ALL, None),
            P(ALL, None),
        ),
        check_vma=False,
    )
```

```python
import functools
import typing

import jax
import jax.numpy as jnp
from jax import lax
from jax.experimental import pallas as pl
from jax.experimental.pallas import tpu as pltpu
from jax.sharding import PartitionSpec as P

DP, REP, SUB = "dp", "rep", "sub"
SEQ = (REP, SUB)
ALL = (DP, REP, SUB)
HD = 64
WIN = 512
BYTE_VALUES = 256


PRECISE = lax.Precision.HIGHEST
NEG_BIG = -1e30
EPSILON = 1e-06
SCORE_SCALE = 0.125


def passed_along(x, axis, by):
    devices = lax.axis_size(axis)
    pairs = [(i, i + by) for i in range(devices) if 0 <= i + by < devices]
    return lax.ppermute(x, axis, pairs)


def matmul(matrix_a, matrix_b):
    return jnp.dot(matrix_a, matrix_b, preferred_element_type=jnp.float32)


def times_t(matrix_a, matrix_b):
    return lax.dot_general(
        matrix_a, matrix_b, (((1,), (1,)), ((), ())), preferred_element_type=jnp.float32
    )


def t_times(matrix_a, matrix_b):
    return lax.dot_general(
        matrix_a, matrix_b, (((0,), (0,)), ((), ())), preferred_element_type=jnp.float32
    )


def normalize(values, gains):
    inv_rms = lax.rsqrt(jnp.mean(values * values, axis=-1, keepdims=True) + EPSILON)
    normed = values * inv_rms
    return ((normed * gains).astype(jnp.bfloat16), normed, inv_rms)


def norm_back(grad_out, normed, inv_rms, gains):
    grad_gain = jnp.sum(grad_out * normed, axis=0)
    scaled_grad = grad_out * gains
    grad_in = inv_rms * (
        scaled_grad - normed * jnp.mean(scaled_grad * normed, axis=-1, keepdims=True)
    )
    return (grad_in, grad_gain)


def soft_forward(scores, allowed):
    masked = jnp.where(allowed, scores, NEG_BIG)
    row_max = jnp.max(masked, axis=-1, keepdims=True)
    exps = jnp.exp(masked - row_max)
    row_sum = jnp.sum(exps, axis=-1, keepdims=True)
    return (exps / row_sum, row_max + jnp.log(row_sum))


def soft_again(scores, allowed, log_total):
    return jnp.where(allowed, jnp.exp(scores - log_total), 0.0)


def soft_back(probs_full, grad_probs):
    row_total = jnp.sum(probs_full * grad_probs, axis=-1, keepdims=True)
    return (probs_full * (grad_probs - row_total)).astype(jnp.bfloat16)


def window_mask(first_query, first_key, row_count, col_count):
    query_pos = first_query + jnp.arange(row_count, dtype=jnp.int32)
    key_pos = first_key + jnp.arange(col_count, dtype=jnp.int32)
    near = (
        (key_pos[None, :] <= query_pos[:, None])
        & (key_pos[None, :] > query_pos[:, None] - WIN)
        & (key_pos[None, :] >= 0)
    )
    return near[None]


MESH_ID = pl.DeviceIdType.MESH
SLOTS = 96
GATHER_LAGS = (1, 2, 3)


HASH, GATHER, FORWARD = range(3)


SCHEDULE = (
    (GATHER, 0),
    (HASH, 0),
    (GATHER, 1),
    (HASH, 1),
    (HASH, 2),
    (GATHER, 2),
    (HASH, 3),
    (GATHER, 3),
    (HASH, 4),
    (GATHER, 4),
    (HASH, 5),
    (GATHER, 5),
    (HASH, 6),
    (GATHER, 6),
    (HASH, 7),
    (FORWARD, 2),
    (GATHER, 7),
    (FORWARD, 2),
    (GATHER, 8),
    (FORWARD, 1),
    (GATHER, 9),
    (FORWARD, 2),
    (GATHER, 10),
    (FORWARD, 1),
    (GATHER, 11),
    (FORWARD, 2),
    (GATHER, 12),
    (FORWARD, 2),
    (GATHER, 13),
    (FORWARD, 3),
)
VMEM_CAP = 60 * 1024 * 1024


class Place:
    def __init__(self, dp_count):
        self.n = dp_count
        self.z = lax.axis_index(DP)
        self.x = lax.axis_index(REP)
        sub = lax.axis_index(SUB)
        self.y = sub // 2
        self.c = sub % 2
        self.started, self.maybe = [], []

    def at(self, dz=0, dx=0, dy=0, dc=0):
        z = lax.rem(self.z + dz, self.n) if dz else self.z
        x = 1 - self.x if dx else self.x
        y = 1 - self.y if dy else self.y
        c = 1 - self.c if dc else self.c
        return (z, x, y * 2 + c)

    def greet(self):
        barrier = pltpu.get_barrier_semaphore()
        peers = [
            self.at(dx=dx, dy=dy, dc=dc)
            for dx in range(2)
            for dy in range(2)
            for dc in range(2)
            if dx + dy + dc > 0
        ]
        peers += [self.at(dz=j) for j in range(1, self.n)]
        for peer in peers:
            pl.semaphore_signal(barrier, inc=1, device_id=peer, device_id_type=MESH_ID)
        pl.semaphore_wait(barrier, len(peers))

    def send_if(self, there, src, dst, send_sem, recv_sem, peer):
        copy = pltpu.make_async_remote_copy(
            src_ref=src,
            dst_ref=dst,
            send_sem=send_sem,
            recv_sem=recv_sem,
            device_id=peer,
            device_id_type=MESH_ID,
        )
        pl.when(there)(copy.start)
        self.maybe.append((there, copy))

    def send(self, src, dst, send_sem, recv_sem, peer):
        copy = pltpu.make_async_remote_copy(
            src_ref=src,
            dst_ref=dst,
            send_sem=send_sem,
            recv_sem=recv_sem,
            device_id=peer,
            device_id_type=MESH_ID,
        )
        copy.start()
        self.started.append(copy)
        return copy

    def expect(self, dst, recv_sem):
        pltpu.make_async_remote_copy(
            src_ref=dst,
            dst_ref=dst,
            send_sem=recv_sem,
            recv_sem=recv_sem,
            device_id=self.at(dc=1),
            device_id_type=MESH_ID,
        ).wait_recv()

    def sent(self, copy):
        copy.wait_send()
        self.started = [other for other in self.started if other is not copy]

    def finish(self):
        for copy in self.started:
            copy.wait_send()
        for there, copy in self.maybe:
            pl.when(there)(copy.wait_send)
        self.started, self.maybe = [], []


def add_into(dst, src, blocks, width):
    def step(i, carry):
        total = dst(i)[...].astype(jnp.float32) + src(i)[...].astype(jnp.float32)
        dst(i)[...] = total.astype(jnp.bfloat16)
        return carry

    lax.fori_loop(0, blocks, step, 0)


class Reduction:
    def __init__(self, here, p0, r1a, r1b, r2a, r2b, sems, index):
        self.here, self.p0 = here, p0
        self.r1a, self.r1b, self.r2a, self.r2b = r1a, r1b, r2a, r2b
        self.sems, self.i = sems, index
        self.planes, _, _, self.rows, cols = p0.shape
        self.half = cols // 2
        self.left = pl.ds(0, self.half)
        self.right = pl.ds(self.half, self.half)

    def sem(self, k):
        return self.sems.at[self.i, k, 0], self.sems.at[self.i, k, 1]

    def first(self):
        h = self.here
        self.s1a = h.send(
            self.p0.at[:, 1 - h.x, :, :, self.left], self.r1a, *self.sem(0), h.at(dx=1)
        )
        self.s1b = h.send(
            self.p0.at[:, :, 1 - h.y, :, self.right], self.r1b, *self.sem(1), h.at(dy=1)
        )

    def second(self):
        h = self.here
        self.s1a.wait_recv()
        add_into(
            lambda i: self.p0.at[i // 2, h.x, i % 2, :, self.left],
            lambda i: self.r1a.at[i // 2, i % 2],
            2 * self.planes,
            self.half,
        )
        self.s2a = h.send(
            self.p0.at[:, h.x, 1 - h.y, :, self.left], self.r2a, *self.sem(2), h.at(dy=1)
        )
        self.s1b.wait_recv()
        add_into(
            lambda i: self.p0.at[i // 2, i % 2, h.y, :, self.right],
            lambda i: self.r1b.at[i // 2, i % 2],
            2 * self.planes,
            self.half,
        )
        self.s2b = h.send(
            self.p0.at[:, 1 - h.x, h.y, :, self.right], self.r2b, *self.sem(3), h.at(dx=1)
        )

    def third(self):
        h = self.here
        self.s2a.wait_recv()
        add_into(
            lambda i: self.p0.at[i, h.x, h.y, :, self.left],
            lambda i: self.r2a.at[i],
            self.planes,
            self.half,
        )
        self.s2b.wait_recv()
        add_into(
            lambda i: self.p0.at[i, h.x, h.y, :, self.right],
            lambda i: self.r2b.at[i],
            self.planes,
            self.half,
        )
        return self.p0.at[:, h.x, h.y]


EXTRA_IN = 5
F32, LOW = jnp.float32, jnp.bfloat16
class Kept(typing.NamedTuple):
    x_attn: typing.Any
    queries: typing.Any
    key_values: typing.Any
    lse: typing.Any
    attended: typing.Any
    h_mid: typing.Any
    x_ffn: typing.Any
    gate_pre: typing.Any
    up_pre: typing.Any
    hidden: typing.Any
    h_out: typing.Any
    byte_states: typing.Any
    x_cross: typing.Any
    pooled: typing.Any
    p_query: typing.Any
    p_key: typing.Any
    p_value: typing.Any
    cross_lse: typing.Any
    p_attended: typing.Any
    patch_states: typing.Any


def kept_shapes(t, w, f, p):
    one = jax.ShapeDtypeStruct
    return Kept(
        x_attn=one((t, w), LOW),
        queries=one((t, w), LOW),
        key_values=one((2, 3 * t, w), LOW),
        lse=one((t, 128), F32),
        attended=one((t, w), LOW),
        h_mid=one((t, w), F32),
        x_ffn=one((t, w), LOW),
        gate_pre=one((t, f), F32),
        up_pre=one((t, f), F32),
        hidden=one((t, f), LOW),
        h_out=one((t, w), F32),
        byte_states=one((t, w), LOW),
        x_cross=one((t, w), LOW),
        pooled=one((p, w), LOW),
        p_query=one((p, w), LOW),
        p_key=one((t, w), LOW),
        p_value=one((t, w), LOW),
        cross_lse=one((p, 128), F32),
        p_attended=one((p, w), LOW),
        patch_states=one((p, w), LOW),
    )


def forward_steps(here, fulls, embedded, extra_in, extra_out, slots, scratch):
    byte_ids, byte_table, gains, starts, ends = extra_in
    out = Kept(*extra_out)
    gate_w, up_w, x_halo, load_sems, halo_sems = scratch
    tokens, width = embedded.shape
    heads = width // HD
    n = here.n
    z, x, y, c = here.z, here.x, here.y, here.c
    rank = (x * 2 + y) * 2 + c
    loads = {}
    kv = out.key_values

    def load(i, *targets):
        copies = []
        for b, target in enumerate(targets):
            rows = target.shape[0]
            copy = pltpu.make_async_copy(
                fulls[i].at[pl.ds(b * rows, rows)], target, load_sems.at[i, b]
            )
            copy.start()
            copies.append(copy)
        loads[i] = copies

    def load_slot(i, slot):
        for b in range(4):
            copy = pltpu.make_async_copy(
                fulls[i].at[pl.ds(b * (width // 4), width // 4)],
                slots[slot].at[b // 2, b % 2],
                load_sems.at[i, b],
            )
            copy.start()
            loads.setdefault(i, []).append(copy)

    def wait(*weights):
        for i in weights:
            for copy in loads[i]:
                copy.wait()

    def through(a, slot):
        return matmul(a, slots[slot][...].reshape(width, width))

    def embed():
        load_slot(0, 0)
        load_slot(1, 1)
        load_slot(2, 2)
        ids = lax.broadcasted_iota(jnp.int32, (tokens, BYTE_VALUES), 1)
        pick = jnp.where(byte_ids[...] == ids, 1.0, 0.0).astype(LOW)
        embedded[...] = embedded[...] + matmul(pick, byte_table[...])
        out.x_attn[...] = normalize(embedded[...], gains[0:1])[0]
        halo_send()

    def halo_send():
        target = jnp.minimum(rank + 2, 7)
        here.send_if(
            rank + 2 < 8,
            out.x_attn,
            x_halo.at[0],
            halo_sems.at[0, 0],
            halo_sems.at[0, 1],
            (z, target // 4, lax.rem(target, 4)),
        )
        here.send_if(
            c == 0, out.x_attn, x_halo.at[1], halo_sems.at[1, 0], halo_sems.at[1, 1], here.at(dc=1)
        )

    def project():
        wait(0, 1, 2)
        a = out.x_attn[...]
        out.queries[...] = through(a, 0).astype(LOW)
        kv[0, 2 * tokens :] = through(a, 1).astype(LOW)
        kv[1, 2 * tokens :] = through(a, 2).astype(LOW)

    def halo():
        there = rank >= 2

        @pl.when(there)
        def _():
            here.expect(x_halo.at[0], halo_sems.at[0, 1])

        here.send_if(
            there & (c == 1),
            x_halo.at[0],
            x_halo.at[1],
            halo_sems.at[1, 0],
            halo_sems.at[1, 1],
            here.at(dc=1),
        )

        @pl.when(there | (c == 1))
        def _():
            here.expect(x_halo.at[1], halo_sems.at[1, 1])

        @pl.when(jnp.logical_not(there))
        def _():
            x_halo[0] = jnp.zeros_like(x_halo[0])

        @pl.when(rank == 0)
        def _():
            x_halo[1] = jnp.zeros_like(x_halo[1])

        a = x_halo[...].reshape(2 * tokens, width)
        kv[0, : 2 * tokens] = through(a, 1).astype(LOW)
        kv[1, : 2 * tokens] = through(a, 2).astype(LOW)

    lane = lax.broadcasted_iota(jnp.int32, (1, 128), 1)
    sides = [jnp.where(lane < HD, 1.0, 0.0).astype(LOW), jnp.where(lane < HD, 0.0, 1.0).astype(LOW)]

    def attend(first):
        row = lax.broadcasted_iota(jnp.int32, (tokens, tokens), 0)
        col = lax.broadcasted_iota(jnp.int32, (tokens, tokens), 1)
        mine = col <= row
        far_bias = jnp.where(rank >= 2, 0.0, NEG_BIG)
        near_bias = jnp.where(rank >= 1, 0.0, NEG_BIG)
        if first == 0:
            out.lse[...] = jnp.zeros_like(out.lse)
        else:
            load_slot(3, 3)

        def heads_pair(pair, carry):
            span = pl.ds(pl.multiple_of(pair * 128, 128), 128)
            q2 = out.queries[:, span]
            k2, v2 = kv[0, :, span], kv[1, :, span]
            halves = []
            for side in range(2):
                scores = times_t(q2 * sides[side], k2) * SCORE_SCALE
                edge = jnp.where(mine, scores[:, 2 * tokens :], scores[:, :tokens] + far_bias)
                middle = scores[:, tokens : 2 * tokens] + near_bias
                top = jnp.maximum(
                    jnp.max(edge, axis=1, keepdims=True), jnp.max(middle, axis=1, keepdims=True)
                )
                edge, middle = jnp.exp(edge - top), jnp.exp(middle - top)
                total = jnp.sum(edge, axis=1, keepdims=True) + jnp.sum(
                    middle, axis=1, keepdims=True
                )
                inverse = 1.0 / total
                edge, middle = edge * inverse, middle * inverse
                probs = jnp.concatenate(
                    [
                        jnp.where(mine, 0.0, edge).astype(LOW),
                        middle.astype(LOW),
                        jnp.where(mine, edge, 0.0).astype(LOW),
                    ],
                    axis=1,
                )
                halves.append(matmul(probs, v2))
                where = lane == pair * 2 + side
                out.lse[...] = jnp.where(where, top + jnp.log(total), out.lse[...])
            out.attended[:, span] = jnp.where(lane < HD, halves[0], halves[1]).astype(LOW)
            return carry

        lax.fori_loop(first * heads // 4, (first + 1) * heads // 4, heads_pair, 0)

    def attention_out():
        wait(3)
        h_mid = embedded[...] + through(out.attended[...], 3)
        out.h_mid[...] = h_mid
        out.x_ffn[...] = normalize(h_mid, gains[1:2])[0]

    def down_block(t):
        return slots[t // 4].at[t // 2 % 2, t % 2]

    tile = 256
    tiles = gate_w.shape[1] // tile

    def feed_forward():
        for t in range(tiles):
            copy = pltpu.make_async_copy(
                fulls[6].at[pl.ds(t * tile, tile)], down_block(t), down_sems.at[t]
            )
            copy.start()
            loads.setdefault(6, []).append(copy)
        wait(4, 5)
        a = out.x_ffn[...]

        def columns(t, carry):
            span = pl.ds(pl.multiple_of(t * tile, tile), tile)
            gate = matmul(a, gate_w[:, span])
            up = matmul(a, up_w[:, span])
            out.gate_pre[:, span] = gate
            out.up_pre[:, span] = up
            out.hidden[:, span] = (gate * jax.nn.sigmoid(gate) * up).astype(LOW)
            return carry

        lax.fori_loop(0, tiles, columns, 0)

    def feed_out():
        wait(6)
        total = out.h_mid[...]
        for t in range(tiles):
            total = total + matmul(
                out.hidden[:, t * tile : (t + 1) * tile], down_block(t)[...]
            )
        out.h_out[...] = total
        out.byte_states[...] = total.astype(LOW)
        out.x_cross[...] = normalize(total, gains[2:3])[0]

    byte_pos = lax.broadcasted_iota(jnp.int32, (starts.shape[0], tokens), 1)

    def member():
        return (byte_pos >= starts[...]) & (byte_pos < ends[...])

    pooled_f = []

    def cross_keys():
        inside = jnp.where(member(), 1.0, 0.0).astype(LOW)
        length = (ends[...] - starts[...]).astype(F32)
        pooled = matmul(inside, out.x_cross[...]) / length
        pooled_f.append(pooled)
        out.pooled[...] = pooled.astype(LOW)
        wait(8, 9)
        a = out.x_cross[...]
        out.p_key[...] = through(a, 4).astype(LOW)
        out.p_value[...] = through(a, 5).astype(LOW)

    def cross_query():
        wait(7)
        out.p_query[...] = through(out.pooled[...], 3).astype(LOW)
        allowed = member()
        out.cross_lse[...] = jnp.zeros_like(out.cross_lse)

        def heads_pair(pair, carry):
            span = pl.ds(pl.multiple_of(pair * 128, 128), 128)
            q2, k2, v2 = out.p_query[:, span], out.p_key[:, span], out.p_value[:, span]
            halves = []
            for side in range(2):
                scores = times_t(q2 * sides[side], k2) * SCORE_SCALE
                masked = jnp.where(allowed, scores, NEG_BIG)
                top = jnp.max(masked, axis=1, keepdims=True)
                exps = jnp.exp(masked - top)
                total = jnp.sum(exps, axis=1, keepdims=True)
                halves.append(matmul((exps / total).astype(LOW), v2))
                where = lane == pair * 2 + side
                out.cross_lse[...] = jnp.where(
                    where, top + jnp.log(total), out.cross_lse[...]
                )
            out.p_attended[:, span] = jnp.where(lane < HD, halves[0], halves[1]).astype(LOW)
            return carry

        lax.fori_loop(0, heads // 2, heads_pair, 0)

    def cross_out():
        wait(10)
        states = pooled_f[0] + through(out.p_attended[...], 0)
        out.patch_states[...] = states.astype(LOW)

    down_sems = load_sems.at[6]
    return [
        ((0, 1, 2), embed),
        ((), project),
        ((), halo),
        ((), lambda: attend(0)),
        ((3,), lambda: attend(1)),
        ((), attention_out),
        ((4, 5), lambda: (load(4, gate_w), load(5, up_w))),
        ((6,), feed_forward),
        ((8, 9), lambda: (load_slot(8, 4), load_slot(9, 5))),
        ((), feed_out),
        ((7,), lambda: load_slot(7, 3)),
        ((), cross_keys),
        ((10,), lambda: load_slot(10, 0)),
        ((), cross_query),
        ((), cross_out),
    ]


def fetch_kernel(dp_count, weight_count, steps_of, tokens, gram_count, used_lines, *refs):
    shards = refs[:weight_count]
    refs = list(refs[weight_count:])

    def take(number):
        taken = refs[:number]
        del refs[:number]
        return taken

    ids, table = take(2)
    extra_in = take(EXTRA_IN)
    fulls = take(weight_count)
    embedded, lists = take(2)
    extra_out = take(len(Kept._fields))
    (
        all_ids,
        send0,
        p0,
        r1a,
        r1b,
        r2a,
        r2b,
        r3,
        g_rows,
        core_sems,
        stage_sems,
        z_sems,
        local_sems,
        w_send,
        w_recv,
        z_send,
        id_sems,
        places,
        entries,
        *extra_scratch,
    ) = refs
    here = Place(dp_count)
    n = dp_count
    z, x, y, c = here.z, here.x, here.y, here.c

    class Weight:
        def __init__(self, number, i, part, parts, kind):
            self.i = number
            self.kind = kind
            rows, cols = shards[i].shape
            self.by_cols = rows // 8 % 16 != 0
            self.all_rows, self.count = rows, rows // parts
            self.first = part * self.count
            self.shard = shards[i].at[pl.ds(self.first, self.count)]
            self.full = fulls[i]
            self.step = (cols if self.by_cols else rows // parts) // 8
            near, far = (x, y) if kind == 0 else (y, x)
            self.q = (c * 2 + far) * 2 + near

        def on(self, plane):
            return self.full.at[pl.ds(plane * self.all_rows + self.first, self.count)]

        def cut(self, ref, start, count):
            span = pl.ds(start * self.step, count * self.step)
            if self.by_cols:
                return ref.at[:, span]
            return ref.at[span, :]

        def local(self):
            here.send(
                self.shard,
                self.on(z),
                local_sems.at[self.i, 0],
                local_sems.at[self.i, 1],
                here.at(dc=1),
            )

        def stage(self, k, j, start, count, src_ref, plane, peer):
            here.send(
                self.cut(src_ref, start, count),
                self.cut(self.on(plane), start, count),
                w_send.at[self.i, k, j - 1],
                w_recv.at[self.i, k, j - 1],
                peer,
            )

        def came(self, k, j, start, count):
            plane = lax.rem(z + n - j, n)
            here.expect(
                self.cut(self.on(plane), start, count), w_recv.at[self.i, k, j - 1]
            )
            return plane

        def hop(self, there, up, k, plane, src_ref):
            peer = jnp.clip(z + 1 if up else z - 1, 0, n - 1)
            here.send_if(
                there,
                self.cut(src_ref, self.q, 1),
                self.cut(self.on(plane), self.q, 1),
                z_send.at[self.i, 0 if up else 1, k],
                w_recv.at[self.i, 0, (k + 1 if up else n - k - 1) - 1],
                (peer, x, y * 2 + c),
            )

        def along_z(self):
            self.hop(z + 1 < n, True, 0, z, self.shard)
            self.hop(z >= 1, False, 0, z, self.shard)

        def onward(self, k):
            for up in (True, False):
                there = (z >= k) & (z + 1 < n) if up else (z + k < n) & (z >= 1)
                plane = jnp.clip(z - k if up else z + k, 0, n - 1)
                j = k if up else n - k

                @pl.when(there)
                def _():
                    self.came(0, j, self.q, 1)

                self.hop(there, up, k, plane, self.on(plane))

        def near(self):
            for j in range(1, n):
                plane = lax.rem(z + n - j, n)

                @pl.when((z == 0) | (z == n - 1))
                def _():
                    self.came(0, j, self.q, 1)

                peer = here.at(dx=1) if self.kind == 0 else here.at(dy=1)
                self.stage(1, j, self.q, 1, self.on(plane), plane, peer)

        def far(self):
            other = self.q + 1 - 2 * (self.q % 2)
            for j in range(1, n):
                plane = self.came(1, j, other, 1)
                peer = here.at(dy=1) if self.kind == 0 else here.at(dx=1)
                self.stage(2, j, self.q // 2 * 2, 2, self.on(plane), plane, peer)

        def across(self):
            pair = self.q // 2
            other = pair + 1 - 2 * (pair % 2)
            for j in range(1, n):
                plane = self.came(2, j, other * 2, 2)
                self.stage(3, j, c * 4, 4, self.on(plane), plane, here.at(dc=1))

        def done(self):
            for j in range(1, n):
                self.came(3, j, (1 - c) * 4, 4)
            here.expect(self.on(z), local_sems.at[self.i, 1])

    weights = []
    for first, second in steps_of:
        pair = []
        for kind, (i, part, parts) in enumerate((first, second)):
            pair.append(Weight(2 * len(weights) + kind, i, part, parts, kind))
        weights.append(pair)

    def each(t, name):
        if 0 <= t < len(weights):
            for w in weights[t]:
                name(w)

    def gather_ids():
        all_ids[z, x, y, c] = ids[...]
        mine = all_ids.at[z, x, y, c]
        here.send(mine, mine, id_sems.at[0, 0], id_sems.at[0, 1], here.at(dc=1))
        here.expect(all_ids.at[z, x, y, 1 - c], id_sems.at[0, 1])
        pair = all_ids.at[z, x, y]
        here.send(pair, pair, id_sems.at[1, 0], id_sems.at[1, 1], here.at(dx=1))
        here.expect(all_ids.at[z, 1 - x, y], id_sems.at[1, 1])
        four = all_ids.at[z, :, y]
        here.send(four, four, id_sems.at[2, 0], id_sems.at[2, 1], here.at(dy=1))
        here.expect(all_ids.at[z, :, 1 - y], id_sems.at[2, 1])
        plane = all_ids.at[z]
        for j in range(1, n):
            here.send(plane, plane, id_sems.at[2 + j, 0], id_sems.at[2 + j, 1], here.at(dz=j))
        for j in range(1, n):
            here.expect(all_ids.at[lax.rem(z + n - j, n)], id_sems.at[2 + j, 1])

    def list_rows():
        lines, lanes = ids.shape
        sources = n * 8
        total = sources * lines
        rows_dev = table.shape[0]
        local = all_ids[...].reshape(total, lanes) - ((z * 2 + x) * 4 + y * 2 + c) * rows_dev
        inside = (local >= 0) & (local < rows_dev)
        flags = jnp.where(inside, 1.0, 0.0).astype(jnp.bfloat16)
        row = lax.broadcasted_iota(jnp.int32, (lanes, lanes), 0)
        col = lax.broadcasted_iota(jnp.int32, (lanes, lanes), 1)
        place = matmul(flags, jnp.where(row < col, 1.0, 0.0).astype(jnp.bfloat16))
        held = matmul(flags, jnp.ones((lanes, lanes), jnp.bfloat16)).astype(jnp.bfloat16)
        row = lax.broadcasted_iota(jnp.int32, (total, total), 0)
        col = lax.broadcasted_iota(jnp.int32, (total, total), 1)
        before = (row // lines == col // lines) & (col < row)
        place = place + matmul(jnp.where(before, 1.0, 0.0).astype(jnp.bfloat16), held)
        places[...] = jnp.where(inside, place.astype(jnp.int32), -1)
        line = lax.broadcasted_iota(jnp.int32, (total, lanes), 0)
        lane = lax.broadcasted_iota(jnp.int32, (total, lanes), 1)
        index = lax.rem(line, lines) * lanes + lane
        entries[...] = local * 256 + index // gram_count + 1
        slot = lax.broadcasted_iota(jnp.int32, (SLOTS, lanes), 0)

        def source(s, carry):
            span = pl.ds(pl.multiple_of(s * lines, lines), lines)
            where, what = places[span], entries[span]
            found = jnp.zeros((SLOTS, lanes), jnp.int32)
            for line in range(used_lines):
                hit = where[line : line + 1] == slot
                found = found + jnp.where(hit, what[line : line + 1], 0)
            lists[s] = jnp.sum(found, axis=1, keepdims=True) - 1
            return carry

        lax.fori_loop(0, sources, source, 0)

    row_iota = lax.broadcasted_iota(jnp.int32, (4 * SLOTS, table.shape[0]), 1)
    byte_iota = lax.broadcasted_iota(jnp.int32, (SLOTS, tokens), 1)

    def partial_sums(plane, core, write):
        asked = [lists[plane * 8 + place * 2 + core] for place in range(4)]
        rows = jnp.right_shift(jnp.concatenate(asked, axis=0), 8)
        pick = (rows == row_iota).astype(jnp.bfloat16)
        g_rows[...] = matmul(pick, table[...]).astype(jnp.bfloat16)
        for place in range(4):
            source = plane * 8 + place * 2 + core
            entry = lists[source]
            to_byte = (jnp.bitwise_and(entry, 255) == byte_iota).astype(jnp.bfloat16)
            sums = t_times(to_byte, g_rows[place * SLOTS : (place + 1) * SLOTS, :])
            write(place, sums)

    units = []
    for u in range(n):
        units.append(
            Reduction(
                here,
                p0.at[pl.ds(u, 1)],
                r1a.at[pl.ds(u, 1)],
                r1b.at[pl.ds(u, 1)],
                r2a.at[pl.ds(u, 1)],
                r2b.at[pl.ds(u, 1)],
                stage_sems,
                u,
            )
        )
    core_copies = [None] * n
    z_copies = [None] * n

    def plane_of(u):
        return lax.rem(z + u + 1, n)

    def hash_a(u):
        slot = u % 2
        if u >= 2:
            here.sent(core_copies[u - 2])

        def write(place, sums):
            send0[slot, place // 2, place % 2] = sums.astype(jnp.bfloat16)

        partial_sums(plane_of(u), 1 - c, write)
        core_copies[u] = here.send(
            send0.at[slot], p0.at[u], core_sems.at[u, 0], core_sems.at[u, 1], here.at(dc=1)
        )

    def hash_b(u):
        core_copies[u].wait_recv()

        def write(place, sums):
            total = sums + p0[u, place // 2, place % 2].astype(jnp.float32)
            p0[u, place // 2, place % 2] = total.astype(jnp.bfloat16)

        partial_sums(plane_of(u), c, write)
        units[u].first()

    def hash_c(u):
        units[u].second()

    def hash_d(u):
        mine = units[u].third()
        if u < n - 1:
            z_copies[u] = here.send(
                mine.at[0], r3.at[u], z_sems.at[u, 0], z_sems.at[u, 1], here.at(dz=u + 1)
            )

    def hash_e():
        for u in range(n - 1):
            z_copies[u].wait_recv()
        total = p0[n - 1, x, y].astype(jnp.float32)
        for u in range(n - 1):
            total = total + r3[u].astype(jnp.float32)
        embedded[...] = total
        for copy in core_copies[-2:] + z_copies[:-1]:
            here.sent(copy)
        for unit in units:
            for copy in (unit.s1a, unit.s1b, unit.s2a, unit.s2b):
                here.sent(copy)

    here.greet()
    lag1, lag2, lag3 = GATHER_LAGS
    for t in range(n - 1):
        each(t, Weight.along_z)
        for k in range(1, n - 1):
            if k <= t:
                each(t - k, lambda w, k=k: w.onward(k))
    gather_ids()
    list_rows()
    hash_steps = []
    for t in range(n + 3):
        group = []
        for u, stage in ((t, hash_a), (t - 1, hash_b), (t - 2, hash_c), (t - 3, hash_d)):
            if 0 <= u < n:
                group.append(lambda u=u, stage=stage: stage(u))
        hash_steps.append(group)
    hash_steps.append([hash_e])
    layer = forward_steps(
        here,
        fulls,
        embedded,
        extra_in,
        extra_out,
        [p0.at[u] for u in range(n)] + [send0.at[u] for u in range(2)],
        extra_scratch,
    )
    gather_done, runs = set(), iter(layer)
    for what, number in SCHEDULE:
        if what == HASH:
            for run in hash_steps[number]:
                run()
        elif what == GATHER:
            each(number + n - 1, Weight.along_z)
            for k in range(1, n - 1):
                each(number + n - 1 - k, lambda w, k=k: w.onward(k))
            each(number, Weight.near)
            each(number - lag1, Weight.far)
            each(number - lag1, Weight.local)
            each(number - lag2, Weight.across)
            each(number - lag3, Weight.done)
            if 0 <= number - lag3 < len(steps_of):
                gather_done |= {i for i, _, _ in steps_of[number - lag3]}
        else:
            for _ in range(number):
                needs, run = next(runs)
                assert gather_done.issuperset(needs)
                run()
    assert next(runs, None) is None
    here.finish()


def fetch(hash_ids, table, shards, extra, steps_of, dp_count):
    width = table.shape[1]
    tokens, gram_count = hash_ids.shape
    count = len(shards)
    hbm = pl.BlockSpec(memory_space=pl.ANY)
    vmem = pl.BlockSpec(memory_space=pltpu.VMEM)
    n, half = dp_count, width // 2
    low = jnp.bfloat16
    dma = pltpu.SemaphoreType.DMA
    used_lines = tokens * gram_count // 128
    lines = -(-used_lines // 8) * 8
    ids = hash_ids.reshape(used_lines, 128)
    ids = jnp.concatenate([ids, jnp.full((lines - used_lines, 128), -1, jnp.int32)])
    gathers = 2 * len(steps_of)
    ff = shards[4].shape[1]
    extra_out = list(kept_shapes(tokens, width, ff, extra[3].shape[0]))
    results = pl.pallas_call(
        functools.partial(fetch_kernel, n, count, steps_of, tokens, gram_count, used_lines),
        out_shape=[jax.ShapeDtypeStruct((n * w.shape[0], w.shape[1]), w.dtype) for w in shards]
        + [
            jax.ShapeDtypeStruct((tokens, width), jnp.float32),
            jax.ShapeDtypeStruct((n * 8, SLOTS, 1), jnp.int32),
        ]
        + extra_out,
        in_specs=[hbm] * count + [vmem, vmem] + [vmem] * len(extra),
        out_specs=[hbm] * count + [vmem, vmem] + [vmem] * len(extra_out),
        scratch_shapes=[
            pltpu.VMEM((n, 2, 2, 2, lines, 128), jnp.int32),
            pltpu.VMEM((2, 2, 2, tokens, width), low),
            pltpu.VMEM((n, 2, 2, tokens, width), low),
            pltpu.VMEM((n, 2, tokens, half), low),
            pltpu.VMEM((n, 2, tokens, half), low),
            pltpu.VMEM((n, tokens, half), low),
            pltpu.VMEM((n, tokens, half), low),
            pltpu.VMEM((n - 1, tokens, width), low),
            pltpu.VMEM((4 * SLOTS, width), low),
            dma((n, 2)),
            dma((n, 4, 2)),
            dma((n - 1, 2)),
            dma((gathers, 2)),
            dma((gathers, 4, n - 1)),
            dma((gathers, 4, n - 1)),
            dma((gathers, 2, n - 1)),
            dma((2 + n, 2)),
            pltpu.VMEM((n * 8 * lines, 128), jnp.int32),
            pltpu.VMEM((n * 8 * lines, 128), jnp.int32),
            pltpu.VMEM((n * shards[4].shape[0], ff), low),
            pltpu.VMEM((n * shards[5].shape[0], ff), low),
            pltpu.VMEM((2, tokens, width), low),
            dma((count, max(n, ff // 256))),
            dma((2, 2)),
        ],
        compiler_params=pltpu.CompilerParams(
            collective_id=0, has_side_effects=True, vmem_limit_bytes=VMEM_CAP
        ),
        name="fetch",
    )(*shards, ids, table, *extra)
    return results[:count], results[count], results[count + 1], Kept(*results[count + 2 :])


LAGS = (2, 3, 5)


class GradSums:
    def __init__(self, here, units, lefts_in, rights_in, outs, take, pool_count):
        count = len(units)
        self.here, self.units = here, units
        self.lefts_in, self.rights_in, self.outs = lefts_in, rights_in, outs
        self.lefts, self.rights = take(len(lefts_in)), take(len(rights_in))
        self.pools = take(pool_count)
        self.r1a, self.r1b, self.r2a, self.r2b, self.r3 = (take(count) for _ in range(5))
        self.left_sems, self.right_sems, self.stage_sems, self.z_sems = take(4)
        self.left_copies, self.right_copies = {}, {}
        self.sums = [None] * count
        self.using = {}
        self.mine_of = [None] * count
        self.sent_of = [None] * count

    def bring(self, source, target, sems, i, split):
        here = self.here
        copies = []
        theirs = target.at[0]
        if source is not None:
            theirs = source.at[1 - here.c] if split else source
            mine = source.at[here.c] if split else source
            local = pltpu.make_async_copy(mine, target.at[0], sems.at[i, 0])
            local.start()
            copies.append(local.wait)
        remote = here.send(theirs, target.at[1], sems.at[i, 1], sems.at[i, 2], here.at(dc=1))
        copies.append(remote.wait_recv)
        return copies

    def left(self, i):
        if i not in self.left_copies:
            self.left_copies[i] = self.bring(
                self.lefts_in[i], self.lefts[i], self.left_sems, i, True
            )

    def right(self, i):
        if i not in self.right_copies:
            self.right_copies[i] = self.bring(
                self.rights_in[i], self.rights[i], self.right_sems, i, False
            )

    def need(self, i):
        self.left(self.units[i][0])
        self.right(self.units[i][1])

    def product(self, i):
        here, n = self.here, self.here.n
        left, right, pool, slot = self.units[i]
        self.need(i)
        for copies in (self.left_copies[left], self.right_copies[right]):
            for wait in copies:
                wait()
            copies.clear()
        for copy in self.using.get((pool, slot), []):
            here.sent(copy)
        p0 = self.pools[pool].at[slot]
        xt, g = self.lefts[left], self.rights[right]
        k, depth = xt.shape[2], xt.shape[3]
        cols = g.shape[2]
        chunks = 1 if k <= 32 else n
        planes = n // chunks
        tile = 256

        def columns(t, carry):
            span = pl.ds(pl.multiple_of(t * tile, tile), tile)
            for chunk in range(chunks):
                total = None
                for who in range(2):
                    rows = xt[who, chunk * planes * 4 : (chunk + 1) * planes * 4]
                    part = matmul(rows.reshape(planes * 4 * k, depth), g[who, :, span])
                    total = part if total is None else total + part
                p0[chunk * planes : (chunk + 1) * planes, :, :, :, span] = total.astype(
                    jnp.bfloat16
                ).reshape(planes, 2, 2, k, tile)
            return carry

        lax.fori_loop(0, cols // tile, columns, 0)
        unit = Reduction(
            here, p0, self.r1a[i], self.r1b[i], self.r2a[i], self.r2b[i], self.stage_sems, i
        )
        unit.first()
        self.sums[i] = unit
        self.using[(pool, slot)] = [unit.s1a, unit.s1b]

    def second(self, i):
        self.sums[i].second()
        self.using[self.units[i][2:]] += [self.sums[i].s2a, self.sums[i].s2b]

    def third(self, i):
        here, n = self.here, self.here.n
        mine = self.sums[i].third()
        self.sent_of[i] = []
        for j in range(1, n):
            self.sent_of[i].append(
                here.send(
                    mine.at[lax.rem(here.z + j, n)],
                    self.r3[i].at[j - 1],
                    self.z_sems.at[i, j - 1, 0],
                    self.z_sems.at[i, j - 1, 1],
                    here.at(dz=j),
                )
            )
        self.using[self.units[i][2:]] += self.sent_of[i]
        self.mine_of[i] = mine

    def final(self, i):
        total = self.mine_of[i][self.here.z].astype(jnp.float32)
        for j in range(1, self.here.n):
            self.sent_of[i][j - 1].wait_recv()
            total = total + self.r3[i][j - 1].astype(jnp.float32)
        self.outs[i][...] = total

    def move(self, t, lags):
        lag2, lag3, lag4 = lags
        count = len(self.units)
        if 0 <= t - lag2 < count:
            self.second(t - lag2)
        if 0 <= t - lag3 < count:
            self.third(t - lag3)
        if 0 <= t - lag4 < count:
            self.final(t - lag4)


def plan_sums(pairs, left_shapes, right_shapes, n, most):
    low = jnp.bfloat16
    dma = pltpu.SemaphoreType.DMA
    shapes, units, seen = [], [], {}
    for left, right in pairs:
        shape = (left_shapes[left][2], right_shapes[right][1])
        seen[shape] = seen.get(shape, 0) + 1
        shapes.append(shape)
    classes = list(seen)
    slots = [min(seen[s], most) for s in classes]
    used = {s: 0 for s in classes}
    for (left, right), shape in zip(pairs, shapes):
        pool = classes.index(shape)
        units.append((left, right, pool, used[shape] % slots[pool]))
        used[shape] += 1
    count = len(pairs)
    scratch = [pltpu.VMEM(shape, low) for shape in left_shapes]
    scratch += [pltpu.VMEM((2, *shape), low) for shape in right_shapes]
    scratch += [pltpu.VMEM((s, n, 2, 2, *shape), low) for s, shape in zip(slots, classes)]
    halves = [(k, cols // 2) for k, cols in shapes]
    for _ in range(2):
        scratch += [pltpu.VMEM((n, 2, *half), low) for half in halves]
    for _ in range(2):
        scratch += [pltpu.VMEM((n, *half), low) for half in halves]
    scratch += [pltpu.VMEM((n - 1, *shape), low) for shape in shapes]
    scratch += [
        dma((len(left_shapes), 3)),
        dma((len(right_shapes), 3)),
        dma((count, 4, 2)),
        dma((count, n - 1, 2)),
    ]
    return units, shapes, scratch, len(classes)


def taker(refs):
    refs = list(refs)

    def take(number):
        taken = refs[:number]
        del refs[:number]
        return taken

    return take


def last_kernel(dp_count, units, left_count, right_count, pool_count, *refs):
    n = dp_count
    count = len(units)
    take = taker(refs)
    lefts_in, rights_in = take(left_count), take(right_count)
    embed_in, gains_in, lists, rows_of = take(4)
    outs = take(count)
    gains_out, table_grad, counts, stacked_last, rows_last = take(5)
    here = Place(n)
    sums = GradSums(here, units, lefts_in, rights_in, outs, take, pool_count)
    gathered, stacked = take(2)
    gain_send, gain_recv, gain_sems, own_sem, near_sems, plane_sems = take(6)
    z, x, y, c = here.z, here.x, here.y, here.c

    here.greet()

    own = pltpu.make_async_copy(embed_in, gathered.at[z, x, y, c], own_sem)
    own.start()
    for j in range(1, n):
        here.send(
            embed_in,
            gathered.at[z, x, y, c],
            plane_sems.at[j - 1, 0],
            plane_sems.at[j - 1, 1],
            here.at(dz=j),
        )
    width = embed_in.shape[1]
    left_half, right_half = pl.ds(0, width // 2), pl.ds(width // 2, width // 2)

    def embed_near(j):
        plane = lax.rem(z + n - j, n)
        if j:
            here.expect(gathered.at[plane, x, y, c], plane_sems.at[j - 1, 1])
        else:
            own.wait()
        a = gathered.at[plane, x, y, c, :, left_half]
        b = gathered.at[plane, x, y, c, :, right_half]
        here.send(a, a, near_sems.at[j, 0, 0], near_sems.at[j, 0, 1], here.at(dx=1))
        here.send(b, b, near_sems.at[j, 1, 0], near_sems.at[j, 1, 1], here.at(dy=1))

    def embed_far(j):
        plane = lax.rem(z + n - j, n)
        here.expect(gathered.at[plane, 1 - x, y, c, :, left_half], near_sems.at[j, 0, 1])
        here.expect(gathered.at[plane, x, 1 - y, c, :, right_half], near_sems.at[j, 1, 1])
        a = gathered.at[plane, :, y, c, :, left_half]
        b = gathered.at[plane, x, :, c, :, right_half]
        here.send(a, a, near_sems.at[j, 2, 0], near_sems.at[j, 2, 1], here.at(dy=1))
        here.send(b, b, near_sems.at[j, 3, 0], near_sems.at[j, 3, 1], here.at(dx=1))

    def embed_across(j):
        plane = lax.rem(z + n - j, n)
        here.expect(gathered.at[plane, :, 1 - y, c, :, left_half], near_sems.at[j, 2, 1])
        here.expect(gathered.at[plane, 1 - x, :, c, :, right_half], near_sems.at[j, 3, 1])
        a = gathered.at[plane, :, :, c]
        here.send(a, a, near_sems.at[j, 4, 0], near_sems.at[j, 4, 1], here.at(dc=1))

    def spread(j):
        plane = lax.rem(z + n - j, n)
        here.expect(gathered.at[plane, :, :, 1 - c], near_sems.at[j, 4, 1])
        byte_iota = lax.broadcasted_iota(jnp.int32, (SLOTS, embed_in.shape[0]), 1)
        for s in range(8):
            asked = jnp.bitwise_and(lists[plane * 8 + s], 255)
            pick = (asked == byte_iota).astype(jnp.bfloat16)
            grads = gathered[plane, s // 4, s // 2 % 2, s % 2]
            target = stacked_last if j == n - 1 else stacked
            target[s * SLOTS : (s + 1) * SLOTS, :] = matmul(pick, grads).astype(jnp.bfloat16)
        if j == n - 1:
            rows_last[...] = rows_of[plane]
            return
        row_iota = lax.broadcasted_iota(jnp.int32, (table_grad.shape[0], 8 * SLOTS), 0)
        onto = (rows_of[plane] == row_iota).astype(jnp.float32)
        uses = jnp.sum(onto, axis=1, keepdims=True)
        added = matmul(onto.astype(jnp.bfloat16), stacked[...])
        if j == 0:
            counts[...] = uses
            table_grad[...] = added
        else:
            counts[...] += uses
            table_grad[...] += added

    def gains(stage):
        if stage == 0:
            gain_send[0] = gains_in[...]
        elif stage <= 3:
            here.expect(gain_recv.at[stage - 1], gain_sems.at[stage - 1, 1])
            gain_send[stage] = gain_send[stage - 1] + gain_recv[stage - 1]
        if stage < 3:
            peer = (here.at(dc=1), here.at(dx=1), here.at(dy=1))[stage]
            here.send(
                gain_send.at[stage],
                gain_recv.at[stage],
                gain_sems.at[stage, 0],
                gain_sems.at[stage, 1],
                peer,
            )
        elif stage == 3:
            for j in range(1, n):
                here.send(
                    gain_send.at[3],
                    gain_recv.at[2 + j],
                    gain_sems.at[2 + j, 0],
                    gain_sems.at[2 + j, 1],
                    here.at(dz=j),
                )
        else:
            total = gain_send[3]
            for j in range(1, n):
                here.expect(gain_recv.at[2 + j], gain_sems.at[2 + j, 1])
                total = total + gain_recv[2 + j]
            gains_out[...] = total

    for i in range(count):
        sums.need(i)
    for t in range(max(count + LAGS[2], n + 5)):
        if t < count:
            sums.product(t)
        if t == 0:
            embed_near(0)
        if 0 <= t - 1 < 5:
            gains(t - 1)
        if 1 <= t - 2 < n:
            embed_near(t - 2)
        sums.move(t, LAGS)
        if 0 <= t - 3 < n:
            embed_far(t - 3)
        if 0 <= t - 4 < n:
            embed_across(t - 4)
        if 0 <= t - 5 < n:
            spread(t - 5)
    here.finish()


def last_sums(pairs, lefts, rights, embed_low, gains, entries, rows_dev, dp_count):
    n = dp_count
    low = jnp.bfloat16
    dma = pltpu.SemaphoreType.DMA
    hbm = pl.BlockSpec(memory_space=pl.ANY)
    vmem = pl.BlockSpec(memory_space=pltpu.VMEM)
    units, shapes, scratch, pool_count = plan_sums(
        pairs, [a.shape for a in lefts], [a.shape for a in rights], n, 6
    )
    count = len(pairs)
    tokens, width = embed_low.shape
    rows_of = jnp.right_shift(entries, 8).reshape(n, 1, 8 * SLOTS)
    scratch += [
        pltpu.VMEM((n, 2, 2, 2, tokens, width), low),
        pltpu.VMEM((8 * SLOTS, width), low),
        pltpu.VMEM((4, 8, width), jnp.float32),
        pltpu.VMEM((2 + n, 8, width), jnp.float32),
        dma((2 + n, 2)),
        dma,
        dma((n, 5, 2)),
        dma((n - 1, 2)),
    ]
    results = pl.pallas_call(
        functools.partial(last_kernel, n, units, len(lefts), len(rights), pool_count),
        out_shape=[jax.ShapeDtypeStruct(shape, jnp.float32) for shape in shapes]
        + [
            jax.ShapeDtypeStruct((8, width), jnp.float32),
            jax.ShapeDtypeStruct((rows_dev, width), jnp.float32),
            jax.ShapeDtypeStruct((rows_dev, 1), jnp.float32),
            jax.ShapeDtypeStruct((8 * SLOTS, width), low),
            jax.ShapeDtypeStruct((1, 8 * SLOTS), jnp.int32),
        ],
        in_specs=[hbm] * (len(lefts) + len(rights)) + [vmem] * 4,
        out_specs=[vmem] * (count + 5),
        scratch_shapes=scratch,
        compiler_params=pltpu.CompilerParams(
            collective_id=2, has_side_effects=True, vmem_limit_bytes=VMEM_CAP
        ),
        name="last_sums",
    )(*lefts, *rights, embed_low, gains, entries, rows_of)
    return results[:count], *results[count:]


BACK_PAIRS = ((4, 8), (3, 6), (3, 7), (2, 5), (1, 4), (0, 0), (0, 1), (0, 2), (0, 3))


class Streamed(typing.NamedTuple):
    gate_pre: typing.Any
    up_pre: typing.Any
    h_out: typing.Any
    h_mid: typing.Any
    embedded: typing.Any
    key_values: typing.Any
    w_query: typing.Any
    w_key: typing.Any
    w_value: typing.Any
    w_out: typing.Any
    w_gate: typing.Any
    w_up: typing.Any
    w_down: typing.Any
    c_query: typing.Any
    c_key: typing.Any
    c_value: typing.Any
    c_out: typing.Any
    cot_patches: typing.Any


def back_kernel(dp_count, units, pool_count, *refs):
    n = dp_count
    take = taker(refs)
    lefts_in = take(5)
    hbm = Streamed(*take(len(Streamed._fields)))
    (cot_bytes, p_query, p_key, p_value, cross_lse, gains, starts, ends, queries, lse) = take(10)
    outs = take(len(units))
    grad_gains, g_attn, g_query, g_key, g_value, g_embed = take(6)
    here = Place(n)
    sums = GradSums(here, units, lefts_in, [None] * 8 + [hbm.cot_patches], outs, take, pool_count)
    w, tile_pre, grad_out, grad_ffn, grad_mid, kv, halo = take(7)
    w_sems, tile_sems, pre_sems, kv_sems, halo_sems = take(5)
    g_gate = [sums.rights[0].at[0], sums.rights[2].at[0]]
    g_up = [sums.rights[1].at[0], sums.rights[3].at[0]]
    g_branch, g_pquery, g_pkey, g_pvalue, cot_patches = [ref.at[0] for ref in sums.rights[4:]]
    tokens, width = cot_bytes.shape
    patches = p_query.shape[0]
    tile = 256
    first_tiles = g_gate[0].shape[1] // tile
    tiles = first_tiles + g_gate[1].shape[1] // tile
    rank = (here.x * 2 + here.y) * 2 + here.c
    lane = lax.broadcasted_iota(jnp.int32, (1, 128), 1)
    sides = [jnp.where(lane < HD, 1.0, 0.0).astype(LOW), jnp.where(lane < HD, 0.0, 1.0).astype(LOW)]
    byte_pos = lax.broadcasted_iota(jnp.int32, (patches, tokens), 1)

    here.greet()

    def load_w(slot, source):
        copy = pltpu.make_async_copy(source, w.at[slot], w_sems.at[slot])
        copy.start()
        return copy

    def load_pre(source):
        copies = []
        for b in range(width // tile):
            copy = pltpu.make_async_copy(
                source.at[:, pl.ds(b * tile, tile)],
                tile_pre.at[b // 2, b % 2],
                pre_sems.at[b],
            )
            copy.start()
            copies.append(copy)
        return copies

    def pre_rows(copies):
        for copy in copies:
            copy.wait()
        return jnp.concatenate([tile_pre[b // 2, b % 2] for b in range(width // tile)], axis=1)

    for i in (4, 3, 2, 1, 0):
        sums.left(i)
    sums.right(8)
    cross = [load_w(i, a) for i, a in enumerate((hbm.c_out, hbm.c_query, hbm.c_key, hbm.c_value))]
    h_out_copies = load_pre(hbm.h_out)

    def tile_copies(t):
        slot = lax.rem(t, 2)
        span = pl.ds(pl.multiple_of(t * tile, tile), tile)
        return [
            pltpu.make_async_copy(source, target, tile_sems.at[slot, k])
            for k, (source, target) in enumerate(
                (
                    (hbm.w_gate.at[:, span], w.at[slot, :, pl.ds(0, tile)]),
                    (hbm.w_up.at[:, span], w.at[slot, :, pl.ds(tile, tile)]),
                    (hbm.w_down.at[span], w.at[2, pl.ds(pl.multiple_of(slot * tile, tile), tile)]),
                    (hbm.gate_pre.at[:, span], tile_pre.at[slot, 0]),
                    (hbm.up_pre.at[:, span], tile_pre.at[slot, 1]),
                )
            )
        ]

    def member():
        return (byte_pos >= starts[...]) & (byte_pos < ends[...])

    def head_lse(ref, head):
        return jnp.sum(jnp.where(lane == head, ref[...], 0.0), axis=1, keepdims=True)

    def cross_heads():
        cross[0].wait()
        allowed = member()
        grad_ffn[:patches] = times_t(cot_patches[...], w[0]).astype(LOW).astype(F32)

        def heads_pair(pair, carry):
            span = pl.ds(pl.multiple_of(pair * 128, 128), 128)
            q2, k2, v2 = p_query[:, span], p_key[:, span], p_value[:, span]
            gp2 = grad_ffn[:patches, span].astype(LOW)
            parts = []
            for side in range(2):
                total = head_lse(cross_lse, pair * 2 + side)
                scores = times_t(q2 * sides[side], k2) * SCORE_SCALE
                probs = jnp.where(allowed, jnp.exp(jnp.where(allowed, scores, total) - total), 0.0)
                grad_score = soft_back(probs, times_t(gp2 * sides[side], v2))
                parts.append(
                    (
                        matmul(grad_score, k2),
                        t_times(grad_score, q2),
                        t_times(probs.astype(LOW), gp2),
                    )
                )
            mine = lane < HD
            g_pquery[:, span] = (jnp.where(mine, parts[0][0], parts[1][0]) * SCORE_SCALE).astype(LOW)
            g_pkey[:, span] = (jnp.where(mine, parts[0][1], parts[1][1]) * SCORE_SCALE).astype(LOW)
            g_pvalue[:, span] = jnp.where(mine, parts[0][2], parts[1][2]).astype(LOW)
            return carry

        lax.fori_loop(0, width // 128, heads_pair, 0)
        for i in (5, 6, 7):
            sums.right(i)

    def split(v):
        high = v.astype(LOW)
        return high, (v - high.astype(F32)).astype(LOW)

    def unit_of(v):
        inv_rms = lax.rsqrt(jnp.mean(v * v, axis=-1, keepdims=True) + EPSILON)
        return v * inv_rms, inv_rms

    def through_norm(grad, rows, number):
        normed, inv_rms = unit_of(rows)
        grad_in, grad_gain = norm_back(
            grad.astype(LOW).astype(F32), normed, inv_rms, gains[number : number + 1]
        )
        grad_gains[number : number + 1] = grad_gain[None]
        return grad_in

    loaded = {}

    def cross_in():
        for copy in cross[1:]:
            copy.wait()
        length = (ends[...] - starts[...]).astype(F32)
        grad_pooled = cot_patches[...].astype(F32) + times_t(g_pquery[...], w[1]).astype(
            LOW
        ).astype(F32)
        high, rest = split(grad_pooled / length)
        inside = jnp.where(member(), 1.0, 0.0).astype(LOW)
        grad_x = t_times(inside, high) + t_times(inside, rest)
        grad_x = grad_x + times_t(g_pkey[...], w[2]) + times_t(g_pvalue[...], w[3])
        grad_gains[...] = jnp.zeros_like(grad_gains)
        total = cot_bytes[...].astype(F32) + through_norm(grad_x, pre_rows(h_out_copies), 2)
        grad_out[...] = total
        g_branch[...] = total.astype(LOW)
        grad_ffn[...] = jnp.zeros_like(grad_ffn)
        sums.right(4)
        loaded[3] = load_w(3, hbm.w_out)

    def feed(part):
        first, last = ((0, first_tiles), (first_tiles, tiles))[part]
        for copy in tile_copies(first):
            copy.start()

        def one(t, carry):
            slot = lax.rem(t, 2)
            for copy in tile_copies(t):
                copy.wait()

            @pl.when(t + 1 < last)
            def _():
                for copy in tile_copies(t + 1):
                    copy.start()

            span = pl.ds(pl.multiple_of((t - first) * tile, tile), tile)
            down_rows = w[2, pl.ds(pl.multiple_of(slot * tile, tile), tile)]
            grad_hidden = times_t(g_branch[...], down_rows).astype(LOW).astype(F32)
            gate, up = tile_pre[slot, 0], tile_pre[slot, 1]
            sig = jax.nn.sigmoid(gate)
            gg = (grad_hidden * up * sig * (1.0 + gate * (1.0 - sig))).astype(LOW)
            gu = (grad_hidden * (gate * sig)).astype(LOW)
            g_gate[part][:, span] = gg
            g_up[part][:, span] = gu
            grad_ffn[...] += times_t(gg, w[slot, :, :tile]) + times_t(
                gu, w[slot, :, tile : 2 * tile]
            )
            return carry

        lax.fori_loop(first, last, one, 0)
        sums.right(2 * part)
        sums.right(2 * part + 1)

    def feed_in():
        copies = load_pre(hbm.h_mid)
        loaded[3].wait()
        grad_mid[...] = grad_out[...] + through_norm(grad_ffn[...], pre_rows(copies), 1)
        g_attn[...] = grad_mid[...].astype(LOW)
        g_query[...] = times_t(g_attn[...], w[3]).astype(LOW)
        loaded[1] = load_w(1, hbm.w_query)
        loaded[2] = load_w(2, hbm.w_key)
        loaded[3] = load_w(3, hbm.w_value)
        loaded[0] = load_pre(hbm.embedded)

    own_key, own_value = grad_ffn, grad_out
    sent = w.at[0]

    def kv_copy(pair):
        slot = lax.rem(pair, 2)
        span = pl.ds(pl.multiple_of(pair * 128, 128), 128)
        return pltpu.make_async_copy(hbm.key_values.at[:, :, span], kv.at[slot], kv_sems.at[slot])

    def attend(first, last):
        row = lax.broadcasted_iota(jnp.int32, (tokens, tokens), 0)
        col = lax.broadcasted_iota(jnp.int32, (tokens, tokens), 1)
        mine = col <= row
        far_bias = jnp.where(rank >= 2, 0.0, NEG_BIG)
        near_bias = jnp.where(rank >= 1, 0.0, NEG_BIG)
        kv_copy(first).start()

        def three(edge, middle):
            return jnp.concatenate(
                [
                    jnp.where(mine, 0.0, edge).astype(LOW),
                    middle.astype(LOW),
                    jnp.where(mine, edge, 0.0).astype(LOW),
                ],
                axis=1,
            )

        def heads_pair(pair, carry):
            kv_copy(pair).wait()

            @pl.when(pair + 1 < last)
            def _():
                kv_copy(pair + 1).start()

            slot = lax.rem(pair, 2)
            span = pl.ds(pl.multiple_of(pair * 128, 128), 128)
            q2, ga2 = queries[:, span], g_query[:, span]
            k2, v2 = kv[slot, 0], kv[slot, 1]
            parts = []
            for side in range(2):
                total = head_lse(lse, pair * 2 + side)
                scores = times_t(q2 * sides[side], k2) * SCORE_SCALE
                edge = jnp.where(mine, scores[:, 2 * tokens :], scores[:, :tokens] + far_bias)
                edge = jnp.exp(edge - total)
                middle = jnp.exp(scores[:, tokens : 2 * tokens] + near_bias - total)
                grad_prob = times_t(ga2 * sides[side], v2)
                grad_edge = jnp.where(mine, grad_prob[:, 2 * tokens :], grad_prob[:, :tokens])
                grad_middle = grad_prob[:, tokens : 2 * tokens]
                row_total = jnp.sum(edge * grad_edge, axis=1, keepdims=True) + jnp.sum(
                    middle * grad_middle, axis=1, keepdims=True
                )
                grad_score = three(edge * (grad_edge - row_total), middle * (grad_middle - row_total))
                parts.append(
                    (
                        matmul(grad_score, k2),
                        t_times(grad_score, q2),
                        t_times(three(edge, middle), ga2),
                    )
                )
            left = lane < HD
            g_query[:, span] = (jnp.where(left, parts[0][0], parts[1][0]) * SCORE_SCALE).astype(LOW)
            for number, own, scale in ((1, own_key, SCORE_SCALE), (2, own_value, 1.0)):
                grad = jnp.where(left, parts[0][number], parts[1][number]) * scale
                own[:, span] = grad[2 * tokens :]
                start = (number - 1) * 2 * tokens
                sent[start : start + 2 * tokens, span] = grad[: 2 * tokens].astype(LOW)
            return carry

        lax.fori_loop(first, last, heads_pair, 0)

    there = rank >= 2

    def part_of(number, back, span):
        return sent.at[pl.ds((2 * number + 2 - back) * tokens, tokens), span]

    def halo_parts(half):
        span = pl.ds(half * (width // 2), width // 2)
        return [(number, span, 2 * number + half) for number in range(2)]

    def halo_pair(half):
        for number, span, sem in halo_parts(half):
            here.send_if(
                there | (here.c == 1),
                part_of(number, 1, span),
                halo.at[1, number, :, span],
                halo_sems.at[1, sem, 0],
                halo_sems.at[1, sem, 1],
                here.at(dc=1),
            )

    def halo_send(half):
        for number, span, sem in halo_parts(half):

            @pl.when(there | (here.c == 0))
            def _():
                here.expect(halo.at[1, number, :, span], halo_sems.at[1, sem, 1])

            part = part_of(number, 2, span)

            @pl.when(there & (here.c == 1))
            def _():
                added = part[...].astype(F32) + halo[1, number, :, span].astype(F32)
                part[...] = added.astype(LOW)

            target = jnp.maximum(rank - 2, 0)
            here.send_if(
                there,
                part,
                halo.at[0, number, :, span],
                halo_sems.at[0, sem, 0],
                halo_sems.at[0, sem, 1],
                (here.z, target // 4, lax.rem(target, 4)),
            )

    def halo_add():
        for number, own, grad in ((0, own_key, g_key), (1, own_value, g_value)):

            @pl.when(here.c == 0)
            def _():
                own[...] += halo[1, number].astype(F32)

            @pl.when(rank + 2 < 8)
            def _():
                for half in range(2):
                    _, span, sem = halo_parts(half)[number]
                    here.expect(halo.at[0, number, :, span], halo_sems.at[0, sem, 1])
                own[...] += halo[0, number].astype(F32)

            grad[...] = own[...].astype(LOW)

    def embed_in():
        for slot in (1, 2, 3):
            loaded[slot].wait()
        grad = times_t(g_query[...], w[1]) + times_t(g_key[...], w[2]) + times_t(g_value[...], w[3])
        total = grad_mid[...] + through_norm(grad, pre_rows(loaded[0]), 0)
        g_embed[...] = total.astype(LOW)

    sums.product(0)
    cross_heads()
    sums.product(1)
    sums.product(2)
    sums.product(3)
    cross_in()
    sums.second(0)
    sums.product(4)
    sums.second(1)
    feed(0)
    sums.product(5)
    sums.product(6)
    sums.second(2)
    sums.third(0)
    feed(1)
    sums.product(7)
    sums.product(8)
    sums.second(3)
    sums.third(1)
    feed_in()
    sums.second(4)
    sums.third(2)
    pairs = width // 128
    quarter = pairs // 4
    attend(0, quarter)
    sums.second(5)
    sums.third(3)
    sums.third(4)
    attend(quarter, 2 * quarter)
    halo_pair(0)
    halo_send(0)
    sums.second(6)
    sums.third(5)
    attend(2 * quarter, 3 * quarter)
    sums.second(7)
    sums.third(6)
    attend(3 * quarter, pairs)
    halo_pair(1)
    halo_send(1)
    sums.second(8)
    sums.third(7)
    for i in range(4):
        sums.final(i)
    halo_add()
    sums.third(8)
    embed_in()
    for i in range(4, 9):
        sums.final(i)
    here.finish()


def back_sums(lefts, streamed, kept, dp_count):
    n = dp_count
    low = jnp.bfloat16
    dma = pltpu.SemaphoreType.DMA
    hbm = pl.BlockSpec(memory_space=pl.ANY)
    vmem = pl.BlockSpec(memory_space=pltpu.VMEM)
    tokens, ff = streamed.gate_pre.shape
    patches, width = streamed.cot_patches.shape
    tile = 256
    first = (ff // tile + 1) // 2 * tile
    one = jax.ShapeDtypeStruct
    right_shapes = [(tokens, first)] * 2 + [(tokens, ff - first)] * 2
    right_shapes += [(tokens, width), (patches, width)]
    right_shapes += [(tokens, width)] * 2 + [(patches, width)]
    units, shapes, scratch, pool_count = plan_sums(
        BACK_PAIRS, [a.shape for a in lefts], right_shapes, n, 4
    )
    count = len(units)
    scratch += [
        pltpu.VMEM((4, width, width), low),
        pltpu.VMEM((2, 2, tokens, tile), F32),
        pltpu.VMEM((tokens, width), F32),
        pltpu.VMEM((tokens, width), F32),
        pltpu.VMEM((tokens, width), F32),
        pltpu.VMEM((2, 2, 3 * tokens, 128), low),
        pltpu.VMEM((2, 2, tokens, width), low),
        dma((4,)),
        dma((2, 5)),
        dma((width // tile,)),
        dma((2,)),
        dma((2, 4, 2)),
    ]
    results = pl.pallas_call(
        functools.partial(back_kernel, n, units, pool_count),
        out_shape=[one(shape, F32) for shape in shapes]
        + [one((8, width), F32)]
        + [one((tokens, width), low)] * 5,
        in_specs=[hbm] * (len(lefts) + len(streamed)) + [vmem] * len(kept),
        out_specs=[vmem] * (count + 6),
        scratch_shapes=scratch,
        compiler_params=pltpu.CompilerParams(
            collective_id=1, has_side_effects=True, vmem_limit_bytes=63 * 1024 * 1024
        ),
        name="back_sums",
    )(*lefts, *streamed, *kept)
    return results[:count], results[count:]


def finish_kernel(cuts, rows, stacked, table_in, counts_in, *refs):
    wholes, refs = refs[: len(cuts)], list(refs[len(cuts) :])
    halves = [refs.pop(0) for _ in range(4)]
    table, counts = refs.pop(0), refs.pop(0)
    row = lax.broadcasted_iota(jnp.int32, (table.shape[0], rows.shape[1]), 0)
    onto = (rows[...] == row + pl.program_id(0) * table.shape[0]).astype(jnp.float32)
    counts[...] = (counts_in[...] + jnp.sum(onto, axis=1, keepdims=True)).astype(jnp.int32)
    table[...] = table_in[...] + matmul(onto.astype(jnp.bfloat16), stacked[...])

    @pl.when(pl.program_id(0) == 0)
    def _():
        core = lax.axis_index(SUB) % 2
        for cut, source, target in zip(cuts, wholes, refs):
            if cut == source.shape[0]:
                target[...] = source[...]
            else:
                target[...] = jnp.where(core == 0, source[:cut], source[source.shape[0] - cut :])
        for k in range(2):
            left, right = halves[k], halves[2 + k]
            target = refs[len(cuts) + k]
            target[:, : left.shape[1]] = left[...]
            target[:, left.shape[1] :] = right[...]


def finish(table_grad, counts, stacked, rows, wholes, cuts, halves):
    rows_dev, width = table_grad.shape
    block = 256
    one = jax.ShapeDtypeStruct

    def whole(shape):
        return pl.BlockSpec(shape, lambda i: (0, 0))

    def blocks(cols):
        return pl.BlockSpec((block, cols), lambda i: (i, 0))

    shapes = [(cut, a.shape[1]) for a, cut in zip(wholes, cuts)]
    shapes += [(a.shape[0], a.shape[1] + b.shape[1]) for a, b in zip(halves[:2], halves[2:])]
    return pl.pallas_call(
        functools.partial(finish_kernel, cuts),
        grid=(-(-rows_dev // block),),
        out_shape=[one((rows_dev, width), F32), one((rows_dev, 1), jnp.int32)]
        + [one(shape, F32) for shape in shapes],
        in_specs=[whole(rows.shape), whole(stacked.shape), blocks(width), blocks(1)]
        + [whole(a.shape) for a in (*wholes, *halves)],
        out_specs=[blocks(width), blocks(1)] + [whole(shape) for shape in shapes],
        compiler_params=pltpu.CompilerParams(vmem_limit_bytes=VMEM_CAP),
        name="finish",
    )(rows, stacked, table_grad, counts, *wholes, *halves)


WEIGHT_STEPS = tuple(((i, 0, 2), (i, 1, 2)) for i in (0, 1, 2, 3, 4, 5, 6, 8, 9, 7, 10))


def by_rows(a, dp_count):
    depth, total = a.shape
    pairs = dp_count * 4
    both = total // pairs
    a = a.T.reshape(pairs, both, depth)
    rows = -(-(both // 2) // 16) * 16
    return jnp.stack([a[:, :rows], a[:, both - rows :]])


def body(
    byte_ids,
    hash_ids,
    lengths,
    byte_table,
    hash_table,
    norm_attn,
    norm_ffn,
    norm_cross,
    w_query,
    w_key,
    w_value,
    w_out,
    w_gate,
    w_up,
    w_down,
    c_query,
    c_key,
    c_value,
    c_out,
    cot_bytes,
    cot_patches,
):
    dp_count = lax.axis_size(DP)
    rs_count = lax.axis_size(SEQ)
    all_count = dp_count * rs_count
    rank_seq = lax.axis_index(SEQ)
    rank_table = lax.axis_index(DP) * rs_count + rank_seq
    tokens, gram_count = hash_ids.shape
    rows_dev, model_width = hash_table.shape
    head_count = model_width // HD
    request_count = tokens * gram_count
    slot_count = 2 * request_count // all_count
    flat_ids = hash_ids.reshape(request_count)
    owners = flat_ids // rows_dev
    ordering = jnp.argsort(owners, stable=True)
    owners_sorted = owners[ordering]
    per_owner = jnp.sum(
        (owners[:, None] == jnp.arange(all_count, dtype=jnp.int32)[None, :]).astype(jnp.int32),
        axis=0,
    )
    first_slot = jnp.cumsum(per_owner) - per_owner
    place_sorted = (
        owners_sorted * slot_count
        + jnp.arange(request_count, dtype=jnp.int32)
        - first_slot[owners_sorted]
    )
    placement = jnp.zeros((request_count,), jnp.int32).at[ordering].set(place_sorted)
    requests = jnp.full((all_count * slot_count,), -1, jnp.int32).at[placement].set(flat_ids)
    requests = requests.reshape(dp_count, rs_count, slot_count)
    incoming = lax.all_to_all(
        lax.all_to_all(requests, DP, split_axis=0, concat_axis=0, tiled=True),
        SEQ,
        split_axis=1,
        concat_axis=1,
        tiled=True,
    )
    present = incoming >= 0
    safe_rows = jnp.where(present, incoming - rank_table * rows_dev, 0)
    served = jnp.where(present[..., None], hash_table[safe_rows], jnp.zeros((), jnp.bfloat16))
    returned = lax.all_to_all(
        lax.all_to_all(served, DP, split_axis=0, concat_axis=0, tiled=True),
        SEQ,
        split_axis=1,
        concat_axis=1,
        tiled=True,
    )
    fetched = returned.reshape(all_count * slot_count, model_width)[placement]
    fetched = fetched.astype(jnp.float32).reshape(tokens, gram_count, model_width)
    one_hot = byte_ids[:, None] == jnp.arange(BYTE_VALUES, dtype=jnp.int32)[None, :]
    embedded = matmul(one_hot.astype(jnp.bfloat16), byte_table) + jnp.sum(fetched, axis=1)
    row_counts = (
        jnp.zeros((rows_dev,), jnp.int32)
        .at[safe_rows.reshape(-1)]
        .add(present.reshape(-1).astype(jnp.int32))
    )
    weight_list = (
        w_query,
        w_key,
        w_value,
        w_out,
        w_gate,
        w_up,
        w_down,
        c_query,
        c_key,
        c_value,
        c_out,
    )
    gathered = (
        lax.all_gather(weight_list[0], DP, axis=0, tiled=True),
        lax.all_gather(weight_list[1], DP, axis=0, tiled=True),
        lax.all_gather(weight_list[2], DP, axis=0, tiled=True),
        lax.all_gather(weight_list[3], DP, axis=0, tiled=True),
        lax.all_gather(weight_list[4], DP, axis=0, tiled=True),
        lax.all_gather(weight_list[5], DP, axis=0, tiled=True),
        lax.all_gather(weight_list[6], DP, axis=0, tiled=True),
        lax.all_gather(weight_list[7], DP, axis=0, tiled=True),
        lax.all_gather(weight_list[8], DP, axis=0, tiled=True),
        lax.all_gather(weight_list[9], DP, axis=0, tiled=True),
        lax.all_gather(weight_list[10], DP, axis=0, tiled=True),
    )
    (
        full_query,
        full_key,
        full_value,
        full_out,
        full_gate,
        full_up,
        full_down,
        full_cquery,
        full_ckey,
        full_cvalue,
        full_cout,
    ) = gathered
    x_attn, normed_attn, scale_attn = normalize(embedded, norm_attn)
    queries = matmul(x_attn, full_query).astype(jnp.bfloat16).reshape(tokens, head_count, HD)
    key_rows = matmul(x_attn, full_key).astype(jnp.bfloat16).reshape(tokens, head_count, HD)
    value_rows = matmul(x_attn, full_value).astype(jnp.bfloat16).reshape(tokens, head_count, HD)
    behind = (WIN - 2) // tokens + 1
    key_parts = []
    value_parts = []
    for offset_back in range(behind, 0, -1):
        far_keys, far_values = passed_along((key_rows, value_rows), SEQ, offset_back)
        key_parts.append(far_keys)
        value_parts.append(far_values)
    all_keys = jnp.concatenate(key_parts + [key_rows], axis=0)
    all_values = jnp.concatenate(value_parts + [value_rows], axis=0)
    q_rows = min(tokens, 512)
    key_span = (WIN - 1 + q_rows - 1) // q_rows * q_rows
    base_key = (rank_seq - behind) * tokens
    block_index = 0
    q_start = block_index * q_rows
    k_start = behind * tokens + q_start - key_span
    allowed = window_mask(
        rank_seq * tokens + q_start, base_key + k_start, q_rows, q_rows + key_span
    )
    scores = (
        jnp.einsum("qhd,khd->hqk", queries, all_keys, preferred_element_type=jnp.float32)
        * SCORE_SCALE
    )
    prob_block, log_total = soft_forward(scores, allowed)
    attended_parts = jnp.einsum(
        "hqk,khd->qhd",
        prob_block.astype(jnp.bfloat16),
        all_values,
        preferred_element_type=jnp.float32,
    )
    lse_parts = [log_total]
    attended = attended_parts.astype(jnp.bfloat16).reshape(tokens, model_width)
    h_mid = embedded + matmul(attended, full_out)
    x_ffn, normed_ffn, scale_ffn = normalize(h_mid, norm_ffn)
    gate_pre = matmul(x_ffn, full_gate)
    up_pre = matmul(x_ffn, full_up)
    gate_sig = jax.nn.sigmoid(gate_pre)
    silu_val = gate_pre * gate_sig
    hidden = (silu_val * up_pre).astype(jnp.bfloat16)
    h_out = h_mid + matmul(hidden, full_down)
    byte_states = h_out.astype(jnp.bfloat16)
    x_cross, normed_cross, scale_cross = normalize(h_out, norm_cross)
    patch_len = lengths[0]
    patch_count = patch_len.shape[0]
    patch_end = jnp.cumsum(patch_len)
    patch_start = patch_end - patch_len
    byte_pos = jnp.arange(tokens, dtype=jnp.int32)
    member = (byte_pos[None, :] >= patch_start[:, None]) & (byte_pos[None, :] < patch_end[:, None])
    length_f = patch_len.astype(jnp.float32)[:, None]
    pooled = matmul(member.astype(jnp.bfloat16), x_cross) / length_f
    pooled_low = pooled.astype(jnp.bfloat16)
    p_query = (
        matmul(pooled_low, full_cquery).astype(jnp.bfloat16).reshape(patch_count, head_count, HD)
    )
    p_key = matmul(x_cross, full_ckey).astype(jnp.bfloat16).reshape(tokens, head_count, HD)
    p_value = matmul(x_cross, full_cvalue).astype(jnp.bfloat16).reshape(tokens, head_count, HD)
    cross_scores = (
        jnp.einsum("phd,thd->hpt", p_query, p_key, preferred_element_type=jnp.float32) * SCORE_SCALE
    )
    cross_prob, cross_lse = soft_forward(cross_scores, member[None])
    p_attended = (
        jnp.einsum(
            "hpt,thd->phd",
            cross_prob.astype(jnp.bfloat16),
            p_value,
            preferred_element_type=jnp.float32,
        )
        .astype(jnp.bfloat16)
        .reshape(patch_count, model_width)
    )
    patch_states = (pooled + matmul(p_attended, full_cout)).astype(jnp.bfloat16)
    grad_c_out = t_times(p_attended, cot_patches)
    grad_patt = (
        times_t(cot_patches, full_cout).astype(jnp.bfloat16).reshape(patch_count, head_count, HD)
    )
    cross_again = (
        jnp.einsum("phd,thd->hpt", p_query, p_key, preferred_element_type=jnp.float32) * SCORE_SCALE
    )
    cross_full = soft_again(cross_again, member[None], cross_lse)
    grad_cprob = jnp.einsum("phd,thd->hpt", grad_patt, p_value, preferred_element_type=jnp.float32)
    grad_cscore = soft_back(cross_full, grad_cprob)
    grad_pquery = (
        (
            jnp.einsum("hpt,thd->phd", grad_cscore, p_key, preferred_element_type=jnp.float32)
            * SCORE_SCALE
        )
        .astype(jnp.bfloat16)
        .reshape(patch_count, model_width)
    )
    grad_pkey = (
        (
            jnp.einsum("hpt,phd->thd", grad_cscore, p_query, preferred_element_type=jnp.float32)
            * SCORE_SCALE
        )
        .astype(jnp.bfloat16)
        .reshape(tokens, model_width)
    )
    grad_pvalue = (
        jnp.einsum(
            "hpt,phd->thd",
            cross_full.astype(jnp.bfloat16),
            grad_patt,
            preferred_element_type=jnp.float32,
        )
        .astype(jnp.bfloat16)
        .reshape(tokens, model_width)
    )
    grad_c_query = t_times(pooled_low, grad_pquery)
    grad_c_key = t_times(x_cross, grad_pkey)
    grad_c_value = t_times(x_cross, grad_pvalue)
    grad_pooled = cot_patches.astype(jnp.float32) + times_t(grad_pquery, full_cquery).astype(
        jnp.bfloat16
    ).astype(jnp.float32)
    to_bytes = lax.dot_general(
        member.astype(jnp.float32),
        grad_pooled / length_f,
        (((0,), (0,)), ((), ())),
        precision=PRECISE,
    )
    grad_xcross = (
        times_t(grad_pkey, full_ckey) + times_t(grad_pvalue, full_cvalue) + to_bytes
    ).astype(jnp.bfloat16)
    grad_hout_norm, grad_norm_cross = norm_back(
        grad_xcross.astype(jnp.float32), normed_cross, scale_cross, norm_cross
    )
    grad_hout = cot_bytes.astype(jnp.float32) + grad_hout_norm
    grad_branch_f = grad_hout.astype(jnp.bfloat16)
    grad_w_down = t_times(hidden, grad_branch_f)
    grad_hidden = times_t(grad_branch_f, full_down).astype(jnp.bfloat16).astype(jnp.float32)
    grad_gate = (grad_hidden * up_pre * gate_sig * (1.0 + gate_pre * (1.0 - gate_sig))).astype(
        jnp.bfloat16
    )
    grad_up = (grad_hidden * silu_val).astype(jnp.bfloat16)
    grad_w_gate = t_times(x_ffn, grad_gate)
    grad_w_up = t_times(x_ffn, grad_up)
    grad_xffn = (times_t(grad_gate, full_gate) + times_t(grad_up, full_up)).astype(jnp.bfloat16)
    grad_hmid_norm, grad_norm_ffn = norm_back(
        grad_xffn.astype(jnp.float32), normed_ffn, scale_ffn, norm_ffn
    )
    grad_hmid = grad_hout + grad_hmid_norm
    grad_branch_a = grad_hmid.astype(jnp.bfloat16)
    grad_w_out = t_times(attended, grad_branch_a)
    grad_att = times_t(grad_branch_a, full_out).astype(jnp.bfloat16).reshape(tokens, head_count, HD)
    grad_keys_all = jnp.zeros(((behind + 1) * tokens, head_count, HD), jnp.float32)
    grad_values_all = jnp.zeros(((behind + 1) * tokens, head_count, HD), jnp.float32)
    block_index = 0
    q_start = block_index * q_rows
    k_start = behind * tokens + q_start - key_span
    k_stop = k_start + q_rows + key_span
    allowed = window_mask(
        rank_seq * tokens + q_start, base_key + k_start, q_rows, q_rows + key_span
    )
    scores = (
        jnp.einsum("qhd,khd->hqk", queries, all_keys, preferred_element_type=jnp.float32)
        * SCORE_SCALE
    )
    prob_block = soft_again(scores, allowed, lse_parts[block_index])
    grad_prob = jnp.einsum("qhd,khd->hqk", grad_att, all_values, preferred_element_type=jnp.float32)
    grad_score = soft_back(prob_block, grad_prob)
    grad_q_parts = (
        jnp.einsum("hqk,khd->qhd", grad_score, all_keys, preferred_element_type=jnp.float32)
        * SCORE_SCALE
    )
    grad_keys_all = grad_keys_all.at[k_start:k_stop].add(
        jnp.einsum("hqk,qhd->khd", grad_score, queries, preferred_element_type=jnp.float32)
        * SCORE_SCALE
    )
    grad_values_all = grad_values_all.at[k_start:k_stop].add(
        jnp.einsum(
            "hqk,qhd->khd",
            prob_block.astype(jnp.bfloat16),
            grad_att,
            preferred_element_type=jnp.float32,
        )
    )
    grad_keys = grad_keys_all[behind * tokens :]
    grad_values = grad_values_all[behind * tokens :]
    for offset_back in range(behind, 0, -1):
        part_index = behind - offset_back
        far_grad_k, far_grad_v = (
            passed_along(
                grad_keys_all[part_index * tokens : (part_index + 1) * tokens].astype(jnp.bfloat16),
                SEQ,
                -offset_back,
            ).astype(jnp.float32),
            passed_along(
                grad_values_all[part_index * tokens : (part_index + 1) * tokens].astype(
                    jnp.bfloat16
                ),
                SEQ,
                -offset_back,
            ).astype(jnp.float32),
        )
        grad_keys = grad_keys + far_grad_k
        grad_values = grad_values + far_grad_v
    grad_queries = grad_q_parts.astype(jnp.bfloat16).reshape(tokens, model_width)
    grad_keys_low = grad_keys.astype(jnp.bfloat16).reshape(tokens, model_width)
    grad_values_low = grad_values.astype(jnp.bfloat16).reshape(tokens, model_width)
    grad_w_query = t_times(x_attn, grad_queries)
    grad_w_key = t_times(x_attn, grad_keys_low)
    grad_w_value = t_times(x_attn, grad_values_low)
    grad_xattn = (
        times_t(grad_queries, full_query)
        + times_t(grad_keys_low, full_key)
        + times_t(grad_values_low, full_value)
    ).astype(jnp.bfloat16)
    grad_embed_norm, grad_norm_attn = norm_back(
        grad_xattn.astype(jnp.float32), normed_attn, scale_attn, norm_attn
    )
    grad_embed = grad_hmid + grad_embed_norm
    embed_grad = grad_embed.astype(jnp.bfloat16)
    grad_byte_table = lax.dot_general(
        one_hot.astype(jnp.float32), grad_embed, (((0,), (0,)), ((), ())), precision=PRECISE
    )
    per_request = jnp.broadcast_to(
        grad_embed[:, None, :], (tokens, gram_count, model_width)
    ).reshape(request_count, model_width)
    outgoing = (
        jnp.zeros((all_count * slot_count, model_width), jnp.float32).at[placement].set(per_request)
    )
    outgoing = outgoing.reshape(dp_count, rs_count, slot_count, model_width)
    arrived = lax.all_to_all(
        lax.all_to_all(
            outgoing.astype(jnp.bfloat16), DP, split_axis=0, concat_axis=0, tiled=True
        ),
        SEQ,
        split_axis=1,
        concat_axis=1,
        tiled=True,
    ).astype(outgoing.dtype)
    hash_table_grad = (
        jnp.zeros((rows_dev, model_width), jnp.float32)
        .at[safe_rows.reshape(-1)]
        .add(jnp.where(present[..., None], arrived, 0.0).reshape(-1, model_width))
    )
    summed_all = (
        lax.psum_scatter(grad_norm_attn, ALL, scatter_dimension=0, tiled=True),
        lax.psum_scatter(grad_norm_ffn, ALL, scatter_dimension=0, tiled=True),
        lax.psum_scatter(grad_norm_cross, ALL, scatter_dimension=0, tiled=True),
        lax.psum_scatter(grad_w_query, ALL, scatter_dimension=0, tiled=True),
        lax.psum_scatter(grad_w_key, ALL, scatter_dimension=0, tiled=True),
        lax.psum_scatter(grad_w_value, ALL, scatter_dimension=0, tiled=True),
        lax.psum_scatter(grad_w_out, ALL, scatter_dimension=0, tiled=True),
        lax.psum_scatter(grad_w_gate, ALL, scatter_dimension=0, tiled=True),
        lax.psum_scatter(grad_w_up, ALL, scatter_dimension=0, tiled=True),
        lax.psum_scatter(grad_w_down, ALL, scatter_dimension=0, tiled=True),
        lax.psum_scatter(grad_c_query, ALL, scatter_dimension=0, tiled=True),
        lax.psum_scatter(grad_c_key, ALL, scatter_dimension=0, tiled=True),
        lax.psum_scatter(grad_c_value, ALL, scatter_dimension=0, tiled=True),
        lax.psum_scatter(grad_c_out, ALL, scatter_dimension=0, tiled=True),
        lax.psum_scatter(grad_byte_table, ALL, scatter_dimension=0, tiled=True),
    )
    (
        out_norm_attn,
        out_norm_ffn,
        out_norm_cross,
        out_query,
        out_key,
        out_value,
        out_proj,
        out_gate,
        out_up,
        out_down,
        out_cquery,
        out_ckey,
        out_cvalue,
        out_cout,
        out_bytes,
    ) = summed_all
    return (
        byte_states,
        patch_states,
        embed_grad,
        out_bytes,
        hash_table_grad,
        row_counts,
        out_norm_attn,
        out_norm_ffn,
        out_norm_cross,
        out_query,
        out_key,
        out_value,
        out_proj,
        out_gate,
        out_up,
        out_down,
        out_cquery,
        out_ckey,
        out_cvalue,
        out_cout,
    )


def fast_body(
    byte_ids,
    hash_ids,
    lengths,
    byte_table,
    hash_table,
    norm_attn,
    norm_ffn,
    norm_cross,
    w_query,
    w_key,
    w_value,
    w_out,
    w_gate,
    w_up,
    w_down,
    c_query,
    c_key,
    c_value,
    c_out,
    cot_bytes,
    cot_patches,
):
    dp_count = lax.axis_size(DP)
    rs_count = lax.axis_size(SEQ)
    all_count = dp_count * rs_count
    rank_table = lax.axis_index(ALL)
    rows_dev, model_width = hash_table.shape
    patch_len = lengths[0]
    patch_end = jnp.cumsum(patch_len)[:, None]
    patch_start = patch_end - patch_len[:, None]
    gains = jnp.concatenate(
        [norm_attn[None], norm_ffn[None], norm_cross[None], jnp.zeros((5, model_width), jnp.float32)]
    )
    full, embedded, entries, kept = fetch(
        hash_ids,
        hash_table,
        (
            w_query,
            w_key,
            w_value,
            w_out,
            w_gate,
            w_up,
            w_down,
            c_query,
            c_key,
            c_value,
            c_out,
        ),
        (byte_ids[:, None], byte_table, gains, patch_start, patch_end),
        WEIGHT_STEPS,
        dp_count,
    )
    lefts = [
        by_rows(a, dp_count)
        for a in (kept.x_ffn, kept.hidden, kept.pooled, kept.x_cross, kept.p_attended)
    ]
    sums, results = back_sums(
        lefts,
        Streamed(
            kept.gate_pre,
            kept.up_pre,
            kept.h_out,
            kept.h_mid,
            embedded,
            kept.key_values,
            *full,
            cot_patches,
        ),
        (
            cot_bytes,
            kept.p_query,
            kept.p_key,
            kept.p_value,
            kept.cross_lse,
            gains,
            patch_start,
            patch_end,
            kept.queries,
            kept.lse,
        ),
        dp_count,
    )
    first_sums = sums
    gain_rows, grad_branch_a, grad_queries, grad_keys, grad_values, embed_grad = results
    one_hot = byte_ids[:, None] == jnp.arange(BYTE_VALUES, dtype=jnp.int32)[None, :]
    lefts = [
        by_rows(a, dp_count) for a in (kept.x_attn, kept.attended, one_hot.astype(jnp.bfloat16))
    ]
    rights = [grad_queries, grad_keys, grad_values, grad_branch_a, embed_grad]
    sums, gain_sums, *table_parts = last_sums(
        [(1, 3), (0, 0), (0, 1), (0, 2), (2, 4)],
        lefts,
        rights,
        embed_grad,
        gain_rows,
        entries,
        rows_dev,
        dp_count,
    )
    wholes = (*sums, *first_sums[:5])
    cuts = [a.shape[0] for a in wholes]
    cuts[4] = BYTE_VALUES // all_count
    cuts[9] = kept.hidden.shape[1] // all_count
    (
        hash_table_grad,
        counts,
        out_proj,
        out_query,
        out_key,
        out_value,
        out_bytes,
        out_cout,
        out_ckey,
        out_cvalue,
        out_cquery,
        out_down,
        out_gate,
        out_up,
    ) = finish(*table_parts, wholes, tuple(cuts), first_sums[5:])
    row_counts = counts[:, 0]
    own_gains = lax.dynamic_slice_in_dim(
        gain_sums, rank_table * (model_width // all_count), model_width // all_count, 1
    )
    return (
        kept.byte_states,
        kept.patch_states,
        embed_grad,
        out_bytes,
        hash_table_grad,
        row_counts,
        own_gains[0],
        own_gains[1],
        own_gains[2],
        out_query,
        out_key,
        out_value,
        out_proj,
        out_gate,
        out_up,
        out_down,
        out_cquery,
        out_ckey,
        out_cvalue,
        out_cout,
    )


def solution(mesh):
    fits = mesh.shape[REP] == 2 and mesh.shape[SUB] == 4 and mesh.shape[DP] <= 4
    return jax.shard_map(
        fast_body if fits else body,
        mesh=mesh,
        in_specs=(
            P(ALL),
            P(ALL, None),
            P(ALL, None),
            P(),
            P(ALL, None),
            P(),
            P(),
            P(),
            P(DP, None),
            P(DP, None),
            P(DP, None),
            P(DP, None),
            P(DP, None),
            P(DP, None),
            P(DP, None),
            P(DP, None),
            P(DP, None),
            P(DP, None),
            P(DP, None),
            P(ALL, None),
            P(ALL, None),
        ),
        out_specs=(
            P(ALL, None),
            P(ALL, None),
            P(ALL, None),
            P(ALL, None),
            P(ALL, None),
            P(ALL),
            P(ALL),
            P(ALL),
            P(ALL),
            P(ALL, None),
            P(ALL, None),
            P(ALL, None),
            P(ALL, None),
            P(ALL, None),
            P(ALL, None),
            P(ALL, None),
            P(ALL, None),
            P(ALL, None),
            P(ALL, None),
            P(ALL, None),
        ),
        check_vma=False,
    )
```

```python
import functools
import typing

import jax
import jax.numpy as jnp
from jax import lax
from jax.experimental import pallas as pl
from jax.experimental.pallas import tpu as pltpu
from jax.sharding import PartitionSpec as P

DP, REP, SUB = "dp", "rep", "sub"
SEQ = (REP, SUB)
ALL = (DP, REP, SUB)
HD = 64
WIN = 512
BYTE_VALUES = 256


PRECISE = lax.Precision.HIGHEST
NEG_BIG = -1e30
EPSILON = 1e-06
SCORE_SCALE = 0.125


def passed_along(x, axis, by):
    devices = lax.axis_size(axis)
    pairs = [(i, i + by) for i in range(devices) if 0 <= i + by < devices]
    return lax.ppermute(x, axis, pairs)


def matmul(matrix_a, matrix_b):
    return jnp.dot(matrix_a, matrix_b, preferred_element_type=jnp.float32)


def times_t(matrix_a, matrix_b):
    return lax.dot_general(
        matrix_a, matrix_b, (((1,), (1,)), ((), ())), preferred_element_type=jnp.float32
    )


def t_times(matrix_a, matrix_b):
    return lax.dot_general(
        matrix_a, matrix_b, (((0,), (0,)), ((), ())), preferred_element_type=jnp.float32
    )


def normalize(values, gains):
    inv_rms = lax.rsqrt(jnp.mean(values * values, axis=-1, keepdims=True) + EPSILON)
    normed = values * inv_rms
    return ((normed * gains).astype(jnp.bfloat16), normed, inv_rms)


def norm_back(grad_out, normed, inv_rms, gains):
    grad_gain = jnp.sum(grad_out * normed, axis=0)
    scaled_grad = grad_out * gains
    grad_in = inv_rms * (
        scaled_grad - normed * jnp.mean(scaled_grad * normed, axis=-1, keepdims=True)
    )
    return (grad_in, grad_gain)


def soft_forward(scores, allowed):
    masked = jnp.where(allowed, scores, NEG_BIG)
    row_max = jnp.max(masked, axis=-1, keepdims=True)
    exps = jnp.exp(masked - row_max)
    row_sum = jnp.sum(exps, axis=-1, keepdims=True)
    return (exps / row_sum, row_max + jnp.log(row_sum))


def soft_again(scores, allowed, log_total):
    return jnp.where(allowed, jnp.exp(scores - log_total), 0.0)


def soft_back(probs_full, grad_probs):
    row_total = jnp.sum(probs_full * grad_probs, axis=-1, keepdims=True)
    return (probs_full * (grad_probs - row_total)).astype(jnp.bfloat16)


def window_mask(first_query, first_key, row_count, col_count):
    query_pos = first_query + jnp.arange(row_count, dtype=jnp.int32)
    key_pos = first_key + jnp.arange(col_count, dtype=jnp.int32)
    near = (
        (key_pos[None, :] <= query_pos[:, None])
        & (key_pos[None, :] > query_pos[:, None] - WIN)
        & (key_pos[None, :] >= 0)
    )
    return near[None]


MESH_ID = pl.DeviceIdType.MESH
SLOTS = 96
GATHER_LAGS = (1, 2, 3)


HASH, GATHER, FORWARD = range(3)


SCHEDULE = (
    (GATHER, 0),
    (HASH, 0),
    (GATHER, 1),
    (HASH, 1),
    (HASH, 2),
    (GATHER, 2),
    (HASH, 3),
    (GATHER, 3),
    (HASH, 4),
    (GATHER, 4),
    (HASH, 5),
    (GATHER, 5),
    (HASH, 6),
    (GATHER, 6),
    (HASH, 7),
    (FORWARD, 2),
    (GATHER, 7),
    (FORWARD, 2),
    (GATHER, 8),
    (FORWARD, 2),
    (GATHER, 9),
    (FORWARD, 2),
    (GATHER, 10),
    (GATHER, 11),
    (FORWARD, 2),
    (GATHER, 12),
    (FORWARD, 2),
    (GATHER, 13),
    (FORWARD, 3),
)
VMEM_CAP = 60 * 1024 * 1024


class Place:
    def __init__(self, dp_count):
        self.n = dp_count
        self.z = lax.axis_index(DP)
        self.x = lax.axis_index(REP)
        sub = lax.axis_index(SUB)
        self.y = sub // 2
        self.c = sub % 2
        self.started, self.maybe = [], []

    def at(self, dz=0, dx=0, dy=0, dc=0):
        z = lax.rem(self.z + dz, self.n) if dz else self.z
        x = 1 - self.x if dx else self.x
        y = 1 - self.y if dy else self.y
        c = 1 - self.c if dc else self.c
        return (z, x, y * 2 + c)

    def greet(self):
        barrier = pltpu.get_barrier_semaphore()
        peers = [
            self.at(dx=dx, dy=dy, dc=dc)
            for dx in range(2)
            for dy in range(2)
            for dc in range(2)
            if dx + dy + dc > 0
        ]
        peers += [self.at(dz=j) for j in range(1, self.n)]
        for peer in peers:
            pl.semaphore_signal(barrier, inc=1, device_id=peer, device_id_type=MESH_ID)
        pl.semaphore_wait(barrier, len(peers))

    def send_if(self, there, src, dst, send_sem, recv_sem, peer):
        copy = pltpu.make_async_remote_copy(
            src_ref=src,
            dst_ref=dst,
            send_sem=send_sem,
            recv_sem=recv_sem,
            device_id=peer,
            device_id_type=MESH_ID,
        )
        pl.when(there)(copy.start)
        self.maybe.append((there, copy))

    def send(self, src, dst, send_sem, recv_sem, peer):
        copy = pltpu.make_async_remote_copy(
            src_ref=src,
            dst_ref=dst,
            send_sem=send_sem,
            recv_sem=recv_sem,
            device_id=peer,
            device_id_type=MESH_ID,
        )
        copy.start()
        self.started.append(copy)
        return copy

    def expect(self, dst, recv_sem):
        pltpu.make_async_remote_copy(
            src_ref=dst,
            dst_ref=dst,
            send_sem=recv_sem,
            recv_sem=recv_sem,
            device_id=self.at(dc=1),
            device_id_type=MESH_ID,
        ).wait_recv()

    def sent(self, copy):
        copy.wait_send()
        self.started = [other for other in self.started if other is not copy]

    def finish(self):
        for copy in self.started:
            copy.wait_send()
        for there, copy in self.maybe:
            pl.when(there)(copy.wait_send)
        self.started, self.maybe = [], []


def add_into(dst, src, blocks, width):
    def step(i, carry):
        total = dst(i)[...].astype(jnp.float32) + src(i)[...].astype(jnp.float32)
        dst(i)[...] = total.astype(jnp.bfloat16)
        return carry

    lax.fori_loop(0, blocks, step, 0)


class Reduction:
    def __init__(self, here, p0, r1a, r1b, r2a, r2b, sems, index):
        self.here, self.p0 = here, p0
        self.r1a, self.r1b, self.r2a, self.r2b = r1a, r1b, r2a, r2b
        self.sems, self.i = sems, index
        self.planes, _, _, self.rows, cols = p0.shape
        self.half = cols // 2
        self.left = pl.ds(0, self.half)
        self.right = pl.ds(self.half, self.half)

    def sem(self, k):
        return self.sems.at[self.i, k, 0], self.sems.at[self.i, k, 1]

    def first(self):
        h = self.here
        self.s1a = h.send(
            self.p0.at[:, 1 - h.x, :, :, self.left], self.r1a, *self.sem(0), h.at(dx=1)
        )
        self.s1b = h.send(
            self.p0.at[:, :, 1 - h.y, :, self.right], self.r1b, *self.sem(1), h.at(dy=1)
        )

    def second(self):
        h = self.here
        self.s1a.wait_recv()
        add_into(
            lambda i: self.p0.at[i // 2, h.x, i % 2, :, self.left],
            lambda i: self.r1a.at[i // 2, i % 2],
            2 * self.planes,
            self.half,
        )
        self.s2a = h.send(
            self.p0.at[:, h.x, 1 - h.y, :, self.left], self.r2a, *self.sem(2), h.at(dy=1)
        )
        self.s1b.wait_recv()
        add_into(
            lambda i: self.p0.at[i // 2, i % 2, h.y, :, self.right],
            lambda i: self.r1b.at[i // 2, i % 2],
            2 * self.planes,
            self.half,
        )
        self.s2b = h.send(
            self.p0.at[:, 1 - h.x, h.y, :, self.right], self.r2b, *self.sem(3), h.at(dx=1)
        )

    def third(self):
        h = self.here
        self.s2a.wait_recv()
        add_into(
            lambda i: self.p0.at[i, h.x, h.y, :, self.left],
            lambda i: self.r2a.at[i],
            self.planes,
            self.half,
        )
        self.s2b.wait_recv()
        add_into(
            lambda i: self.p0.at[i, h.x, h.y, :, self.right],
            lambda i: self.r2b.at[i],
            self.planes,
            self.half,
        )
        return self.p0.at[:, h.x, h.y]


EXTRA_IN = 5
F32, LOW = jnp.float32, jnp.bfloat16
class Kept(typing.NamedTuple):
    x_attn: typing.Any
    queries: typing.Any
    key_values: typing.Any
    lse: typing.Any
    attended: typing.Any
    h_mid: typing.Any
    x_ffn: typing.Any
    gate_pre: typing.Any
    up_pre: typing.Any
    hidden: typing.Any
    h_out: typing.Any
    byte_states: typing.Any
    x_cross: typing.Any
    pooled: typing.Any
    p_query: typing.Any
    p_key: typing.Any
    p_value: typing.Any
    cross_lse: typing.Any
    p_attended: typing.Any
    patch_states: typing.Any


def kept_shapes(t, w, f, p):
    one = jax.ShapeDtypeStruct
    return Kept(
        x_attn=one((t, w), LOW),
        queries=one((t, w), LOW),
        key_values=one((2, 3 * t, w), LOW),
        lse=one((t, 128), F32),
        attended=one((t, w), LOW),
        h_mid=one((t, w), F32),
        x_ffn=one((t, w), LOW),
        gate_pre=one((t, f), F32),
        up_pre=one((t, f), F32),
        hidden=one((t, f), LOW),
        h_out=one((t, w), F32),
        byte_states=one((t, w), LOW),
        x_cross=one((t, w), LOW),
        pooled=one((p, w), LOW),
        p_query=one((p, w), LOW),
        p_key=one((t, w), LOW),
        p_value=one((t, w), LOW),
        cross_lse=one((p, 128), F32),
        p_attended=one((p, w), LOW),
        patch_states=one((p, w), LOW),
    )


def forward_steps(here, fulls, embedded, extra_in, extra_out, slots, scratch):
    byte_ids, byte_table, gains, starts, ends = extra_in
    gate_w, up_w, x_halo, load_sems, halo_sems, *buffers, flush_sems = scratch
    out = Kept(*extra_out)
    flushed = (out.gate_pre, out.up_pre, out.key_values)
    out = out._replace(gate_pre=buffers[0], up_pre=buffers[1], key_values=buffers[2])
    flushes = []

    def flush(i):
        copy = pltpu.make_async_copy(buffers[i], flushed[i], flush_sems.at[i])
        copy.start()
        flushes.append(copy)

    tokens, width = embedded.shape
    heads = width // HD
    n = here.n
    z, x, y, c = here.z, here.x, here.y, here.c
    rank = (x * 2 + y) * 2 + c
    loads = {}
    kv = out.key_values

    def load(i, *targets):
        copies = []
        for b, target in enumerate(targets):
            rows = target.shape[0]
            copy = pltpu.make_async_copy(
                fulls[i].at[pl.ds(b * rows, rows)], target, load_sems.at[i, b]
            )
            copy.start()
            copies.append(copy)
        loads[i] = copies

    def load_slot(i, slot):
        for b in range(4):
            copy = pltpu.make_async_copy(
                fulls[i].at[pl.ds(b * (width // 4), width // 4)],
                slots[slot].at[b // 2, b % 2],
                load_sems.at[i, b],
            )
            copy.start()
            loads.setdefault(i, []).append(copy)

    def wait(*weights):
        for i in weights:
            for copy in loads[i]:
                copy.wait()

    def through(a, slot):
        return matmul(a, slots[slot][...].reshape(width, width))

    def embed():
        load_slot(0, 0)
        load_slot(1, 1)
        load_slot(2, 2)
        ids = lax.broadcasted_iota(jnp.int32, (tokens, BYTE_VALUES), 1)
        pick = jnp.where(byte_ids[...] == ids, 1.0, 0.0).astype(LOW)
        embedded[...] = embedded[...] + matmul(pick, byte_table[...])
        out.x_attn[...] = normalize(embedded[...], gains[0:1])[0]
        halo_send()

    def halo_send():
        target = jnp.minimum(rank + 2, 7)
        here.send_if(
            rank + 2 < 8,
            out.x_attn,
            x_halo.at[0],
            halo_sems.at[0, 0],
            halo_sems.at[0, 1],
            (z, target // 4, lax.rem(target, 4)),
        )
        here.send_if(
            c == 0, out.x_attn, x_halo.at[1], halo_sems.at[1, 0], halo_sems.at[1, 1], here.at(dc=1)
        )

    def project():
        wait(0, 1, 2)
        a = out.x_attn[...]
        out.queries[...] = through(a, 0).astype(LOW)
        kv[0, 2 * tokens :] = through(a, 1).astype(LOW)
        kv[1, 2 * tokens :] = through(a, 2).astype(LOW)

    def halo():
        there = rank >= 2

        @pl.when(there)
        def _():
            here.expect(x_halo.at[0], halo_sems.at[0, 1])

        here.send_if(
            there & (c == 1),
            x_halo.at[0],
            x_halo.at[1],
            halo_sems.at[1, 0],
            halo_sems.at[1, 1],
            here.at(dc=1),
        )

        @pl.when(there | (c == 1))
        def _():
            here.expect(x_halo.at[1], halo_sems.at[1, 1])

        @pl.when(jnp.logical_not(there))
        def _():
            x_halo[0] = jnp.zeros_like(x_halo[0])

        @pl.when(rank == 0)
        def _():
            x_halo[1] = jnp.zeros_like(x_halo[1])

        a = x_halo[...].reshape(2 * tokens, width)
        kv[0, : 2 * tokens] = through(a, 1).astype(LOW)
        kv[1, : 2 * tokens] = through(a, 2).astype(LOW)
        flush(2)

    lane = lax.broadcasted_iota(jnp.int32, (1, 128), 1)
    sides = [jnp.where(lane < HD, 1.0, 0.0).astype(LOW), jnp.where(lane < HD, 0.0, 1.0).astype(LOW)]

    def attend(first):
        row = lax.broadcasted_iota(jnp.int32, (tokens, tokens), 0)
        col = lax.broadcasted_iota(jnp.int32, (tokens, tokens), 1)
        mine = col <= row
        far_bias = jnp.where(rank >= 2, 0.0, NEG_BIG)
        near_bias = jnp.where(rank >= 1, 0.0, NEG_BIG)
        if first == 0:
            out.lse[...] = jnp.zeros_like(out.lse)
        else:
            load_slot(3, 3)

        def heads_pair(pair, carry):
            span = pl.ds(pl.multiple_of(pair * 128, 128), 128)
            q2 = out.queries[:, span]
            k2, v2 = kv[0, :, span], kv[1, :, span]
            halves = []
            for side in range(2):
                scores = times_t(q2 * sides[side], k2) * SCORE_SCALE
                edge = jnp.where(mine, scores[:, 2 * tokens :], scores[:, :tokens] + far_bias)
                middle = scores[:, tokens : 2 * tokens] + near_bias
                top = jnp.maximum(
                    jnp.max(edge, axis=1, keepdims=True), jnp.max(middle, axis=1, keepdims=True)
                )
                edge, middle = jnp.exp(edge - top), jnp.exp(middle - top)
                total = jnp.sum(edge, axis=1, keepdims=True) + jnp.sum(
                    middle, axis=1, keepdims=True
                )
                inverse = 1.0 / total
                edge, middle = edge * inverse, middle * inverse
                probs = jnp.concatenate(
                    [
                        jnp.where(mine, 0.0, edge).astype(LOW),
                        middle.astype(LOW),
                        jnp.where(mine, edge, 0.0).astype(LOW),
                    ],
                    axis=1,
                )
                halves.append(matmul(probs, v2))
                where = lane == pair * 2 + side
                out.lse[...] = jnp.where(where, top + jnp.log(total), out.lse[...])
            out.attended[:, span] = jnp.where(lane < HD, halves[0], halves[1]).astype(LOW)
            return carry

        lax.fori_loop(first * heads // 4, (first + 1) * heads // 4, heads_pair, 0)

    def attention_out():
        wait(3)
        h_mid = embedded[...] + through(out.attended[...], 3)
        out.h_mid[...] = h_mid
        out.x_ffn[...] = normalize(h_mid, gains[1:2])[0]

    def down_block(t):
        return slots[t // 4].at[t // 2 % 2, t % 2]

    tile = 256
    tiles = gate_w.shape[1] // tile

    def feed_forward():
        for t in range(tiles):
            copy = pltpu.make_async_copy(
                fulls[6].at[pl.ds(t * tile, tile)], down_block(t), down_sems.at[t]
            )
            copy.start()
            loads.setdefault(6, []).append(copy)
        wait(4, 5)
        a = out.x_ffn[...]

        def columns(t, carry):
            span = pl.ds(pl.multiple_of(t * tile, tile), tile)
            gate = matmul(a, gate_w[:, span])
            up = matmul(a, up_w[:, span])
            out.gate_pre[:, span] = gate
            out.up_pre[:, span] = up
            out.hidden[:, span] = (gate * jax.nn.sigmoid(gate) * up).astype(LOW)
            return carry

        lax.fori_loop(0, tiles, columns, 0)
        flush(0)
        flush(1)

    def feed_out():
        wait(6)
        total = out.h_mid[...]
        for t in range(tiles):
            total = total + matmul(
                out.hidden[:, t * tile : (t + 1) * tile], down_block(t)[...]
            )
        out.h_out[...] = total
        out.byte_states[...] = total.astype(LOW)
        out.x_cross[...] = normalize(total, gains[2:3])[0]

    byte_pos = lax.broadcasted_iota(jnp.int32, (starts.shape[0], tokens), 1)

    def member():
        return (byte_pos >= starts[...]) & (byte_pos < ends[...])

    pooled_f = []

    def cross_keys():
        inside = jnp.where(member(), 1.0, 0.0).astype(LOW)
        length = (ends[...] - starts[...]).astype(F32)
        pooled = matmul(inside, out.x_cross[...]) / length
        pooled_f.append(pooled)
        out.pooled[...] = pooled.astype(LOW)
        wait(8, 9)
        a = out.x_cross[...]
        out.p_key[...] = through(a, 4).astype(LOW)
        out.p_value[...] = through(a, 5).astype(LOW)

    def cross_query():
        wait(7)
        out.p_query[...] = through(out.pooled[...], 3).astype(LOW)
        allowed = member()
        out.cross_lse[...] = jnp.zeros_like(out.cross_lse)

        def heads_pair(pair, carry):
            span = pl.ds(pl.multiple_of(pair * 128, 128), 128)
            q2, k2, v2 = out.p_query[:, span], out.p_key[:, span], out.p_value[:, span]
            halves = []
            for side in range(2):
                scores = times_t(q2 * sides[side], k2) * SCORE_SCALE
                masked = jnp.where(allowed, scores, NEG_BIG)
                top = jnp.max(masked, axis=1, keepdims=True)
                exps = jnp.exp(masked - top)
                total = jnp.sum(exps, axis=1, keepdims=True)
                halves.append(matmul((exps / total).astype(LOW), v2))
                where = lane == pair * 2 + side
                out.cross_lse[...] = jnp.where(
                    where, top + jnp.log(total), out.cross_lse[...]
                )
            out.p_attended[:, span] = jnp.where(lane < HD, halves[0], halves[1]).astype(LOW)
            return carry

        lax.fori_loop(0, heads // 2, heads_pair, 0)

    def cross_out():
        wait(10)
        states = pooled_f[0] + through(out.p_attended[...], 0)
        out.patch_states[...] = states.astype(LOW)
        for copy in flushes:
            copy.wait()

    down_sems = load_sems.at[6]
    return [
        ((0, 1, 2), embed),
        ((), project),
        ((), halo),
        ((), lambda: attend(0)),
        ((4, 5), lambda: (load(4, gate_w), load(5, up_w))),
        ((3,), lambda: attend(1)),
        ((), attention_out),
        ((6,), feed_forward),
        ((8, 9), lambda: (load_slot(8, 4), load_slot(9, 5))),
        ((), feed_out),
        ((7,), lambda: load_slot(7, 3)),
        ((), cross_keys),
        ((10,), lambda: load_slot(10, 0)),
        ((), cross_query),
        ((), cross_out),
    ]


def fetch_kernel(dp_count, weight_count, steps_of, tokens, gram_count, used_lines, *refs):
    shards = refs[:weight_count]
    refs = list(refs[weight_count:])

    def take(number):
        taken = refs[:number]
        del refs[:number]
        return taken

    ids, table = take(2)
    extra_in = take(EXTRA_IN)
    fulls = take(weight_count)
    embedded, lists = take(2)
    extra_out = take(len(Kept._fields))
    (
        all_ids,
        send0,
        p0,
        r1a,
        r1b,
        r2a,
        r2b,
        r3,
        g_rows,
        core_sems,
        stage_sems,
        z_sems,
        local_sems,
        w_send,
        w_recv,
        z_send,
        id_sems,
        places,
        entries,
        *extra_scratch,
    ) = refs
    here = Place(dp_count)
    n = dp_count
    z, x, y, c = here.z, here.x, here.y, here.c

    class Weight:
        def __init__(self, number, i, part, parts, kind):
            self.i = number
            self.kind = kind
            rows, cols = shards[i].shape
            self.by_cols = rows // 8 % 16 != 0
            self.all_rows, self.count = rows, rows // parts
            self.first = part * self.count
            self.shard = shards[i].at[pl.ds(self.first, self.count)]
            self.full = fulls[i]
            self.step = (cols if self.by_cols else rows // parts) // 8
            near, far = (x, y) if kind == 0 else (y, x)
            self.q = (c * 2 + far) * 2 + near

        def on(self, plane):
            return self.full.at[pl.ds(plane * self.all_rows + self.first, self.count)]

        def cut(self, ref, start, count):
            span = pl.ds(start * self.step, count * self.step)
            if self.by_cols:
                return ref.at[:, span]
            return ref.at[span, :]

        def local(self):
            here.send(
                self.shard,
                self.on(z),
                local_sems.at[self.i, 0],
                local_sems.at[self.i, 1],
                here.at(dc=1),
            )

        def stage(self, k, j, start, count, src_ref, plane, peer):
            here.send(
                self.cut(src_ref, start, count),
                self.cut(self.on(plane), start, count),
                w_send.at[self.i, k, j - 1],
                w_recv.at[self.i, k, j - 1],
                peer,
            )

        def came(self, k, j, start, count):
            plane = lax.rem(z + n - j, n)
            here.expect(
                self.cut(self.on(plane), start, count), w_recv.at[self.i, k, j - 1]
            )
            return plane

        def hop(self, there, up, k, plane, src_ref):
            peer = jnp.clip(z + 1 if up else z - 1, 0, n - 1)
            here.send_if(
                there,
                self.cut(src_ref, self.q, 1),
                self.cut(self.on(plane), self.q, 1),
                z_send.at[self.i, 0 if up else 1, k],
                w_recv.at[self.i, 0, (k + 1 if up else n - k - 1) - 1],
                (peer, x, y * 2 + c),
            )

        def along_z(self):
            self.hop(z + 1 < n, True, 0, z, self.shard)
            self.hop(z >= 1, False, 0, z, self.shard)

        def onward(self, k):
            for up in (True, False):
                there = (z >= k) & (z + 1 < n) if up else (z + k < n) & (z >= 1)
                plane = jnp.clip(z - k if up else z + k, 0, n - 1)
                j = k if up else n - k

                @pl.when(there)
                def _():
                    self.came(0, j, self.q, 1)

                self.hop(there, up, k, plane, self.on(plane))

        def near(self):
            for j in range(1, n):
                plane = lax.rem(z + n - j, n)

                @pl.when((z == 0) | (z == n - 1))
                def _():
                    self.came(0, j, self.q, 1)

                peer = here.at(dx=1) if self.kind == 0 else here.at(dy=1)
                self.stage(1, j, self.q, 1, self.on(plane), plane, peer)

        def far(self):
            other = self.q + 1 - 2 * (self.q % 2)
            for j in range(1, n):
                plane = self.came(1, j, other, 1)
                peer = here.at(dy=1) if self.kind == 0 else here.at(dx=1)
                self.stage(2, j, self.q // 2 * 2, 2, self.on(plane), plane, peer)

        def across(self):
            pair = self.q // 2
            other = pair + 1 - 2 * (pair % 2)
            for j in range(1, n):
                plane = self.came(2, j, other * 2, 2)
                self.stage(3, j, c * 4, 4, self.on(plane), plane, here.at(dc=1))

        def done(self):
            for j in range(1, n):
                self.came(3, j, (1 - c) * 4, 4)
            here.expect(self.on(z), local_sems.at[self.i, 1])

    weights = []
    for first, second in steps_of:
        pair = []
        for kind, (i, part, parts) in enumerate((first, second)):
            pair.append(Weight(2 * len(weights) + kind, i, part, parts, kind))
        weights.append(pair)

    def each(t, name):
        if 0 <= t < len(weights):
            for w in weights[t]:
                name(w)

    def gather_ids():
        all_ids[z, x, y, c] = ids[...]
        mine = all_ids.at[z, x, y, c]
        here.send(mine, mine, id_sems.at[0, 0], id_sems.at[0, 1], here.at(dc=1))
        here.expect(all_ids.at[z, x, y, 1 - c], id_sems.at[0, 1])
        pair = all_ids.at[z, x, y]
        here.send(pair, pair, id_sems.at[1, 0], id_sems.at[1, 1], here.at(dx=1))
        here.expect(all_ids.at[z, 1 - x, y], id_sems.at[1, 1])
        four = all_ids.at[z, :, y]
        here.send(four, four, id_sems.at[2, 0], id_sems.at[2, 1], here.at(dy=1))
        here.expect(all_ids.at[z, :, 1 - y], id_sems.at[2, 1])
        plane = all_ids.at[z]
        for j in range(1, n):
            here.send(plane, plane, id_sems.at[2 + j, 0], id_sems.at[2 + j, 1], here.at(dz=j))
        for j in range(1, n):
            here.expect(all_ids.at[lax.rem(z + n - j, n)], id_sems.at[2 + j, 1])

    def list_rows():
        lines, lanes = ids.shape
        sources = n * 8
        total = sources * lines
        rows_dev = table.shape[0]
        local = all_ids[...].reshape(total, lanes) - ((z * 2 + x) * 4 + y * 2 + c) * rows_dev
        inside = (local >= 0) & (local < rows_dev)
        flags = jnp.where(inside, 1.0, 0.0).astype(jnp.bfloat16)
        row = lax.broadcasted_iota(jnp.int32, (lanes, lanes), 0)
        col = lax.broadcasted_iota(jnp.int32, (lanes, lanes), 1)
        place = matmul(flags, jnp.where(row < col, 1.0, 0.0).astype(jnp.bfloat16))
        held = matmul(flags, jnp.ones((lanes, lanes), jnp.bfloat16)).astype(jnp.bfloat16)
        row = lax.broadcasted_iota(jnp.int32, (total, total), 0)
        col = lax.broadcasted_iota(jnp.int32, (total, total), 1)
        before = (row // lines == col // lines) & (col < row)
        place = place + matmul(jnp.where(before, 1.0, 0.0).astype(jnp.bfloat16), held)
        places[...] = jnp.where(inside, place.astype(jnp.int32), -1)
        line = lax.broadcasted_iota(jnp.int32, (total, lanes), 0)
        lane = lax.broadcasted_iota(jnp.int32, (total, lanes), 1)
        index = lax.rem(line, lines) * lanes + lane
        entries[...] = local * 256 + index // gram_count + 1
        slot = lax.broadcasted_iota(jnp.int32, (SLOTS, lanes), 0)

        def source(s, carry):
            span = pl.ds(pl.multiple_of(s * lines, lines), lines)
            where, what = places[span], entries[span]
            found = jnp.zeros((SLOTS, lanes), jnp.int32)
            for line in range(used_lines):
                hit = where[line : line + 1] == slot
                found = found + jnp.where(hit, what[line : line + 1], 0)
            lists[s] = jnp.sum(found, axis=1, keepdims=True) - 1
            return carry

        lax.fori_loop(0, sources, source, 0)

    row_iota = lax.broadcasted_iota(jnp.int32, (4 * SLOTS, table.shape[0]), 1)
    byte_iota = lax.broadcasted_iota(jnp.int32, (SLOTS, tokens), 1)

    def partial_sums(plane, core, write):
        asked = [lists[plane * 8 + place * 2 + core] for place in range(4)]
        rows = jnp.right_shift(jnp.concatenate(asked, axis=0), 8)
        pick = (rows == row_iota).astype(jnp.bfloat16)
        g_rows[...] = matmul(pick, table[...]).astype(jnp.bfloat16)
        for place in range(4):
            source = plane * 8 + place * 2 + core
            entry = lists[source]
            to_byte = (jnp.bitwise_and(entry, 255) == byte_iota).astype(jnp.bfloat16)
            sums = t_times(to_byte, g_rows[place * SLOTS : (place + 1) * SLOTS, :])
            write(place, sums)

    units = []
    for u in range(n):
        units.append(
            Reduction(
                here,
                p0.at[pl.ds(u, 1)],
                r1a.at[pl.ds(u, 1)],
                r1b.at[pl.ds(u, 1)],
                r2a.at[pl.ds(u, 1)],
                r2b.at[pl.ds(u, 1)],
                stage_sems,
                u,
            )
        )
    core_copies = [None] * n
    z_copies = [None] * n

    def plane_of(u):
        return lax.rem(z + u + 1, n)

    def hash_a(u):
        slot = u % 2
        if u >= 2:
            here.sent(core_copies[u - 2])

        def write(place, sums):
            send0[slot, place // 2, place % 2] = sums.astype(jnp.bfloat16)

        partial_sums(plane_of(u), 1 - c, write)
        core_copies[u] = here.send(
            send0.at[slot], p0.at[u], core_sems.at[u, 0], core_sems.at[u, 1], here.at(dc=1)
        )

    def hash_b(u):
        core_copies[u].wait_recv()

        def write(place, sums):
            total = sums + p0[u, place // 2, place % 2].astype(jnp.float32)
            p0[u, place // 2, place % 2] = total.astype(jnp.bfloat16)

        partial_sums(plane_of(u), c, write)
        units[u].first()

    def hash_c(u):
        units[u].second()

    def hash_d(u):
        mine = units[u].third()
        if u < n - 1:
            z_copies[u] = here.send(
                mine.at[0], r3.at[u], z_sems.at[u, 0], z_sems.at[u, 1], here.at(dz=u + 1)
            )

    def hash_e():
        for u in range(n - 1):
            z_copies[u].wait_recv()
        total = p0[n - 1, x, y].astype(jnp.float32)
        for u in range(n - 1):
            total = total + r3[u].astype(jnp.float32)
        embedded[...] = total
        for copy in core_copies[-2:] + z_copies[:-1]:
            here.sent(copy)
        for unit in units:
            for copy in (unit.s1a, unit.s1b, unit.s2a, unit.s2b):
                here.sent(copy)

    here.greet()
    lag1, lag2, lag3 = GATHER_LAGS
    for t in range(n - 1):
        each(t, Weight.along_z)
        for k in range(1, n - 1):
            if k <= t:
                each(t - k, lambda w, k=k: w.onward(k))
    gather_ids()
    list_rows()
    hash_steps = []
    for t in range(n + 3):
        group = []
        for u, stage in ((t, hash_a), (t - 1, hash_b), (t - 2, hash_c), (t - 3, hash_d)):
            if 0 <= u < n:
                group.append(lambda u=u, stage=stage: stage(u))
        hash_steps.append(group)
    hash_steps.append([hash_e])
    layer = forward_steps(
        here,
        fulls,
        embedded,
        extra_in,
        extra_out,
        [p0.at[u] for u in range(n)] + [send0.at[u] for u in range(2)],
        extra_scratch,
    )
    gather_done, runs = set(), iter(layer)
    for what, number in SCHEDULE:
        if what == HASH:
            for run in hash_steps[number]:
                run()
        elif what == GATHER:
            each(number + n - 1, Weight.along_z)
            for k in range(1, n - 1):
                each(number + n - 1 - k, lambda w, k=k: w.onward(k))
            each(number, Weight.near)
            each(number - lag1, Weight.far)
            each(number - lag1, Weight.local)
            each(number - lag2, Weight.across)
            each(number - lag3, Weight.done)
            if 0 <= number - lag3 < len(steps_of):
                gather_done |= {i for i, _, _ in steps_of[number - lag3]}
        else:
            for _ in range(number):
                needs, run = next(runs)
                assert gather_done.issuperset(needs)
                run()
    assert next(runs, None) is None
    here.finish()


def fetch(hash_ids, table, shards, extra, steps_of, dp_count):
    width = table.shape[1]
    tokens, gram_count = hash_ids.shape
    count = len(shards)
    hbm = pl.BlockSpec(memory_space=pl.ANY)
    vmem = pl.BlockSpec(memory_space=pltpu.VMEM)
    n, half = dp_count, width // 2
    low = jnp.bfloat16
    dma = pltpu.SemaphoreType.DMA
    used_lines = tokens * gram_count // 128
    lines = -(-used_lines // 8) * 8
    ids = hash_ids.reshape(used_lines, 128)
    ids = jnp.concatenate([ids, jnp.full((lines - used_lines, 128), -1, jnp.int32)])
    gathers = 2 * len(steps_of)
    ff = shards[4].shape[1]
    extra_out = list(kept_shapes(tokens, width, ff, extra[3].shape[0]))
    out_places = Kept(*[vmem] * len(extra_out))
    out_places = list(out_places._replace(gate_pre=hbm, up_pre=hbm, key_values=hbm))
    results = pl.pallas_call(
        functools.partial(fetch_kernel, n, count, steps_of, tokens, gram_count, used_lines),
        out_shape=[jax.ShapeDtypeStruct((n * w.shape[0], w.shape[1]), w.dtype) for w in shards]
        + [
            jax.ShapeDtypeStruct((tokens, width), jnp.float32),
            jax.ShapeDtypeStruct((n * 8, SLOTS, 1), jnp.int32),
        ]
        + extra_out,
        in_specs=[hbm] * count + [vmem, vmem] + [vmem] * len(extra),
        out_specs=[hbm] * count + [vmem, vmem] + out_places,
        scratch_shapes=[
            pltpu.VMEM((n, 2, 2, 2, lines, 128), jnp.int32),
            pltpu.VMEM((2, 2, 2, tokens, width), low),
            pltpu.VMEM((n, 2, 2, tokens, width), low),
            pltpu.VMEM((n, 2, tokens, half), low),
            pltpu.VMEM((n, 2, tokens, half), low),
            pltpu.VMEM((n, tokens, half), low),
            pltpu.VMEM((n, tokens, half), low),
            pltpu.VMEM((n - 1, tokens, width), low),
            pltpu.VMEM((4 * SLOTS, width), low),
            dma((n, 2)),
            dma((n, 4, 2)),
            dma((n - 1, 2)),
            dma((gathers, 2)),
            dma((gathers, 4, n - 1)),
            dma((gathers, 4, n - 1)),
            dma((gathers, 2, n - 1)),
            dma((2 + n, 2)),
            pltpu.VMEM((n * 8 * lines, 128), jnp.int32),
            pltpu.VMEM((n * 8 * lines, 128), jnp.int32),
            pltpu.VMEM((n * shards[4].shape[0], ff), low),
            pltpu.VMEM((n * shards[5].shape[0], ff), low),
            pltpu.VMEM((2, tokens, width), low),
            dma((count, max(n, ff // 256))),
            dma((2, 2)),
            pltpu.VMEM((tokens, ff), F32),
            pltpu.VMEM((tokens, ff), F32),
            pltpu.VMEM((2, 3 * tokens, width), low),
            dma((3,)),
        ],
        compiler_params=pltpu.CompilerParams(
            collective_id=0, has_side_effects=True, vmem_limit_bytes=VMEM_CAP
        ),
        name="fetch",
    )(*shards, ids, table, *extra)
    return results[:count], results[count], results[count + 1], Kept(*results[count + 2 :])


LAGS = (2, 3, 5)


class GradSums:
    def __init__(self, here, units, lefts_in, rights_in, outs, take, pool_count):
        count = len(units)
        self.here, self.units = here, units
        self.lefts_in, self.rights_in, self.outs = lefts_in, rights_in, outs
        self.lefts, self.rights = take(len(lefts_in)), take(len(rights_in))
        self.pools = take(pool_count)
        self.r1a, self.r1b, self.r2a, self.r2b, self.r3 = (take(count) for _ in range(5))
        self.left_sems, self.right_sems, self.stage_sems, self.z_sems = take(4)
        self.left_copies, self.right_copies = {}, {}
        self.sums = [None] * count
        self.using = {}
        self.mine_of = [None] * count
        self.sent_of = [None] * count

    def bring(self, source, target, sems, i, split):
        here = self.here
        copies = []
        theirs = target.at[0]
        if source is not None:
            mine = theirs = source
            if split:
                rows = target.shape[2]
                apart = source.shape[1] - rows
                mine = source.at[:, pl.ds(pl.multiple_of(here.c * apart, 16), rows)]
                theirs = source.at[:, pl.ds(pl.multiple_of((1 - here.c) * apart, 16), rows)]
            local = pltpu.make_async_copy(mine, target.at[0], sems.at[i, 0])
            local.start()
            copies.append(local.wait)
        remote = here.send(theirs, target.at[1], sems.at[i, 1], sems.at[i, 2], here.at(dc=1))
        copies.append(remote.wait_recv)
        return copies

    def left(self, i):
        if i not in self.left_copies:
            self.left_copies[i] = self.bring(
                self.lefts_in[i], self.lefts[i], self.left_sems, i, True
            )

    def right(self, i):
        if i not in self.right_copies:
            self.right_copies[i] = self.bring(
                self.rights_in[i], self.rights[i], self.right_sems, i, False
            )

    def need(self, i):
        self.left(self.units[i][0])
        self.right(self.units[i][1])

    def product(self, i):
        here, n = self.here, self.here.n
        left, right, pool, slot = self.units[i]
        self.need(i)
        for copies in (self.left_copies[left], self.right_copies[right]):
            for wait in copies:
                wait()
            copies.clear()
        for copy in self.using.get((pool, slot), []):
            here.sent(copy)
        p0 = self.pools[pool].at[slot]
        xt, g = self.lefts[left], self.rights[right]
        k, depth = xt.shape[2], xt.shape[3]
        cols = g.shape[2]
        chunks = 1 if k <= 32 else n
        planes = n // chunks
        tile = 256

        def columns(t, carry):
            span = pl.ds(pl.multiple_of(t * tile, tile), tile)
            for chunk in range(chunks):
                total = None
                for who in range(2):
                    rows = xt[who, chunk * planes * 4 : (chunk + 1) * planes * 4]
                    part = matmul(rows.reshape(planes * 4 * k, depth), g[who, :, span])
                    total = part if total is None else total + part
                p0[chunk * planes : (chunk + 1) * planes, :, :, :, span] = total.astype(
                    jnp.bfloat16
                ).reshape(planes, 2, 2, k, tile)
            return carry

        lax.fori_loop(0, cols // tile, columns, 0)
        unit = Reduction(
            here, p0, self.r1a[i], self.r1b[i], self.r2a[i], self.r2b[i], self.stage_sems, i
        )
        unit.first()
        self.sums[i] = unit
        self.using[(pool, slot)] = [unit.s1a, unit.s1b]

    def second(self, i):
        self.sums[i].second()
        self.using[self.units[i][2:]] += [self.sums[i].s2a, self.sums[i].s2b]

    def third(self, i):
        here, n = self.here, self.here.n
        mine = self.sums[i].third()
        self.sent_of[i] = []
        for j in range(1, n):
            self.sent_of[i].append(
                here.send(
                    mine.at[lax.rem(here.z + j, n)],
                    self.r3[i].at[j - 1],
                    self.z_sems.at[i, j - 1, 0],
                    self.z_sems.at[i, j - 1, 1],
                    here.at(dz=j),
                )
            )
        self.using[self.units[i][2:]] += self.sent_of[i]
        self.mine_of[i] = mine

    def final(self, i):
        total = self.mine_of[i][self.here.z].astype(jnp.float32)
        for j in range(1, self.here.n):
            self.sent_of[i][j - 1].wait_recv()
            total = total + self.r3[i][j - 1].astype(jnp.float32)
        self.outs[i][...] = total

    def move(self, t, lags):
        lag2, lag3, lag4 = lags
        count = len(self.units)
        if 0 <= t - lag2 < count:
            self.second(t - lag2)
        if 0 <= t - lag3 < count:
            self.third(t - lag3)
        if 0 <= t - lag4 < count:
            self.final(t - lag4)


def left_shape(a):
    pairs, both, depth = a.shape
    return (2, pairs, -(-(both // 2) // 16) * 16, depth)


def plan_sums(pairs, left_shapes, right_shapes, n, most):
    low = jnp.bfloat16
    dma = pltpu.SemaphoreType.DMA
    shapes, units, seen = [], [], {}
    for left, right in pairs:
        shape = (left_shapes[left][2], right_shapes[right][1])
        seen[shape] = seen.get(shape, 0) + 1
        shapes.append(shape)
    classes = list(seen)
    slots = [min(seen[s], most) for s in classes]
    used = {s: 0 for s in classes}
    for (left, right), shape in zip(pairs, shapes):
        pool = classes.index(shape)
        units.append((left, right, pool, used[shape] % slots[pool]))
        used[shape] += 1
    count = len(pairs)
    scratch = [pltpu.VMEM(shape, low) for shape in left_shapes]
    scratch += [pltpu.VMEM((2, *shape), low) for shape in right_shapes]
    scratch += [pltpu.VMEM((s, n, 2, 2, *shape), low) for s, shape in zip(slots, classes)]
    halves = [(k, cols // 2) for k, cols in shapes]
    for _ in range(2):
        scratch += [pltpu.VMEM((n, 2, *half), low) for half in halves]
    for _ in range(2):
        scratch += [pltpu.VMEM((n, *half), low) for half in halves]
    scratch += [pltpu.VMEM((n - 1, *shape), low) for shape in shapes]
    scratch += [
        dma((len(left_shapes), 3)),
        dma((len(right_shapes), 3)),
        dma((count, 4, 2)),
        dma((count, n - 1, 2)),
    ]
    return units, shapes, scratch, len(classes)


def taker(refs):
    refs = list(refs)

    def take(number):
        taken = refs[:number]
        del refs[:number]
        return taken

    return take


def last_kernel(dp_count, units, left_count, right_count, pool_count, *refs):
    n = dp_count
    count = len(units)
    take = taker(refs)
    lefts_in, rights_in = take(left_count), take(right_count)
    embed_in, gains_in, lists, rows_of = take(4)
    outs = take(count)
    gains_out, table_grad, counts, stacked_last, rows_last = take(5)
    here = Place(n)
    sums = GradSums(here, units, lefts_in, rights_in, outs, take, pool_count)
    gathered, stacked = take(2)
    gain_send, gain_recv, gain_sems, own_sem, near_sems, plane_sems = take(6)
    z, x, y, c = here.z, here.x, here.y, here.c

    here.greet()

    own = pltpu.make_async_copy(embed_in, gathered.at[z, x, y, c], own_sem)
    own.start()
    for j in range(1, n):
        here.send(
            embed_in,
            gathered.at[z, x, y, c],
            plane_sems.at[j - 1, 0],
            plane_sems.at[j - 1, 1],
            here.at(dz=j),
        )
    width = embed_in.shape[1]
    left_half, right_half = pl.ds(0, width // 2), pl.ds(width // 2, width // 2)

    def embed_near(j):
        plane = lax.rem(z + n - j, n)
        if j:
            here.expect(gathered.at[plane, x, y, c], plane_sems.at[j - 1, 1])
        else:
            own.wait()
        a = gathered.at[plane, x, y, c, :, left_half]
        b = gathered.at[plane, x, y, c, :, right_half]
        here.send(a, a, near_sems.at[j, 0, 0], near_sems.at[j, 0, 1], here.at(dx=1))
        here.send(b, b, near_sems.at[j, 1, 0], near_sems.at[j, 1, 1], here.at(dy=1))

    def embed_far(j):
        plane = lax.rem(z + n - j, n)
        here.expect(gathered.at[plane, 1 - x, y, c, :, left_half], near_sems.at[j, 0, 1])
        here.expect(gathered.at[plane, x, 1 - y, c, :, right_half], near_sems.at[j, 1, 1])
        a = gathered.at[plane, :, y, c, :, left_half]
        b = gathered.at[plane, x, :, c, :, right_half]
        here.send(a, a, near_sems.at[j, 2, 0], near_sems.at[j, 2, 1], here.at(dy=1))
        here.send(b, b, near_sems.at[j, 3, 0], near_sems.at[j, 3, 1], here.at(dx=1))

    def embed_across(j):
        plane = lax.rem(z + n - j, n)
        here.expect(gathered.at[plane, :, 1 - y, c, :, left_half], near_sems.at[j, 2, 1])
        here.expect(gathered.at[plane, 1 - x, :, c, :, right_half], near_sems.at[j, 3, 1])
        a = gathered.at[plane, :, :, c]
        here.send(a, a, near_sems.at[j, 4, 0], near_sems.at[j, 4, 1], here.at(dc=1))

    def spread(j):
        plane = lax.rem(z + n - j, n)
        here.expect(gathered.at[plane, :, :, 1 - c], near_sems.at[j, 4, 1])
        byte_iota = lax.broadcasted_iota(jnp.int32, (SLOTS, embed_in.shape[0]), 1)
        for s in range(8):
            asked = jnp.bitwise_and(lists[plane * 8 + s], 255)
            pick = (asked == byte_iota).astype(jnp.bfloat16)
            grads = gathered[plane, s // 4, s // 2 % 2, s % 2]
            target = stacked_last if j == n - 1 else stacked
            target[s * SLOTS : (s + 1) * SLOTS, :] = matmul(pick, grads).astype(jnp.bfloat16)
        if j == n - 1:
            rows_last[...] = rows_of[plane]
            return
        row_iota = lax.broadcasted_iota(jnp.int32, (table_grad.shape[0], 8 * SLOTS), 0)
        onto = (rows_of[plane] == row_iota).astype(jnp.float32)
        uses = jnp.sum(onto, axis=1, keepdims=True)
        added = matmul(onto.astype(jnp.bfloat16), stacked[...])
        if j == 0:
            counts[...] = uses
            table_grad[...] = added
        else:
            counts[...] += uses
            table_grad[...] += added

    def gains(stage):
        if stage == 0:
            gain_send[0] = gains_in[...]
        elif stage <= 3:
            here.expect(gain_recv.at[stage - 1], gain_sems.at[stage - 1, 1])
            gain_send[stage] = gain_send[stage - 1] + gain_recv[stage - 1]
        if stage < 3:
            peer = (here.at(dc=1), here.at(dx=1), here.at(dy=1))[stage]
            here.send(
                gain_send.at[stage],
                gain_recv.at[stage],
                gain_sems.at[stage, 0],
                gain_sems.at[stage, 1],
                peer,
            )
        elif stage == 3:
            for j in range(1, n):
                here.send(
                    gain_send.at[3],
                    gain_recv.at[2 + j],
                    gain_sems.at[2 + j, 0],
                    gain_sems.at[2 + j, 1],
                    here.at(dz=j),
                )
        else:
            total = gain_send[3]
            for j in range(1, n):
                here.expect(gain_recv.at[2 + j], gain_sems.at[2 + j, 1])
                total = total + gain_recv[2 + j]
            gains_out[...] = total

    for i in range(count):
        sums.need(i)
    for t in range(max(count + LAGS[2], n + 5)):
        if t < count:
            sums.product(t)
        if t == 0:
            embed_near(0)
        if 0 <= t - 1 < 5:
            gains(t - 1)
        if 1 <= t - 2 < n:
            embed_near(t - 2)
        sums.move(t, LAGS)
        if 0 <= t - 3 < n:
            embed_far(t - 3)
        if 0 <= t - 4 < n:
            embed_across(t - 4)
        if 0 <= t - 5 < n:
            spread(t - 5)
    here.finish()


def last_sums(pairs, lefts, rights, embed_low, gains, entries, rows_dev, dp_count):
    n = dp_count
    low = jnp.bfloat16
    dma = pltpu.SemaphoreType.DMA
    hbm = pl.BlockSpec(memory_space=pl.ANY)
    vmem = pl.BlockSpec(memory_space=pltpu.VMEM)
    units, shapes, scratch, pool_count = plan_sums(
        pairs, [left_shape(a) for a in lefts], [a.shape for a in rights], n, 6
    )
    count = len(pairs)
    tokens, width = embed_low.shape
    rows_of = jnp.right_shift(entries, 8).reshape(n, 1, 8 * SLOTS)
    scratch += [
        pltpu.VMEM((n, 2, 2, 2, tokens, width), low),
        pltpu.VMEM((8 * SLOTS, width), low),
        pltpu.VMEM((4, 8, width), jnp.float32),
        pltpu.VMEM((2 + n, 8, width), jnp.float32),
        dma((2 + n, 2)),
        dma,
        dma((n, 5, 2)),
        dma((n - 1, 2)),
    ]
    results = pl.pallas_call(
        functools.partial(last_kernel, n, units, len(lefts), len(rights), pool_count),
        out_shape=[jax.ShapeDtypeStruct(shape, jnp.float32) for shape in shapes]
        + [
            jax.ShapeDtypeStruct((8, width), jnp.float32),
            jax.ShapeDtypeStruct((rows_dev, width), jnp.float32),
            jax.ShapeDtypeStruct((rows_dev, 1), jnp.float32),
            jax.ShapeDtypeStruct((8 * SLOTS, width), low),
            jax.ShapeDtypeStruct((1, 8 * SLOTS), jnp.int32),
        ],
        in_specs=[hbm] * (len(lefts) + len(rights)) + [vmem] * 4,
        out_specs=[vmem] * (count + 5),
        scratch_shapes=scratch,
        compiler_params=pltpu.CompilerParams(
            collective_id=2, has_side_effects=True, vmem_limit_bytes=VMEM_CAP
        ),
        name="last_sums",
    )(*lefts, *rights, embed_low, gains, entries, rows_of)
    return results[:count], *results[count:]


BACK_PAIRS = ((4, 8), (3, 6), (3, 7), (2, 5), (1, 4), (0, 0), (0, 1), (0, 2), (0, 3))


class Streamed(typing.NamedTuple):
    gate_pre: typing.Any
    up_pre: typing.Any
    h_out: typing.Any
    h_mid: typing.Any
    embedded: typing.Any
    key_values: typing.Any
    w_query: typing.Any
    w_key: typing.Any
    w_value: typing.Any
    w_out: typing.Any
    w_gate: typing.Any
    w_up: typing.Any
    w_down: typing.Any
    c_query: typing.Any
    c_key: typing.Any
    c_value: typing.Any
    c_out: typing.Any
    cot_patches: typing.Any


def back_kernel(dp_count, units, pool_count, *refs):
    n = dp_count
    take = taker(refs)
    lefts_in = take(5)
    hbm = Streamed(*take(len(Streamed._fields)))
    (cot_bytes, p_query, p_key, p_value, cross_lse, gains, starts, ends, queries, lse) = take(10)
    outs = take(len(units))
    grad_gains, g_attn, g_query, g_key, g_value, g_embed = take(6)
    here = Place(n)
    sums = GradSums(here, units, lefts_in, [None] * 8 + [hbm.cot_patches], outs, take, pool_count)
    w, tile_pre, grad_out, grad_ffn, grad_mid, kv, halo = take(7)
    w_sems, tile_sems, pre_sems, kv_sems, halo_sems = take(5)
    g_gate = [sums.rights[0].at[0], sums.rights[2].at[0]]
    g_up = [sums.rights[1].at[0], sums.rights[3].at[0]]
    g_branch, g_pquery, g_pkey, g_pvalue, cot_patches = [ref.at[0] for ref in sums.rights[4:]]
    tokens, width = cot_bytes.shape
    patches = p_query.shape[0]
    tile = 256
    first_tiles = g_gate[0].shape[1] // tile
    tiles = first_tiles + g_gate[1].shape[1] // tile
    rank = (here.x * 2 + here.y) * 2 + here.c
    lane = lax.broadcasted_iota(jnp.int32, (1, 128), 1)
    sides = [jnp.where(lane < HD, 1.0, 0.0).astype(LOW), jnp.where(lane < HD, 0.0, 1.0).astype(LOW)]
    byte_pos = lax.broadcasted_iota(jnp.int32, (patches, tokens), 1)

    here.greet()

    def load_w(slot, source):
        copy = pltpu.make_async_copy(source, w.at[slot], w_sems.at[slot])
        copy.start()
        return copy

    def load_pre(source):
        copies = []
        for b in range(width // tile):
            copy = pltpu.make_async_copy(
                source.at[:, pl.ds(b * tile, tile)],
                tile_pre.at[b // 2, b % 2],
                pre_sems.at[b],
            )
            copy.start()
            copies.append(copy)
        return copies

    def pre_rows(copies):
        for copy in copies:
            copy.wait()
        return jnp.concatenate([tile_pre[b // 2, b % 2] for b in range(width // tile)], axis=1)

    for i in (4, 3, 2, 1, 0):
        sums.left(i)
    sums.right(8)
    cross = [load_w(i, a) for i, a in enumerate((hbm.c_out, hbm.c_query, hbm.c_key, hbm.c_value))]
    h_out_copies = load_pre(hbm.h_out)

    def tile_copies(t):
        slot = lax.rem(t, 2)
        span = pl.ds(pl.multiple_of(t * tile, tile), tile)
        return [
            pltpu.make_async_copy(source, target, tile_sems.at[slot, k])
            for k, (source, target) in enumerate(
                (
                    (hbm.w_gate.at[:, span], w.at[slot, :, pl.ds(0, tile)]),
                    (hbm.w_up.at[:, span], w.at[slot, :, pl.ds(tile, tile)]),
                    (hbm.w_down.at[span], w.at[2, pl.ds(pl.multiple_of(slot * tile, tile), tile)]),
                    (hbm.gate_pre.at[:, span], tile_pre.at[slot, 0]),
                    (hbm.up_pre.at[:, span], tile_pre.at[slot, 1]),
                )
            )
        ]

    def member():
        return (byte_pos >= starts[...]) & (byte_pos < ends[...])

    def head_lse(ref, head):
        return jnp.sum(jnp.where(lane == head, ref[...], 0.0), axis=1, keepdims=True)

    def cross_heads():
        cross[0].wait()
        allowed = member()
        grad_ffn[:patches] = times_t(cot_patches[...], w[0]).astype(LOW).astype(F32)

        def heads_pair(pair, carry):
            span = pl.ds(pl.multiple_of(pair * 128, 128), 128)
            q2, k2, v2 = p_query[:, span], p_key[:, span], p_value[:, span]
            gp2 = grad_ffn[:patches, span].astype(LOW)
            parts = []
            for side in range(2):
                total = head_lse(cross_lse, pair * 2 + side)
                scores = times_t(q2 * sides[side], k2) * SCORE_SCALE
                probs = jnp.where(allowed, jnp.exp(jnp.where(allowed, scores, total) - total), 0.0)
                grad_score = soft_back(probs, times_t(gp2 * sides[side], v2))
                parts.append(
                    (
                        matmul(grad_score, k2),
                        t_times(grad_score, q2),
                        t_times(probs.astype(LOW), gp2),
                    )
                )
            mine = lane < HD
            g_pquery[:, span] = (jnp.where(mine, parts[0][0], parts[1][0]) * SCORE_SCALE).astype(LOW)
            g_pkey[:, span] = (jnp.where(mine, parts[0][1], parts[1][1]) * SCORE_SCALE).astype(LOW)
            g_pvalue[:, span] = jnp.where(mine, parts[0][2], parts[1][2]).astype(LOW)
            return carry

        lax.fori_loop(0, width // 128, heads_pair, 0)
        for i in (5, 6, 7):
            sums.right(i)

    def split(v):
        high = v.astype(LOW)
        return high, (v - high.astype(F32)).astype(LOW)

    def unit_of(v):
        inv_rms = lax.rsqrt(jnp.mean(v * v, axis=-1, keepdims=True) + EPSILON)
        return v * inv_rms, inv_rms

    def through_norm(grad, rows, number):
        normed, inv_rms = unit_of(rows)
        grad_in, grad_gain = norm_back(
            grad.astype(LOW).astype(F32), normed, inv_rms, gains[number : number + 1]
        )
        grad_gains[number : number + 1] = grad_gain[None]
        return grad_in

    loaded = {}

    def cross_in():
        for copy in cross[1:]:
            copy.wait()
        length = (ends[...] - starts[...]).astype(F32)
        grad_pooled = cot_patches[...].astype(F32) + times_t(g_pquery[...], w[1]).astype(
            LOW
        ).astype(F32)
        high, rest = split(grad_pooled / length)
        inside = jnp.where(member(), 1.0, 0.0).astype(LOW)
        grad_x = t_times(inside, high) + t_times(inside, rest)
        grad_x = grad_x + times_t(g_pkey[...], w[2]) + times_t(g_pvalue[...], w[3])
        grad_gains[...] = jnp.zeros_like(grad_gains)
        total = cot_bytes[...].astype(F32) + through_norm(grad_x, pre_rows(h_out_copies), 2)
        grad_out[...] = total
        g_branch[...] = total.astype(LOW)
        grad_ffn[...] = jnp.zeros_like(grad_ffn)
        sums.right(4)
        loaded[3] = load_w(3, hbm.w_out)

    def feed(part):
        first, last = ((0, first_tiles), (first_tiles, tiles))[part]
        for copy in tile_copies(first):
            copy.start()

        def one(t, carry):
            slot = lax.rem(t, 2)
            for copy in tile_copies(t):
                copy.wait()

            @pl.when(t + 1 < last)
            def _():
                for copy in tile_copies(t + 1):
                    copy.start()

            span = pl.ds(pl.multiple_of((t - first) * tile, tile), tile)
            down_rows = w[2, pl.ds(pl.multiple_of(slot * tile, tile), tile)]
            grad_hidden = times_t(g_branch[...], down_rows).astype(LOW).astype(F32)
            gate, up = tile_pre[slot, 0], tile_pre[slot, 1]
            sig = jax.nn.sigmoid(gate)
            gg = (grad_hidden * up * sig * (1.0 + gate * (1.0 - sig))).astype(LOW)
            gu = (grad_hidden * (gate * sig)).astype(LOW)
            g_gate[part][:, span] = gg
            g_up[part][:, span] = gu
            grad_ffn[...] += times_t(gg, w[slot, :, :tile]) + times_t(
                gu, w[slot, :, tile : 2 * tile]
            )
            return carry

        lax.fori_loop(first, last, one, 0)
        sums.right(2 * part)
        sums.right(2 * part + 1)

    def feed_in():
        copies = load_pre(hbm.h_mid)
        loaded[3].wait()
        grad_mid[...] = grad_out[...] + through_norm(grad_ffn[...], pre_rows(copies), 1)
        g_attn[...] = grad_mid[...].astype(LOW)
        g_query[...] = times_t(g_attn[...], w[3]).astype(LOW)
        loaded[1] = load_w(1, hbm.w_query)
        loaded[2] = load_w(2, hbm.w_key)
        loaded[3] = load_w(3, hbm.w_value)
        loaded[0] = load_pre(hbm.embedded)

    own_key, own_value = grad_ffn, grad_out
    sent = w.at[0]

    def kv_copy(pair):
        slot = lax.rem(pair, 2)
        span = pl.ds(pl.multiple_of(pair * 128, 128), 128)
        return pltpu.make_async_copy(hbm.key_values.at[:, :, span], kv.at[slot], kv_sems.at[slot])

    def attend(first, last):
        row = lax.broadcasted_iota(jnp.int32, (tokens, tokens), 0)
        col = lax.broadcasted_iota(jnp.int32, (tokens, tokens), 1)
        mine = col <= row
        far_bias = jnp.where(rank >= 2, 0.0, NEG_BIG)
        near_bias = jnp.where(rank >= 1, 0.0, NEG_BIG)
        kv_copy(first).start()

        def three(edge, middle):
            return jnp.concatenate(
                [
                    jnp.where(mine, 0.0, edge).astype(LOW),
                    middle.astype(LOW),
                    jnp.where(mine, edge, 0.0).astype(LOW),
                ],
                axis=1,
            )

        def heads_pair(pair, carry):
            kv_copy(pair).wait()

            @pl.when(pair + 1 < last)
            def _():
                kv_copy(pair + 1).start()

            slot = lax.rem(pair, 2)
            span = pl.ds(pl.multiple_of(pair * 128, 128), 128)
            q2, ga2 = queries[:, span], g_query[:, span]
            k2, v2 = kv[slot, 0], kv[slot, 1]
            parts = []
            for side in range(2):
                total = head_lse(lse, pair * 2 + side)
                scores = times_t(q2 * sides[side], k2) * SCORE_SCALE
                edge = jnp.where(mine, scores[:, 2 * tokens :], scores[:, :tokens] + far_bias)
                edge = jnp.exp(edge - total)
                middle = jnp.exp(scores[:, tokens : 2 * tokens] + near_bias - total)
                grad_prob = times_t(ga2 * sides[side], v2)
                grad_edge = jnp.where(mine, grad_prob[:, 2 * tokens :], grad_prob[:, :tokens])
                grad_middle = grad_prob[:, tokens : 2 * tokens]
                row_total = jnp.sum(edge * grad_edge, axis=1, keepdims=True) + jnp.sum(
                    middle * grad_middle, axis=1, keepdims=True
                )
                grad_score = three(edge * (grad_edge - row_total), middle * (grad_middle - row_total))
                parts.append(
                    (
                        matmul(grad_score, k2),
                        t_times(grad_score, q2),
                        t_times(three(edge, middle), ga2),
                    )
                )
            left = lane < HD
            g_query[:, span] = (jnp.where(left, parts[0][0], parts[1][0]) * SCORE_SCALE).astype(LOW)
            for number, own, scale in ((1, own_key, SCORE_SCALE), (2, own_value, 1.0)):
                grad = jnp.where(left, parts[0][number], parts[1][number]) * scale
                own[:, span] = grad[2 * tokens :]
                start = (number - 1) * 2 * tokens
                sent[start : start + 2 * tokens, span] = grad[: 2 * tokens].astype(LOW)
            return carry

        lax.fori_loop(first, last, heads_pair, 0)

    there = rank >= 2

    def part_of(number, back, span):
        return sent.at[pl.ds((2 * number + 2 - back) * tokens, tokens), span]

    def halo_parts(half):
        span = pl.ds(half * (width // 2), width // 2)
        return [(number, span, 2 * number + half) for number in range(2)]

    def halo_pair(half):
        for number, span, sem in halo_parts(half):
            here.send_if(
                there | (here.c == 1),
                part_of(number, 1, span),
                halo.at[1, number, :, span],
                halo_sems.at[1, sem, 0],
                halo_sems.at[1, sem, 1],
                here.at(dc=1),
            )

    def halo_send(half):
        for number, span, sem in halo_parts(half):

            @pl.when(there | (here.c == 0))
            def _():
                here.expect(halo.at[1, number, :, span], halo_sems.at[1, sem, 1])

            part = part_of(number, 2, span)

            @pl.when(there & (here.c == 1))
            def _():
                added = part[...].astype(F32) + halo[1, number, :, span].astype(F32)
                part[...] = added.astype(LOW)

            target = jnp.maximum(rank - 2, 0)
            here.send_if(
                there,
                part,
                halo.at[0, number, :, span],
                halo_sems.at[0, sem, 0],
                halo_sems.at[0, sem, 1],
                (here.z, target // 4, lax.rem(target, 4)),
            )

    def halo_add():
        for number, own, grad in ((0, own_key, g_key), (1, own_value, g_value)):

            @pl.when(here.c == 0)
            def _():
                own[...] += halo[1, number].astype(F32)

            @pl.when(rank + 2 < 8)
            def _():
                for half in range(2):
                    _, span, sem = halo_parts(half)[number]
                    here.expect(halo.at[0, number, :, span], halo_sems.at[0, sem, 1])
                own[...] += halo[0, number].astype(F32)

            grad[...] = own[...].astype(LOW)

    def embed_in():
        for slot in (1, 2, 3):
            loaded[slot].wait()
        grad = times_t(g_query[...], w[1]) + times_t(g_key[...], w[2]) + times_t(g_value[...], w[3])
        total = grad_mid[...] + through_norm(grad, pre_rows(loaded[0]), 0)
        g_embed[...] = total.astype(LOW)

    sums.product(0)
    cross_heads()
    sums.product(1)
    sums.product(2)
    sums.product(3)
    cross_in()
    sums.second(0)
    sums.product(4)
    sums.second(1)
    feed(0)
    sums.product(5)
    sums.product(6)
    sums.second(2)
    sums.third(0)
    feed(1)
    sums.product(7)
    sums.product(8)
    sums.second(3)
    sums.third(1)
    feed_in()
    sums.second(4)
    sums.third(2)
    pairs = width // 128
    quarter = pairs // 4
    attend(0, quarter)
    sums.second(5)
    sums.third(3)
    sums.third(4)
    attend(quarter, 2 * quarter)
    halo_pair(0)
    halo_send(0)
    sums.second(6)
    sums.third(5)
    attend(2 * quarter, 3 * quarter)
    sums.second(7)
    sums.third(6)
    attend(3 * quarter, pairs)
    halo_pair(1)
    halo_send(1)
    sums.second(8)
    sums.third(7)
    for i in range(4):
        sums.final(i)
    halo_add()
    sums.third(8)
    embed_in()
    for i in range(4, 9):
        sums.final(i)
    here.finish()


def back_sums(lefts, streamed, kept, dp_count):
    n = dp_count
    low = jnp.bfloat16
    dma = pltpu.SemaphoreType.DMA
    hbm = pl.BlockSpec(memory_space=pl.ANY)
    vmem = pl.BlockSpec(memory_space=pltpu.VMEM)
    tokens, ff = streamed.gate_pre.shape
    patches, width = streamed.cot_patches.shape
    tile = 256
    first = (ff // tile + 1) // 2 * tile
    one = jax.ShapeDtypeStruct
    right_shapes = [(tokens, first)] * 2 + [(tokens, ff - first)] * 2
    right_shapes += [(tokens, width), (patches, width)]
    right_shapes += [(tokens, width)] * 2 + [(patches, width)]
    units, shapes, scratch, pool_count = plan_sums(
        BACK_PAIRS, [left_shape(a) for a in lefts], right_shapes, n, 4
    )
    count = len(units)
    scratch += [
        pltpu.VMEM((4, width, width), low),
        pltpu.VMEM((2, 2, tokens, tile), F32),
        pltpu.VMEM((tokens, width), F32),
        pltpu.VMEM((tokens, width), F32),
        pltpu.VMEM((tokens, width), F32),
        pltpu.VMEM((2, 2, 3 * tokens, 128), low),
        pltpu.VMEM((2, 2, tokens, width), low),
        dma((4,)),
        dma((2, 5)),
        dma((width // tile,)),
        dma((2,)),
        dma((2, 4, 2)),
    ]
    results = pl.pallas_call(
        functools.partial(back_kernel, n, units, pool_count),
        out_shape=[one(shape, F32) for shape in shapes]
        + [one((8, width), F32)]
        + [one((tokens, width), low)] * 5,
        in_specs=[hbm] * (len(lefts) + len(streamed)) + [vmem] * len(kept),
        out_specs=[vmem] * (count + 6),
        scratch_shapes=scratch,
        compiler_params=pltpu.CompilerParams(
            collective_id=1, has_side_effects=True, vmem_limit_bytes=63 * 1024 * 1024
        ),
        name="back_sums",
    )(*lefts, *streamed, *kept)
    return results[:count], results[count:]


def finish_kernel(cuts, rows, stacked, table_in, counts_in, *refs):
    wholes, refs = refs[: len(cuts)], list(refs[len(cuts) :])
    halves = [refs.pop(0) for _ in range(4)]
    table, counts = refs.pop(0), refs.pop(0)
    row = lax.broadcasted_iota(jnp.int32, (table.shape[0], rows.shape[1]), 0)
    onto = (rows[...] == row + pl.program_id(0) * table.shape[0]).astype(jnp.float32)
    counts[...] = (counts_in[...] + jnp.sum(onto, axis=1, keepdims=True)).astype(jnp.int32)
    table[...] = table_in[...] + matmul(onto.astype(jnp.bfloat16), stacked[...])

    @pl.when(pl.program_id(0) == 0)
    def _():
        core = lax.axis_index(SUB) % 2
        for cut, source, target in zip(cuts, wholes, refs):
            if cut == source.shape[0]:
                target[...] = source[...]
            else:
                target[...] = jnp.where(core == 0, source[:cut], source[source.shape[0] - cut :])
        for k in range(2):
            left, right = halves[k], halves[2 + k]
            target = refs[len(cuts) + k]
            target[:, : left.shape[1]] = left[...]
            target[:, left.shape[1] :] = right[...]


def finish(table_grad, counts, stacked, rows, wholes, cuts, halves):
    rows_dev, width = table_grad.shape
    block = 256
    one = jax.ShapeDtypeStruct

    def whole(shape):
        return pl.BlockSpec(shape, lambda i: (0, 0))

    def blocks(cols):
        return pl.BlockSpec((block, cols), lambda i: (i, 0))

    shapes = [(cut, a.shape[1]) for a, cut in zip(wholes, cuts)]
    shapes += [(a.shape[0], a.shape[1] + b.shape[1]) for a, b in zip(halves[:2], halves[2:])]
    return pl.pallas_call(
        functools.partial(finish_kernel, cuts),
        grid=(-(-rows_dev // block),),
        out_shape=[one((rows_dev, width), F32), one((rows_dev, 1), jnp.int32)]
        + [one(shape, F32) for shape in shapes],
        in_specs=[whole(rows.shape), whole(stacked.shape), blocks(width), blocks(1)]
        + [whole(a.shape) for a in (*wholes, *halves)],
        out_specs=[blocks(width), blocks(1)] + [whole(shape) for shape in shapes],
        compiler_params=pltpu.CompilerParams(vmem_limit_bytes=VMEM_CAP),
        name="finish",
    )(rows, stacked, table_grad, counts, *wholes, *halves)


WEIGHT_STEPS = tuple(((i, 0, 2), (i, 1, 2)) for i in (0, 1, 2, 3, 4, 5, 6, 8, 9, 7, 10))


def by_rows(a, dp_count):
    depth, total = a.shape
    return a.T.reshape(dp_count * 4, total // (dp_count * 4), depth)


def body(
    byte_ids,
    hash_ids,
    lengths,
    byte_table,
    hash_table,
    norm_attn,
    norm_ffn,
    norm_cross,
    w_query,
    w_key,
    w_value,
    w_out,
    w_gate,
    w_up,
    w_down,
    c_query,
    c_key,
    c_value,
    c_out,
    cot_bytes,
    cot_patches,
):
    dp_count = lax.axis_size(DP)
    rs_count = lax.axis_size(SEQ)
    all_count = dp_count * rs_count
    rank_seq = lax.axis_index(SEQ)
    rank_table = lax.axis_index(DP) * rs_count + rank_seq
    tokens, gram_count = hash_ids.shape
    rows_dev, model_width = hash_table.shape
    head_count = model_width // HD
    request_count = tokens * gram_count
    slot_count = 2 * request_count // all_count
    flat_ids = hash_ids.reshape(request_count)
    owners = flat_ids // rows_dev
    ordering = jnp.argsort(owners, stable=True)
    owners_sorted = owners[ordering]
    per_owner = jnp.sum(
        (owners[:, None] == jnp.arange(all_count, dtype=jnp.int32)[None, :]).astype(jnp.int32),
        axis=0,
    )
    first_slot = jnp.cumsum(per_owner) - per_owner
    place_sorted = (
        owners_sorted * slot_count
        + jnp.arange(request_count, dtype=jnp.int32)
        - first_slot[owners_sorted]
    )
    placement = jnp.zeros((request_count,), jnp.int32).at[ordering].set(place_sorted)
    requests = jnp.full((all_count * slot_count,), -1, jnp.int32).at[placement].set(flat_ids)
    requests = requests.reshape(dp_count, rs_count, slot_count)
    incoming = lax.all_to_all(
        lax.all_to_all(requests, DP, split_axis=0, concat_axis=0, tiled=True),
        SEQ,
        split_axis=1,
        concat_axis=1,
        tiled=True,
    )
    present = incoming >= 0
    safe_rows = jnp.where(present, incoming - rank_table * rows_dev, 0)
    served = jnp.where(present[..., None], hash_table[safe_rows], jnp.zeros((), jnp.bfloat16))
    returned = lax.all_to_all(
        lax.all_to_all(served, DP, split_axis=0, concat_axis=0, tiled=True),
        SEQ,
        split_axis=1,
        concat_axis=1,
        tiled=True,
    )
    fetched = returned.reshape(all_count * slot_count, model_width)[placement]
    fetched = fetched.astype(jnp.float32).reshape(tokens, gram_count, model_width)
    one_hot = byte_ids[:, None] == jnp.arange(BYTE_VALUES, dtype=jnp.int32)[None, :]
    embedded = matmul(one_hot.astype(jnp.bfloat16), byte_table) + jnp.sum(fetched, axis=1)
    row_counts = (
        jnp.zeros((rows_dev,), jnp.int32)
        .at[safe_rows.reshape(-1)]
        .add(present.reshape(-1).astype(jnp.int32))
    )
    weight_list = (
        w_query,
        w_key,
        w_value,
        w_out,
        w_gate,
        w_up,
        w_down,
        c_query,
        c_key,
        c_value,
        c_out,
    )
    gathered = (
        lax.all_gather(weight_list[0], DP, axis=0, tiled=True),
        lax.all_gather(weight_list[1], DP, axis=0, tiled=True),
        lax.all_gather(weight_list[2], DP, axis=0, tiled=True),
        lax.all_gather(weight_list[3], DP, axis=0, tiled=True),
        lax.all_gather(weight_list[4], DP, axis=0, tiled=True),
        lax.all_gather(weight_list[5], DP, axis=0, tiled=True),
        lax.all_gather(weight_list[6], DP, axis=0, tiled=True),
        lax.all_gather(weight_list[7], DP, axis=0, tiled=True),
        lax.all_gather(weight_list[8], DP, axis=0, tiled=True),
        lax.all_gather(weight_list[9], DP, axis=0, tiled=True),
        lax.all_gather(weight_list[10], DP, axis=0, tiled=True),
    )
    (
        full_query,
        full_key,
        full_value,
        full_out,
        full_gate,
        full_up,
        full_down,
        full_cquery,
        full_ckey,
        full_cvalue,
        full_cout,
    ) = gathered
    x_attn, normed_attn, scale_attn = normalize(embedded, norm_attn)
    queries = matmul(x_attn, full_query).astype(jnp.bfloat16).reshape(tokens, head_count, HD)
    key_rows = matmul(x_attn, full_key).astype(jnp.bfloat16).reshape(tokens, head_count, HD)
    value_rows = matmul(x_attn, full_value).astype(jnp.bfloat16).reshape(tokens, head_count, HD)
    behind = (WIN - 2) // tokens + 1
    key_parts = []
    value_parts = []
    for offset_back in range(behind, 0, -1):
        far_keys, far_values = passed_along((key_rows, value_rows), SEQ, offset_back)
        key_parts.append(far_keys)
        value_parts.append(far_values)
    all_keys = jnp.concatenate(key_parts + [key_rows], axis=0)
    all_values = jnp.concatenate(value_parts + [value_rows], axis=0)
    q_rows = min(tokens, 512)
    key_span = (WIN - 1 + q_rows - 1) // q_rows * q_rows
    base_key = (rank_seq - behind) * tokens
    block_index = 0
    q_start = block_index * q_rows
    k_start = behind * tokens + q_start - key_span
    allowed = window_mask(
        rank_seq * tokens + q_start, base_key + k_start, q_rows, q_rows + key_span
    )
    scores = (
        jnp.einsum("qhd,khd->hqk", queries, all_keys, preferred_element_type=jnp.float32)
        * SCORE_SCALE
    )
    prob_block, log_total = soft_forward(scores, allowed)
    attended_parts = jnp.einsum(
        "hqk,khd->qhd",
        prob_block.astype(jnp.bfloat16),
        all_values,
        preferred_element_type=jnp.float32,
    )
    lse_parts = [log_total]
    attended = attended_parts.astype(jnp.bfloat16).reshape(tokens, model_width)
    h_mid = embedded + matmul(attended, full_out)
    x_ffn, normed_ffn, scale_ffn = normalize(h_mid, norm_ffn)
    gate_pre = matmul(x_ffn, full_gate)
    up_pre = matmul(x_ffn, full_up)
    gate_sig = jax.nn.sigmoid(gate_pre)
    silu_val = gate_pre * gate_sig
    hidden = (silu_val * up_pre).astype(jnp.bfloat16)
    h_out = h_mid + matmul(hidden, full_down)
    byte_states = h_out.astype(jnp.bfloat16)
    x_cross, normed_cross, scale_cross = normalize(h_out, norm_cross)
    patch_len = lengths[0]
    patch_count = patch_len.shape[0]
    patch_end = jnp.cumsum(patch_len)
    patch_start = patch_end - patch_len
    byte_pos = jnp.arange(tokens, dtype=jnp.int32)
    member = (byte_pos[None, :] >= patch_start[:, None]) & (byte_pos[None, :] < patch_end[:, None])
    length_f = patch_len.astype(jnp.float32)[:, None]
    pooled = matmul(member.astype(jnp.bfloat16), x_cross) / length_f
    pooled_low = pooled.astype(jnp.bfloat16)
    p_query = (
        matmul(pooled_low, full_cquery).astype(jnp.bfloat16).reshape(patch_count, head_count, HD)
    )
    p_key = matmul(x_cross, full_ckey).astype(jnp.bfloat16).reshape(tokens, head_count, HD)
    p_value = matmul(x_cross, full_cvalue).astype(jnp.bfloat16).reshape(tokens, head_count, HD)
    cross_scores = (
        jnp.einsum("phd,thd->hpt", p_query, p_key, preferred_element_type=jnp.float32) * SCORE_SCALE
    )
    cross_prob, cross_lse = soft_forward(cross_scores, member[None])
    p_attended = (
        jnp.einsum(
            "hpt,thd->phd",
            cross_prob.astype(jnp.bfloat16),
            p_value,
            preferred_element_type=jnp.float32,
        )
        .astype(jnp.bfloat16)
        .reshape(patch_count, model_width)
    )
    patch_states = (pooled + matmul(p_attended, full_cout)).astype(jnp.bfloat16)
    grad_c_out = t_times(p_attended, cot_patches)
    grad_patt = (
        times_t(cot_patches, full_cout).astype(jnp.bfloat16).reshape(patch_count, head_count, HD)
    )
    cross_again = (
        jnp.einsum("phd,thd->hpt", p_query, p_key, preferred_element_type=jnp.float32) * SCORE_SCALE
    )
    cross_full = soft_again(cross_again, member[None], cross_lse)
    grad_cprob = jnp.einsum("phd,thd->hpt", grad_patt, p_value, preferred_element_type=jnp.float32)
    grad_cscore = soft_back(cross_full, grad_cprob)
    grad_pquery = (
        (
            jnp.einsum("hpt,thd->phd", grad_cscore, p_key, preferred_element_type=jnp.float32)
            * SCORE_SCALE
        )
        .astype(jnp.bfloat16)
        .reshape(patch_count, model_width)
    )
    grad_pkey = (
        (
            jnp.einsum("hpt,phd->thd", grad_cscore, p_query, preferred_element_type=jnp.float32)
            * SCORE_SCALE
        )
        .astype(jnp.bfloat16)
        .reshape(tokens, model_width)
    )
    grad_pvalue = (
        jnp.einsum(
            "hpt,phd->thd",
            cross_full.astype(jnp.bfloat16),
            grad_patt,
            preferred_element_type=jnp.float32,
        )
        .astype(jnp.bfloat16)
        .reshape(tokens, model_width)
    )
    grad_c_query = t_times(pooled_low, grad_pquery)
    grad_c_key = t_times(x_cross, grad_pkey)
    grad_c_value = t_times(x_cross, grad_pvalue)
    grad_pooled = cot_patches.astype(jnp.float32) + times_t(grad_pquery, full_cquery).astype(
        jnp.bfloat16
    ).astype(jnp.float32)
    to_bytes = lax.dot_general(
        member.astype(jnp.float32),
        grad_pooled / length_f,
        (((0,), (0,)), ((), ())),
        precision=PRECISE,
    )
    grad_xcross = (
        times_t(grad_pkey, full_ckey) + times_t(grad_pvalue, full_cvalue) + to_bytes
    ).astype(jnp.bfloat16)
    grad_hout_norm, grad_norm_cross = norm_back(
        grad_xcross.astype(jnp.float32), normed_cross, scale_cross, norm_cross
    )
    grad_hout = cot_bytes.astype(jnp.float32) + grad_hout_norm
    grad_branch_f = grad_hout.astype(jnp.bfloat16)
    grad_w_down = t_times(hidden, grad_branch_f)
    grad_hidden = times_t(grad_branch_f, full_down).astype(jnp.bfloat16).astype(jnp.float32)
    grad_gate = (grad_hidden * up_pre * gate_sig * (1.0 + gate_pre * (1.0 - gate_sig))).astype(
        jnp.bfloat16
    )
    grad_up = (grad_hidden * silu_val).astype(jnp.bfloat16)
    grad_w_gate = t_times(x_ffn, grad_gate)
    grad_w_up = t_times(x_ffn, grad_up)
    grad_xffn = (times_t(grad_gate, full_gate) + times_t(grad_up, full_up)).astype(jnp.bfloat16)
    grad_hmid_norm, grad_norm_ffn = norm_back(
        grad_xffn.astype(jnp.float32), normed_ffn, scale_ffn, norm_ffn
    )
    grad_hmid = grad_hout + grad_hmid_norm
    grad_branch_a = grad_hmid.astype(jnp.bfloat16)
    grad_w_out = t_times(attended, grad_branch_a)
    grad_att = times_t(grad_branch_a, full_out).astype(jnp.bfloat16).reshape(tokens, head_count, HD)
    grad_keys_all = jnp.zeros(((behind + 1) * tokens, head_count, HD), jnp.float32)
    grad_values_all = jnp.zeros(((behind + 1) * tokens, head_count, HD), jnp.float32)
    block_index = 0
    q_start = block_index * q_rows
    k_start = behind * tokens + q_start - key_span
    k_stop = k_start + q_rows + key_span
    allowed = window_mask(
        rank_seq * tokens + q_start, base_key + k_start, q_rows, q_rows + key_span
    )
    scores = (
        jnp.einsum("qhd,khd->hqk", queries, all_keys, preferred_element_type=jnp.float32)
        * SCORE_SCALE
    )
    prob_block = soft_again(scores, allowed, lse_parts[block_index])
    grad_prob = jnp.einsum("qhd,khd->hqk", grad_att, all_values, preferred_element_type=jnp.float32)
    grad_score = soft_back(prob_block, grad_prob)
    grad_q_parts = (
        jnp.einsum("hqk,khd->qhd", grad_score, all_keys, preferred_element_type=jnp.float32)
        * SCORE_SCALE
    )
    grad_keys_all = grad_keys_all.at[k_start:k_stop].add(
        jnp.einsum("hqk,qhd->khd", grad_score, queries, preferred_element_type=jnp.float32)
        * SCORE_SCALE
    )
    grad_values_all = grad_values_all.at[k_start:k_stop].add(
        jnp.einsum(
            "hqk,qhd->khd",
            prob_block.astype(jnp.bfloat16),
            grad_att,
            preferred_element_type=jnp.float32,
        )
    )
    grad_keys = grad_keys_all[behind * tokens :]
    grad_values = grad_values_all[behind * tokens :]
    for offset_back in range(behind, 0, -1):
        part_index = behind - offset_back
        far_grad_k, far_grad_v = (
            passed_along(
                grad_keys_all[part_index * tokens : (part_index + 1) * tokens].astype(jnp.bfloat16),
                SEQ,
                -offset_back,
            ).astype(jnp.float32),
            passed_along(
                grad_values_all[part_index * tokens : (part_index + 1) * tokens].astype(
                    jnp.bfloat16
                ),
                SEQ,
                -offset_back,
            ).astype(jnp.float32),
        )
        grad_keys = grad_keys + far_grad_k
        grad_values = grad_values + far_grad_v
    grad_queries = grad_q_parts.astype(jnp.bfloat16).reshape(tokens, model_width)
    grad_keys_low = grad_keys.astype(jnp.bfloat16).reshape(tokens, model_width)
    grad_values_low = grad_values.astype(jnp.bfloat16).reshape(tokens, model_width)
    grad_w_query = t_times(x_attn, grad_queries)
    grad_w_key = t_times(x_attn, grad_keys_low)
    grad_w_value = t_times(x_attn, grad_values_low)
    grad_xattn = (
        times_t(grad_queries, full_query)
        + times_t(grad_keys_low, full_key)
        + times_t(grad_values_low, full_value)
    ).astype(jnp.bfloat16)
    grad_embed_norm, grad_norm_attn = norm_back(
        grad_xattn.astype(jnp.float32), normed_attn, scale_attn, norm_attn
    )
    grad_embed = grad_hmid + grad_embed_norm
    embed_grad = grad_embed.astype(jnp.bfloat16)
    grad_byte_table = lax.dot_general(
        one_hot.astype(jnp.float32), grad_embed, (((0,), (0,)), ((), ())), precision=PRECISE
    )
    per_request = jnp.broadcast_to(
        grad_embed[:, None, :], (tokens, gram_count, model_width)
    ).reshape(request_count, model_width)
    outgoing = (
        jnp.zeros((all_count * slot_count, model_width), jnp.float32).at[placement].set(per_request)
    )
    outgoing = outgoing.reshape(dp_count, rs_count, slot_count, model_width)
    arrived = lax.all_to_all(
        lax.all_to_all(
            outgoing.astype(jnp.bfloat16), DP, split_axis=0, concat_axis=0, tiled=True
        ),
        SEQ,
        split_axis=1,
        concat_axis=1,
        tiled=True,
    ).astype(outgoing.dtype)
    hash_table_grad = (
        jnp.zeros((rows_dev, model_width), jnp.float32)
        .at[safe_rows.reshape(-1)]
        .add(jnp.where(present[..., None], arrived, 0.0).reshape(-1, model_width))
    )
    summed_all = (
        lax.psum_scatter(grad_norm_attn, ALL, scatter_dimension=0, tiled=True),
        lax.psum_scatter(grad_norm_ffn, ALL, scatter_dimension=0, tiled=True),
        lax.psum_scatter(grad_norm_cross, ALL, scatter_dimension=0, tiled=True),
        lax.psum_scatter(grad_w_query, ALL, scatter_dimension=0, tiled=True),
        lax.psum_scatter(grad_w_key, ALL, scatter_dimension=0, tiled=True),
        lax.psum_scatter(grad_w_value, ALL, scatter_dimension=0, tiled=True),
        lax.psum_scatter(grad_w_out, ALL, scatter_dimension=0, tiled=True),
        lax.psum_scatter(grad_w_gate, ALL, scatter_dimension=0, tiled=True),
        lax.psum_scatter(grad_w_up, ALL, scatter_dimension=0, tiled=True),
        lax.psum_scatter(grad_w_down, ALL, scatter_dimension=0, tiled=True),
        lax.psum_scatter(grad_c_query, ALL, scatter_dimension=0, tiled=True),
        lax.psum_scatter(grad_c_key, ALL, scatter_dimension=0, tiled=True),
        lax.psum_scatter(grad_c_value, ALL, scatter_dimension=0, tiled=True),
        lax.psum_scatter(grad_c_out, ALL, scatter_dimension=0, tiled=True),
        lax.psum_scatter(grad_byte_table, ALL, scatter_dimension=0, tiled=True),
    )
    (
        out_norm_attn,
        out_norm_ffn,
        out_norm_cross,
        out_query,
        out_key,
        out_value,
        out_proj,
        out_gate,
        out_up,
        out_down,
        out_cquery,
        out_ckey,
        out_cvalue,
        out_cout,
        out_bytes,
    ) = summed_all
    return (
        byte_states,
        patch_states,
        embed_grad,
        out_bytes,
        hash_table_grad,
        row_counts,
        out_norm_attn,
        out_norm_ffn,
        out_norm_cross,
        out_query,
        out_key,
        out_value,
        out_proj,
        out_gate,
        out_up,
        out_down,
        out_cquery,
        out_ckey,
        out_cvalue,
        out_cout,
    )


def fast_body(
    byte_ids,
    hash_ids,
    lengths,
    byte_table,
    hash_table,
    norm_attn,
    norm_ffn,
    norm_cross,
    w_query,
    w_key,
    w_value,
    w_out,
    w_gate,
    w_up,
    w_down,
    c_query,
    c_key,
    c_value,
    c_out,
    cot_bytes,
    cot_patches,
):
    dp_count = lax.axis_size(DP)
    rs_count = lax.axis_size(SEQ)
    all_count = dp_count * rs_count
    rank_table = lax.axis_index(ALL)
    rows_dev, model_width = hash_table.shape
    patch_len = lengths[0]
    patch_end = jnp.cumsum(patch_len)[:, None]
    patch_start = patch_end - patch_len[:, None]
    gains = jnp.concatenate(
        [norm_attn[None], norm_ffn[None], norm_cross[None], jnp.zeros((5, model_width), jnp.float32)]
    )
    full, embedded, entries, kept = fetch(
        hash_ids,
        hash_table,
        (
            w_query,
            w_key,
            w_value,
            w_out,
            w_gate,
            w_up,
            w_down,
            c_query,
            c_key,
            c_value,
            c_out,
        ),
        (byte_ids[:, None], byte_table, gains, patch_start, patch_end),
        WEIGHT_STEPS,
        dp_count,
    )
    lefts = [
        by_rows(a, dp_count)
        for a in (kept.x_ffn, kept.hidden, kept.pooled, kept.x_cross, kept.p_attended)
    ]
    sums, results = back_sums(
        lefts,
        Streamed(
            kept.gate_pre,
            kept.up_pre,
            kept.h_out,
            kept.h_mid,
            embedded,
            kept.key_values,
            *full,
            cot_patches,
        ),
        (
            cot_bytes,
            kept.p_query,
            kept.p_key,
            kept.p_value,
            kept.cross_lse,
            gains,
            patch_start,
            patch_end,
            kept.queries,
            kept.lse,
        ),
        dp_count,
    )
    first_sums = sums
    gain_rows, grad_branch_a, grad_queries, grad_keys, grad_values, embed_grad = results
    one_hot = byte_ids[:, None] == jnp.arange(BYTE_VALUES, dtype=jnp.int32)[None, :]
    lefts = [
        by_rows(a, dp_count) for a in (kept.x_attn, kept.attended, one_hot.astype(jnp.bfloat16))
    ]
    rights = [grad_queries, grad_keys, grad_values, grad_branch_a, embed_grad]
    sums, gain_sums, *table_parts = last_sums(
        [(1, 3), (0, 0), (0, 1), (0, 2), (2, 4)],
        lefts,
        rights,
        embed_grad,
        gain_rows,
        entries,
        rows_dev,
        dp_count,
    )
    wholes = (*sums, *first_sums[:5])
    cuts = [a.shape[0] for a in wholes]
    cuts[4] = BYTE_VALUES // all_count
    cuts[9] = kept.hidden.shape[1] // all_count
    (
        hash_table_grad,
        counts,
        out_proj,
        out_query,
        out_key,
        out_value,
        out_bytes,
        out_cout,
        out_ckey,
        out_cvalue,
        out_cquery,
        out_down,
        out_gate,
        out_up,
    ) = finish(*table_parts, wholes, tuple(cuts), first_sums[5:])
    row_counts = counts[:, 0]
    own_gains = lax.dynamic_slice_in_dim(
        gain_sums, rank_table * (model_width // all_count), model_width // all_count, 1
    )
    return (
        kept.byte_states,
        kept.patch_states,
        embed_grad,
        out_bytes,
        hash_table_grad,
        row_counts,
        own_gains[0],
        own_gains[1],
        own_gains[2],
        out_query,
        out_key,
        out_value,
        out_proj,
        out_gate,
        out_up,
        out_down,
        out_cquery,
        out_ckey,
        out_cvalue,
        out_cout,
    )


def solution(mesh):
    fits = mesh.shape[REP] == 2 and mesh.shape[SUB] == 4 and mesh.shape[DP] <= 4
    return jax.shard_map(
        fast_body if fits else body,
        mesh=mesh,
        in_specs=(
            P(ALL),
            P(ALL, None),
            P(ALL, None),
            P(),
            P(ALL, None),
            P(),
            P(),
            P(),
            P(DP, None),
            P(DP, None),
            P(DP, None),
            P(DP, None),
            P(DP, None),
            P(DP, None),
            P(DP, None),
            P(DP, None),
            P(DP, None),
            P(DP, None),
            P(DP, None),
            P(ALL, None),
            P(ALL, None),
        ),
        out_specs=(
            P(ALL, None),
            P(ALL, None),
            P(ALL, None),
            P(ALL, None),
            P(ALL, None),
            P(ALL),
            P(ALL),
            P(ALL),
            P(ALL),
            P(ALL, None),
            P(ALL, None),
            P(ALL, None),
            P(ALL, None),
            P(ALL, None),
            P(ALL, None),
            P(ALL, None),
            P(ALL, None),
            P(ALL, None),
            P(ALL, None),
            P(ALL, None),
        ),
        check_vma=False,
    )
```

```python
import functools
import typing

import jax
import jax.numpy as jnp
from jax import lax
from jax.experimental import pallas as pl
from jax.experimental.pallas import tpu as pltpu
from jax.sharding import PartitionSpec as P

DP, REP, SUB = "dp", "rep", "sub"
SEQ = (REP, SUB)
ALL = (DP, REP, SUB)
HD = 64
WIN = 512
BYTE_VALUES = 256


PRECISE = lax.Precision.HIGHEST
NEG_BIG = -1e30
EPSILON = 1e-06
SCORE_SCALE = 0.125


def passed_along(x, axis, by):
    devices = lax.axis_size(axis)
    pairs = [(i, i + by) for i in range(devices) if 0 <= i + by < devices]
    return lax.ppermute(x, axis, pairs)


def matmul(matrix_a, matrix_b):
    return jnp.dot(matrix_a, matrix_b, preferred_element_type=jnp.float32)


def times_t(matrix_a, matrix_b):
    return lax.dot_general(
        matrix_a, matrix_b, (((1,), (1,)), ((), ())), preferred_element_type=jnp.float32
    )


def t_times(matrix_a, matrix_b):
    return lax.dot_general(
        matrix_a, matrix_b, (((0,), (0,)), ((), ())), preferred_element_type=jnp.float32
    )


def normalize(values, gains):
    inv_rms = lax.rsqrt(jnp.mean(values * values, axis=-1, keepdims=True) + EPSILON)
    normed = values * inv_rms
    return ((normed * gains).astype(jnp.bfloat16), normed, inv_rms)


def norm_back(grad_out, normed, inv_rms, gains):
    grad_gain = jnp.sum(grad_out * normed, axis=0)
    scaled_grad = grad_out * gains
    grad_in = inv_rms * (
        scaled_grad - normed * jnp.mean(scaled_grad * normed, axis=-1, keepdims=True)
    )
    return (grad_in, grad_gain)


def soft_forward(scores, allowed):
    masked = jnp.where(allowed, scores, NEG_BIG)
    row_max = jnp.max(masked, axis=-1, keepdims=True)
    exps = jnp.exp(masked - row_max)
    row_sum = jnp.sum(exps, axis=-1, keepdims=True)
    return (exps / row_sum, row_max + jnp.log(row_sum))


def soft_again(scores, allowed, log_total):
    return jnp.where(allowed, jnp.exp(scores - log_total), 0.0)


def soft_back(probs_full, grad_probs):
    row_total = jnp.sum(probs_full * grad_probs, axis=-1, keepdims=True)
    return (probs_full * (grad_probs - row_total)).astype(jnp.bfloat16)


def window_mask(first_query, first_key, row_count, col_count):
    query_pos = first_query + jnp.arange(row_count, dtype=jnp.int32)
    key_pos = first_key + jnp.arange(col_count, dtype=jnp.int32)
    near = (
        (key_pos[None, :] <= query_pos[:, None])
        & (key_pos[None, :] > query_pos[:, None] - WIN)
        & (key_pos[None, :] >= 0)
    )
    return near[None]


MESH_ID = pl.DeviceIdType.MESH
SLOTS = 96
GATHER_LAGS = (1, 2, 3)


HASH, GATHER, FORWARD = range(3)


SCHEDULE = (
    (GATHER, 0),
    (HASH, 0),
    (GATHER, 1),
    (HASH, 1),
    (HASH, 2),
    (GATHER, 2),
    (HASH, 3),
    (GATHER, 3),
    (HASH, 4),
    (GATHER, 4),
    (HASH, 5),
    (GATHER, 5),
    (HASH, 6),
    (GATHER, 6),
    (HASH, 7),
    (FORWARD, 2),
    (GATHER, 7),
    (FORWARD, 2),
    (GATHER, 8),
    (FORWARD, 2),
    (GATHER, 9),
    (FORWARD, 2),
    (GATHER, 10),
    (GATHER, 11),
    (FORWARD, 2),
    (GATHER, 12),
    (FORWARD, 2),
    (GATHER, 13),
    (FORWARD, 3),
)
VMEM_CAP = 60 * 1024 * 1024


class Place:
    def __init__(self, dp_count):
        self.n = dp_count
        self.z = lax.axis_index(DP)
        self.x = lax.axis_index(REP)
        sub = lax.axis_index(SUB)
        self.y = sub // 2
        self.c = sub % 2
        self.started, self.maybe = [], []

    def at(self, dz=0, dx=0, dy=0, dc=0):
        z = lax.rem(self.z + dz, self.n) if dz else self.z
        x = 1 - self.x if dx else self.x
        y = 1 - self.y if dy else self.y
        c = 1 - self.c if dc else self.c
        return (z, x, y * 2 + c)

    def greet(self):
        barrier = pltpu.get_barrier_semaphore()
        peers = [
            self.at(dx=dx, dy=dy, dc=dc)
            for dx in range(2)
            for dy in range(2)
            for dc in range(2)
            if dx + dy + dc > 0
        ]
        peers += [self.at(dz=j) for j in range(1, self.n)]
        for peer in peers:
            pl.semaphore_signal(barrier, inc=1, device_id=peer, device_id_type=MESH_ID)
        pl.semaphore_wait(barrier, len(peers))

    def send_if(self, there, src, dst, send_sem, recv_sem, peer):
        copy = pltpu.make_async_remote_copy(
            src_ref=src,
            dst_ref=dst,
            send_sem=send_sem,
            recv_sem=recv_sem,
            device_id=peer,
            device_id_type=MESH_ID,
        )
        pl.when(there)(copy.start)
        self.maybe.append((there, copy))

    def send(self, src, dst, send_sem, recv_sem, peer):
        copy = pltpu.make_async_remote_copy(
            src_ref=src,
            dst_ref=dst,
            send_sem=send_sem,
            recv_sem=recv_sem,
            device_id=peer,
            device_id_type=MESH_ID,
        )
        copy.start()
        self.started.append(copy)
        return copy

    def expect(self, dst, recv_sem):
        pltpu.make_async_remote_copy(
            src_ref=dst,
            dst_ref=dst,
            send_sem=recv_sem,
            recv_sem=recv_sem,
            device_id=self.at(dc=1),
            device_id_type=MESH_ID,
        ).wait_recv()

    def sent(self, copy):
        copy.wait_send()
        self.started = [other for other in self.started if other is not copy]

    def finish(self):
        for copy in self.started:
            copy.wait_send()
        for there, copy in self.maybe:
            pl.when(there)(copy.wait_send)
        self.started, self.maybe = [], []


def add_into(dst, src, blocks, width):
    def step(i, carry):
        total = dst(i)[...].astype(jnp.float32) + src(i)[...].astype(jnp.float32)
        dst(i)[...] = total.astype(jnp.bfloat16)
        return carry

    lax.fori_loop(0, blocks, step, 0)


class Reduction:
    def __init__(self, here, p0, r1a, r1b, r2a, r2b, sems, index):
        self.here, self.p0 = here, p0
        self.r1a, self.r1b, self.r2a, self.r2b = r1a, r1b, r2a, r2b
        self.sems, self.i = sems, index
        self.planes, _, _, self.rows, cols = p0.shape
        self.half = cols // 2
        self.left = pl.ds(0, self.half)
        self.right = pl.ds(self.half, self.half)

    def sem(self, k):
        return self.sems.at[self.i, k, 0], self.sems.at[self.i, k, 1]

    def first(self):
        h = self.here
        self.s1a = h.send(
            self.p0.at[:, 1 - h.x, :, :, self.left], self.r1a, *self.sem(0), h.at(dx=1)
        )
        self.s1b = h.send(
            self.p0.at[:, :, 1 - h.y, :, self.right], self.r1b, *self.sem(1), h.at(dy=1)
        )

    def second(self):
        h = self.here
        self.s1a.wait_recv()
        add_into(
            lambda i: self.p0.at[i // 2, h.x, i % 2, :, self.left],
            lambda i: self.r1a.at[i // 2, i % 2],
            2 * self.planes,
            self.half,
        )
        self.s2a = h.send(
            self.p0.at[:, h.x, 1 - h.y, :, self.left], self.r2a, *self.sem(2), h.at(dy=1)
        )
        self.s1b.wait_recv()
        add_into(
            lambda i: self.p0.at[i // 2, i % 2, h.y, :, self.right],
            lambda i: self.r1b.at[i // 2, i % 2],
            2 * self.planes,
            self.half,
        )
        self.s2b = h.send(
            self.p0.at[:, 1 - h.x, h.y, :, self.right], self.r2b, *self.sem(3), h.at(dx=1)
        )

    def third(self):
        h = self.here
        self.s2a.wait_recv()
        add_into(
            lambda i: self.p0.at[i, h.x, h.y, :, self.left],
            lambda i: self.r2a.at[i],
            self.planes,
            self.half,
        )
        self.s2b.wait_recv()
        add_into(
            lambda i: self.p0.at[i, h.x, h.y, :, self.right],
            lambda i: self.r2b.at[i],
            self.planes,
            self.half,
        )
        return self.p0.at[:, h.x, h.y]


EXTRA_IN = 5
F32, LOW = jnp.float32, jnp.bfloat16
class Kept(typing.NamedTuple):
    x_attn: typing.Any
    queries: typing.Any
    key_values: typing.Any
    lse: typing.Any
    attended: typing.Any
    h_mid: typing.Any
    x_ffn: typing.Any
    gate_pre: typing.Any
    up_pre: typing.Any
    hidden: typing.Any
    h_out: typing.Any
    byte_states: typing.Any
    x_cross: typing.Any
    pooled: typing.Any
    p_query: typing.Any
    p_key: typing.Any
    p_value: typing.Any
    cross_lse: typing.Any
    p_attended: typing.Any
    patch_states: typing.Any


def kept_shapes(t, w, f, p):
    one = jax.ShapeDtypeStruct
    return Kept(
        x_attn=one((t, w), LOW),
        queries=one((t, w), LOW),
        key_values=one((2, 3 * t, w), LOW),
        lse=one((t, 128), F32),
        attended=one((t, w), LOW),
        h_mid=one((t, w), F32),
        x_ffn=one((t, w), LOW),
        gate_pre=one((t, f), F32),
        up_pre=one((t, f), F32),
        hidden=one((t, f), LOW),
        h_out=one((t, w), F32),
        byte_states=one((t, w), LOW),
        x_cross=one((t, w), LOW),
        pooled=one((p, w), LOW),
        p_query=one((p, w), LOW),
        p_key=one((t, w), LOW),
        p_value=one((t, w), LOW),
        cross_lse=one((p, 128), F32),
        p_attended=one((p, w), LOW),
        patch_states=one((p, w), LOW),
    )


def forward_steps(here, fulls, embedded, extra_in, extra_out, slots, scratch):
    byte_ids, byte_table, gains, starts, ends = extra_in
    gate_w, up_w, x_halo, load_sems, halo_sems, *buffers, flush_sems = scratch
    out = Kept(*extra_out)
    flushed = (out.gate_pre, out.up_pre, out.key_values)
    out = out._replace(gate_pre=buffers[0], up_pre=buffers[1], key_values=buffers[2])
    flushes = []

    def flush(i):
        copy = pltpu.make_async_copy(buffers[i], flushed[i], flush_sems.at[i])
        copy.start()
        flushes.append(copy)

    tokens, width = embedded.shape
    heads = width // HD
    n = here.n
    z, x, y, c = here.z, here.x, here.y, here.c
    rank = (x * 2 + y) * 2 + c
    loads = {}
    kv = out.key_values

    def load(i, *targets):
        copies = []
        for b, target in enumerate(targets):
            rows = target.shape[0]
            copy = pltpu.make_async_copy(
                fulls[i].at[pl.ds(b * rows, rows)], target, load_sems.at[i, b]
            )
            copy.start()
            copies.append(copy)
        loads[i] = copies

    def load_slot(i, slot):
        for b in range(4):
            copy = pltpu.make_async_copy(
                fulls[i].at[pl.ds(b * (width // 4), width // 4)],
                slots[slot].at[b // 2, b % 2],
                load_sems.at[i, b],
            )
            copy.start()
            loads.setdefault(i, []).append(copy)

    def wait(*weights):
        for i in weights:
            for copy in loads[i]:
                copy.wait()

    def through(a, slot):
        return matmul(a, slots[slot][...].reshape(width, width))

    def embed():
        load_slot(0, 0)
        load_slot(1, 1)
        load_slot(2, 2)
        ids = lax.broadcasted_iota(jnp.int32, (tokens, BYTE_VALUES), 1)
        pick = jnp.where(byte_ids[...] == ids, 1.0, 0.0).astype(LOW)
        embedded[...] = embedded[...] + matmul(pick, byte_table[...])
        out.x_attn[...] = normalize(embedded[...], gains[0:1])[0]
        halo_send()

    def halo_send():
        target = jnp.minimum(rank + 2, 7)
        here.send_if(
            rank + 2 < 8,
            out.x_attn,
            x_halo.at[0],
            halo_sems.at[0, 0],
            halo_sems.at[0, 1],
            (z, target // 4, lax.rem(target, 4)),
        )
        here.send_if(
            c == 0, out.x_attn, x_halo.at[1], halo_sems.at[1, 0], halo_sems.at[1, 1], here.at(dc=1)
        )

    def project():
        wait(0, 1, 2)
        a = out.x_attn[...]
        out.queries[...] = through(a, 0).astype(LOW)
        kv[0, 2 * tokens :] = through(a, 1).astype(LOW)
        kv[1, 2 * tokens :] = through(a, 2).astype(LOW)

    def halo():
        there = rank >= 2

        @pl.when(there)
        def _():
            here.expect(x_halo.at[0], halo_sems.at[0, 1])

        here.send_if(
            there & (c == 1),
            x_halo.at[0],
            x_halo.at[1],
            halo_sems.at[1, 0],
            halo_sems.at[1, 1],
            here.at(dc=1),
        )

        @pl.when(there | (c == 1))
        def _():
            here.expect(x_halo.at[1], halo_sems.at[1, 1])

        @pl.when(jnp.logical_not(there))
        def _():
            x_halo[0] = jnp.zeros_like(x_halo[0])

        @pl.when(rank == 0)
        def _():
            x_halo[1] = jnp.zeros_like(x_halo[1])

        a = x_halo[...].reshape(2 * tokens, width)
        kv[0, : 2 * tokens] = through(a, 1).astype(LOW)
        kv[1, : 2 * tokens] = through(a, 2).astype(LOW)
        flush(2)

    lane = lax.broadcasted_iota(jnp.int32, (1, 128), 1)
    sides = [jnp.where(lane < HD, 1.0, 0.0).astype(LOW), jnp.where(lane < HD, 0.0, 1.0).astype(LOW)]

    def attend(first):
        row = lax.broadcasted_iota(jnp.int32, (tokens, tokens), 0)
        col = lax.broadcasted_iota(jnp.int32, (tokens, tokens), 1)
        mine = col <= row
        far_bias = jnp.where(rank >= 2, 0.0, NEG_BIG)
        near_bias = jnp.where(rank >= 1, 0.0, NEG_BIG)
        if first == 0:
            out.lse[...] = jnp.zeros_like(out.lse)
        else:
            load_slot(3, 3)

        def heads_pair(pair, carry):
            span = pl.ds(pl.multiple_of(pair * 128, 128), 128)
            q2 = out.queries[:, span]
            k2, v2 = kv[0, :, span], kv[1, :, span]
            halves = []
            for side in range(2):
                scores = times_t(q2 * sides[side], k2) * SCORE_SCALE
                edge = jnp.where(mine, scores[:, 2 * tokens :], scores[:, :tokens] + far_bias)
                middle = scores[:, tokens : 2 * tokens] + near_bias
                top = jnp.maximum(
                    jnp.max(edge, axis=1, keepdims=True), jnp.max(middle, axis=1, keepdims=True)
                )
                edge, middle = jnp.exp(edge - top), jnp.exp(middle - top)
                total = jnp.sum(edge, axis=1, keepdims=True) + jnp.sum(
                    middle, axis=1, keepdims=True
                )
                inverse = 1.0 / total
                edge, middle = edge * inverse, middle * inverse
                probs = jnp.concatenate(
                    [
                        jnp.where(mine, 0.0, edge).astype(LOW),
                        middle.astype(LOW),
                        jnp.where(mine, edge, 0.0).astype(LOW),
                    ],
                    axis=1,
                )
                halves.append(matmul(probs, v2))
                where = lane == pair * 2 + side
                out.lse[...] = jnp.where(where, top + jnp.log(total), out.lse[...])
            out.attended[:, span] = jnp.where(lane < HD, halves[0], halves[1]).astype(LOW)
            return carry

        lax.fori_loop(first * heads // 4, (first + 1) * heads // 4, heads_pair, 0)

    def attention_out():
        wait(3)
        h_mid = embedded[...] + through(out.attended[...], 3)
        out.h_mid[...] = h_mid
        out.x_ffn[...] = normalize(h_mid, gains[1:2])[0]

    def down_block(t):
        return slots[t // 4].at[t // 2 % 2, t % 2]

    tile = 256
    tiles = gate_w.shape[1] // tile

    def feed_forward():
        for t in range(tiles):
            copy = pltpu.make_async_copy(
                fulls[6].at[pl.ds(t * tile, tile)], down_block(t), down_sems.at[t]
            )
            copy.start()
            loads.setdefault(6, []).append(copy)
        wait(4, 5)
        a = out.x_ffn[...]

        def columns(t, carry):
            span = pl.ds(pl.multiple_of(t * tile, tile), tile)
            gate = matmul(a, gate_w[:, span])
            up = matmul(a, up_w[:, span])
            out.gate_pre[:, span] = gate
            out.up_pre[:, span] = up
            out.hidden[:, span] = (gate * jax.nn.sigmoid(gate) * up).astype(LOW)
            return carry

        lax.fori_loop(0, tiles, columns, 0)
        flush(0)
        flush(1)

    def feed_out():
        wait(6)
        total = out.h_mid[...]
        for t in range(tiles):
            total = total + matmul(
                out.hidden[:, t * tile : (t + 1) * tile], down_block(t)[...]
            )
        out.h_out[...] = total
        out.byte_states[...] = total.astype(LOW)
        out.x_cross[...] = normalize(total, gains[2:3])[0]

    byte_pos = lax.broadcasted_iota(jnp.int32, (starts.shape[0], tokens), 1)

    def member():
        return (byte_pos >= starts[...]) & (byte_pos < ends[...])

    pooled_f = []

    def cross_keys():
        inside = jnp.where(member(), 1.0, 0.0).astype(LOW)
        length = (ends[...] - starts[...]).astype(F32)
        pooled = matmul(inside, out.x_cross[...]) / length
        pooled_f.append(pooled)
        out.pooled[...] = pooled.astype(LOW)
        wait(8, 9)
        a = out.x_cross[...]
        out.p_key[...] = through(a, 4).astype(LOW)
        out.p_value[...] = through(a, 5).astype(LOW)

    def cross_query():
        wait(7)
        out.p_query[...] = through(out.pooled[...], 3).astype(LOW)
        allowed = member()
        out.cross_lse[...] = jnp.zeros_like(out.cross_lse)

        def heads_pair(pair, carry):
            span = pl.ds(pl.multiple_of(pair * 128, 128), 128)
            q2, k2, v2 = out.p_query[:, span], out.p_key[:, span], out.p_value[:, span]
            halves = []
            for side in range(2):
                scores = times_t(q2 * sides[side], k2) * SCORE_SCALE
                masked = jnp.where(allowed, scores, NEG_BIG)
                top = jnp.max(masked, axis=1, keepdims=True)
                exps = jnp.exp(masked - top)
                total = jnp.sum(exps, axis=1, keepdims=True)
                halves.append(matmul((exps / total).astype(LOW), v2))
                where = lane == pair * 2 + side
                out.cross_lse[...] = jnp.where(
                    where, top + jnp.log(total), out.cross_lse[...]
                )
            out.p_attended[:, span] = jnp.where(lane < HD, halves[0], halves[1]).astype(LOW)
            return carry

        lax.fori_loop(0, heads // 2, heads_pair, 0)

    def cross_out():
        wait(10)
        states = pooled_f[0] + through(out.p_attended[...], 0)
        out.patch_states[...] = states.astype(LOW)
        for copy in flushes:
            copy.wait()

    down_sems = load_sems.at[6]
    return [
        ((0, 1, 2), embed),
        ((), project),
        ((), halo),
        ((), lambda: attend(0)),
        ((4, 5), lambda: (load(4, gate_w), load(5, up_w))),
        ((3,), lambda: attend(1)),
        ((), attention_out),
        ((6,), feed_forward),
        ((8, 9), lambda: (load_slot(8, 4), load_slot(9, 5))),
        ((), feed_out),
        ((7,), lambda: load_slot(7, 3)),
        ((), cross_keys),
        ((10,), lambda: load_slot(10, 0)),
        ((), cross_query),
        ((), cross_out),
    ]


def fetch_kernel(dp_count, weight_count, steps_of, tokens, gram_count, used_lines, *refs):
    shards = refs[:weight_count]
    refs = list(refs[weight_count:])

    def take(number):
        taken = refs[:number]
        del refs[:number]
        return taken

    ids, table = take(2)
    extra_in = take(EXTRA_IN)
    fulls = take(weight_count)
    embedded, lists = take(2)
    extra_out = take(len(Kept._fields))
    (
        all_ids,
        send0,
        p0,
        r1a,
        r1b,
        r2a,
        r2b,
        r3,
        g_rows,
        core_sems,
        stage_sems,
        z_sems,
        local_sems,
        w_send,
        w_recv,
        z_send,
        id_sems,
        places,
        entries,
        *extra_scratch,
    ) = refs
    here = Place(dp_count)
    n = dp_count
    z, x, y, c = here.z, here.x, here.y, here.c

    class Weight:
        def __init__(self, number, i, part, parts, kind):
            self.i = number
            self.kind = kind
            rows, cols = shards[i].shape
            self.by_cols = rows // 8 % 16 != 0
            self.all_rows, self.count = rows, rows // parts
            self.first = part * self.count
            self.shard = shards[i].at[pl.ds(self.first, self.count)]
            self.full = fulls[i]
            self.step = (cols if self.by_cols else rows // parts) // 8
            near, far = (x, y) if kind == 0 else (y, x)
            self.q = (c * 2 + far) * 2 + near

        def on(self, plane):
            return self.full.at[pl.ds(plane * self.all_rows + self.first, self.count)]

        def cut(self, ref, start, count):
            span = pl.ds(start * self.step, count * self.step)
            if self.by_cols:
                return ref.at[:, span]
            return ref.at[span, :]

        def local(self):
            here.send(
                self.shard,
                self.on(z),
                local_sems.at[self.i, 0],
                local_sems.at[self.i, 1],
                here.at(dc=1),
            )

        def stage(self, k, j, start, count, src_ref, plane, peer):
            here.send(
                self.cut(src_ref, start, count),
                self.cut(self.on(plane), start, count),
                w_send.at[self.i, k, j - 1],
                w_recv.at[self.i, k, j - 1],
                peer,
            )

        def came(self, k, j, start, count):
            plane = lax.rem(z + n - j, n)
            here.expect(
                self.cut(self.on(plane), start, count), w_recv.at[self.i, k, j - 1]
            )
            return plane

        def hop(self, there, up, k, plane, src_ref):
            peer = jnp.clip(z + 1 if up else z - 1, 0, n - 1)
            here.send_if(
                there,
                self.cut(src_ref, self.q, 1),
                self.cut(self.on(plane), self.q, 1),
                z_send.at[self.i, 0 if up else 1, k],
                w_recv.at[self.i, 0, (k + 1 if up else n - k - 1) - 1],
                (peer, x, y * 2 + c),
            )

        def along_z(self):
            self.hop(z + 1 < n, True, 0, z, self.shard)
            self.hop(z >= 1, False, 0, z, self.shard)

        def onward(self, k):
            for up in (True, False):
                there = (z >= k) & (z + 1 < n) if up else (z + k < n) & (z >= 1)
                plane = jnp.clip(z - k if up else z + k, 0, n - 1)
                j = k if up else n - k

                @pl.when(there)
                def _():
                    self.came(0, j, self.q, 1)

                self.hop(there, up, k, plane, self.on(plane))

        def near(self):
            for j in range(1, n):
                plane = lax.rem(z + n - j, n)

                @pl.when((z == 0) | (z == n - 1))
                def _():
                    self.came(0, j, self.q, 1)

                peer = here.at(dx=1) if self.kind == 0 else here.at(dy=1)
                self.stage(1, j, self.q, 1, self.on(plane), plane, peer)

        def far(self):
            other = self.q + 1 - 2 * (self.q % 2)
            for j in range(1, n):
                plane = self.came(1, j, other, 1)
                peer = here.at(dy=1) if self.kind == 0 else here.at(dx=1)
                self.stage(2, j, self.q // 2 * 2, 2, self.on(plane), plane, peer)

        def across(self):
            pair = self.q // 2
            other = pair + 1 - 2 * (pair % 2)
            for j in range(1, n):
                plane = self.came(2, j, other * 2, 2)
                self.stage(3, j, c * 4, 4, self.on(plane), plane, here.at(dc=1))

        def done(self):
            for j in range(1, n):
                self.came(3, j, (1 - c) * 4, 4)
            here.expect(self.on(z), local_sems.at[self.i, 1])

    weights = []
    for first, second in steps_of:
        pair = []
        for kind, (i, part, parts) in enumerate((first, second)):
            pair.append(Weight(2 * len(weights) + kind, i, part, parts, kind))
        weights.append(pair)

    def each(t, name):
        if 0 <= t < len(weights):
            for w in weights[t]:
                name(w)

    def gather_ids():
        all_ids[z, x, y, c] = ids[...]
        mine = all_ids.at[z, x, y, c]
        here.send(mine, mine, id_sems.at[0, 0], id_sems.at[0, 1], here.at(dc=1))
        here.expect(all_ids.at[z, x, y, 1 - c], id_sems.at[0, 1])
        pair = all_ids.at[z, x, y]
        here.send(pair, pair, id_sems.at[1, 0], id_sems.at[1, 1], here.at(dx=1))
        here.expect(all_ids.at[z, 1 - x, y], id_sems.at[1, 1])
        four = all_ids.at[z, :, y]
        here.send(four, four, id_sems.at[2, 0], id_sems.at[2, 1], here.at(dy=1))
        here.expect(all_ids.at[z, :, 1 - y], id_sems.at[2, 1])
        plane = all_ids.at[z]
        for j in range(1, n):
            here.send(plane, plane, id_sems.at[2 + j, 0], id_sems.at[2 + j, 1], here.at(dz=j))
        for j in range(1, n):
            here.expect(all_ids.at[lax.rem(z + n - j, n)], id_sems.at[2 + j, 1])

    def list_rows():
        lines, lanes = ids.shape
        sources = n * 8
        total = sources * lines
        rows_dev = table.shape[0]
        local = all_ids[...].reshape(total, lanes) - ((z * 2 + x) * 4 + y * 2 + c) * rows_dev
        inside = (local >= 0) & (local < rows_dev)
        flags = jnp.where(inside, 1.0, 0.0).astype(jnp.bfloat16)
        row = lax.broadcasted_iota(jnp.int32, (lanes, lanes), 0)
        col = lax.broadcasted_iota(jnp.int32, (lanes, lanes), 1)
        place = matmul(flags, jnp.where(row < col, 1.0, 0.0).astype(jnp.bfloat16))
        held = matmul(flags, jnp.ones((lanes, lanes), jnp.bfloat16)).astype(jnp.bfloat16)
        row = lax.broadcasted_iota(jnp.int32, (total, total), 0)
        col = lax.broadcasted_iota(jnp.int32, (total, total), 1)
        before = (row // lines == col // lines) & (col < row)
        place = place + matmul(jnp.where(before, 1.0, 0.0).astype(jnp.bfloat16), held)
        places[...] = jnp.where(inside, place.astype(jnp.int32), -1)
        line = lax.broadcasted_iota(jnp.int32, (total, lanes), 0)
        lane = lax.broadcasted_iota(jnp.int32, (total, lanes), 1)
        index = lax.rem(line, lines) * lanes + lane
        entries[...] = local * 256 + index // gram_count + 1
        slot = lax.broadcasted_iota(jnp.int32, (SLOTS, lanes), 0)

        def source(s, carry):
            span = pl.ds(pl.multiple_of(s * lines, lines), lines)
            where, what = places[span], entries[span]
            found = jnp.zeros((SLOTS, lanes), jnp.int32)
            for line in range(used_lines):
                hit = where[line : line + 1] == slot
                found = found + jnp.where(hit, what[line : line + 1], 0)
            lists[s] = jnp.sum(found, axis=1, keepdims=True) - 1
            return carry

        lax.fori_loop(0, sources, source, 0)

    row_iota = lax.broadcasted_iota(jnp.int32, (4 * SLOTS, table.shape[0]), 1)
    byte_iota = lax.broadcasted_iota(jnp.int32, (SLOTS, tokens), 1)

    def partial_sums(plane, core, write):
        asked = [lists[plane * 8 + place * 2 + core] for place in range(4)]
        rows = jnp.right_shift(jnp.concatenate(asked, axis=0), 8)
        pick = (rows == row_iota).astype(jnp.bfloat16)
        g_rows[...] = matmul(pick, table[...]).astype(jnp.bfloat16)
        for place in range(4):
            source = plane * 8 + place * 2 + core
            entry = lists[source]
            to_byte = (jnp.bitwise_and(entry, 255) == byte_iota).astype(jnp.bfloat16)
            sums = t_times(to_byte, g_rows[place * SLOTS : (place + 1) * SLOTS, :])
            write(place, sums)

    units = []
    for u in range(n):
        units.append(
            Reduction(
                here,
                p0.at[pl.ds(u, 1)],
                r1a.at[pl.ds(u, 1)],
                r1b.at[pl.ds(u, 1)],
                r2a.at[pl.ds(u, 1)],
                r2b.at[pl.ds(u, 1)],
                stage_sems,
                u,
            )
        )
    core_copies = [None] * n
    z_copies = [None] * n

    def plane_of(u):
        return lax.rem(z + u + 1, n)

    def hash_a(u):
        slot = u % 2
        if u >= 2:
            here.sent(core_copies[u - 2])

        def write(place, sums):
            send0[slot, place // 2, place % 2] = sums.astype(jnp.bfloat16)

        partial_sums(plane_of(u), 1 - c, write)
        core_copies[u] = here.send(
            send0.at[slot], p0.at[u], core_sems.at[u, 0], core_sems.at[u, 1], here.at(dc=1)
        )

    def hash_b(u):
        core_copies[u].wait_recv()

        def write(place, sums):
            total = sums + p0[u, place // 2, place % 2].astype(jnp.float32)
            p0[u, place // 2, place % 2] = total.astype(jnp.bfloat16)

        partial_sums(plane_of(u), c, write)
        units[u].first()

    def hash_c(u):
        units[u].second()

    def hash_d(u):
        mine = units[u].third()
        if u < n - 1:
            z_copies[u] = here.send(
                mine.at[0], r3.at[u], z_sems.at[u, 0], z_sems.at[u, 1], here.at(dz=u + 1)
            )

    def hash_e():
        for u in range(n - 1):
            z_copies[u].wait_recv()
        total = p0[n - 1, x, y].astype(jnp.float32)
        for u in range(n - 1):
            total = total + r3[u].astype(jnp.float32)
        embedded[...] = total
        for copy in core_copies[-2:] + z_copies[:-1]:
            here.sent(copy)
        for unit in units:
            for copy in (unit.s1a, unit.s1b, unit.s2a, unit.s2b):
                here.sent(copy)

    here.greet()
    lag1, lag2, lag3 = GATHER_LAGS
    for t in range(n - 1):
        each(t, Weight.along_z)
        for k in range(1, n - 1):
            if k <= t:
                each(t - k, lambda w, k=k: w.onward(k))
    gather_ids()
    list_rows()
    hash_steps = []
    for t in range(n + 3):
        group = []
        for u, stage in ((t, hash_a), (t - 1, hash_b), (t - 2, hash_c), (t - 3, hash_d)):
            if 0 <= u < n:
                group.append(lambda u=u, stage=stage: stage(u))
        hash_steps.append(group)
    hash_steps.append([hash_e])
    layer = forward_steps(
        here,
        fulls,
        embedded,
        extra_in,
        extra_out,
        [p0.at[u] for u in range(n)] + [send0.at[u] for u in range(2)],
        extra_scratch,
    )
    gather_done, runs = set(), iter(layer)
    for what, number in SCHEDULE:
        if what == HASH:
            for run in hash_steps[number]:
                run()
        elif what == GATHER:
            each(number + n - 1, Weight.along_z)
            for k in range(1, n - 1):
                each(number + n - 1 - k, lambda w, k=k: w.onward(k))
            each(number, Weight.near)
            each(number - lag1, Weight.far)
            each(number - lag1, Weight.local)
            each(number - lag2, Weight.across)
            each(number - lag3, Weight.done)
            if 0 <= number - lag3 < len(steps_of):
                gather_done |= {i for i, _, _ in steps_of[number - lag3]}
        else:
            for _ in range(number):
                needs, run = next(runs)
                assert gather_done.issuperset(needs)
                run()
    assert next(runs, None) is None
    here.finish()


def fetch(hash_ids, table, shards, extra, steps_of, dp_count):
    width = table.shape[1]
    tokens, gram_count = hash_ids.shape
    count = len(shards)
    hbm = pl.BlockSpec(memory_space=pl.ANY)
    vmem = pl.BlockSpec(memory_space=pltpu.VMEM)
    n, half = dp_count, width // 2
    low = jnp.bfloat16
    dma = pltpu.SemaphoreType.DMA
    used_lines = tokens * gram_count // 128
    lines = -(-used_lines // 8) * 8
    ids = hash_ids.reshape(used_lines, 128)
    ids = jnp.concatenate([ids, jnp.full((lines - used_lines, 128), -1, jnp.int32)])
    gathers = 2 * len(steps_of)
    ff = shards[4].shape[1]
    extra_out = list(kept_shapes(tokens, width, ff, extra[3].shape[0]))
    out_places = Kept(*[vmem] * len(extra_out))
    out_places = list(out_places._replace(gate_pre=hbm, up_pre=hbm, key_values=hbm))
    results = pl.pallas_call(
        functools.partial(fetch_kernel, n, count, steps_of, tokens, gram_count, used_lines),
        out_shape=[jax.ShapeDtypeStruct((n * w.shape[0], w.shape[1]), w.dtype) for w in shards]
        + [
            jax.ShapeDtypeStruct((tokens, width), jnp.float32),
            jax.ShapeDtypeStruct((n * 8, SLOTS, 1), jnp.int32),
        ]
        + extra_out,
        in_specs=[hbm] * count + [vmem, vmem] + [vmem] * len(extra),
        out_specs=[hbm] * count + [vmem, vmem] + out_places,
        scratch_shapes=[
            pltpu.VMEM((n, 2, 2, 2, lines, 128), jnp.int32),
            pltpu.VMEM((2, 2, 2, tokens, width), low),
            pltpu.VMEM((n, 2, 2, tokens, width), low),
            pltpu.VMEM((n, 2, tokens, half), low),
            pltpu.VMEM((n, 2, tokens, half), low),
            pltpu.VMEM((n, tokens, half), low),
            pltpu.VMEM((n, tokens, half), low),
            pltpu.VMEM((n - 1, tokens, width), low),
            pltpu.VMEM((4 * SLOTS, width), low),
            dma((n, 2)),
            dma((n, 4, 2)),
            dma((n - 1, 2)),
            dma((gathers, 2)),
            dma((gathers, 4, n - 1)),
            dma((gathers, 4, n - 1)),
            dma((gathers, 2, n - 1)),
            dma((2 + n, 2)),
            pltpu.VMEM((n * 8 * lines, 128), jnp.int32),
            pltpu.VMEM((n * 8 * lines, 128), jnp.int32),
            pltpu.VMEM((n * shards[4].shape[0], ff), low),
            pltpu.VMEM((n * shards[5].shape[0], ff), low),
            pltpu.VMEM((2, tokens, width), low),
            dma((count, max(n, ff // 256))),
            dma((2, 2)),
            pltpu.VMEM((tokens, ff), F32),
            pltpu.VMEM((tokens, ff), F32),
            pltpu.VMEM((2, 3 * tokens, width), low),
            dma((3,)),
        ],
        compiler_params=pltpu.CompilerParams(
            collective_id=0, has_side_effects=True, vmem_limit_bytes=VMEM_CAP
        ),
        name="fetch",
    )(*shards, ids, table, *extra)
    return results[:count], results[count], results[count + 1], Kept(*results[count + 2 :])


LAGS = (1, 2, 4)


class GradSums:
    def __init__(self, here, units, lefts_in, rights_in, outs, take, pool_count):
        count = len(units)
        self.here, self.units = here, units
        self.lefts_in, self.rights_in, self.outs = lefts_in, rights_in, outs
        self.lefts, self.rights = take(len(lefts_in)), take(len(rights_in))
        self.pools = take(pool_count)
        self.r1a, self.r1b, self.r2a, self.r2b, self.r3 = (take(count) for _ in range(5))
        self.left_sems, self.right_sems, self.stage_sems, self.z_sems = take(4)
        self.left_copies, self.right_copies = {}, {}
        self.sums = [None] * count
        self.using = {}
        self.mine_of = [None] * count
        self.sent_of = [None] * count

    def bring(self, source, target, sems, i, split):
        here = self.here
        copies = []
        theirs = target.at[0]
        if source is not None:
            mine = theirs = source
            if split:
                rows = target.shape[2]
                apart = source.shape[1] - rows
                mine = source.at[:, pl.ds(pl.multiple_of(here.c * apart, 16), rows)]
                theirs = source.at[:, pl.ds(pl.multiple_of((1 - here.c) * apart, 16), rows)]
            local = pltpu.make_async_copy(mine, target.at[0], sems.at[i, 0])
            local.start()
            copies.append(local.wait)
        remote = here.send(theirs, target.at[1], sems.at[i, 1], sems.at[i, 2], here.at(dc=1))
        copies.append(remote.wait_recv)
        return copies

    def left(self, i):
        if i not in self.left_copies:
            self.left_copies[i] = self.bring(
                self.lefts_in[i], self.lefts[i], self.left_sems, i, True
            )

    def right(self, i):
        if i not in self.right_copies:
            self.right_copies[i] = self.bring(
                self.rights_in[i], self.rights[i], self.right_sems, i, False
            )

    def need(self, i):
        self.left(self.units[i][0])
        self.right(self.units[i][1])

    def product(self, i):
        here, n = self.here, self.here.n
        left, right, pool, slot = self.units[i]
        self.need(i)
        for copies in (self.left_copies[left], self.right_copies[right]):
            for wait in copies:
                wait()
            copies.clear()
        for copy in self.using.get((pool, slot), []):
            here.sent(copy)
        p0 = self.pools[pool].at[slot]
        xt, g = self.lefts[left], self.rights[right]
        k, depth = xt.shape[2], xt.shape[3]
        cols = g.shape[2]
        chunks = 1 if k <= 32 else n
        planes = n // chunks
        tile = 256

        def columns(t, carry):
            span = pl.ds(pl.multiple_of(t * tile, tile), tile)
            for chunk in range(chunks):
                total = None
                for who in range(2):
                    rows = xt[who, chunk * planes * 4 : (chunk + 1) * planes * 4]
                    part = matmul(rows.reshape(planes * 4 * k, depth), g[who, :, span])
                    total = part if total is None else total + part
                p0[chunk * planes : (chunk + 1) * planes, :, :, :, span] = total.astype(
                    jnp.bfloat16
                ).reshape(planes, 2, 2, k, tile)
            return carry

        lax.fori_loop(0, cols // tile, columns, 0)
        unit = Reduction(
            here, p0, self.r1a[i], self.r1b[i], self.r2a[i], self.r2b[i], self.stage_sems, i
        )
        unit.first()
        self.sums[i] = unit
        self.using[(pool, slot)] = [unit.s1a, unit.s1b]

    def second(self, i):
        self.sums[i].second()
        self.using[self.units[i][2:]] += [self.sums[i].s2a, self.sums[i].s2b]

    def third(self, i):
        here, n = self.here, self.here.n
        mine = self.sums[i].third()
        self.sent_of[i] = []
        for j in range(1, n):
            self.sent_of[i].append(
                here.send(
                    mine.at[lax.rem(here.z + j, n)],
                    self.r3[i].at[j - 1],
                    self.z_sems.at[i, j - 1, 0],
                    self.z_sems.at[i, j - 1, 1],
                    here.at(dz=j),
                )
            )
        self.using[self.units[i][2:]] += self.sent_of[i]
        self.mine_of[i] = mine

    def final(self, i):
        total = self.mine_of[i][self.here.z].astype(jnp.float32)
        for j in range(1, self.here.n):
            self.sent_of[i][j - 1].wait_recv()
            total = total + self.r3[i][j - 1].astype(jnp.float32)
        self.outs[i][...] = total

    def move(self, t, lags):
        lag2, lag3, lag4 = lags
        count = len(self.units)
        if 0 <= t - lag2 < count:
            self.second(t - lag2)
        if 0 <= t - lag3 < count:
            self.third(t - lag3)
        if 0 <= t - lag4 < count:
            self.final(t - lag4)


def left_shape(a):
    pairs, both, depth = a.shape
    return (2, pairs, -(-(both // 2) // 16) * 16, depth)


def plan_sums(pairs, left_shapes, right_shapes, n, most):
    low = jnp.bfloat16
    dma = pltpu.SemaphoreType.DMA
    shapes, units, seen = [], [], {}
    for left, right in pairs:
        shape = (left_shapes[left][2], right_shapes[right][1])
        seen[shape] = seen.get(shape, 0) + 1
        shapes.append(shape)
    classes = list(seen)
    slots = [min(seen[s], most) for s in classes]
    used = {s: 0 for s in classes}
    for (left, right), shape in zip(pairs, shapes):
        pool = classes.index(shape)
        units.append((left, right, pool, used[shape] % slots[pool]))
        used[shape] += 1
    count = len(pairs)
    scratch = [pltpu.VMEM(shape, low) for shape in left_shapes]
    scratch += [pltpu.VMEM((2, *shape), low) for shape in right_shapes]
    scratch += [pltpu.VMEM((s, n, 2, 2, *shape), low) for s, shape in zip(slots, classes)]
    halves = [(k, cols // 2) for k, cols in shapes]
    for _ in range(2):
        scratch += [pltpu.VMEM((n, 2, *half), low) for half in halves]
    for _ in range(2):
        scratch += [pltpu.VMEM((n, *half), low) for half in halves]
    scratch += [pltpu.VMEM((n - 1, *shape), low) for shape in shapes]
    scratch += [
        dma((len(left_shapes), 3)),
        dma((len(right_shapes), 3)),
        dma((count, 4, 2)),
        dma((count, n - 1, 2)),
    ]
    return units, shapes, scratch, len(classes)


def taker(refs):
    refs = list(refs)

    def take(number):
        taken = refs[:number]
        del refs[:number]
        return taken

    return take


def last_kernel(dp_count, units, left_count, right_count, pool_count, *refs):
    n = dp_count
    count = len(units)
    take = taker(refs)
    lefts_in, rights_in = take(left_count), take(right_count)
    embed_in, gains_in, lists, rows_of = take(4)
    outs = take(count)
    gains_out, table_grad, counts, stacked_last, rows_last = take(5)
    here = Place(n)
    sums = GradSums(here, units, lefts_in, rights_in, outs, take, pool_count)
    gathered, stacked = take(2)
    gain_send, gain_recv, gain_sems, own_sem, near_sems, plane_sems = take(6)
    z, x, y, c = here.z, here.x, here.y, here.c

    here.greet()

    own = pltpu.make_async_copy(embed_in, gathered.at[z, x, y, c], own_sem)
    own.start()
    for j in range(1, n):
        here.send(
            embed_in,
            gathered.at[z, x, y, c],
            plane_sems.at[j - 1, 0],
            plane_sems.at[j - 1, 1],
            here.at(dz=j),
        )
    width = embed_in.shape[1]
    left_half, right_half = pl.ds(0, width // 2), pl.ds(width // 2, width // 2)

    def embed_near(j):
        plane = lax.rem(z + n - j, n)
        if j:
            here.expect(gathered.at[plane, x, y, c], plane_sems.at[j - 1, 1])
        else:
            own.wait()
        a = gathered.at[plane, x, y, c, :, left_half]
        b = gathered.at[plane, x, y, c, :, right_half]
        here.send(a, a, near_sems.at[j, 0, 0], near_sems.at[j, 0, 1], here.at(dx=1))
        here.send(b, b, near_sems.at[j, 1, 0], near_sems.at[j, 1, 1], here.at(dy=1))

    def embed_far(j):
        plane = lax.rem(z + n - j, n)
        here.expect(gathered.at[plane, 1 - x, y, c, :, left_half], near_sems.at[j, 0, 1])
        here.expect(gathered.at[plane, x, 1 - y, c, :, right_half], near_sems.at[j, 1, 1])
        a = gathered.at[plane, :, y, c, :, left_half]
        b = gathered.at[plane, x, :, c, :, right_half]
        here.send(a, a, near_sems.at[j, 2, 0], near_sems.at[j, 2, 1], here.at(dy=1))
        here.send(b, b, near_sems.at[j, 3, 0], near_sems.at[j, 3, 1], here.at(dx=1))

    def embed_across(j):
        plane = lax.rem(z + n - j, n)
        here.expect(gathered.at[plane, :, 1 - y, c, :, left_half], near_sems.at[j, 2, 1])
        here.expect(gathered.at[plane, 1 - x, :, c, :, right_half], near_sems.at[j, 3, 1])
        a = gathered.at[plane, :, :, c]
        here.send(a, a, near_sems.at[j, 4, 0], near_sems.at[j, 4, 1], here.at(dc=1))

    def spread(j):
        plane = lax.rem(z + n - j, n)
        here.expect(gathered.at[plane, :, :, 1 - c], near_sems.at[j, 4, 1])
        byte_iota = lax.broadcasted_iota(jnp.int32, (SLOTS, embed_in.shape[0]), 1)
        for s in range(8):
            asked = jnp.bitwise_and(lists[plane * 8 + s], 255)
            pick = (asked == byte_iota).astype(jnp.bfloat16)
            grads = gathered[plane, s // 4, s // 2 % 2, s % 2]
            target = stacked_last if j == n - 1 else stacked
            target[s * SLOTS : (s + 1) * SLOTS, :] = matmul(pick, grads).astype(jnp.bfloat16)
        if j == n - 1:
            rows_last[...] = rows_of[plane]
            return
        row_iota = lax.broadcasted_iota(jnp.int32, (table_grad.shape[0], 8 * SLOTS), 0)
        onto = (rows_of[plane] == row_iota).astype(jnp.float32)
        uses = jnp.sum(onto, axis=1, keepdims=True)
        added = matmul(onto.astype(jnp.bfloat16), stacked[...])
        if j == 0:
            counts[...] = uses
            table_grad[...] = added
        else:
            counts[...] += uses
            table_grad[...] += added

    def gains(stage):
        if stage == 0:
            gain_send[0] = gains_in[...]
        elif stage <= 3:
            here.expect(gain_recv.at[stage - 1], gain_sems.at[stage - 1, 1])
            gain_send[stage] = gain_send[stage - 1] + gain_recv[stage - 1]
        if stage < 3:
            peer = (here.at(dc=1), here.at(dx=1), here.at(dy=1))[stage]
            here.send(
                gain_send.at[stage],
                gain_recv.at[stage],
                gain_sems.at[stage, 0],
                gain_sems.at[stage, 1],
                peer,
            )
        elif stage == 3:
            for j in range(1, n):
                here.send(
                    gain_send.at[3],
                    gain_recv.at[2 + j],
                    gain_sems.at[2 + j, 0],
                    gain_sems.at[2 + j, 1],
                    here.at(dz=j),
                )
        else:
            total = gain_send[3]
            for j in range(1, n):
                here.expect(gain_recv.at[2 + j], gain_sems.at[2 + j, 1])
                total = total + gain_recv[2 + j]
            gains_out[...] = total

    for i in range(count):
        sums.need(i)
    for t in range(max(count + LAGS[2], n + 5)):
        if t < count:
            sums.product(t)
        if t == 0:
            embed_near(0)
        if 0 <= t - 1 < 5:
            gains(t - 1)
        if 1 <= t - 2 < n:
            embed_near(t - 2)
        sums.move(t, LAGS)
        if 0 <= t - 3 < n:
            embed_far(t - 3)
        if 0 <= t - 4 < n:
            embed_across(t - 4)
        if 0 <= t - 5 < n:
            spread(t - 5)
    here.finish()


def last_sums(pairs, lefts, rights, embed_low, gains, entries, rows_dev, dp_count):
    n = dp_count
    low = jnp.bfloat16
    dma = pltpu.SemaphoreType.DMA
    hbm = pl.BlockSpec(memory_space=pl.ANY)
    vmem = pl.BlockSpec(memory_space=pltpu.VMEM)
    units, shapes, scratch, pool_count = plan_sums(
        pairs, [left_shape(a) for a in lefts], [a.shape for a in rights], n, 6
    )
    count = len(pairs)
    tokens, width = embed_low.shape
    rows_of = jnp.right_shift(entries, 8).reshape(n, 1, 8 * SLOTS)
    scratch += [
        pltpu.VMEM((n, 2, 2, 2, tokens, width), low),
        pltpu.VMEM((8 * SLOTS, width), low),
        pltpu.VMEM((4, 8, width), jnp.float32),
        pltpu.VMEM((2 + n, 8, width), jnp.float32),
        dma((2 + n, 2)),
        dma,
        dma((n, 5, 2)),
        dma((n - 1, 2)),
    ]
    results = pl.pallas_call(
        functools.partial(last_kernel, n, units, len(lefts), len(rights), pool_count),
        out_shape=[jax.ShapeDtypeStruct(shape, jnp.float32) for shape in shapes]
        + [
            jax.ShapeDtypeStruct((8, width), jnp.float32),
            jax.ShapeDtypeStruct((rows_dev, width), jnp.float32),
            jax.ShapeDtypeStruct((rows_dev, 1), jnp.float32),
            jax.ShapeDtypeStruct((8 * SLOTS, width), low),
            jax.ShapeDtypeStruct((1, 8 * SLOTS), jnp.int32),
        ],
        in_specs=[hbm] * (len(lefts) + len(rights)) + [vmem] * 4,
        out_specs=[vmem] * (count + 5),
        scratch_shapes=scratch,
        compiler_params=pltpu.CompilerParams(
            collective_id=2, has_side_effects=True, vmem_limit_bytes=VMEM_CAP
        ),
        name="last_sums",
    )(*lefts, *rights, embed_low, gains, entries, rows_of)
    return results[:count], *results[count:]


BACK_PAIRS = ((4, 8), (3, 6), (3, 7), (2, 5), (1, 4), (0, 0), (0, 1), (0, 2), (0, 3))


class Streamed(typing.NamedTuple):
    gate_pre: typing.Any
    up_pre: typing.Any
    h_out: typing.Any
    h_mid: typing.Any
    embedded: typing.Any
    key_values: typing.Any
    w_query: typing.Any
    w_key: typing.Any
    w_value: typing.Any
    w_out: typing.Any
    w_gate: typing.Any
    w_up: typing.Any
    w_down: typing.Any
    c_query: typing.Any
    c_key: typing.Any
    c_value: typing.Any
    c_out: typing.Any
    cot_patches: typing.Any


def back_kernel(dp_count, units, pool_count, *refs):
    n = dp_count
    take = taker(refs)
    lefts_in = take(5)
    hbm = Streamed(*take(len(Streamed._fields)))
    (cot_bytes, p_query, p_key, p_value, cross_lse, gains, starts, ends, queries, lse) = take(10)
    outs = take(len(units))
    grad_gains, g_attn, g_query, g_key, g_value, g_embed = take(6)
    here = Place(n)
    sums = GradSums(here, units, lefts_in, [None] * 8 + [hbm.cot_patches], outs, take, pool_count)
    w, tile_pre, grad_out, grad_ffn, grad_mid, kv, halo = take(7)
    w_sems, tile_sems, pre_sems, kv_sems, halo_sems = take(5)
    g_gate = [sums.rights[0].at[0], sums.rights[2].at[0]]
    g_up = [sums.rights[1].at[0], sums.rights[3].at[0]]
    g_branch, g_pquery, g_pkey, g_pvalue, cot_patches = [ref.at[0] for ref in sums.rights[4:]]
    tokens, width = cot_bytes.shape
    patches = p_query.shape[0]
    tile = 256
    first_tiles = g_gate[0].shape[1] // tile
    tiles = first_tiles + g_gate[1].shape[1] // tile
    rank = (here.x * 2 + here.y) * 2 + here.c
    lane = lax.broadcasted_iota(jnp.int32, (1, 128), 1)
    sides = [jnp.where(lane < HD, 1.0, 0.0).astype(LOW), jnp.where(lane < HD, 0.0, 1.0).astype(LOW)]
    byte_pos = lax.broadcasted_iota(jnp.int32, (patches, tokens), 1)

    here.greet()

    def load_w(slot, source):
        copy = pltpu.make_async_copy(source, w.at[slot], w_sems.at[slot])
        copy.start()
        return copy

    def load_pre(source):
        copies = []
        for b in range(width // tile):
            copy = pltpu.make_async_copy(
                source.at[:, pl.ds(b * tile, tile)],
                tile_pre.at[b // 2, b % 2],
                pre_sems.at[b],
            )
            copy.start()
            copies.append(copy)
        return copies

    def pre_rows(copies):
        for copy in copies:
            copy.wait()
        return jnp.concatenate([tile_pre[b // 2, b % 2] for b in range(width // tile)], axis=1)

    for i in (4, 3, 2, 1, 0):
        sums.left(i)
    sums.right(8)
    cross = [load_w(i, a) for i, a in enumerate((hbm.c_out, hbm.c_query, hbm.c_key, hbm.c_value))]
    h_out_copies = load_pre(hbm.h_out)

    def tile_copies(t):
        slot = lax.rem(t, 2)
        span = pl.ds(pl.multiple_of(t * tile, tile), tile)
        return [
            pltpu.make_async_copy(source, target, tile_sems.at[slot, k])
            for k, (source, target) in enumerate(
                (
                    (hbm.w_gate.at[:, span], w.at[slot, :, pl.ds(0, tile)]),
                    (hbm.w_up.at[:, span], w.at[slot, :, pl.ds(tile, tile)]),
                    (hbm.w_down.at[span], w.at[2, pl.ds(pl.multiple_of(slot * tile, tile), tile)]),
                    (hbm.gate_pre.at[:, span], tile_pre.at[slot, 0]),
                    (hbm.up_pre.at[:, span], tile_pre.at[slot, 1]),
                )
            )
        ]

    def member():
        return (byte_pos >= starts[...]) & (byte_pos < ends[...])

    def head_lse(ref, head):
        return jnp.sum(jnp.where(lane == head, ref[...], 0.0), axis=1, keepdims=True)

    def cross_heads():
        cross[0].wait()
        allowed = member()
        grad_ffn[:patches] = times_t(cot_patches[...], w[0]).astype(LOW).astype(F32)

        def heads_pair(pair, carry):
            span = pl.ds(pl.multiple_of(pair * 128, 128), 128)
            q2, k2, v2 = p_query[:, span], p_key[:, span], p_value[:, span]
            gp2 = grad_ffn[:patches, span].astype(LOW)
            parts = []
            for side in range(2):
                total = head_lse(cross_lse, pair * 2 + side)
                scores = times_t(q2 * sides[side], k2) * SCORE_SCALE
                probs = jnp.where(allowed, jnp.exp(jnp.where(allowed, scores, total) - total), 0.0)
                grad_score = soft_back(probs, times_t(gp2 * sides[side], v2))
                parts.append(
                    (
                        matmul(grad_score, k2),
                        t_times(grad_score, q2),
                        t_times(probs.astype(LOW), gp2),
                    )
                )
            mine = lane < HD
            g_pquery[:, span] = (jnp.where(mine, parts[0][0], parts[1][0]) * SCORE_SCALE).astype(LOW)
            g_pkey[:, span] = (jnp.where(mine, parts[0][1], parts[1][1]) * SCORE_SCALE).astype(LOW)
            g_pvalue[:, span] = jnp.where(mine, parts[0][2], parts[1][2]).astype(LOW)
            return carry

        lax.fori_loop(0, width // 128, heads_pair, 0)
        for i in (5, 6, 7):
            sums.right(i)

    def split(v):
        high = v.astype(LOW)
        return high, (v - high.astype(F32)).astype(LOW)

    def unit_of(v):
        inv_rms = lax.rsqrt(jnp.mean(v * v, axis=-1, keepdims=True) + EPSILON)
        return v * inv_rms, inv_rms

    def through_norm(grad, rows, number):
        normed, inv_rms = unit_of(rows)
        grad_in, grad_gain = norm_back(
            grad.astype(LOW).astype(F32), normed, inv_rms, gains[number : number + 1]
        )
        grad_gains[number : number + 1] = grad_gain[None]
        return grad_in

    loaded = {}

    def cross_in():
        for copy in cross[1:]:
            copy.wait()
        length = (ends[...] - starts[...]).astype(F32)
        grad_pooled = cot_patches[...].astype(F32) + times_t(g_pquery[...], w[1]).astype(
            LOW
        ).astype(F32)
        high, rest = split(grad_pooled / length)
        inside = jnp.where(member(), 1.0, 0.0).astype(LOW)
        grad_x = t_times(inside, high) + t_times(inside, rest)
        grad_x = grad_x + times_t(g_pkey[...], w[2]) + times_t(g_pvalue[...], w[3])
        grad_gains[...] = jnp.zeros_like(grad_gains)
        total = cot_bytes[...].astype(F32) + through_norm(grad_x, pre_rows(h_out_copies), 2)
        grad_out[...] = total
        g_branch[...] = total.astype(LOW)
        grad_ffn[...] = jnp.zeros_like(grad_ffn)
        sums.right(4)
        loaded[3] = load_w(3, hbm.w_out)

    def feed(part):
        first, last = ((0, first_tiles), (first_tiles, tiles))[part]
        for copy in tile_copies(first):
            copy.start()

        def one(t, carry):
            slot = lax.rem(t, 2)
            for copy in tile_copies(t):
                copy.wait()

            @pl.when(t + 1 < last)
            def _():
                for copy in tile_copies(t + 1):
                    copy.start()

            span = pl.ds(pl.multiple_of((t - first) * tile, tile), tile)
            down_rows = w[2, pl.ds(pl.multiple_of(slot * tile, tile), tile)]
            grad_hidden = times_t(g_branch[...], down_rows).astype(LOW).astype(F32)
            gate, up = tile_pre[slot, 0], tile_pre[slot, 1]
            sig = jax.nn.sigmoid(gate)
            gg = (grad_hidden * up * sig * (1.0 + gate * (1.0 - sig))).astype(LOW)
            gu = (grad_hidden * (gate * sig)).astype(LOW)
            g_gate[part][:, span] = gg
            g_up[part][:, span] = gu
            grad_ffn[...] += times_t(gg, w[slot, :, :tile]) + times_t(
                gu, w[slot, :, tile : 2 * tile]
            )
            return carry

        lax.fori_loop(first, last, one, 0)
        sums.right(2 * part)
        sums.right(2 * part + 1)

    def feed_in():
        copies = load_pre(hbm.h_mid)
        loaded[3].wait()
        grad_mid[...] = grad_out[...] + through_norm(grad_ffn[...], pre_rows(copies), 1)
        g_attn[...] = grad_mid[...].astype(LOW)
        g_query[...] = times_t(g_attn[...], w[3]).astype(LOW)
        loaded[1] = load_w(1, hbm.w_query)
        loaded[2] = load_w(2, hbm.w_key)
        loaded[3] = load_w(3, hbm.w_value)
        loaded[0] = load_pre(hbm.embedded)

    own_key, own_value = grad_ffn, grad_out
    sent = w.at[0]

    def kv_copy(pair):
        slot = lax.rem(pair, 2)
        span = pl.ds(pl.multiple_of(pair * 128, 128), 128)
        return pltpu.make_async_copy(hbm.key_values.at[:, :, span], kv.at[slot], kv_sems.at[slot])

    def attend(first, last):
        row = lax.broadcasted_iota(jnp.int32, (tokens, tokens), 0)
        col = lax.broadcasted_iota(jnp.int32, (tokens, tokens), 1)
        mine = col <= row
        far_bias = jnp.where(rank >= 2, 0.0, NEG_BIG)
        near_bias = jnp.where(rank >= 1, 0.0, NEG_BIG)
        kv_copy(first).start()

        def three(edge, middle):
            return jnp.concatenate(
                [
                    jnp.where(mine, 0.0, edge).astype(LOW),
                    middle.astype(LOW),
                    jnp.where(mine, edge, 0.0).astype(LOW),
                ],
                axis=1,
            )

        def heads_pair(pair, carry):
            kv_copy(pair).wait()

            @pl.when(pair + 1 < last)
            def _():
                kv_copy(pair + 1).start()

            slot = lax.rem(pair, 2)
            span = pl.ds(pl.multiple_of(pair * 128, 128), 128)
            q2, ga2 = queries[:, span], g_query[:, span]
            k2, v2 = kv[slot, 0], kv[slot, 1]
            parts = []
            for side in range(2):
                total = head_lse(lse, pair * 2 + side)
                scores = times_t(q2 * sides[side], k2) * SCORE_SCALE
                edge = jnp.where(mine, scores[:, 2 * tokens :], scores[:, :tokens] + far_bias)
                edge = jnp.exp(edge - total)
                middle = jnp.exp(scores[:, tokens : 2 * tokens] + near_bias - total)
                grad_prob = times_t(ga2 * sides[side], v2)
                grad_edge = jnp.where(mine, grad_prob[:, 2 * tokens :], grad_prob[:, :tokens])
                grad_middle = grad_prob[:, tokens : 2 * tokens]
                row_total = jnp.sum(edge * grad_edge, axis=1, keepdims=True) + jnp.sum(
                    middle * grad_middle, axis=1, keepdims=True
                )
                grad_score = three(edge * (grad_edge - row_total), middle * (grad_middle - row_total))
                parts.append(
                    (
                        matmul(grad_score, k2),
                        t_times(grad_score, q2),
                        t_times(three(edge, middle), ga2),
                    )
                )
            left = lane < HD
            g_query[:, span] = (jnp.where(left, parts[0][0], parts[1][0]) * SCORE_SCALE).astype(LOW)
            for number, own, scale in ((1, own_key, SCORE_SCALE), (2, own_value, 1.0)):
                grad = jnp.where(left, parts[0][number], parts[1][number]) * scale
                own[:, span] = grad[2 * tokens :]
                start = (number - 1) * 2 * tokens
                sent[start : start + 2 * tokens, span] = grad[: 2 * tokens].astype(LOW)
            return carry

        lax.fori_loop(first, last, heads_pair, 0)

    there = rank >= 2

    def part_of(number, back, span):
        return sent.at[pl.ds((2 * number + 2 - back) * tokens, tokens), span]

    def halo_parts(half):
        span = pl.ds(half * (width // 2), width // 2)
        return [(number, span, 2 * number + half) for number in range(2)]

    def halo_pair(half):
        for number, span, sem in halo_parts(half):
            here.send_if(
                there | (here.c == 1),
                part_of(number, 1, span),
                halo.at[1, number, :, span],
                halo_sems.at[1, sem, 0],
                halo_sems.at[1, sem, 1],
                here.at(dc=1),
            )

    def halo_send(half):
        for number, span, sem in halo_parts(half):

            @pl.when(there | (here.c == 0))
            def _():
                here.expect(halo.at[1, number, :, span], halo_sems.at[1, sem, 1])

            part = part_of(number, 2, span)

            @pl.when(there & (here.c == 1))
            def _():
                added = part[...].astype(F32) + halo[1, number, :, span].astype(F32)
                part[...] = added.astype(LOW)

            target = jnp.maximum(rank - 2, 0)
            here.send_if(
                there,
                part,
                halo.at[0, number, :, span],
                halo_sems.at[0, sem, 0],
                halo_sems.at[0, sem, 1],
                (here.z, target // 4, lax.rem(target, 4)),
            )

    def halo_add():
        for number, own, grad in ((0, own_key, g_key), (1, own_value, g_value)):

            @pl.when(here.c == 0)
            def _():
                own[...] += halo[1, number].astype(F32)

            @pl.when(rank + 2 < 8)
            def _():
                for half in range(2):
                    _, span, sem = halo_parts(half)[number]
                    here.expect(halo.at[0, number, :, span], halo_sems.at[0, sem, 1])
                own[...] += halo[0, number].astype(F32)

            grad[...] = own[...].astype(LOW)

    def embed_in():
        for slot in (1, 2, 3):
            loaded[slot].wait()
        grad = times_t(g_query[...], w[1]) + times_t(g_key[...], w[2]) + times_t(g_value[...], w[3])
        total = grad_mid[...] + through_norm(grad, pre_rows(loaded[0]), 0)
        g_embed[...] = total.astype(LOW)

    sums.product(0)
    cross_heads()
    sums.product(1)
    sums.product(2)
    sums.product(3)
    cross_in()
    sums.second(0)
    sums.product(4)
    sums.second(1)
    feed(0)
    sums.product(5)
    sums.product(6)
    sums.second(2)
    sums.third(0)
    feed(1)
    sums.product(7)
    sums.product(8)
    sums.second(3)
    sums.third(1)
    feed_in()
    sums.second(4)
    sums.third(2)
    pairs = width // 128
    quarter = pairs // 4
    attend(0, quarter)
    sums.second(5)
    sums.third(3)
    sums.third(4)
    attend(quarter, 2 * quarter)
    halo_pair(0)
    halo_send(0)
    sums.second(6)
    sums.third(5)
    attend(2 * quarter, 3 * quarter)
    sums.second(7)
    sums.third(6)
    attend(3 * quarter, pairs)
    halo_pair(1)
    halo_send(1)
    sums.second(8)
    sums.third(7)
    for i in range(4):
        sums.final(i)
    halo_add()
    sums.third(8)
    embed_in()
    for i in range(4, 9):
        sums.final(i)
    here.finish()


def back_sums(lefts, streamed, kept, dp_count):
    n = dp_count
    low = jnp.bfloat16
    dma = pltpu.SemaphoreType.DMA
    hbm = pl.BlockSpec(memory_space=pl.ANY)
    vmem = pl.BlockSpec(memory_space=pltpu.VMEM)
    tokens, ff = streamed.gate_pre.shape
    patches, width = streamed.cot_patches.shape
    tile = 256
    first = (ff // tile + 1) // 2 * tile
    one = jax.ShapeDtypeStruct
    right_shapes = [(tokens, first)] * 2 + [(tokens, ff - first)] * 2
    right_shapes += [(tokens, width), (patches, width)]
    right_shapes += [(tokens, width)] * 2 + [(patches, width)]
    units, shapes, scratch, pool_count = plan_sums(
        BACK_PAIRS, [left_shape(a) for a in lefts], right_shapes, n, 4
    )
    count = len(units)
    scratch += [
        pltpu.VMEM((4, width, width), low),
        pltpu.VMEM((2, 2, tokens, tile), F32),
        pltpu.VMEM((tokens, width), F32),
        pltpu.VMEM((tokens, width), F32),
        pltpu.VMEM((tokens, width), F32),
        pltpu.VMEM((2, 2, 3 * tokens, 128), low),
        pltpu.VMEM((2, 2, tokens, width), low),
        dma((4,)),
        dma((2, 5)),
        dma((width // tile,)),
        dma((2,)),
        dma((2, 4, 2)),
    ]
    results = pl.pallas_call(
        functools.partial(back_kernel, n, units, pool_count),
        out_shape=[one(shape, F32) for shape in shapes]
        + [one((8, width), F32)]
        + [one((tokens, width), low)] * 5,
        in_specs=[hbm] * (len(lefts) + len(streamed)) + [vmem] * len(kept),
        out_specs=[vmem] * (count + 6),
        scratch_shapes=scratch,
        compiler_params=pltpu.CompilerParams(
            collective_id=1, has_side_effects=True, vmem_limit_bytes=63 * 1024 * 1024
        ),
        name="back_sums",
    )(*lefts, *streamed, *kept)
    return results[:count], results[count:]


def finish_kernel(cuts, rows, stacked, table_in, counts_in, *refs):
    wholes, refs = refs[: len(cuts)], list(refs[len(cuts) :])
    halves = [refs.pop(0) for _ in range(4)]
    table, counts = refs.pop(0), refs.pop(0)
    row = lax.broadcasted_iota(jnp.int32, (table.shape[0], rows.shape[1]), 0)
    onto = (rows[...] == row + pl.program_id(0) * table.shape[0]).astype(jnp.float32)
    counts[...] = (counts_in[...] + jnp.sum(onto, axis=1, keepdims=True)).astype(jnp.int32)
    table[...] = table_in[...] + matmul(onto.astype(jnp.bfloat16), stacked[...])

    @pl.when(pl.program_id(0) == 0)
    def _():
        core = lax.axis_index(SUB) % 2
        for cut, source, target in zip(cuts, wholes, refs):
            if cut == source.shape[0]:
                target[...] = source[...]
            else:
                target[...] = jnp.where(core == 0, source[:cut], source[source.shape[0] - cut :])
        for k in range(2):
            left, right = halves[k], halves[2 + k]
            target = refs[len(cuts) + k]
            target[:, : left.shape[1]] = left[...]
            target[:, left.shape[1] :] = right[...]


def finish(table_grad, counts, stacked, rows, wholes, cuts, halves):
    rows_dev, width = table_grad.shape
    block = 512
    one = jax.ShapeDtypeStruct

    def whole(shape):
        return pl.BlockSpec(shape, lambda i: (0, 0))

    def blocks(cols):
        return pl.BlockSpec((block, cols), lambda i: (i, 0))

    shapes = [(cut, a.shape[1]) for a, cut in zip(wholes, cuts)]
    shapes += [(a.shape[0], a.shape[1] + b.shape[1]) for a, b in zip(halves[:2], halves[2:])]
    return pl.pallas_call(
        functools.partial(finish_kernel, cuts),
        grid=(-(-rows_dev // block),),
        out_shape=[one((rows_dev, width), F32), one((rows_dev, 1), jnp.int32)]
        + [one(shape, F32) for shape in shapes],
        in_specs=[whole(rows.shape), whole(stacked.shape), blocks(width), blocks(1)]
        + [whole(a.shape) for a in (*wholes, *halves)],
        out_specs=[blocks(width), blocks(1)] + [whole(shape) for shape in shapes],
        compiler_params=pltpu.CompilerParams(vmem_limit_bytes=VMEM_CAP),
        name="finish",
    )(rows, stacked, table_grad, counts, *wholes, *halves)


WEIGHT_STEPS = tuple(((i, 0, 2), (i, 1, 2)) for i in (0, 1, 2, 3, 4, 5, 6, 8, 9, 7, 10))


def by_rows(a, dp_count):
    depth, total = a.shape
    return a.T.reshape(dp_count * 4, total // (dp_count * 4), depth)


def body(
    byte_ids,
    hash_ids,
    lengths,
    byte_table,
    hash_table,
    norm_attn,
    norm_ffn,
    norm_cross,
    w_query,
    w_key,
    w_value,
    w_out,
    w_gate,
    w_up,
    w_down,
    c_query,
    c_key,
    c_value,
    c_out,
    cot_bytes,
    cot_patches,
):
    dp_count = lax.axis_size(DP)
    rs_count = lax.axis_size(SEQ)
    all_count = dp_count * rs_count
    rank_seq = lax.axis_index(SEQ)
    rank_table = lax.axis_index(DP) * rs_count + rank_seq
    tokens, gram_count = hash_ids.shape
    rows_dev, model_width = hash_table.shape
    head_count = model_width // HD
    request_count = tokens * gram_count
    slot_count = 2 * request_count // all_count
    flat_ids = hash_ids.reshape(request_count)
    owners = flat_ids // rows_dev
    ordering = jnp.argsort(owners, stable=True)
    owners_sorted = owners[ordering]
    per_owner = jnp.sum(
        (owners[:, None] == jnp.arange(all_count, dtype=jnp.int32)[None, :]).astype(jnp.int32),
        axis=0,
    )
    first_slot = jnp.cumsum(per_owner) - per_owner
    place_sorted = (
        owners_sorted * slot_count
        + jnp.arange(request_count, dtype=jnp.int32)
        - first_slot[owners_sorted]
    )
    placement = jnp.zeros((request_count,), jnp.int32).at[ordering].set(place_sorted)
    requests = jnp.full((all_count * slot_count,), -1, jnp.int32).at[placement].set(flat_ids)
    requests = requests.reshape(dp_count, rs_count, slot_count)
    incoming = lax.all_to_all(
        lax.all_to_all(requests, DP, split_axis=0, concat_axis=0, tiled=True),
        SEQ,
        split_axis=1,
        concat_axis=1,
        tiled=True,
    )
    present = incoming >= 0
    safe_rows = jnp.where(present, incoming - rank_table * rows_dev, 0)
    served = jnp.where(present[..., None], hash_table[safe_rows], jnp.zeros((), jnp.bfloat16))
    returned = lax.all_to_all(
        lax.all_to_all(served, DP, split_axis=0, concat_axis=0, tiled=True),
        SEQ,
        split_axis=1,
        concat_axis=1,
        tiled=True,
    )
    fetched = returned.reshape(all_count * slot_count, model_width)[placement]
    fetched = fetched.astype(jnp.float32).reshape(tokens, gram_count, model_width)
    one_hot = byte_ids[:, None] == jnp.arange(BYTE_VALUES, dtype=jnp.int32)[None, :]
    embedded = matmul(one_hot.astype(jnp.bfloat16), byte_table) + jnp.sum(fetched, axis=1)
    row_counts = (
        jnp.zeros((rows_dev,), jnp.int32)
        .at[safe_rows.reshape(-1)]
        .add(present.reshape(-1).astype(jnp.int32))
    )
    weight_list = (
        w_query,
        w_key,
        w_value,
        w_out,
        w_gate,
        w_up,
        w_down,
        c_query,
        c_key,
        c_value,
        c_out,
    )
    gathered = (
        lax.all_gather(weight_list[0], DP, axis=0, tiled=True),
        lax.all_gather(weight_list[1], DP, axis=0, tiled=True),
        lax.all_gather(weight_list[2], DP, axis=0, tiled=True),
        lax.all_gather(weight_list[3], DP, axis=0, tiled=True),
        lax.all_gather(weight_list[4], DP, axis=0, tiled=True),
        lax.all_gather(weight_list[5], DP, axis=0, tiled=True),
        lax.all_gather(weight_list[6], DP, axis=0, tiled=True),
        lax.all_gather(weight_list[7], DP, axis=0, tiled=True),
        lax.all_gather(weight_list[8], DP, axis=0, tiled=True),
        lax.all_gather(weight_list[9], DP, axis=0, tiled=True),
        lax.all_gather(weight_list[10], DP, axis=0, tiled=True),
    )
    (
        full_query,
        full_key,
        full_value,
        full_out,
        full_gate,
        full_up,
        full_down,
        full_cquery,
        full_ckey,
        full_cvalue,
        full_cout,
    ) = gathered
    x_attn, normed_attn, scale_attn = normalize(embedded, norm_attn)
    queries = matmul(x_attn, full_query).astype(jnp.bfloat16).reshape(tokens, head_count, HD)
    key_rows = matmul(x_attn, full_key).astype(jnp.bfloat16).reshape(tokens, head_count, HD)
    value_rows = matmul(x_attn, full_value).astype(jnp.bfloat16).reshape(tokens, head_count, HD)
    behind = (WIN - 2) // tokens + 1
    key_parts = []
    value_parts = []
    for offset_back in range(behind, 0, -1):
        far_keys, far_values = passed_along((key_rows, value_rows), SEQ, offset_back)
        key_parts.append(far_keys)
        value_parts.append(far_values)
    all_keys = jnp.concatenate(key_parts + [key_rows], axis=0)
    all_values = jnp.concatenate(value_parts + [value_rows], axis=0)
    q_rows = min(tokens, 512)
    key_span = (WIN - 1 + q_rows - 1) // q_rows * q_rows
    base_key = (rank_seq - behind) * tokens
    block_index = 0
    q_start = block_index * q_rows
    k_start = behind * tokens + q_start - key_span
    allowed = window_mask(
        rank_seq * tokens + q_start, base_key + k_start, q_rows, q_rows + key_span
    )
    scores = (
        jnp.einsum("qhd,khd->hqk", queries, all_keys, preferred_element_type=jnp.float32)
        * SCORE_SCALE
    )
    prob_block, log_total = soft_forward(scores, allowed)
    attended_parts = jnp.einsum(
        "hqk,khd->qhd",
        prob_block.astype(jnp.bfloat16),
        all_values,
        preferred_element_type=jnp.float32,
    )
    lse_parts = [log_total]
    attended = attended_parts.astype(jnp.bfloat16).reshape(tokens, model_width)
    h_mid = embedded + matmul(attended, full_out)
    x_ffn, normed_ffn, scale_ffn = normalize(h_mid, norm_ffn)
    gate_pre = matmul(x_ffn, full_gate)
    up_pre = matmul(x_ffn, full_up)
    gate_sig = jax.nn.sigmoid(gate_pre)
    silu_val = gate_pre * gate_sig
    hidden = (silu_val * up_pre).astype(jnp.bfloat16)
    h_out = h_mid + matmul(hidden, full_down)
    byte_states = h_out.astype(jnp.bfloat16)
    x_cross, normed_cross, scale_cross = normalize(h_out, norm_cross)
    patch_len = lengths[0]
    patch_count = patch_len.shape[0]
    patch_end = jnp.cumsum(patch_len)
    patch_start = patch_end - patch_len
    byte_pos = jnp.arange(tokens, dtype=jnp.int32)
    member = (byte_pos[None, :] >= patch_start[:, None]) & (byte_pos[None, :] < patch_end[:, None])
    length_f = patch_len.astype(jnp.float32)[:, None]
    pooled = matmul(member.astype(jnp.bfloat16), x_cross) / length_f
    pooled_low = pooled.astype(jnp.bfloat16)
    p_query = (
        matmul(pooled_low, full_cquery).astype(jnp.bfloat16).reshape(patch_count, head_count, HD)
    )
    p_key = matmul(x_cross, full_ckey).astype(jnp.bfloat16).reshape(tokens, head_count, HD)
    p_value = matmul(x_cross, full_cvalue).astype(jnp.bfloat16).reshape(tokens, head_count, HD)
    cross_scores = (
        jnp.einsum("phd,thd->hpt", p_query, p_key, preferred_element_type=jnp.float32) * SCORE_SCALE
    )
    cross_prob, cross_lse = soft_forward(cross_scores, member[None])
    p_attended = (
        jnp.einsum(
            "hpt,thd->phd",
            cross_prob.astype(jnp.bfloat16),
            p_value,
            preferred_element_type=jnp.float32,
        )
        .astype(jnp.bfloat16)
        .reshape(patch_count, model_width)
    )
    patch_states = (pooled + matmul(p_attended, full_cout)).astype(jnp.bfloat16)
    grad_c_out = t_times(p_attended, cot_patches)
    grad_patt = (
        times_t(cot_patches, full_cout).astype(jnp.bfloat16).reshape(patch_count, head_count, HD)
    )
    cross_again = (
        jnp.einsum("phd,thd->hpt", p_query, p_key, preferred_element_type=jnp.float32) * SCORE_SCALE
    )
    cross_full = soft_again(cross_again, member[None], cross_lse)
    grad_cprob = jnp.einsum("phd,thd->hpt", grad_patt, p_value, preferred_element_type=jnp.float32)
    grad_cscore = soft_back(cross_full, grad_cprob)
    grad_pquery = (
        (
            jnp.einsum("hpt,thd->phd", grad_cscore, p_key, preferred_element_type=jnp.float32)
            * SCORE_SCALE
        )
        .astype(jnp.bfloat16)
        .reshape(patch_count, model_width)
    )
    grad_pkey = (
        (
            jnp.einsum("hpt,phd->thd", grad_cscore, p_query, preferred_element_type=jnp.float32)
            * SCORE_SCALE
        )
        .astype(jnp.bfloat16)
        .reshape(tokens, model_width)
    )
    grad_pvalue = (
        jnp.einsum(
            "hpt,phd->thd",
            cross_full.astype(jnp.bfloat16),
            grad_patt,
            preferred_element_type=jnp.float32,
        )
        .astype(jnp.bfloat16)
        .reshape(tokens, model_width)
    )
    grad_c_query = t_times(pooled_low, grad_pquery)
    grad_c_key = t_times(x_cross, grad_pkey)
    grad_c_value = t_times(x_cross, grad_pvalue)
    grad_pooled = cot_patches.astype(jnp.float32) + times_t(grad_pquery, full_cquery).astype(
        jnp.bfloat16
    ).astype(jnp.float32)
    to_bytes = lax.dot_general(
        member.astype(jnp.float32),
        grad_pooled / length_f,
        (((0,), (0,)), ((), ())),
        precision=PRECISE,
    )
    grad_xcross = (
        times_t(grad_pkey, full_ckey) + times_t(grad_pvalue, full_cvalue) + to_bytes
    ).astype(jnp.bfloat16)
    grad_hout_norm, grad_norm_cross = norm_back(
        grad_xcross.astype(jnp.float32), normed_cross, scale_cross, norm_cross
    )
    grad_hout = cot_bytes.astype(jnp.float32) + grad_hout_norm
    grad_branch_f = grad_hout.astype(jnp.bfloat16)
    grad_w_down = t_times(hidden, grad_branch_f)
    grad_hidden = times_t(grad_branch_f, full_down).astype(jnp.bfloat16).astype(jnp.float32)
    grad_gate = (grad_hidden * up_pre * gate_sig * (1.0 + gate_pre * (1.0 - gate_sig))).astype(
        jnp.bfloat16
    )
    grad_up = (grad_hidden * silu_val).astype(jnp.bfloat16)
    grad_w_gate = t_times(x_ffn, grad_gate)
    grad_w_up = t_times(x_ffn, grad_up)
    grad_xffn = (times_t(grad_gate, full_gate) + times_t(grad_up, full_up)).astype(jnp.bfloat16)
    grad_hmid_norm, grad_norm_ffn = norm_back(
        grad_xffn.astype(jnp.float32), normed_ffn, scale_ffn, norm_ffn
    )
    grad_hmid = grad_hout + grad_hmid_norm
    grad_branch_a = grad_hmid.astype(jnp.bfloat16)
    grad_w_out = t_times(attended, grad_branch_a)
    grad_att = times_t(grad_branch_a, full_out).astype(jnp.bfloat16).reshape(tokens, head_count, HD)
    grad_keys_all = jnp.zeros(((behind + 1) * tokens, head_count, HD), jnp.float32)
    grad_values_all = jnp.zeros(((behind + 1) * tokens, head_count, HD), jnp.float32)
    block_index = 0
    q_start = block_index * q_rows
    k_start = behind * tokens + q_start - key_span
    k_stop = k_start + q_rows + key_span
    allowed = window_mask(
        rank_seq * tokens + q_start, base_key + k_start, q_rows, q_rows + key_span
    )
    scores = (
        jnp.einsum("qhd,khd->hqk", queries, all_keys, preferred_element_type=jnp.float32)
        * SCORE_SCALE
    )
    prob_block = soft_again(scores, allowed, lse_parts[block_index])
    grad_prob = jnp.einsum("qhd,khd->hqk", grad_att, all_values, preferred_element_type=jnp.float32)
    grad_score = soft_back(prob_block, grad_prob)
    grad_q_parts = (
        jnp.einsum("hqk,khd->qhd", grad_score, all_keys, preferred_element_type=jnp.float32)
        * SCORE_SCALE
    )
    grad_keys_all = grad_keys_all.at[k_start:k_stop].add(
        jnp.einsum("hqk,qhd->khd", grad_score, queries, preferred_element_type=jnp.float32)
        * SCORE_SCALE
    )
    grad_values_all = grad_values_all.at[k_start:k_stop].add(
        jnp.einsum(
            "hqk,qhd->khd",
            prob_block.astype(jnp.bfloat16),
            grad_att,
            preferred_element_type=jnp.float32,
        )
    )
    grad_keys = grad_keys_all[behind * tokens :]
    grad_values = grad_values_all[behind * tokens :]
    for offset_back in range(behind, 0, -1):
        part_index = behind - offset_back
        far_grad_k, far_grad_v = (
            passed_along(
                grad_keys_all[part_index * tokens : (part_index + 1) * tokens].astype(jnp.bfloat16),
                SEQ,
                -offset_back,
            ).astype(jnp.float32),
            passed_along(
                grad_values_all[part_index * tokens : (part_index + 1) * tokens].astype(
                    jnp.bfloat16
                ),
                SEQ,
                -offset_back,
            ).astype(jnp.float32),
        )
        grad_keys = grad_keys + far_grad_k
        grad_values = grad_values + far_grad_v
    grad_queries = grad_q_parts.astype(jnp.bfloat16).reshape(tokens, model_width)
    grad_keys_low = grad_keys.astype(jnp.bfloat16).reshape(tokens, model_width)
    grad_values_low = grad_values.astype(jnp.bfloat16).reshape(tokens, model_width)
    grad_w_query = t_times(x_attn, grad_queries)
    grad_w_key = t_times(x_attn, grad_keys_low)
    grad_w_value = t_times(x_attn, grad_values_low)
    grad_xattn = (
        times_t(grad_queries, full_query)
        + times_t(grad_keys_low, full_key)
        + times_t(grad_values_low, full_value)
    ).astype(jnp.bfloat16)
    grad_embed_norm, grad_norm_attn = norm_back(
        grad_xattn.astype(jnp.float32), normed_attn, scale_attn, norm_attn
    )
    grad_embed = grad_hmid + grad_embed_norm
    embed_grad = grad_embed.astype(jnp.bfloat16)
    grad_byte_table = lax.dot_general(
        one_hot.astype(jnp.float32), grad_embed, (((0,), (0,)), ((), ())), precision=PRECISE
    )
    per_request = jnp.broadcast_to(
        grad_embed[:, None, :], (tokens, gram_count, model_width)
    ).reshape(request_count, model_width)
    outgoing = (
        jnp.zeros((all_count * slot_count, model_width), jnp.float32).at[placement].set(per_request)
    )
    outgoing = outgoing.reshape(dp_count, rs_count, slot_count, model_width)
    arrived = lax.all_to_all(
        lax.all_to_all(
            outgoing.astype(jnp.bfloat16), DP, split_axis=0, concat_axis=0, tiled=True
        ),
        SEQ,
        split_axis=1,
        concat_axis=1,
        tiled=True,
    ).astype(outgoing.dtype)
    hash_table_grad = (
        jnp.zeros((rows_dev, model_width), jnp.float32)
        .at[safe_rows.reshape(-1)]
        .add(jnp.where(present[..., None], arrived, 0.0).reshape(-1, model_width))
    )
    summed_all = (
        lax.psum_scatter(grad_norm_attn, ALL, scatter_dimension=0, tiled=True),
        lax.psum_scatter(grad_norm_ffn, ALL, scatter_dimension=0, tiled=True),
        lax.psum_scatter(grad_norm_cross, ALL, scatter_dimension=0, tiled=True),
        lax.psum_scatter(grad_w_query, ALL, scatter_dimension=0, tiled=True),
        lax.psum_scatter(grad_w_key, ALL, scatter_dimension=0, tiled=True),
        lax.psum_scatter(grad_w_value, ALL, scatter_dimension=0, tiled=True),
        lax.psum_scatter(grad_w_out, ALL, scatter_dimension=0, tiled=True),
        lax.psum_scatter(grad_w_gate, ALL, scatter_dimension=0, tiled=True),
        lax.psum_scatter(grad_w_up, ALL, scatter_dimension=0, tiled=True),
        lax.psum_scatter(grad_w_down, ALL, scatter_dimension=0, tiled=True),
        lax.psum_scatter(grad_c_query, ALL, scatter_dimension=0, tiled=True),
        lax.psum_scatter(grad_c_key, ALL, scatter_dimension=0, tiled=True),
        lax.psum_scatter(grad_c_value, ALL, scatter_dimension=0, tiled=True),
        lax.psum_scatter(grad_c_out, ALL, scatter_dimension=0, tiled=True),
        lax.psum_scatter(grad_byte_table, ALL, scatter_dimension=0, tiled=True),
    )
    (
        out_norm_attn,
        out_norm_ffn,
        out_norm_cross,
        out_query,
        out_key,
        out_value,
        out_proj,
        out_gate,
        out_up,
        out_down,
        out_cquery,
        out_ckey,
        out_cvalue,
        out_cout,
        out_bytes,
    ) = summed_all
    return (
        byte_states,
        patch_states,
        embed_grad,
        out_bytes,
        hash_table_grad,
        row_counts,
        out_norm_attn,
        out_norm_ffn,
        out_norm_cross,
        out_query,
        out_key,
        out_value,
        out_proj,
        out_gate,
        out_up,
        out_down,
        out_cquery,
        out_ckey,
        out_cvalue,
        out_cout,
    )


def fast_body(
    byte_ids,
    hash_ids,
    lengths,
    byte_table,
    hash_table,
    norm_attn,
    norm_ffn,
    norm_cross,
    w_query,
    w_key,
    w_value,
    w_out,
    w_gate,
    w_up,
    w_down,
    c_query,
    c_key,
    c_value,
    c_out,
    cot_bytes,
    cot_patches,
):
    dp_count = lax.axis_size(DP)
    rs_count = lax.axis_size(SEQ)
    all_count = dp_count * rs_count
    rank_table = lax.axis_index(ALL)
    rows_dev, model_width = hash_table.shape
    patch_len = lengths[0]
    patch_end = jnp.cumsum(patch_len)[:, None]
    patch_start = patch_end - patch_len[:, None]
    gains = jnp.concatenate(
        [norm_attn[None], norm_ffn[None], norm_cross[None], jnp.zeros((5, model_width), jnp.float32)]
    )
    full, embedded, entries, kept = fetch(
        hash_ids,
        hash_table,
        (
            w_query,
            w_key,
            w_value,
            w_out,
            w_gate,
            w_up,
            w_down,
            c_query,
            c_key,
            c_value,
            c_out,
        ),
        (byte_ids[:, None], byte_table, gains, patch_start, patch_end),
        WEIGHT_STEPS,
        dp_count,
    )
    lefts = [
        by_rows(a, dp_count)
        for a in (kept.x_ffn, kept.hidden, kept.pooled, kept.x_cross, kept.p_attended)
    ]
    sums, results = back_sums(
        lefts,
        Streamed(
            kept.gate_pre,
            kept.up_pre,
            kept.h_out,
            kept.h_mid,
            embedded,
            kept.key_values,
            *full,
            cot_patches,
        ),
        (
            cot_bytes,
            kept.p_query,
            kept.p_key,
            kept.p_value,
            kept.cross_lse,
            gains,
            patch_start,
            patch_end,
            kept.queries,
            kept.lse,
        ),
        dp_count,
    )
    first_sums = sums
    gain_rows, grad_branch_a, grad_queries, grad_keys, grad_values, embed_grad = results
    one_hot = byte_ids[:, None] == jnp.arange(BYTE_VALUES, dtype=jnp.int32)[None, :]
    lefts = [
        by_rows(a, dp_count) for a in (kept.x_attn, kept.attended, one_hot.astype(jnp.bfloat16))
    ]
    rights = [grad_queries, grad_keys, grad_values, grad_branch_a, embed_grad]
    sums, gain_sums, *table_parts = last_sums(
        [(1, 3), (0, 0), (0, 1), (0, 2), (2, 4)],
        lefts,
        rights,
        embed_grad,
        gain_rows,
        entries,
        rows_dev,
        dp_count,
    )
    wholes = (*sums, *first_sums[:5])
    cuts = [a.shape[0] for a in wholes]
    cuts[4] = BYTE_VALUES // all_count
    cuts[9] = kept.hidden.shape[1] // all_count
    (
        hash_table_grad,
        counts,
        out_proj,
        out_query,
        out_key,
        out_value,
        out_bytes,
        out_cout,
        out_ckey,
        out_cvalue,
        out_cquery,
        out_down,
        out_gate,
        out_up,
    ) = finish(*table_parts, wholes, tuple(cuts), first_sums[5:])
    row_counts = counts[:, 0]
    own_gains = lax.dynamic_slice_in_dim(
        gain_sums, rank_table * (model_width // all_count), model_width // all_count, 1
    )
    return (
        kept.byte_states,
        kept.patch_states,
        embed_grad,
        out_bytes,
        hash_table_grad,
        row_counts,
        own_gains[0],
        own_gains[1],
        own_gains[2],
        out_query,
        out_key,
        out_value,
        out_proj,
        out_gate,
        out_up,
        out_down,
        out_cquery,
        out_ckey,
        out_cvalue,
        out_cout,
    )


def solution(mesh):
    fits = mesh.shape[REP] == 2 and mesh.shape[SUB] == 4 and mesh.shape[DP] <= 4
    return jax.shard_map(
        fast_body if fits else body,
        mesh=mesh,
        in_specs=(
            P(ALL),
            P(ALL, None),
            P(ALL, None),
            P(),
            P(ALL, None),
            P(),
            P(),
            P(),
            P(DP, None),
            P(DP, None),
            P(DP, None),
            P(DP, None),
            P(DP, None),
            P(DP, None),
            P(DP, None),
            P(DP, None),
            P(DP, None),
            P(DP, None),
            P(DP, None),
            P(ALL, None),
            P(ALL, None),
        ),
        out_specs=(
            P(ALL, None),
            P(ALL, None),
            P(ALL, None),
            P(ALL, None),
            P(ALL, None),
            P(ALL),
            P(ALL),
            P(ALL),
            P(ALL),
            P(ALL, None),
            P(ALL, None),
            P(ALL, None),
            P(ALL, None),
            P(ALL, None),
            P(ALL, None),
            P(ALL, None),
            P(ALL, None),
            P(ALL, None),
            P(ALL, None),
            P(ALL, None),
        ),
        check_vma=False,
    )
```
